32 devices in a mesh: segment: 2 (over x), dp: 4 (over z), rep: 4 (over y, core).
Axes of the slice: x: 2, y: 2, z: 4, core: 2. Of those that a mesh axis runs over, the one named last changes fastest.
Arguments:
- block_input: bfloat16 [16384, 512], P(('dp', 'rep')), may hold values from -6 to 6
- cotangent: bfloat16 [16384, 512], P(('dp', 'rep')), may hold values from -6 to 6
- window_group: int32 [16, 2], P(('dp', 'rep')), may hold values from 0 to 1, as said below
- w_qkv: bfloat16 [2, 512, 1536], P('segment'), may hold values from -0.25 to 0.25
- w_out: bfloat16 [2, 512, 512], P('segment'), may hold values from -1 to 1
- w_up: bfloat16 [2, 512, 2048], P('segment'), may hold values from -0.25 to 0.25
- w_down: bfloat16 [2, 2048, 512], P('segment'), may hold values from -0.125 to 0.125
- up_bias: bfloat16 [2, 2048], P('segment'), may hold values from -3 to 3
- norm_gains: bfloat16 [2, 2, 512], P('segment'), may hold values from 0.25 to 1.75
- biases: bfloat16 [2, 4, 512], P('segment'), may hold values from -2 to 2
Outputs:
- ends: float32 [2, 16384, 512], P('segment', ('dp', 'rep'))
- grad_qkv: float32 [2, 512, 1536], P('segment', 'dp')
- grad_out: float32 [2, 512, 512], P('segment', 'dp')
- grad_up: float32 [2, 512, 2048], P('segment', 'dp')
- grad_down: float32 [2, 2048, 512], P('segment', 'dp')
- grad_up_bias: float32 [2, 2048], P('segment', 'dp')
- grad_norm_gains: float32 [2, 2, 512], P('segment', None, 'dp')
- grad_biases: float32 [2, 4, 512], P('segment', None, 'dp')
The draws below stay inside these ranges and needn't reach their ends.
Inputs may be any that keep to these rules, and one draw needn't show every extreme that they name: `window_group`: in every row, half of the 2 entries are 1 and half are 0.
All inputs are finite; a program needn't handle non-finite values.
Results may differ from the reference program's by a relative error of at most 0.019.
Values may be sent and summed in bfloat16 or wider, within the bound.
A program may use at most 128 MiB of HBM per device.

```python
import math
import jax
import jax.numpy as jnp
from jax import lax

D = 512
HEADS = 8
HEAD_DIM = 64
FF = 2048
MB_TOK = 512
MB_DEV = 2
WINDOW = 256
LAYERS = 2
GROUPS = 16
TOKENS = 16384


def draw_window_group(key, part):
    key = jax.random.fold_in(key, 7)
    pattern = (jnp.arange(MB_DEV) % 2).astype(jnp.int32)
    row_keys = jax.random.split(key, GROUPS)
    return jax.vmap(lambda row_key: jax.random.permutation(row_key, pattern))(row_keys)


def spiked(values, own_key, source, target, blocks, factor):
    owner, partner = [(jnp.arange(values.shape[dim]) // (values.shape[dim] // blocks)).reshape([-1 if axis == dim else 1 for axis in range(values.ndim)]) for dim in (source, target)]
    chosen = jax.random.permutation(own_key, blocks)[partner]
    strong = (owner == chosen) | (owner == (partner + blocks // 2) % blocks)
    return jnp.where(strong, factor * values, values)


def level_of(key, extent, cuts, smallest, largest):
    loudness = 1.0
    for axis_at, parts in cuts:
        steps = jax.random.uniform(jax.random.fold_in(jax.random.fold_in(key, 6), axis_at), (parts,), jnp.float32, smallest / len(cuts), largest / len(cuts))
        loudness = loudness * jnp.repeat(jnp.exp(steps), extent[axis_at] // parts).reshape((-1,) + (1,) * (len(extent) - 1 - axis_at))
    return loudness


def bell_draw(own_key, extent, scale, most, shards=(), held_as=jnp.bfloat16):
    entries = scale * jax.random.normal(own_key, extent, jnp.float32)
    if shards:
        entries = entries * level_of(own_key, extent, shards, -0.22, 0.18)
    return jnp.clip(entries, -most, most).astype(held_as)


def bell_draw_with(own_key, dims, spread, most, pieces, heavy, dtype=jnp.bfloat16):
    result = spread * jax.random.normal(own_key, dims, jnp.float32)
    if pieces:
        result = result * level_of(own_key, dims, pieces, -0.22, 0.18)
    return jnp.clip(spiked(result, jax.random.fold_in(own_key, 3), *heavy), -most, most).astype(dtype)


def setup_inputs(seed: int = 0) -> dict:
    seeds = jax.random.split(jax.random.key(seed), 11)
    block_input = bell_draw_with(seeds[0], (TOKENS, D), 1.0, 6.0, ((0, 16),), (0, 1, 16, 2.0))
    cotangent = bell_draw(seeds[1], (TOKENS, D), 1.0, 6.0, ((0, 16),))
    window_group = draw_window_group(jax.random.fold_in(seeds[10], 71), 0)
    w_qkv = bell_draw(seeds[3], (LAYERS, D, 3 * D), D ** -0.5, 0.25, ((0, 2),))
    w_out = bell_draw(seeds[4], (LAYERS, D, D), (D // 16) ** -0.5, 1.0, ((0, 2),))
    w_up = bell_draw(seeds[5], (LAYERS, D, FF), D ** -0.5, 0.25, ((0, 2),))
    w_down = bell_draw(seeds[6], (LAYERS, FF, D), FF ** -0.5, 0.125, ((0, 2),))
    up_bias = bell_draw(seeds[7], (LAYERS, FF), 0.5, 3.0, ((0, 2),))
    norm_gains = jnp.clip(1.0 + 0.15 * jax.random.normal(seeds[8], (LAYERS, 2, D), jnp.float32), 0.25, 1.75).astype(jnp.bfloat16)
    biases = bell_draw(seeds[9], (LAYERS, 4, D), 0.3, 2.0, ((0, 2),))
    return {"block_input": block_input, "cotangent": cotangent, "window_group": window_group, "w_qkv": w_qkv, "w_out": w_out, "w_up": w_up, "w_down": w_down, "up_bias": up_bias, "norm_gains": norm_gains, "biases": biases}


@jax.custom_vjp
def low(v):
    return lax.optimization_barrier(v.astype(jnp.bfloat16)).astype(jnp.float32)

@jax.custom_vjp
def low_back(v):
    return v

def low_keep(v):
    return (low(v), None)

def low_pass(kept, grad):
    return (grad,)

def back_keep(v):
    return (v, None)

def back_low(kept, grad):
    return (low(grad),)
low.defvjp(low_keep, low_pass)
low_back.defvjp(back_keep, back_low)
highest = lax.Precision.HIGHEST

def window_mask(window_flag):
    position = lax.broadcasted_iota(jnp.int32, (MB_TOK, MB_TOK), 0)
    earlier = lax.broadcasted_iota(jnp.int32, (MB_TOK, MB_TOK), 1)
    window_width = jnp.where(window_flag == 1, MB_TOK, WINDOW).astype(jnp.int32)
    return (earlier <= position) & (position // window_width == earlier // window_width)

def norm_rows(values, norm_gain, norm_shift):
    centred = values - lax.optimization_barrier(jnp.mean(values, axis=-1, keepdims=True))
    variance = lax.optimization_barrier(jnp.mean(centred * centred, axis=-1, keepdims=True))
    return centred * lax.rsqrt(variance + 1e-05) * norm_gain + norm_shift

def attend(qkv_rows, allowed):
    sections = qkv_rows.reshape(MB_TOK, 3, HEADS, HEAD_DIM)
    scores = jnp.einsum('qhe,khe->hqk', sections[:, 0], sections[:, 1], precision=highest) * (1.0 / math.sqrt(HEAD_DIM))
    scores = jnp.where(allowed, low_back(scores), -1e+30)
    row_max = lax.optimization_barrier(jnp.max(scores, axis=-1, keepdims=True))
    raised = jnp.exp(scores - row_max)
    shares = raised / lax.optimization_barrier(jnp.sum(raised, axis=-1, keepdims=True))
    mixture = jnp.einsum('hqk,khe->qhe', low(shares), sections[:, 2], precision=highest)
    return mixture.reshape(MB_TOK, HEADS * HEAD_DIM)

def layer(inputs, w_qkv, w_out, w_up, w_down, up_bias, norm_gains, biases, allowed):
    qkv = low_back(low(jnp.dot(inputs, w_qkv, precision=highest)))
    mixture = low_back(low(jax.checkpoint(attend)(qkv, allowed)))
    branch = low_back(jnp.dot(mixture, w_out, precision=highest)) + biases[0]
    hidden = norm_rows(inputs + branch, norm_gains[0], biases[1])
    pre_act = low_back(jnp.dot(low(hidden), w_up, precision=highest)) + up_bias
    active = low(jax.nn.gelu(pre_act, approximate=False))
    branch_two = low_back(jnp.dot(active, w_down, precision=highest)) + biases[2]
    return norm_rows(hidden + branch_two, norm_gains[1], biases[3])

def forward(inputs, w_qkv, w_out, w_up, w_down, up_bias, norm_gains, biases, allowed):
    current = inputs
    for layer_index in range(LAYERS):
        if layer_index > 0:
            current = low_back(low(current))
        current = layer(current, w_qkv[layer_index], w_out[layer_index], w_up[layer_index], w_down[layer_index], up_bias[layer_index], norm_gains[layer_index], biases[layer_index], allowed)
    return current

def reference(block_input, cotangent, window_group, w_qkv, w_out, w_up, w_down, up_bias, norm_gains, biases):
    float_weights = tuple((array.astype(jnp.float32) for array in (w_qkv, w_out, w_up, w_down, up_bias, norm_gains, biases)))
    batch_count = TOKENS // MB_TOK
    inputs = block_input.astype(jnp.float32).reshape(batch_count, MB_TOK, D)
    cotangents = cotangent.astype(jnp.float32).reshape(batch_count, MB_TOK, D)
    window_flags = window_group.reshape(batch_count).astype(jnp.int32)

    def accumulate(running, record):
        rows_in, rows_cot, window_flag = record
        allowed = window_mask(window_flag)

        def evaluate(values, *weights):
            return forward(values, *weights, allowed)
        output, pullback = jax.vjp(evaluate, rows_in, *float_weights)
        gradients = pullback(rows_cot)
        updated = tuple((total_part + grad_part for total_part, grad_part in zip(running, gradients[1:])))
        return (updated, (output, gradients[0]))
    starting = tuple((jnp.zeros(array.shape, jnp.float32) for array in float_weights))
    running, (outputs, input_grads) = lax.scan(accumulate, starting, (inputs, cotangents, window_flags))
    ends = jnp.stack([input_grads.reshape(TOKENS, D), outputs.reshape(TOKENS, D)])
    return (ends, running[0], running[1], running[2], running[3], running[4], running[5], running[6])
```

```python
import functools
import math

import jax
import jax.numpy as jnp
from jax import lax
from jax.experimental import pallas as pl
from jax.experimental.pallas import tpu as pltpu
from jax.sharding import PartitionSpec as P

MESH = pl.DeviceIdType.MESH
F32 = jnp.float32
BF16 = jnp.bfloat16
HEADS = 8
LANES = 128
PIECES = 4
EPS = 1e-05
GAIN_ONE, GAIN_TWO, BIAS_OUT, BIAS_ONE, BIAS_DOWN, BIAS_TWO, BIAS_UP = range(7)
STATS = 10


def dot_plain(left, right):
    return lax.dot_general(left, right, (((1,), (0,)), ((), ())), preferred_element_type=F32)


def dot_turned(left, right):
    return lax.dot_general(left, right, (((1,), (1,)), ((), ())), preferred_element_type=F32)


def row_mean(values):
    return jnp.sum(values, axis=0, keepdims=True) * (1.0 / values.shape[0])


def fold(values):
    total = values[:, :LANES]
    for start in range(LANES, values.shape[1], LANES):
        total = total + values[:, start : start + LANES]
    return total


def pair_blocks(values):
    half = values.shape[0] // 2
    blank = jnp.zeros((half, values.shape[1]), values.dtype)
    first = jnp.concatenate([values[:half], blank], axis=0)
    second = jnp.concatenate([blank, values[half:]], axis=0)
    return jnp.concatenate([first, second], axis=1)


def layer_kernel(
    dp_count,
    flag_ref,
    x_hbm,
    ct_hbm,
    w_qkv_hbm,
    w_out_hbm,
    w_up_hbm,
    w_down_hbm,
    up_bias_ref,
    gains_ref,
    biases_ref,
    ends_hbm,
    fin_hbm,
    small_hbm,
    w_qkv,
    w_out,
    w_up,
    w_down,
    turned,
    down_turned,
    rows_in,
    x_t,
    qkv,
    keys_rm,
    values_rm,
    share,
    share_off,
    mixture,
    norm_one,
    norm_two,
    inverses,
    hidden_low,
    slope,
    active,
    down_grad,
    branch_grad,
    grad_mix,
    outgoing,
    incoming_grad,
    columns,
    sums,
    key_sums,
    wide_a,
    wide_b,
    ends_v,
    core_in,
    side_in,
    dp_in,
    fin,
    small,
    small_dp,
    small_rep,
    small_out,
    load_sem,
    seg_send,
    seg_recv,
    ends_sem,
    core_send,
    core_recv,
    side_send,
    side_recv,
    dp_send,
    dp_recv,
    join_send,
    join_recv,
    last_send,
    last_recv,
    sdp_send,
    sdp_recv,
    srep_send,
    srep_recv,
    fin_sem,
):
    width = w_out.shape[0]
    piece = x_t.shape[1] // PIECES
    pairs = qkv.shape[1]
    share_rows = width // dp_count
    segment = lax.axis_index("segment")
    dp = lax.axis_index("dp")
    rep = lax.axis_index("rep")
    core = lax.rem(rep, 2)
    side = lax.div(rep, 2)
    other_core = side * 2 + (1 - core)
    other_side = (1 - side) * 2 + core

    loads = [
        (w_qkv_hbm.at[0], w_qkv),
        (w_out_hbm.at[0], w_out),
        (w_up_hbm.at[0], w_up),
    ]
    for block in range(4):
        loads.append((w_down_hbm.at[0, pl.ds(block * width, width), :], w_down.at[block]))
    load_copies = [
        pltpu.make_async_copy(source, target, load_sem.at[index + 1])
        for index, (source, target) in enumerate(loads)
    ]
    first_rows = pltpu.make_async_copy(x_hbm, rows_in, load_sem.at[0])
    last_rows = pltpu.make_async_copy(ct_hbm, rows_in, load_sem.at[0])

    @pl.when(segment == 0)
    def _():
        first_rows.start()

    @pl.when(segment == 1)
    def _():
        last_rows.start()

    for copy in load_copies:
        copy.start()

    barrier = pltpu.get_barrier_semaphore()
    pl.semaphore_signal(
        barrier, inc=1, device_id={"segment": 1 - segment}, device_id_type=MESH
    )
    for step in range(1, 4):
        pl.semaphore_signal(
            barrier, inc=1, device_id={"rep": lax.rem(rep + step, 4)}, device_id_type=MESH
        )
    for step in range(1, dp_count):
        pl.semaphore_signal(
            barrier, inc=1, device_id={"dp": lax.rem(dp + step, dp_count)}, device_id_type=MESH
        )

    params = [gains_ref[0].astype(F32), biases_ref[0].astype(F32)]
    for block in range(4):
        params.append(up_bias_ref[:, block * width : (block + 1) * width].astype(F32))
    params.append(jnp.zeros((16 - STATS, width), F32))
    upright = jnp.concatenate(params, axis=0).T
    for index in range(STATS):
        columns[index] = jnp.broadcast_to(upright[:, index : index + 1], (width, LANES)).astype(BF16)
    for index in range(STATS):
        sums[index] = jnp.zeros((width, LANES), F32)
    key_sums[0] = jnp.zeros(key_sums.shape[1:], F32)

    def column(index):
        part = columns[index].astype(F32)
        return jnp.concatenate([part] * (piece // LANES), axis=1)

    def gather_sum(index, values):
        sums[index] = sums[index] + fold(values)

    for copy in load_copies:
        copy.wait()
    first_rows.wait()

    for block in range(3):
        turned[block] = w_qkv[:, block * width : (block + 1) * width].T
    turned[3] = w_out[...].T
    for block in range(4):
        turned[4 + block] = w_up[:, block * width : (block + 1) * width].T
    for block in range(4):
        down_turned[:, block * width : (block + 1) * width] = w_down[block].T

    pl.semaphore_wait(barrier, 4 + dp_count - 1)

    flag = flag_ref[0, 0].astype(F32)

    def lanes_of(index):
        return pl.ds(pl.multiple_of(index * piece, piece), piece)

    def forward_copy(index):
        return pltpu.make_async_remote_copy(
            src_ref=outgoing.at[index],
            dst_ref=x_t.at[:, lanes_of(index)],
            send_sem=seg_send.at[index],
            recv_sem=seg_recv.at[index],
            device_id={"segment": 1 - segment},
            device_id_type=MESH,
        )

    def backward_copy(index):
        return pltpu.make_async_remote_copy(
            src_ref=outgoing.at[index],
            dst_ref=incoming_grad.at[index],
            send_sem=seg_send.at[index],
            recv_sem=seg_recv.at[index],
            device_id={"segment": 1 - segment},
            device_id_type=MESH,
        )

    def ends_copy(index):
        return pltpu.make_async_copy(ends_v.at[index], ends_hbm.at[index], ends_sem.at[index])

    def own_rows(index):
        half = lax.rem(index, 2)
        whole = jnp.where(index < 2, 1.0, 0.0).astype(F32)
        weight = whole * flag + (1.0 - whole) * (1.0 - flag)
        picked = rows_in[half].astype(F32) * weight + rows_in[2 + half].astype(F32) * (1.0 - weight)
        return picked.T

    def attend(index, has_off):
        lanes = lanes_of(index)

        def one_pair(pair, carry):
            queries = pair_blocks(qkv[0, pair, :, lanes])
            scores = dot_plain(keys_rm[index, pair], queries)
            key_at = lax.broadcasted_iota(jnp.int32, (piece, piece), 0)
            query_at = lax.broadcasted_iota(jnp.int32, (piece, piece), 1)
            allowed = key_at <= query_at
            if has_off:
                scores_off = dot_plain(keys_rm[0, pair], queries)
            half = queries.shape[0] // 2
            for head in range(2):
                span = slice(head * piece, (head + 1) * piece)
                rows = slice(head * half, (head + 1) * half)
                own = jnp.where(allowed, scores[:, span], -1e30)
                top = jnp.max(own, axis=0, keepdims=True)
                if has_off:
                    off = scores_off[:, span]
                    top = jnp.maximum(top, jnp.max(off, axis=0, keepdims=True))
                raised = jnp.exp(own - top)
                total = jnp.sum(raised, axis=0, keepdims=True)
                if has_off:
                    raised_off = jnp.exp(off - top)
                    total = total + jnp.sum(raised_off, axis=0, keepdims=True)
                scale = 1.0 / total
                low = (raised * scale).astype(BF16)
                share[index, pair, head] = low
                mixed = dot_plain(qkv[2, pair, rows, lanes], low)
                if has_off:
                    low_off = (raised_off * scale).astype(BF16)
                    share_off[pair, head] = low_off
                    mixed = mixed + dot_plain(qkv[2, pair, rows, :piece], low_off)
                mixture[pair, rows, lanes] = mixed.astype(BF16)
            return carry

        lax.fori_loop(0, pairs, one_pair, 0)

    def norm(values, index, which, normed_ref):
        lanes = lanes_of(index)
        centred = values - row_mean(values)
        inverse = lax.rsqrt(row_mean(centred * centred) + EPS)
        normed = centred * inverse
        normed_ref[:, lanes] = normed
        inverses[index, which] = inverse
        return normed

    def forward(index):
        lanes = lanes_of(index)

        @pl.when(segment == 0)
        def _():
            x_t[:, lanes] = own_rows(index).astype(BF16)

        @pl.when(segment == 1)
        def _():
            forward_copy(index).wait_recv()

        inputs = x_t[:, lanes]
        queries = dot_plain(turned[0], inputs) * (1.0 / math.sqrt(width // HEADS))
        qkv[0, :, :, lanes] = queries.astype(BF16).reshape(pairs, LANES, piece)
        keys = dot_plain(turned[1], inputs)
        qkv[1, :, :, lanes] = keys.astype(BF16).reshape(pairs, LANES, piece)
        values = dot_plain(turned[2], inputs)
        qkv[2, :, :, lanes] = values.astype(BF16).reshape(pairs, LANES, piece)
        for pair in range(pairs):
            rows = slice(pair * LANES, (pair + 1) * LANES)
            keys_rm[index, pair] = keys[rows].T.astype(BF16)
            values_rm[index, pair] = values[rows].T.astype(BF16)

        @pl.when(index == 1)
        def _():
            attend(index, True)

        @pl.when(index != 1)
        def _():
            attend(index, False)

        branch = dot_plain(turned[3], mixture[:, :, lanes].reshape(width, piece))
        sum_one = x_t[:, lanes].astype(F32) + (branch + column(BIAS_OUT))
        normed = norm(sum_one, index, 0, norm_one)
        hidden = normed * column(GAIN_ONE) + column(BIAS_ONE)
        wide_a[...] = hidden
        hidden_low[:, lanes] = hidden.astype(BF16)

        def up_block(block, carry):
            pre = dot_plain(turned[4 + block], hidden_low[:, lanes]) + column(BIAS_UP + block)
            level = (lax.erf(pre * (1.0 / math.sqrt(2.0))) + 1.0) * 0.5
            active[block, :, lanes] = (pre * level).astype(BF16)
            bell = jnp.exp(-0.5 * pre * pre) * (1.0 / math.sqrt(2.0 * math.pi))
            slope[block, :, lanes] = (level + pre * bell).astype(BF16)
            return carry

        lax.fori_loop(0, 4, up_block, 0)
        branch_two = dot_plain(down_turned[...], active[:, :, lanes].reshape(4 * width, piece))
        sum_two = wide_a[...] + (branch_two + column(BIAS_DOWN))
        normed_two = norm(sum_two, index, 1, norm_two)
        output = normed_two * column(GAIN_TWO) + column(BIAS_TWO)

        @pl.when(segment == 0)
        def _():
            outgoing[index] = output.astype(BF16)
            forward_copy(index).start()

        @pl.when(segment == 1)
        def _():
            ends_v[index] = output.T
            ends_copy(index).start()

    def norm_back(grad, index, which, normed_ref, gain):
        lanes = lanes_of(index)
        normed = normed_ref[:, lanes]
        scaled = grad * column(gain)
        inner = row_mean(scaled * normed)
        return (scaled - row_mean(scaled) - normed * inner) * inverses[index, which]

    def attend_back(index, has_off):
        lanes = lanes_of(index)
        slot = jnp.where(index == 0, 1, 0)
        score_scale = 1.0 / math.sqrt(width // HEADS)

        def one_pair(pair, carry):
            grads = grad_mix[pair]
            blocks = pair_blocks(grads)
            back = dot_plain(values_rm[index, pair], blocks)
            if has_off:
                back_off = dot_plain(values_rm[0, pair], blocks)
            half = grads.shape[0] // 2
            for head in range(2):
                span = slice(head * piece, (head + 1) * piece)
                rows = slice(head * half, (head + 1) * half)
                low = share[index, pair, head]
                wide = low.astype(F32)
                product = wide * back[:, span]
                inner = jnp.sum(product, axis=0, keepdims=True)
                if has_off:
                    low_off = share_off[pair, head]
                    wide_off = low_off.astype(F32)
                    product_off = wide_off * back_off[:, span]
                    inner = inner + jnp.sum(product_off, axis=0, keepdims=True)
                grad_scores = (product - wide * inner).astype(BF16)
                queries = qkv[0, pair, rows, lanes]
                grad_query = dot_plain(qkv[1, pair, rows, lanes], grad_scores)
                grad_key = dot_turned(queries, grad_scores) + key_sums[slot, 0, pair, rows]
                grad_value = dot_turned(grads[rows], low) + key_sums[slot, 1, pair, rows]
                if has_off:
                    grad_off = (product_off - wide_off * inner).astype(BF16)
                    grad_query = grad_query + dot_plain(qkv[1, pair, rows, :piece], grad_off)
                    key_sums[1, 0, pair, rows] = dot_turned(queries, grad_off)
                    key_sums[1, 1, pair, rows] = dot_turned(grads[rows], low_off)
                qkv[0, pair, rows, lanes] = (grad_query * score_scale).astype(BF16)
                qkv[1, pair, rows, lanes] = grad_key.astype(BF16)
                qkv[2, pair, rows, lanes] = grad_value.astype(BF16)
            return carry

        lax.fori_loop(0, pairs, one_pair, 0)

    def backward(index):
        lanes = lanes_of(index)

        @pl.when(segment == 1)
        def _():
            incoming_grad[index] = own_rows(index).astype(BF16)

        @pl.when(segment == 0)
        def _():
            backward_copy(index).wait_recv()

        grad = incoming_grad[index].astype(F32)
        gather_sum(GAIN_TWO, grad * norm_two[:, lanes])
        gather_sum(BIAS_TWO, grad)
        grad_two = norm_back(grad, index, 1, norm_two, GAIN_TWO)
        gather_sum(BIAS_DOWN, grad_two)
        wide_a[...] = grad_two
        down_grad[:, lanes] = grad_two.astype(BF16)

        def down_block(block, carry):
            back = dot_plain(w_down[block], down_grad[:, lanes])
            grad_pre = back * slope[block, :, lanes].astype(F32)
            gather_sum(BIAS_UP + block, grad_pre)
            slope[block, :, lanes] = grad_pre.astype(BF16)
            return carry

        lax.fori_loop(0, 4, down_block, 0)
        grad_hidden = wide_a[...] + dot_plain(
            w_up[...], slope[:, :, lanes].reshape(4 * width, piece)
        )
        gather_sum(GAIN_ONE, grad_hidden * norm_one[:, lanes])
        gather_sum(BIAS_ONE, grad_hidden)
        grad_one = norm_back(grad_hidden, index, 0, norm_one, GAIN_ONE)
        gather_sum(BIAS_OUT, grad_one)
        wide_b[...] = grad_one
        branch_grad[:, lanes] = grad_one.astype(BF16)
        grad_mix[...] = (
            dot_plain(w_out[...], branch_grad[:, lanes]).astype(BF16).reshape(pairs, LANES, piece)
        )

        @pl.when(index == 1)
        def _():
            attend_back(index, True)

        @pl.when(index != 1)
        def _():
            attend_back(index, False)

        grad_input = wide_b[...] + dot_plain(
            w_qkv[...], qkv[:, :, :, lanes].reshape(3 * width, piece)
        )

        @pl.when(segment == 1)
        def _():
            outgoing[index] = grad_input.astype(BF16)
            backward_copy(index).start()

        @pl.when(segment == 0)
        def _():
            ends_v[index] = grad_input.T
            ends_copy(index).start()

    def one_step(step, carry):
        first_index = jnp.where(step < 4, step, jnp.where(step < 6, 5 - step, step - 4))
        last_index = jnp.where(step < 2, step, jnp.where(step < 4, 3 - step, lax.div(step, 2)))
        first_is = jnp.where(step < 4, 1, 0)
        last_is = jnp.where(step < 2, 1, jnp.where(step < 4, 0, 1 - lax.rem(step, 2)))
        index = jnp.where(segment == 0, first_index, last_index)
        is_forward = jnp.where(segment == 0, first_is, last_is)

        @pl.when(is_forward == 1)
        def _():
            forward(index)

        @pl.when(is_forward == 0)
        def _():
            backward(index)

        return carry

    lax.fori_loop(0, 2 * PIECES, one_step, 0)

    def held(group):
        return (w_down, 0) if group == 0 else (turned, 4 if group == 1 else 0)

    def core_copy(group):
        buffer, base = held(group)
        return pltpu.make_async_remote_copy(
            src_ref=buffer.at[pl.ds(base + 2 * (1 - core), 2)],
            dst_ref=core_in.at[group],
            send_sem=core_send.at[group],
            recv_sem=core_recv.at[group],
            device_id={"rep": other_core},
            device_id_type=MESH,
        )

    def side_copy(group):
        buffer, base = held(group)
        return pltpu.make_async_remote_copy(
            src_ref=buffer.at[base + 2 * core + (1 - side)],
            dst_ref=side_in.at[group],
            send_sem=side_send.at[group],
            recv_sem=side_recv.at[group],
            device_id={"rep": other_side},
            device_id_type=MESH,
        )

    def dp_copy(group, step):
        buffer, base = held(group)
        target = lax.rem(dp + step, dp_count)
        rows = pl.ds(pl.multiple_of(target * share_rows, share_rows), share_rows)
        return pltpu.make_async_remote_copy(
            src_ref=buffer.at[base + 2 * core + side, rows],
            dst_ref=dp_in.at[group, step - 1],
            send_sem=dp_send.at[group, step - 1],
            recv_sem=dp_recv.at[group, step - 1],
            device_id={"dp": target},
            device_id_type=MESH,
        )

    def join_copy(group):
        return pltpu.make_async_remote_copy(
            src_ref=fin.at[group, 2 * core + side],
            dst_ref=fin.at[group, 2 * core + side],
            send_sem=join_send.at[group],
            recv_sem=join_recv.at[group],
            device_id={"rep": other_side},
            device_id_type=MESH,
        )

    def last_copy(group):
        return pltpu.make_async_remote_copy(
            src_ref=fin.at[group, pl.ds(2 * core, 2)],
            dst_ref=fin.at[group, pl.ds(2 * core, 2)],
            send_sem=last_send.at[group],
            recv_sem=last_recv.at[group],
            device_id={"rep": other_core},
            device_id_type=MESH,
        )

    def down_sums():
        part = 4 * share_rows
        count = width // part

        def one(block, carry):
            result = dot_turned(active[block], down_grad[...]).astype(BF16)
            for each in range(count):
                for position in range(4):
                    start = each * part + position * share_rows
                    target = pl.multiple_of((block * count + each) * share_rows, share_rows)
                    w_down[position, pl.ds(target, share_rows), :] = result[
                        start : start + share_rows
                    ]
            return carry

        lax.fori_loop(0, 4, one, 0)

    def up_sums():
        def one(block, carry):
            turned[4 + block] = dot_turned(hidden_low[...], slope[block]).astype(BF16)
            return carry

        lax.fori_loop(0, 4, one, 0)

    def qkv_sums():
        def one(block, carry):
            turned[block] = dot_turned(
                x_t[...], qkv[block].reshape(width, PIECES * piece)
            ).astype(BF16)
            return carry

        lax.fori_loop(0, 3, one, 0)
        turned[3] = dot_turned(
            mixture[...].reshape(width, PIECES * piece), branch_grad[...]
        ).astype(BF16)

    def after_core(group):
        buffer, base = held(group)
        copy = core_copy(group)
        copy.wait_send()
        copy.wait_recv()
        first = base + 2 * core + (1 - side)
        buffer[first] = (
            buffer[first].astype(F32) + core_in[group, 1 - side].astype(F32)
        ).astype(BF16)
        side_copy(group).start()

    def after_side(group):
        buffer, base = held(group)
        copy = side_copy(group)
        copy.wait_send()
        copy.wait_recv()
        second = base + 2 * core + side
        buffer[second] = (
            buffer[second].astype(F32)
            + core_in[group, side].astype(F32)
            + side_in[group].astype(F32)
        ).astype(BF16)
        for step in range(1, dp_count):
            dp_copy(group, step).start()

    def after_dp(group):
        buffer, base = held(group)
        rows = pl.ds(pl.multiple_of(dp * share_rows, share_rows), share_rows)
        total = buffer[base + 2 * core + side, rows, :].astype(F32)
        for step in range(1, dp_count):
            copy = dp_copy(group, step)
            copy.wait_send()
            copy.wait_recv()
            total = total + dp_in[group, step - 1].astype(F32)
        fin[group, 2 * core + side] = total.astype(BF16)
        join_copy(group).start()

    def after_join(group):
        copy = join_copy(group)
        copy.wait_send()
        copy.wait_recv()
        last_copy(group).start()

    def fin_copy(group):
        return pltpu.make_async_copy(fin.at[group], fin_hbm.at[group], fin_sem.at[group])

    def after_last(group):
        copy = last_copy(group)
        copy.wait_send()
        copy.wait_recv()
        fin_copy(group).start()

    def small_dp_copy(step):
        target = lax.rem(dp + step, dp_count)
        return pltpu.make_async_remote_copy(
            src_ref=small.at[target],
            dst_ref=small_dp.at[step - 1],
            send_sem=sdp_send.at[step - 1],
            recv_sem=sdp_recv.at[step - 1],
            device_id={"dp": target},
            device_id_type=MESH,
        )

    def small_rep_copy(step):
        return pltpu.make_async_remote_copy(
            src_ref=small_rep.at[rep],
            dst_ref=small_rep.at[rep],
            send_sem=srep_send.at[step - 1],
            recv_sem=srep_recv.at[step - 1],
            device_id={"rep": lax.rem(rep + step, 4)},
            device_id_type=MESH,
        )

    down_sums()
    core_copy(0).start()
    up_sums()
    core_copy(1).start()
    after_core(0)
    qkv_sums()
    core_copy(2).start()
    after_core(1)

    rows_of = [jnp.sum(sums[index].T, axis=0, keepdims=True) for index in range(STATS)]
    small[...] = jnp.zeros(small.shape, F32)
    for share_index in range(dp_count):
        for index in range(BIAS_UP):
            start = share_index * share_rows
            small[share_index, index : index + 1, :share_rows] = rows_of[index][
                :, start : start + share_rows
            ]
        for part in range(4):
            start = (share_index * 4 + part) * share_rows
            block, start = start // width, start % width
            small[share_index, BIAS_UP + part : BIAS_UP + part + 1, :share_rows] = rows_of[
                BIAS_UP + block
            ][:, start : start + share_rows]
    for step in range(1, dp_count):
        small_dp_copy(step).start()

    after_core(2)
    after_side(0)
    small_total = small[dp]
    for step in range(1, dp_count):
        copy = small_dp_copy(step)
        copy.wait_send()
        copy.wait_recv()
        small_total = small_total + small_dp[step - 1]
    small_rep[rep] = small_total
    for step in range(1, 4):
        small_rep_copy(step).start()
    after_side(1)
    after_dp(0)
    after_side(2)
    after_join(0)
    after_dp(1)
    after_last(0)
    after_join(1)
    for step in range(1, 4):
        copy = small_rep_copy(step)
        copy.wait_send()
        copy.wait_recv()
    small_out[...] = (small_rep[0] + small_rep[1]) + (small_rep[2] + small_rep[3])
    small_copy = pltpu.make_async_copy(small_out, small_hbm, load_sem.at[0])
    small_copy.start()
    after_last(1)
    after_dp(2)
    after_join(2)
    after_last(2)

    for index in range(PIECES):

        @pl.when(segment == 0)
        def _():
            forward_copy(index).wait_send()

        @pl.when(segment == 1)
        def _():
            backward_copy(index).wait_send()

        ends_copy(index).wait()
    for group in range(3):
        fin_copy(group).wait()
    small_copy.wait()


def finish_kernel(
    flag_ref,
    ends_in,
    fin,
    small,
    ends,
    grad_qkv,
    grad_out,
    grad_up,
    grad_down,
    grad_up_bias,
    grad_gains,
    grad_biases,
    sem,
):
    half = ends_in.shape[0] // 2
    share_rows, width = fin.shape[2:]
    start = pl.multiple_of(half * (1 - flag_ref[0, 0]), half)
    copies = [
        pltpu.make_async_copy(
            ends_in.at[pl.ds(0, half)], ends.at[0, pl.ds(start, half)], sem.at[0]
        ),
        pltpu.make_async_copy(
            ends_in.at[pl.ds(half, half)], ends.at[0, pl.ds(half - start, half)], sem.at[1]
        ),
    ]
    for copy in copies:
        copy.start()
    for position in range(4):
        columns = slice(position * width, (position + 1) * width)
        rows = slice(position * share_rows, (position + 1) * share_rows)
        grad_down[0, rows, :] = fin[0, position].astype(F32)
        grad_up[0, :, columns] = fin[1, position].astype(F32)
        if position < 3:
            grad_qkv[0, :, columns] = fin[2, position].astype(F32)
        else:
            grad_out[0] = fin[2, position].astype(F32)
        grad_up_bias[:, rows] = small[BIAS_UP + position : BIAS_UP + position + 1, :share_rows]
    grad_gains[0] = small[:2, :share_rows]
    grad_biases[0] = small[2:BIAS_UP, :share_rows]
    for copy in copies:
        copy.wait()


def on_device(
    dp_count,
    block_input,
    cotangent,
    window_group,
    w_qkv,
    w_out,
    w_up,
    w_down,
    up_bias,
    norm_gains,
    biases,
):
    rows, width = block_input.shape
    piece = rows // PIECES
    pairs = width // LANES
    share_rows = width // dp_count
    small_width = max(share_rows, LANES)
    any_spec = pl.BlockSpec(memory_space=pl.ANY)
    vmem_spec = pl.BlockSpec(memory_space=pltpu.VMEM)
    smem_spec = pl.BlockSpec(memory_space=pltpu.SMEM)
    dma = pltpu.SemaphoreType.DMA
    vmem = pltpu.VMEM
    ends_in, fin, small = pl.pallas_call(
        functools.partial(layer_kernel, dp_count),
        out_shape=(
            jax.ShapeDtypeStruct((PIECES, piece, width), F32),
            jax.ShapeDtypeStruct((3, 4, share_rows, width), BF16),
            jax.ShapeDtypeStruct((16, small_width), F32),
        ),
        in_specs=[smem_spec] + [any_spec] * 6 + [vmem_spec] * 3,
        out_specs=(any_spec,) * 3,
        scratch_shapes=[
            vmem((width, 3 * width), BF16),
            vmem((width, width), BF16),
            vmem((width, 4 * width), BF16),
            vmem((4, width, width), BF16),
            vmem((8, width, width), BF16),
            vmem((width, 4 * width), BF16),
            vmem((PIECES, piece, width), BF16),
            vmem((width, rows), BF16),
            vmem((3, pairs, LANES, rows), BF16),
            vmem((PIECES, pairs, piece, LANES), BF16),
            vmem((PIECES, pairs, piece, LANES), BF16),
            vmem((PIECES, pairs, 2, piece, piece), BF16),
            vmem((pairs, 2, piece, piece), BF16),
            vmem((pairs, LANES, rows), BF16),
            vmem((width, rows), F32),
            vmem((width, rows), F32),
            vmem((PIECES, 2, 1, piece), F32),
            vmem((width, rows), BF16),
            vmem((4, width, rows), BF16),
            vmem((4, width, rows), BF16),
            vmem((width, rows), BF16),
            vmem((width, rows), BF16),
            vmem((pairs, LANES, piece), BF16),
            vmem((PIECES, width, piece), BF16),
            vmem((PIECES, width, piece), BF16),
            vmem((STATS, width, LANES), BF16),
            vmem((STATS, width, LANES), F32),
            vmem((2, 2, pairs, LANES, piece), F32),
            vmem((width, piece), F32),
            vmem((width, piece), F32),
            vmem((PIECES, piece, width), F32),
            vmem((3, 2, width, width), BF16),
            vmem((3, width, width), BF16),
            vmem((3, dp_count - 1, share_rows, width), BF16),
            vmem((3, 4, share_rows, width), BF16),
            vmem((dp_count, 16, small_width), F32),
            vmem((dp_count - 1, 16, small_width), F32),
            vmem((4, 16, small_width), F32),
            vmem((16, small_width), F32),
            dma((8,)),
            dma((PIECES,)),
            dma((PIECES,)),
            dma((PIECES,)),
            dma((3,)),
            dma((3,)),
            dma((3,)),
            dma((3,)),
            dma((3, dp_count - 1)),
            dma((3, dp_count - 1)),
            dma((3,)),
            dma((3,)),
            dma((3,)),
            dma((3,)),
            dma((dp_count - 1,)),
            dma((dp_count - 1,)),
            dma((3,)),
            dma((3,)),
            dma((3,)),
        ],
        compiler_params=pltpu.CompilerParams(
            collective_id=0, has_side_effects=True, vmem_limit_bytes=63 * 1024 * 1024
        ),
    )(
        window_group,
        block_input.reshape(PIECES, piece, width),
        cotangent.reshape(PIECES, piece, width),
        w_qkv,
        w_out,
        w_up,
        w_down,
        up_bias,
        norm_gains,
        biases,
    )
    return pl.pallas_call(
        finish_kernel,
        out_shape=(
            jax.ShapeDtypeStruct((1, rows, width), F32),
            jax.ShapeDtypeStruct((1, share_rows, 3 * width), F32),
            jax.ShapeDtypeStruct((1, share_rows, width), F32),
            jax.ShapeDtypeStruct((1, share_rows, 4 * width), F32),
            jax.ShapeDtypeStruct((1, 4 * share_rows, width), F32),
            jax.ShapeDtypeStruct((1, 4 * share_rows), F32),
            jax.ShapeDtypeStruct((1, 2, share_rows), F32),
            jax.ShapeDtypeStruct((1, 4, share_rows), F32),
        ),
        in_specs=[smem_spec, any_spec, vmem_spec, vmem_spec],
        out_specs=(any_spec,) + (vmem_spec,) * 7,
        scratch_shapes=[dma((2,))],
        compiler_params=pltpu.CompilerParams(vmem_limit_bytes=32 * 1024 * 1024),
    )(window_group, ends_in.reshape(rows, width), fin, small)


def solution(mesh):
    return jax.shard_map(
        functools.partial(on_device, mesh.shape["dp"]),
        mesh=mesh,
        in_specs=(
            P(("dp", "rep"), None),
            P(("dp", "rep"), None),
            P(("dp", "rep"), None),
            P("segment", None, None),
            P("segment", None, None),
            P("segment", None, None),
            P("segment", None, None),
            P("segment", None),
            P("segment", None, None),
            P("segment", None, None),
        ),
        out_specs=(
            P("segment", ("dp", "rep"), None),
            P("segment", "dp", None),
            P("segment", "dp", None),
            P("segment", "dp", None),
            P("segment", "dp", None),
            P("segment", "dp"),
            P("segment", None, "dp"),
            P("segment", None, "dp"),
        ),
        check_vma=False,
    )
```

```python
import functools
import math

import jax
import jax.numpy as jnp
from jax import lax
from jax.experimental import pallas as pl
from jax.experimental.pallas import tpu as pltpu
from jax.sharding import PartitionSpec as P

MESH = pl.DeviceIdType.MESH
F32 = jnp.float32
BF16 = jnp.bfloat16
HEADS = 8
LANES = 128
PIECES = 4
EPS = 1e-05
GAIN_ONE, GAIN_TWO, BIAS_OUT, BIAS_ONE, BIAS_DOWN, BIAS_TWO, BIAS_UP = range(7)
STATS = 10
CHUNK = 64


def dot_plain(left, right):
    return lax.dot_general(left, right, (((1,), (0,)), ((), ())), preferred_element_type=F32)


def dot_turned(left, right):
    return lax.dot_general(left, right, (((1,), (1,)), ((), ())), preferred_element_type=F32)


def fold(values):
    total = values[:, :LANES]
    for start in range(LANES, values.shape[1], LANES):
        total = total + values[:, start : start + LANES]
    return total


def pair_blocks(values):
    half = values.shape[0] // 2
    blank = jnp.zeros((half, values.shape[1]), values.dtype)
    first = jnp.concatenate([values[:half], blank], axis=0)
    second = jnp.concatenate([blank, values[half:]], axis=0)
    return jnp.concatenate([first, second], axis=1)


def layer_kernel(
    dp_count,
    flag_ref,
    x_hbm,
    ct_hbm,
    w_qkv_hbm,
    w_out_hbm,
    w_up_hbm,
    w_down_hbm,
    up_bias_ref,
    gains_ref,
    biases_ref,
    ends_hbm,
    fin_hbm,
    small_hbm,
    w_qkv,
    w_out,
    w_up,
    w_down,
    turned,
    down_turned,
    rows_in,
    x_t,
    qkv,
    keys_rm,
    values_rm,
    share,
    share_off,
    mixture,
    norm_one,
    norm_two,
    inverses,
    hidden_low,
    slope,
    active,
    down_grad,
    branch_grad,
    grad_mix,
    outgoing,
    incoming_grad,
    columns,
    sums,
    key_sums,
    score_grad,
    wide_a,
    wide_b,
    ends_v,
    core_in,
    side_in,
    dp_in,
    fin,
    small,
    small_dp,
    small_rep,
    small_out,
    load_sem,
    seg_send,
    seg_recv,
    ends_sem,
    core_send,
    core_recv,
    side_send,
    side_recv,
    dp_send,
    dp_recv,
    join_send,
    join_recv,
    last_send,
    last_recv,
    sdp_send,
    sdp_recv,
    srep_send,
    srep_recv,
    fin_sem,
):
    width = w_out.shape[0]
    piece = x_t.shape[1] // PIECES
    pairs = qkv.shape[1]
    share_rows = width // dp_count
    segment = lax.axis_index("segment")
    dp = lax.axis_index("dp")
    rep = lax.axis_index("rep")
    core = lax.rem(rep, 2)
    side = lax.div(rep, 2)
    other_core = side * 2 + (1 - core)
    other_side = (1 - side) * 2 + core

    loads = [
        (w_qkv_hbm.at[0], w_qkv),
        (w_out_hbm.at[0], w_out),
        (w_up_hbm.at[0], w_up),
    ]
    for block in range(4):
        loads.append((w_down_hbm.at[0, pl.ds(block * width, width), :], w_down.at[block]))
    load_copies = [
        pltpu.make_async_copy(source, target, load_sem.at[index + 1])
        for index, (source, target) in enumerate(loads)
    ]
    first_rows = pltpu.make_async_copy(x_hbm, rows_in, load_sem.at[0])
    last_rows = pltpu.make_async_copy(ct_hbm, rows_in, load_sem.at[0])

    @pl.when(segment == 0)
    def _():
        first_rows.start()

    @pl.when(segment == 1)
    def _():
        last_rows.start()

    for copy in load_copies:
        copy.start()

    barrier = pltpu.get_barrier_semaphore()
    pl.semaphore_signal(
        barrier, inc=1, device_id={"segment": 1 - segment}, device_id_type=MESH
    )
    for step in range(1, 4):
        pl.semaphore_signal(
            barrier, inc=1, device_id={"rep": lax.rem(rep + step, 4)}, device_id_type=MESH
        )
    for step in range(1, dp_count):
        pl.semaphore_signal(
            barrier, inc=1, device_id={"dp": lax.rem(dp + step, dp_count)}, device_id_type=MESH
        )

    params = [gains_ref[0].astype(F32), biases_ref[0].astype(F32)]
    for block in range(4):
        params.append(up_bias_ref[:, block * width : (block + 1) * width].astype(F32))
    params.append(jnp.zeros((16 - STATS, width), F32))
    upright = jnp.concatenate(params, axis=0).T
    for index in range(STATS):
        columns[index] = jnp.broadcast_to(upright[:, index : index + 1], (width, LANES)).astype(BF16)
    for index in range(STATS):
        sums[index] = jnp.zeros((width, LANES), F32)
    key_sums[0] = jnp.zeros(key_sums.shape[1:], F32)

    chunks = [slice(start, start + CHUNK) for start in range(0, width, CHUNK)]

    for copy in load_copies:
        copy.wait()
    first_rows.wait()

    for block in range(3):
        turned[block] = w_qkv[:, block * width : (block + 1) * width].T
    turned[3] = w_out[...].T
    for block in range(4):
        turned[4 + block] = w_up[:, block * width : (block + 1) * width].T
    for block in range(4):
        down_turned[:, block * width : (block + 1) * width] = w_down[block].T

    pl.semaphore_wait(barrier, 4 + dp_count - 1)

    flag = flag_ref[0, 0].astype(F32)

    def lanes_of(index):
        return pl.ds(pl.multiple_of(index * piece, piece), piece)

    def forward_copy(index):
        return pltpu.make_async_remote_copy(
            src_ref=outgoing.at[index],
            dst_ref=x_t.at[:, lanes_of(index)],
            send_sem=seg_send.at[index],
            recv_sem=seg_recv.at[index],
            device_id={"segment": 1 - segment},
            device_id_type=MESH,
        )

    def backward_copy(index):
        return pltpu.make_async_remote_copy(
            src_ref=outgoing.at[index],
            dst_ref=incoming_grad.at[index],
            send_sem=seg_send.at[index],
            recv_sem=seg_recv.at[index],
            device_id={"segment": 1 - segment},
            device_id_type=MESH,
        )

    def ends_copy(index):
        return pltpu.make_async_copy(
            ends_v.at[lax.rem(index, 2)], ends_hbm.at[index], ends_sem.at[index]
        )

    def free_ends(index):
        @pl.when(index >= 2)
        def _():
            ends_copy(index - 2).wait()

    def own_rows(index):
        half = lax.rem(index, 2)
        whole = jnp.where(index < 2, 1.0, 0.0).astype(F32)
        weight = whole * flag + (1.0 - whole) * (1.0 - flag)
        picked = rows_in[half].astype(F32) * weight + rows_in[2 + half].astype(F32) * (1.0 - weight)
        return picked.T

    def attend(index, has_off):
        lanes = lanes_of(index)
        half = LANES // 2
        key_at = lax.broadcasted_iota(jnp.int32, (LANES, LANES), 0)
        query_at = lax.broadcasted_iota(jnp.int32, (LANES, LANES), 1)
        allowed = key_at <= query_at
        blank = jnp.zeros((LANES, LANES), BF16)
        for pair in range(pairs):
            queries = pair_blocks(qkv[0, pair, :, lanes])
            scores = dot_plain(keys_rm[index, pair], queries)
            if has_off:
                scores_off = dot_plain(keys_rm[0, pair], queries)
            for head in range(2):
                rows = slice(head * half, (head + 1) * half)
                for part in range(2):
                    start = head * piece + part * LANES
                    span = slice(start, start + LANES)
                    place = slice(part * LANES, (part + 1) * LANES)
                    tiles = [jnp.where(allowed, scores[place, span], -1e30)]
                    if part:
                        tiles.append(scores[:LANES, span])
                    if has_off:
                        tiles.append(scores_off[:LANES, span])
                        tiles.append(scores_off[LANES:, span])
                    top = functools.reduce(jnp.maximum, tiles)
                    top = jnp.max(top, axis=0, keepdims=True)
                    raised = [jnp.exp(tile - top) for tile in tiles]
                    total = functools.reduce(jnp.add, raised)
                    scale = 1.0 / jnp.sum(total, axis=0, keepdims=True)
                    low = [(tile * scale).astype(BF16) for tile in raised]
                    share[index, pair, head, place, place] = low[0]
                    if part:
                        share[index, pair, head, :LANES, place] = low[1]
                    else:
                        share[index, pair, head, LANES:, place] = blank
                    if has_off:
                        share_off[pair, head, :LANES, place] = low[-2]
                        share_off[pair, head, LANES:, place] = low[-1]
                mixed = dot_plain(qkv[2, pair, rows, lanes], share[index, pair, head])
                if has_off:
                    mixed = mixed + dot_plain(qkv[2, pair, rows, :piece], share_off[pair, head])
                mixture[pair, rows, lanes] = mixed.astype(BF16)

    def part_sum(values):
        return jnp.sum(values.reshape(values.shape[0] // 8, 8, values.shape[1]), axis=0)

    def full_mean(parts):
        return jnp.sum(parts, axis=0, keepdims=True) * (1.0 / width)

    def column(index, rows):
        part = columns[index, rows, :].astype(F32)
        return jnp.concatenate([part] * (piece // LANES), axis=1)

    def gather_sum(index, rows, values):
        sums[index, rows, :] = sums[index, rows, :] + fold(values)

    def norm_chunks(index, which, total):
        mean = full_mean(total)
        spread = jnp.zeros((8, piece), F32)
        for rows in chunks:
            centred = wide_a[rows, :] - mean
            spread = spread + part_sum(centred * centred)
        inverse = lax.rsqrt(full_mean(spread) + EPS)
        inverses[index, which] = inverse
        return mean, inverse

    def forward(index):
        lanes = lanes_of(index)

        @pl.when(segment == 0)
        def _():
            x_t[:, lanes] = own_rows(index).astype(BF16)

        @pl.when(segment == 1)
        def _():
            forward_copy(index).wait_recv()

        inputs = x_t[:, lanes]
        score_scale = 1.0 / math.sqrt(width // HEADS)
        for block in range(3):
            result = dot_plain(turned[block], inputs)
            for pair in range(pairs):
                low = result[pair * LANES : (pair + 1) * LANES]
                low = (low * score_scale if block == 0 else low).astype(BF16)
                qkv[block, pair, :, lanes] = low
                if block == 1:
                    keys_rm[index, pair] = low.T
                if block == 2:
                    values_rm[index, pair] = low.T

        @pl.when(index == 1)
        def _():
            attend(index, True)

        @pl.when(index != 1)
        def _():
            attend(index, False)

        branch = dot_plain(turned[3], mixture[:, :, lanes].reshape(width, piece))
        total = jnp.zeros((8, piece), F32)
        for rows in chunks:
            sum_one = x_t[rows, lanes].astype(F32) + (branch[rows] + column(BIAS_OUT, rows))
            wide_a[rows, :] = sum_one
            total = total + part_sum(sum_one)
        mean, inverse = norm_chunks(index, 0, total)
        for rows in chunks:
            normed = (wide_a[rows, :] - mean) * inverse
            norm_one[rows, lanes] = normed
            hidden = normed * column(GAIN_ONE, rows) + column(BIAS_ONE, rows)
            hidden_low[rows, lanes] = hidden.astype(BF16)

        def activate(block, pre_block):
            for rows in chunks:
                pre = pre_block[rows] + column(BIAS_UP + block, rows)
                level = (lax.erf(pre * (1.0 / math.sqrt(2.0))) + 1.0) * 0.5
                active[block, rows, lanes] = (pre * level).astype(BF16)
                bell = jnp.exp(-0.5 * pre * pre) * (1.0 / math.sqrt(2.0 * math.pi))
                slope[block, rows, lanes] = (level + pre * bell).astype(BF16)

        for block in range(4):
            activate(block, dot_plain(turned[4 + block], hidden_low[:, lanes]))
        branch_two = dot_plain(down_turned[...], active[:, :, lanes].reshape(4 * width, piece))
        total = jnp.zeros((8, piece), F32)
        for rows in chunks:
            hidden = norm_one[rows, lanes] * column(GAIN_ONE, rows) + column(BIAS_ONE, rows)
            sum_two = hidden + (branch_two[rows] + column(BIAS_DOWN, rows))
            wide_a[rows, :] = sum_two
            total = total + part_sum(sum_two)
        mean, inverse = norm_chunks(index, 1, total)

        def outputs(rows):
            normed = (wide_a[rows, :] - mean) * inverse
            norm_two[rows, lanes] = normed
            return normed * column(GAIN_TWO, rows) + column(BIAS_TWO, rows)

        @pl.when(segment == 0)
        def _():
            for rows in chunks:
                outgoing[index, rows, :] = outputs(rows).astype(BF16)
            forward_copy(index).start()

        @pl.when(segment == 1)
        def _():
            free_ends(index)
            for start in range(0, width, LANES):
                rows = slice(start, start + LANES)
                ends_v[lax.rem(index, 2), :, rows] = outputs(rows).T
            ends_copy(index).start()

    def attend_back(index, has_off):
        lanes = lanes_of(index)
        slot = jnp.where(index == 0, 1, 0)
        half = LANES // 2
        score_scale = 1.0 / math.sqrt(width // HEADS)
        blank = jnp.zeros((LANES, LANES), BF16)
        for pair in range(pairs):
            grads = grad_mix[pair]
            blocks = pair_blocks(grads)
            back = dot_plain(values_rm[index, pair], blocks)
            if has_off:
                back_off = dot_plain(values_rm[0, pair], blocks)
            for head in range(2):
                rows = slice(head * half, (head + 1) * half)
                for part in range(2):
                    start = head * piece + part * LANES
                    span = slice(start, start + LANES)
                    place = slice(part * LANES, (part + 1) * LANES)
                    shares = [share[index, pair, head, place, place].astype(F32)]
                    backs = [back[place, span]]
                    if part:
                        shares.append(share[index, pair, head, :LANES, place].astype(F32))
                        backs.append(back[:LANES, span])
                    if has_off:
                        for low_half in range(2):
                            keys = slice(low_half * LANES, (low_half + 1) * LANES)
                            shares.append(share_off[pair, head, keys, place].astype(F32))
                            backs.append(back_off[keys, span])
                    products = [left * right for left, right in zip(shares, backs)]
                    inner = jnp.sum(functools.reduce(jnp.add, products), axis=0, keepdims=True)
                    low = [
                        (product - left * inner).astype(BF16)
                        for product, left in zip(products, shares)
                    ]
                    score_grad[head, place, place] = low[0]
                    if part:
                        score_grad[head, :LANES, place] = low[1]
                    else:
                        score_grad[head, LANES:, place] = blank
                    if has_off:
                        score_grad[2 + head, :LANES, place] = low[-2]
                        score_grad[2 + head, LANES:, place] = low[-1]
                queries = qkv[0, pair, rows, lanes]
                grad_scores = score_grad[head]
                grad_query = dot_plain(qkv[1, pair, rows, lanes], grad_scores)
                grad_key = dot_turned(queries, grad_scores) + key_sums[slot, 0, pair, rows]
                grad_value = (
                    dot_turned(grads[rows], share[index, pair, head])
                    + key_sums[slot, 1, pair, rows]
                )
                if has_off:
                    grad_off = score_grad[2 + head]
                    grad_query = grad_query + dot_plain(qkv[1, pair, rows, :piece], grad_off)
                    key_sums[1, 0, pair, rows] = dot_turned(queries, grad_off)
                    key_sums[1, 1, pair, rows] = dot_turned(grads[rows], share_off[pair, head])
                qkv[0, pair, rows, lanes] = (grad_query * score_scale).astype(BF16)
                qkv[1, pair, rows, lanes] = grad_key.astype(BF16)
                qkv[2, pair, rows, lanes] = grad_value.astype(BF16)

    def backward(index):
        lanes = lanes_of(index)

        @pl.when(segment == 1)
        def _():
            incoming_grad[index] = own_rows(index).astype(BF16)

        @pl.when(segment == 0)
        def _():
            backward_copy(index).wait_recv()

        plain = jnp.zeros((8, piece), F32)
        inner = jnp.zeros((8, piece), F32)
        for rows in chunks:
            grad = incoming_grad[index, rows, :].astype(F32)
            product = grad * norm_two[rows, lanes]
            gather_sum(GAIN_TWO, rows, product)
            gather_sum(BIAS_TWO, rows, grad)
            gain = column(GAIN_TWO, rows)
            plain = plain + part_sum(grad * gain)
            inner = inner + part_sum(product * gain)
        plain = full_mean(plain)
        inner = full_mean(inner)
        inverse = inverses[index, 1]
        for rows in chunks:
            scaled = incoming_grad[index, rows, :].astype(F32) * column(GAIN_TWO, rows)
            grad_two = (scaled - plain - norm_two[rows, lanes] * inner) * inverse
            gather_sum(BIAS_DOWN, rows, grad_two)
            wide_a[rows, :] = grad_two
            down_grad[rows, lanes] = grad_two.astype(BF16)

        for block in range(4):
            back = dot_plain(w_down[block], down_grad[:, lanes])
            for rows in chunks:
                grad_pre = back[rows] * slope[block, rows, lanes].astype(F32)
                gather_sum(BIAS_UP + block, rows, grad_pre)
                slope[block, rows, lanes] = grad_pre.astype(BF16)

        through = dot_plain(w_up[...], slope[:, :, lanes].reshape(4 * width, piece))
        plain = jnp.zeros((8, piece), F32)
        inner = jnp.zeros((8, piece), F32)
        for rows in chunks:
            grad_hidden = wide_a[rows, :] + through[rows]
            wide_a[rows, :] = grad_hidden
            product = grad_hidden * norm_one[rows, lanes]
            gather_sum(GAIN_ONE, rows, product)
            gather_sum(BIAS_ONE, rows, grad_hidden)
            gain = column(GAIN_ONE, rows)
            plain = plain + part_sum(grad_hidden * gain)
            inner = inner + part_sum(product * gain)
        plain = full_mean(plain)
        inner = full_mean(inner)
        inverse = inverses[index, 0]
        for rows in chunks:
            scaled = wide_a[rows, :] * column(GAIN_ONE, rows)
            grad_one = (scaled - plain - norm_one[rows, lanes] * inner) * inverse
            gather_sum(BIAS_OUT, rows, grad_one)
            wide_b[rows, :] = grad_one
            branch_grad[rows, lanes] = grad_one.astype(BF16)
        grad_mix[...] = (
            dot_plain(w_out[...], branch_grad[:, lanes]).astype(BF16).reshape(pairs, LANES, piece)
        )

        @pl.when(index == 1)
        def _():
            attend_back(index, True)

        @pl.when(index != 1)
        def _():
            attend_back(index, False)

        through = dot_plain(w_qkv[...], qkv[:, :, :, lanes].reshape(3 * width, piece))

        @pl.when(segment == 1)
        def _():
            for rows in chunks:
                outgoing[index, rows, :] = (wide_b[rows, :] + through[rows]).astype(BF16)
            backward_copy(index).start()

        @pl.when(segment == 0)
        def _():
            free_ends(index)
            for start in range(0, width, LANES):
                rows = slice(start, start + LANES)
                ends_v[lax.rem(index, 2), :, rows] = (wide_b[rows, :] + through[rows]).T
            ends_copy(index).start()

    def one_step(step, carry):
        first_index = jnp.where(step < 4, step, jnp.where(step < 6, 5 - step, step - 4))
        last_index = jnp.where(step < 2, step, jnp.where(step < 4, 3 - step, lax.div(step, 2)))
        first_is = jnp.where(step < 4, 1, 0)
        last_is = jnp.where(step < 2, 1, jnp.where(step < 4, 0, 1 - lax.rem(step, 2)))
        index = jnp.where(segment == 0, first_index, last_index)
        is_forward = jnp.where(segment == 0, first_is, last_is)

        @pl.when(is_forward == 1)
        def _():
            forward(index)

        @pl.when(is_forward == 0)
        def _():
            backward(index)

        return carry

    lax.fori_loop(0, 2 * PIECES, one_step, 0)

    def held(group):
        return (w_down, 0) if group == 0 else (turned, 4 if group == 1 else 0)

    def core_copy(group):
        buffer, base = held(group)
        return pltpu.make_async_remote_copy(
            src_ref=buffer.at[pl.ds(base + 2 * (1 - core), 2)],
            dst_ref=core_in.at[group],
            send_sem=core_send.at[group],
            recv_sem=core_recv.at[group],
            device_id={"rep": other_core},
            device_id_type=MESH,
        )

    def side_copy(group):
        buffer, base = held(group)
        return pltpu.make_async_remote_copy(
            src_ref=buffer.at[base + 2 * core + (1 - side)],
            dst_ref=side_in.at[group],
            send_sem=side_send.at[group],
            recv_sem=side_recv.at[group],
            device_id={"rep": other_side},
            device_id_type=MESH,
        )

    def dp_copy(group, step):
        buffer, base = held(group)
        target = lax.rem(dp + step, dp_count)
        rows = pl.ds(pl.multiple_of(target * share_rows, share_rows), share_rows)
        return pltpu.make_async_remote_copy(
            src_ref=buffer.at[base + 2 * core + side, rows],
            dst_ref=dp_in.at[group, step - 1],
            send_sem=dp_send.at[group, step - 1],
            recv_sem=dp_recv.at[group, step - 1],
            device_id={"dp": target},
            device_id_type=MESH,
        )

    def join_copy(group):
        return pltpu.make_async_remote_copy(
            src_ref=fin.at[group, 2 * core + side],
            dst_ref=fin.at[group, 2 * core + side],
            send_sem=join_send.at[group],
            recv_sem=join_recv.at[group],
            device_id={"rep": other_side},
            device_id_type=MESH,
        )

    def last_copy(group):
        return pltpu.make_async_remote_copy(
            src_ref=fin.at[group, pl.ds(2 * core, 2)],
            dst_ref=fin.at[group, pl.ds(2 * core, 2)],
            send_sem=last_send.at[group],
            recv_sem=last_recv.at[group],
            device_id={"rep": other_core},
            device_id_type=MESH,
        )

    def down_sums():
        part = 4 * share_rows
        count = width // part

        def one(block, carry):
            result = dot_turned(active[block], down_grad[...]).astype(BF16)
            for each in range(count):
                for position in range(4):
                    start = each * part + position * share_rows
                    target = pl.multiple_of((block * count + each) * share_rows, share_rows)
                    w_down[position, pl.ds(target, share_rows), :] = result[
                        start : start + share_rows
                    ]
            return carry

        lax.fori_loop(0, 4, one, 0)

    def up_sums():
        def one(block, carry):
            turned[4 + block] = dot_turned(hidden_low[...], slope[block]).astype(BF16)
            return carry

        lax.fori_loop(0, 4, one, 0)

    def qkv_sums():
        def one(block, carry):
            turned[block] = dot_turned(
                x_t[...], qkv[block].reshape(width, PIECES * piece)
            ).astype(BF16)
            return carry

        lax.fori_loop(0, 3, one, 0)
        turned[3] = dot_turned(
            mixture[...].reshape(width, PIECES * piece), branch_grad[...]
        ).astype(BF16)

    def after_core(group):
        buffer, base = held(group)
        copy = core_copy(group)
        copy.wait_send()
        copy.wait_recv()
        first = base + 2 * core + (1 - side)
        buffer[first] = (
            buffer[first].astype(F32) + core_in[group, 1 - side].astype(F32)
        ).astype(BF16)
        side_copy(group).start()

    def after_side(group):
        buffer, base = held(group)
        copy = side_copy(group)
        copy.wait_send()
        copy.wait_recv()
        second = base + 2 * core + side
        buffer[second] = (
            buffer[second].astype(F32)
            + core_in[group, side].astype(F32)
            + side_in[group].astype(F32)
        ).astype(BF16)
        for step in range(1, dp_count):
            dp_copy(group, step).start()

    def after_dp(group):
        buffer, base = held(group)
        rows = pl.ds(pl.multiple_of(dp * share_rows, share_rows), share_rows)
        total = buffer[base + 2 * core + side, rows, :].astype(F32)
        for step in range(1, dp_count):
            copy = dp_copy(group, step)
            copy.wait_send()
            copy.wait_recv()
            total = total + dp_in[group, step - 1].astype(F32)
        fin[group, 2 * core + side] = total.astype(BF16)
        join_copy(group).start()

    def after_join(group):
        copy = join_copy(group)
        copy.wait_send()
        copy.wait_recv()
        last_copy(group).start()

    def fin_copy(group):
        return pltpu.make_async_copy(fin.at[group], fin_hbm.at[group], fin_sem.at[group])

    def after_last(group):
        copy = last_copy(group)
        copy.wait_send()
        copy.wait_recv()
        fin_copy(group).start()

    def small_dp_copy(step):
        target = lax.rem(dp + step, dp_count)
        return pltpu.make_async_remote_copy(
            src_ref=small.at[target],
            dst_ref=small_dp.at[step - 1],
            send_sem=sdp_send.at[step - 1],
            recv_sem=sdp_recv.at[step - 1],
            device_id={"dp": target},
            device_id_type=MESH,
        )

    def small_rep_copy(step):
        return pltpu.make_async_remote_copy(
            src_ref=small_rep.at[rep],
            dst_ref=small_rep.at[rep],
            send_sem=srep_send.at[step - 1],
            recv_sem=srep_recv.at[step - 1],
            device_id={"rep": lax.rem(rep + step, 4)},
            device_id_type=MESH,
        )

    down_sums()
    core_copy(0).start()
    up_sums()
    core_copy(1).start()
    after_core(0)
    qkv_sums()
    core_copy(2).start()
    after_core(1)

    rows_of = [jnp.sum(sums[index].T, axis=0, keepdims=True) for index in range(STATS)]
    small[...] = jnp.zeros(small.shape, F32)
    for share_index in range(dp_count):
        for index in range(BIAS_UP):
            start = share_index * share_rows
            small[share_index, index : index + 1, :share_rows] = rows_of[index][
                :, start : start + share_rows
            ]
        for part in range(4):
            start = (share_index * 4 + part) * share_rows
            block, start = start // width, start % width
            small[share_index, BIAS_UP + part : BIAS_UP + part + 1, :share_rows] = rows_of[
                BIAS_UP + block
            ][:, start : start + share_rows]
    for step in range(1, dp_count):
        small_dp_copy(step).start()

    after_core(2)
    after_side(0)
    small_total = small[dp]
    for step in range(1, dp_count):
        copy = small_dp_copy(step)
        copy.wait_send()
        copy.wait_recv()
        small_total = small_total + small_dp[step - 1]
    small_rep[rep] = small_total
    for step in range(1, 4):
        small_rep_copy(step).start()
    after_side(1)
    after_dp(0)
    after_side(2)
    after_join(0)
    after_dp(1)
    after_last(0)
    after_join(1)
    for step in range(1, 4):
        copy = small_rep_copy(step)
        copy.wait_send()
        copy.wait_recv()
    small_out[...] = (small_rep[0] + small_rep[1]) + (small_rep[2] + small_rep[3])
    small_copy = pltpu.make_async_copy(small_out, small_hbm, load_sem.at[0])
    small_copy.start()
    after_last(1)
    after_dp(2)
    after_join(2)
    after_last(2)

    for index in range(PIECES):

        @pl.when(segment == 0)
        def _():
            forward_copy(index).wait_send()

        @pl.when(segment == 1)
        def _():
            backward_copy(index).wait_send()

    for index in range(2, PIECES):
        ends_copy(index).wait()
    for group in range(3):
        fin_copy(group).wait()
    small_copy.wait()


def finish_kernel(
    flag_ref,
    ends_in,
    fin,
    small,
    ends,
    grad_qkv,
    grad_out,
    grad_up,
    grad_down,
    grad_up_bias,
    grad_gains,
    grad_biases,
    fin_v,
    wide_qkv,
    wide_out,
    wide_up,
    wide_down,
    ends_sem,
    in_sem,
    out_sem,
):
    half = ends_in.shape[0] // 2
    share_rows, width = fin.shape[2:]
    start = pl.multiple_of(half * (1 - flag_ref[0, 0]), half)
    ends_copies = [
        pltpu.make_async_copy(
            ends_in.at[pl.ds(0, half)], ends.at[0, pl.ds(start, half)], ends_sem.at[0]
        ),
        pltpu.make_async_copy(
            ends_in.at[pl.ds(half, half)], ends.at[0, pl.ds(half - start, half)], ends_sem.at[1]
        ),
    ]
    loads = [
        pltpu.make_async_copy(fin.at[group], fin_v.at[group], in_sem.at[group])
        for group in range(3)
    ]
    stores = [
        pltpu.make_async_copy(wide, target.at[0], out_sem.at[index])
        for index, (wide, target) in enumerate(
            ((wide_down, grad_down), (wide_up, grad_up), (wide_qkv, grad_qkv), (wide_out, grad_out))
        )
    ]
    for copy in loads + ends_copies:
        copy.start()
    loads[0].wait()
    for position in range(4):
        rows = slice(position * share_rows, (position + 1) * share_rows)
        wide_down[rows, :] = fin_v[0, position].astype(F32)
    stores[0].start()
    loads[1].wait()
    for position in range(4):
        wide_up[:, position * width : (position + 1) * width] = fin_v[1, position].astype(F32)
    stores[1].start()
    loads[2].wait()
    for position in range(3):
        wide_qkv[:, position * width : (position + 1) * width] = fin_v[2, position].astype(F32)
    stores[2].start()
    wide_out[...] = fin_v[2, 3].astype(F32)
    stores[3].start()
    for position in range(4):
        rows = slice(position * share_rows, (position + 1) * share_rows)
        grad_up_bias[:, rows] = small[BIAS_UP + position : BIAS_UP + position + 1, :share_rows]
    grad_gains[0] = small[:2, :share_rows]
    grad_biases[0] = small[2:BIAS_UP, :share_rows]
    for copy in stores + ends_copies:
        copy.wait()


def on_device(
    dp_count,
    block_input,
    cotangent,
    window_group,
    w_qkv,
    w_out,
    w_up,
    w_down,
    up_bias,
    norm_gains,
    biases,
):
    rows, width = block_input.shape
    piece = rows // PIECES
    pairs = width // LANES
    share_rows = width // dp_count
    small_width = max(share_rows, LANES)
    any_spec = pl.BlockSpec(memory_space=pl.ANY)
    vmem_spec = pl.BlockSpec(memory_space=pltpu.VMEM)
    smem_spec = pl.BlockSpec(memory_space=pltpu.SMEM)
    dma = pltpu.SemaphoreType.DMA
    vmem = pltpu.VMEM
    ends_in, fin, small = pl.pallas_call(
        functools.partial(layer_kernel, dp_count),
        out_shape=(
            jax.ShapeDtypeStruct((PIECES, piece, width), F32),
            jax.ShapeDtypeStruct((3, 4, share_rows, width), BF16),
            jax.ShapeDtypeStruct((16, small_width), F32),
        ),
        in_specs=[smem_spec] + [any_spec] * 6 + [vmem_spec] * 3,
        out_specs=(any_spec,) * 3,
        scratch_shapes=[
            vmem((width, 3 * width), BF16),
            vmem((width, width), BF16),
            vmem((width, 4 * width), BF16),
            vmem((4, width, width), BF16),
            vmem((8, width, width), BF16),
            vmem((width, 4 * width), BF16),
            vmem((PIECES, piece, width), BF16),
            vmem((width, rows), BF16),
            vmem((3, pairs, LANES, rows), BF16),
            vmem((PIECES, pairs, piece, LANES), BF16),
            vmem((PIECES, pairs, piece, LANES), BF16),
            vmem((PIECES, pairs, 2, piece, piece), BF16),
            vmem((pairs, 2, piece, piece), BF16),
            vmem((pairs, LANES, rows), BF16),
            vmem((width, rows), F32),
            vmem((width, rows), F32),
            vmem((PIECES, 2, 1, piece), F32),
            vmem((width, rows), BF16),
            vmem((4, width, rows), BF16),
            vmem((4, width, rows), BF16),
            vmem((width, rows), BF16),
            vmem((width, rows), BF16),
            vmem((pairs, LANES, piece), BF16),
            vmem((PIECES, width, piece), BF16),
            vmem((PIECES, width, piece), BF16),
            vmem((STATS, width, LANES), BF16),
            vmem((STATS, width, LANES), F32),
            vmem((2, 2, pairs, LANES, piece), F32),
            vmem((4, piece, piece), BF16),
            vmem((width, piece), F32),
            vmem((width, piece), F32),
            vmem((2, piece, width), F32),
            vmem((3, 2, width, width), BF16),
            vmem((3, width, width), BF16),
            vmem((3, dp_count - 1, share_rows, width), BF16),
            vmem((3, 4, share_rows, width), BF16),
            vmem((dp_count, 16, small_width), F32),
            vmem((dp_count - 1, 16, small_width), F32),
            vmem((4, 16, small_width), F32),
            vmem((16, small_width), F32),
            dma((8,)),
            dma((PIECES,)),
            dma((PIECES,)),
            dma((PIECES,)),
            dma((3,)),
            dma((3,)),
            dma((3,)),
            dma((3,)),
            dma((3, dp_count - 1)),
            dma((3, dp_count - 1)),
            dma((3,)),
            dma((3,)),
            dma((3,)),
            dma((3,)),
            dma((dp_count - 1,)),
            dma((dp_count - 1,)),
            dma((3,)),
            dma((3,)),
            dma((3,)),
        ],
        compiler_params=pltpu.CompilerParams(
            collective_id=0, has_side_effects=True, vmem_limit_bytes=63 * 1024 * 1024
        ),
    )(
        window_group,
        block_input.reshape(PIECES, piece, width),
        cotangent.reshape(PIECES, piece, width),
        w_qkv,
        w_out,
        w_up,
        w_down,
        up_bias,
        norm_gains,
        biases,
    )
    return pl.pallas_call(
        finish_kernel,
        out_shape=(
            jax.ShapeDtypeStruct((1, rows, width), F32),
            jax.ShapeDtypeStruct((1, share_rows, 3 * width), F32),
            jax.ShapeDtypeStruct((1, share_rows, width), F32),
            jax.ShapeDtypeStruct((1, share_rows, 4 * width), F32),
            jax.ShapeDtypeStruct((1, 4 * share_rows, width), F32),
            jax.ShapeDtypeStruct((1, 4 * share_rows), F32),
            jax.ShapeDtypeStruct((1, 2, share_rows), F32),
            jax.ShapeDtypeStruct((1, 4, share_rows), F32),
        ),
        in_specs=[smem_spec, any_spec, any_spec, vmem_spec],
        out_specs=(any_spec,) * 5 + (vmem_spec,) * 3,
        scratch_shapes=[
            vmem((3, 4, share_rows, width), BF16),
            vmem((share_rows, 3 * width), F32),
            vmem((share_rows, width), F32),
            vmem((share_rows, 4 * width), F32),
            vmem((4 * share_rows, width), F32),
            dma((2,)),
            dma((3,)),
            dma((4,)),
        ],
        compiler_params=pltpu.CompilerParams(vmem_limit_bytes=63 * 1024 * 1024),
    )(window_group, ends_in.reshape(rows, width), fin, small)


def solution(mesh):
    return jax.shard_map(
        functools.partial(on_device, mesh.shape["dp"]),
        mesh=mesh,
        in_specs=(
            P(("dp", "rep"), None),
            P(("dp", "rep"), None),
            P(("dp", "rep"), None),
            P("segment", None, None),
            P("segment", None, None),
            P("segment", None, None),
            P("segment", None, None),
            P("segment", None),
            P("segment", None, None),
            P("segment", None, None),
        ),
        out_specs=(
            P("segment", ("dp", "rep"), None),
            P("segment", "dp", None),
            P("segment", "dp", None),
            P("segment", "dp", None),
            P("segment", "dp", None),
            P("segment", "dp"),
            P("segment", None, "dp"),
            P("segment", None, "dp"),
        ),
        check_vma=False,
    )
```

```python
import functools
import math

import jax
import jax.numpy as jnp
from jax import lax
from jax.experimental import pallas as pl
from jax.experimental.pallas import tpu as pltpu
from jax.sharding import PartitionSpec as P

MESH = pl.DeviceIdType.MESH
F32 = jnp.float32
BF16 = jnp.bfloat16
HEADS = 8
LANES = 128
PIECES = 4
EPS = 1e-05
GAIN_ONE, GAIN_TWO, BIAS_OUT, BIAS_ONE, BIAS_DOWN, BIAS_TWO, BIAS_UP = range(7)
STATS = 10
CHUNK = 64


def dot_plain(left, right):
    return lax.dot_general(left, right, (((1,), (0,)), ((), ())), preferred_element_type=F32)


def dot_turned(left, right):
    return lax.dot_general(left, right, (((1,), (1,)), ((), ())), preferred_element_type=F32)


def fold(values):
    total = values[:, :LANES]
    for start in range(LANES, values.shape[1], LANES):
        total = total + values[:, start : start + LANES]
    return total


def normal_level(values, bell):
    depth = 1.0 + jnp.abs(values) * (0.3275911 / math.sqrt(2.0))
    near = pl.reciprocal(depth, approx=True)
    near = near * (2.0 - depth * near)
    series = near * (0.5 * 1.061405429) + (0.5 * -1.453152027)
    for factor in (1.421413741, -0.284496736, 0.254829592):
        series = series * near + 0.5 * factor
    upper = series * near * bell
    return jnp.where(values < 0.0, upper, 1.0 - upper)


def pair_blocks(values):
    half = values.shape[0] // 2
    blank = jnp.zeros((half, values.shape[1]), values.dtype)
    first = jnp.concatenate([values[:half], blank], axis=0)
    second = jnp.concatenate([blank, values[half:]], axis=0)
    return jnp.concatenate([first, second], axis=1)


def layer_kernel(
    dp_count,
    flag_ref,
    x_hbm,
    ct_hbm,
    w_qkv_hbm,
    w_out_hbm,
    w_up_hbm,
    w_down_hbm,
    up_bias_ref,
    gains_ref,
    biases_ref,
    ends_hbm,
    fin_hbm,
    small_hbm,
    w_qkv,
    w_out,
    w_up,
    w_down,
    turned,
    down_turned,
    rows_in,
    x_t,
    qkv,
    keys_rm,
    values_rm,
    share,
    share_off,
    mixture,
    norm_one,
    norm_two,
    inverses,
    hidden_low,
    slope,
    active,
    down_grad,
    branch_grad,
    grad_mix,
    outgoing,
    incoming_grad,
    columns,
    sums,
    key_sums,
    score_grad,
    wide_a,
    wide_b,
    ends_v,
    core_in,
    side_in,
    dp_in,
    fin,
    small,
    small_dp,
    small_rep,
    small_out,
    load_sem,
    seg_send,
    seg_recv,
    ends_sem,
    core_send,
    core_recv,
    side_send,
    side_recv,
    dp_send,
    dp_recv,
    join_send,
    join_recv,
    last_send,
    last_recv,
    sdp_send,
    sdp_recv,
    srep_send,
    srep_recv,
    fin_sem,
):
    width = w_out.shape[0]
    piece = x_t.shape[1] // PIECES
    pairs = qkv.shape[1]
    share_rows = width // dp_count
    segment = lax.axis_index("segment")
    dp = lax.axis_index("dp")
    rep = lax.axis_index("rep")
    core = lax.rem(rep, 2)
    side = lax.div(rep, 2)
    other_core = side * 2 + (1 - core)
    other_side = (1 - side) * 2 + core

    loads = [
        (w_qkv_hbm.at[0], w_qkv),
        (w_out_hbm.at[0], w_out),
        (w_up_hbm.at[0], w_up),
    ]
    for block in range(4):
        loads.append((w_down_hbm.at[0, pl.ds(block * width, width), :], w_down.at[block]))
    load_copies = [
        pltpu.make_async_copy(source, target, load_sem.at[index + 1])
        for index, (source, target) in enumerate(loads)
    ]
    first_rows = pltpu.make_async_copy(x_hbm, rows_in, load_sem.at[0])
    last_rows = pltpu.make_async_copy(ct_hbm, rows_in, load_sem.at[0])

    @pl.when(segment == 0)
    def _():
        first_rows.start()

    @pl.when(segment == 1)
    def _():
        last_rows.start()

    for copy in load_copies:
        copy.start()

    barrier = pltpu.get_barrier_semaphore()
    pl.semaphore_signal(
        barrier, inc=1, device_id={"segment": 1 - segment}, device_id_type=MESH
    )
    for step in range(1, 4):
        pl.semaphore_signal(
            barrier, inc=1, device_id={"rep": lax.rem(rep + step, 4)}, device_id_type=MESH
        )
    for step in range(1, dp_count):
        pl.semaphore_signal(
            barrier, inc=1, device_id={"dp": lax.rem(dp + step, dp_count)}, device_id_type=MESH
        )

    params = [gains_ref[0].astype(F32), biases_ref[0].astype(F32)]
    for block in range(4):
        params.append(up_bias_ref[:, block * width : (block + 1) * width].astype(F32))
    params.append(jnp.zeros((16 - STATS, width), F32))
    upright = jnp.concatenate(params, axis=0).T
    for index in range(STATS):
        columns[index] = jnp.broadcast_to(upright[:, index : index + 1], (width, LANES)).astype(BF16)
    for index in range(STATS):
        sums[index] = jnp.zeros((width, LANES), F32)
    key_sums[0] = jnp.zeros(key_sums.shape[1:], F32)

    chunks = [slice(start, start + CHUNK) for start in range(0, width, CHUNK)]

    for copy in load_copies:
        copy.wait()
    first_rows.wait()

    for block in range(3):
        turned[block] = w_qkv[:, block * width : (block + 1) * width].T
    turned[3] = w_out[...].T
    for block in range(4):
        turned[4 + block] = w_up[:, block * width : (block + 1) * width].T
    for block in range(4):
        down_turned[:, block * width : (block + 1) * width] = w_down[block].T

    pl.semaphore_wait(barrier, 4 + dp_count - 1)

    flag = flag_ref[0, 0].astype(F32)

    def lanes_of(index):
        return pl.ds(pl.multiple_of(index * piece, piece), piece)

    def forward_copy(index):
        return pltpu.make_async_remote_copy(
            src_ref=outgoing.at[index],
            dst_ref=x_t.at[:, lanes_of(index)],
            send_sem=seg_send.at[index],
            recv_sem=seg_recv.at[index],
            device_id={"segment": 1 - segment},
            device_id_type=MESH,
        )

    def backward_copy(index):
        return pltpu.make_async_remote_copy(
            src_ref=outgoing.at[index],
            dst_ref=incoming_grad.at[index],
            send_sem=seg_send.at[index],
            recv_sem=seg_recv.at[index],
            device_id={"segment": 1 - segment},
            device_id_type=MESH,
        )

    def ends_copy(index):
        return pltpu.make_async_copy(
            ends_v.at[lax.rem(index, 2)], ends_hbm.at[index], ends_sem.at[index]
        )

    def free_ends(index):
        @pl.when(index >= 2)
        def _():
            ends_copy(index - 2).wait()

    def own_rows(index):
        half = lax.rem(index, 2)
        whole = jnp.where(index < 2, 1.0, 0.0).astype(F32)
        weight = whole * flag + (1.0 - whole) * (1.0 - flag)
        picked = rows_in[half].astype(F32) * weight + rows_in[2 + half].astype(F32) * (1.0 - weight)
        return picked.T

    def attend(index, has_off):
        lanes = lanes_of(index)
        half = LANES // 2
        key_at = lax.broadcasted_iota(jnp.int32, (LANES, LANES), 0)
        query_at = lax.broadcasted_iota(jnp.int32, (LANES, LANES), 1)
        allowed = key_at <= query_at
        blank = jnp.zeros((LANES, LANES), BF16)
        for pair in range(pairs):
            queries = pair_blocks(qkv[0, pair, :, lanes])
            scores = dot_plain(keys_rm[index, pair], queries)
            if has_off:
                scores_off = dot_plain(keys_rm[0, pair], queries)
            for head in range(2):
                rows = slice(head * half, (head + 1) * half)
                for part in range(2):
                    start = head * piece + part * LANES
                    span = slice(start, start + LANES)
                    place = slice(part * LANES, (part + 1) * LANES)
                    tiles = [jnp.where(allowed, scores[place, span], -1e30)]
                    if part:
                        tiles.append(scores[:LANES, span])
                    if has_off:
                        tiles.append(scores_off[:LANES, span])
                        tiles.append(scores_off[LANES:, span])
                    top = functools.reduce(jnp.maximum, tiles)
                    top = jnp.max(top, axis=0, keepdims=True)
                    raised = [jnp.exp(tile - top) for tile in tiles]
                    total = functools.reduce(jnp.add, raised)
                    scale = 1.0 / jnp.sum(total, axis=0, keepdims=True)
                    low = [(tile * scale).astype(BF16) for tile in raised]
                    share[index, pair, head, place, place] = low[0]
                    if part:
                        share[index, pair, head, :LANES, place] = low[1]
                    else:
                        share[index, pair, head, LANES:, place] = blank
                    if has_off:
                        share_off[pair, head, :LANES, place] = low[-2]
                        share_off[pair, head, LANES:, place] = low[-1]
                mixed = dot_plain(qkv[2, pair, rows, lanes], share[index, pair, head])
                if has_off:
                    mixed = mixed + dot_plain(qkv[2, pair, rows, :piece], share_off[pair, head])
                mixture[pair, rows, lanes] = mixed.astype(BF16)

    def part_sum(values):
        return jnp.sum(values.reshape(values.shape[0] // 8, 8, values.shape[1]), axis=0)

    def full_mean(parts):
        return jnp.sum(parts, axis=0, keepdims=True) * (1.0 / width)

    def column(index, rows):
        part = columns[index, rows, :].astype(F32)
        return jnp.concatenate([part] * (piece // LANES), axis=1)

    def gather_sum(index, rows, values):
        sums[index, rows, :] = sums[index, rows, :] + fold(values)

    def norm_chunks(index, which, total):
        mean = full_mean(total)
        spread = jnp.zeros((8, piece), F32)
        for rows in chunks:
            centred = wide_a[rows, :] - mean
            spread = spread + part_sum(centred * centred)
        inverse = lax.rsqrt(full_mean(spread) + EPS)
        inverses[index, which] = inverse
        return mean, inverse

    def forward(index):
        lanes = lanes_of(index)

        @pl.when(segment == 0)
        def _():
            x_t[:, lanes] = own_rows(index).astype(BF16)

        @pl.when(segment == 1)
        def _():
            forward_copy(index).wait_recv()

        inputs = x_t[:, lanes]
        score_scale = 1.0 / math.sqrt(width // HEADS)
        for block in range(3):
            result = dot_plain(turned[block], inputs)
            for pair in range(pairs):
                low = result[pair * LANES : (pair + 1) * LANES]
                low = (low * score_scale if block == 0 else low).astype(BF16)
                qkv[block, pair, :, lanes] = low
                if block == 1:
                    keys_rm[index, pair] = low.T
                if block == 2:
                    values_rm[index, pair] = low.T

        @pl.when(index == 1)
        def _():
            attend(index, True)

        @pl.when(index != 1)
        def _():
            attend(index, False)

        branch = dot_plain(turned[3], mixture[:, :, lanes].reshape(width, piece))
        total = jnp.zeros((8, piece), F32)
        for rows in chunks:
            sum_one = x_t[rows, lanes].astype(F32) + (branch[rows] + column(BIAS_OUT, rows))
            wide_a[rows, :] = sum_one
            total = total + part_sum(sum_one)
        mean, inverse = norm_chunks(index, 0, total)
        for rows in chunks:
            normed = (wide_a[rows, :] - mean) * inverse
            norm_one[rows, lanes] = normed
            hidden = normed * column(GAIN_ONE, rows) + column(BIAS_ONE, rows)
            hidden_low[rows, lanes] = hidden.astype(BF16)

        def activate(block, pre_block):
            for rows in chunks:
                pre = pre_block[rows] + column(BIAS_UP + block, rows)
                bell = jnp.exp2(pre * pre * (-0.5 * math.log2(math.e)))
                level = (lax.erf(pre * (1.0 / math.sqrt(2.0))) + 1.0) * 0.5
                active[block, rows, lanes] = (pre * level).astype(BF16)
                slope[block, rows, lanes] = (
                    level + pre * bell * (1.0 / math.sqrt(2.0 * math.pi))
                ).astype(BF16)

        for block in range(4):
            activate(block, dot_plain(turned[4 + block], hidden_low[:, lanes]))
        branch_two = dot_plain(down_turned[...], active[:, :, lanes].reshape(4 * width, piece))
        total = jnp.zeros((8, piece), F32)
        for rows in chunks:
            hidden = norm_one[rows, lanes] * column(GAIN_ONE, rows) + column(BIAS_ONE, rows)
            sum_two = hidden + (branch_two[rows] + column(BIAS_DOWN, rows))
            wide_a[rows, :] = sum_two
            total = total + part_sum(sum_two)
        mean, inverse = norm_chunks(index, 1, total)

        def outputs(rows):
            normed = (wide_a[rows, :] - mean) * inverse
            norm_two[rows, lanes] = normed
            return normed * column(GAIN_TWO, rows) + column(BIAS_TWO, rows)

        @pl.when(segment == 0)
        def _():
            for rows in chunks:
                outgoing[index, rows, :] = outputs(rows).astype(BF16)
            forward_copy(index).start()

        @pl.when(segment == 1)
        def _():
            free_ends(index)
            for start in range(0, width, LANES):
                rows = slice(start, start + LANES)
                ends_v[lax.rem(index, 2), :, rows] = outputs(rows).T
            ends_copy(index).start()

    def attend_back(index, has_off):
        lanes = lanes_of(index)
        slot = jnp.where(index == 0, 1, 0)
        half = LANES // 2
        score_scale = 1.0 / math.sqrt(width // HEADS)
        blank = jnp.zeros((LANES, LANES), BF16)
        for pair in range(pairs):
            grads = grad_mix[pair]
            blocks = pair_blocks(grads)
            back = dot_plain(values_rm[index, pair], blocks)
            if has_off:
                back_off = dot_plain(values_rm[0, pair], blocks)
            for head in range(2):
                rows = slice(head * half, (head + 1) * half)
                for part in range(2):
                    start = head * piece + part * LANES
                    span = slice(start, start + LANES)
                    place = slice(part * LANES, (part + 1) * LANES)
                    shares = [share[index, pair, head, place, place].astype(F32)]
                    backs = [back[place, span]]
                    if part:
                        shares.append(share[index, pair, head, :LANES, place].astype(F32))
                        backs.append(back[:LANES, span])
                    if has_off:
                        for low_half in range(2):
                            keys = slice(low_half * LANES, (low_half + 1) * LANES)
                            shares.append(share_off[pair, head, keys, place].astype(F32))
                            backs.append(back_off[keys, span])
                    products = [left * right for left, right in zip(shares, backs)]
                    inner = jnp.sum(functools.reduce(jnp.add, products), axis=0, keepdims=True)
                    low = [
                        (product - left * inner).astype(BF16)
                        for product, left in zip(products, shares)
                    ]
                    score_grad[head, place, place] = low[0]
                    if part:
                        score_grad[head, :LANES, place] = low[1]
                    else:
                        score_grad[head, LANES:, place] = blank
                    if has_off:
                        score_grad[2 + head, :LANES, place] = low[-2]
                        score_grad[2 + head, LANES:, place] = low[-1]
                queries = qkv[0, pair, rows, lanes]
                grad_scores = score_grad[head]
                grad_query = dot_plain(qkv[1, pair, rows, lanes], grad_scores)
                grad_key = dot_turned(queries, grad_scores) + key_sums[slot, 0, pair, rows]
                grad_value = (
                    dot_turned(grads[rows], share[index, pair, head])
                    + key_sums[slot, 1, pair, rows]
                )
                if has_off:
                    grad_off = score_grad[2 + head]
                    grad_query = grad_query + dot_plain(qkv[1, pair, rows, :piece], grad_off)
                    key_sums[1, 0, pair, rows] = dot_turned(queries, grad_off)
                    key_sums[1, 1, pair, rows] = dot_turned(grads[rows], share_off[pair, head])
                qkv[0, pair, rows, lanes] = (grad_query * score_scale).astype(BF16)
                qkv[1, pair, rows, lanes] = grad_key.astype(BF16)
                qkv[2, pair, rows, lanes] = grad_value.astype(BF16)

    def backward(index):
        lanes = lanes_of(index)

        @pl.when(segment == 1)
        def _():
            incoming_grad[index] = own_rows(index).astype(BF16)

        @pl.when(segment == 0)
        def _():
            backward_copy(index).wait_recv()

        plain = jnp.zeros((8, piece), F32)
        inner = jnp.zeros((8, piece), F32)
        for rows in chunks:
            grad = incoming_grad[index, rows, :].astype(F32)
            product = grad * norm_two[rows, lanes]
            gather_sum(GAIN_TWO, rows, product)
            gather_sum(BIAS_TWO, rows, grad)
            gain = column(GAIN_TWO, rows)
            plain = plain + part_sum(grad * gain)
            inner = inner + part_sum(product * gain)
        plain = full_mean(plain)
        inner = full_mean(inner)
        inverse = inverses[index, 1]
        for rows in chunks:
            scaled = incoming_grad[index, rows, :].astype(F32) * column(GAIN_TWO, rows)
            grad_two = (scaled - plain - norm_two[rows, lanes] * inner) * inverse
            gather_sum(BIAS_DOWN, rows, grad_two)
            wide_a[rows, :] = grad_two
            down_grad[rows, lanes] = grad_two.astype(BF16)

        for block in range(4):
            back = dot_plain(w_down[block], down_grad[:, lanes])
            for rows in chunks:
                grad_pre = back[rows] * slope[block, rows, lanes].astype(F32)
                gather_sum(BIAS_UP + block, rows, grad_pre)
                slope[block, rows, lanes] = grad_pre.astype(BF16)

        through = dot_plain(w_up[...], slope[:, :, lanes].reshape(4 * width, piece))
        plain = jnp.zeros((8, piece), F32)
        inner = jnp.zeros((8, piece), F32)
        for rows in chunks:
            grad_hidden = wide_a[rows, :] + through[rows]
            wide_a[rows, :] = grad_hidden
            product = grad_hidden * norm_one[rows, lanes]
            gather_sum(GAIN_ONE, rows, product)
            gather_sum(BIAS_ONE, rows, grad_hidden)
            gain = column(GAIN_ONE, rows)
            plain = plain + part_sum(grad_hidden * gain)
            inner = inner + part_sum(product * gain)
        plain = full_mean(plain)
        inner = full_mean(inner)
        inverse = inverses[index, 0]
        for rows in chunks:
            scaled = wide_a[rows, :] * column(GAIN_ONE, rows)
            grad_one = (scaled - plain - norm_one[rows, lanes] * inner) * inverse
            gather_sum(BIAS_OUT, rows, grad_one)
            wide_b[rows, :] = grad_one
            branch_grad[rows, lanes] = grad_one.astype(BF16)
        grad_mix[...] = (
            dot_plain(w_out[...], branch_grad[:, lanes]).astype(BF16).reshape(pairs, LANES, piece)
        )

    def backward_attention(index):
        lanes = lanes_of(index)

        @pl.when(index == 1)
        def _():
            attend_back(index, True)

        @pl.when(index != 1)
        def _():
            attend_back(index, False)

        through = dot_plain(w_qkv[...], qkv[:, :, :, lanes].reshape(3 * width, piece))

        @pl.when(segment == 1)
        def _():
            for rows in chunks:
                outgoing[index, rows, :] = (wide_b[rows, :] + through[rows]).astype(BF16)
            backward_copy(index).start()

        @pl.when(segment == 0)
        def _():
            free_ends(index)
            for start in range(0, width, LANES):
                rows = slice(start, start + LANES)
                ends_v[lax.rem(index, 2), :, rows] = (wide_b[rows, :] + through[rows]).T
            ends_copy(index).start()

    def held(job):
        group = job // 2
        return (w_down, 0) if group == 0 else (turned, 4 if group == 1 else 0)

    def core_copy(job):
        buffer, base = held(job)
        lanes = lanes_in(job)
        return pltpu.make_async_remote_copy(
            src_ref=buffer.at[pl.ds(base + 2 * (1 - core), 2), :, lanes],
            dst_ref=core_in.at[job // 2, :, :, lanes],
            send_sem=core_send.at[job],
            recv_sem=core_recv.at[job],
            device_id={"rep": other_core},
            device_id_type=MESH,
        )

    def side_copy(job):
        buffer, base = held(job)
        lanes = lanes_in(job)
        return pltpu.make_async_remote_copy(
            src_ref=buffer.at[base + 2 * core + (1 - side), :, lanes],
            dst_ref=side_in.at[job // 2, :, lanes],
            send_sem=side_send.at[job],
            recv_sem=side_recv.at[job],
            device_id={"rep": other_side},
            device_id_type=MESH,
        )

    def dp_copy(job, step):
        buffer, base = held(job)
        lanes = lanes_in(job)
        target = lax.rem(dp + step, dp_count)
        rows = pl.ds(pl.multiple_of(target * share_rows, share_rows), share_rows)
        return pltpu.make_async_remote_copy(
            src_ref=buffer.at[base + 2 * core + side, rows, lanes],
            dst_ref=dp_in.at[job // 2, step - 1, :, lanes],
            send_sem=dp_send.at[job, step - 1],
            recv_sem=dp_recv.at[job, step - 1],
            device_id={"dp": target},
            device_id_type=MESH,
        )

    def join_copy(job):
        lanes = lanes_in(job)
        return pltpu.make_async_remote_copy(
            src_ref=fin.at[job // 2, 2 * core + side, :, lanes],
            dst_ref=fin.at[job // 2, 2 * core + side, :, lanes],
            send_sem=join_send.at[job],
            recv_sem=join_recv.at[job],
            device_id={"rep": other_side},
            device_id_type=MESH,
        )

    def last_copy(job):
        lanes = lanes_in(job)
        return pltpu.make_async_remote_copy(
            src_ref=fin.at[job // 2, pl.ds(2 * core, 2), :, lanes],
            dst_ref=fin.at[job // 2, pl.ds(2 * core, 2), :, lanes],
            send_sem=last_send.at[job],
            recv_sem=last_recv.at[job],
            device_id={"rep": other_core},
            device_id_type=MESH,
        )

    def lanes_in(job):
        half = job % 2
        return slice(half * (width // 2), (half + 1) * (width // 2))

    def down_sums(job):
        part = 4 * share_rows
        count = width // part
        lanes = lanes_in(job)

        def one(block, carry):
            result = dot_turned(active[block], down_grad[lanes, :]).astype(BF16)
            for each in range(count):
                for position in range(4):
                    start = each * part + position * share_rows
                    target = pl.multiple_of((block * count + each) * share_rows, share_rows)
                    w_down[position, pl.ds(target, share_rows), lanes] = result[
                        start : start + share_rows
                    ]
            return carry

        lax.fori_loop(0, 4, one, 0)

    def up_sums(job):
        lanes = lanes_in(job)

        def one(block, carry):
            turned[4 + block, :, lanes] = dot_turned(hidden_low[...], slope[block, lanes, :]).astype(
                BF16
            )
            return carry

        lax.fori_loop(0, 4, one, 0)

    def qkv_sums(job):
        lanes = lanes_in(job)
        half_pairs = slice((job % 2) * (pairs // 2), (job % 2 + 1) * (pairs // 2))

        def one(block, carry):
            turned[block, :, lanes] = dot_turned(
                x_t[...], qkv[block, half_pairs].reshape(width // 2, PIECES * piece)
            ).astype(BF16)
            return carry

        lax.fori_loop(0, 3, one, 0)
        turned[3, :, lanes] = dot_turned(
            mixture[...].reshape(width, PIECES * piece), branch_grad[lanes, :]
        ).astype(BF16)

    def sums_of(job):
        (down_sums, up_sums, qkv_sums)[job // 2](job)
        core_copy(job).start()

    def after_core(job):
        buffer, base = held(job)
        lanes = lanes_in(job)
        copy = core_copy(job)
        copy.wait_send()
        copy.wait_recv()
        first = base + 2 * core + (1 - side)
        buffer[first, :, lanes] = (
            buffer[first, :, lanes].astype(F32) + core_in[job // 2, 1 - side, :, lanes].astype(F32)
        ).astype(BF16)

    def after_side(job):
        buffer, base = held(job)
        lanes = lanes_in(job)
        copy = side_copy(job)
        copy.wait_send()
        copy.wait_recv()
        second = base + 2 * core + side
        buffer[second, :, lanes] = (
            buffer[second, :, lanes].astype(F32)
            + core_in[job // 2, side, :, lanes].astype(F32)
            + side_in[job // 2, :, lanes].astype(F32)
        ).astype(BF16)
        for step in range(1, dp_count):
            dp_copy(job, step).start()

    def after_dp(job):
        buffer, base = held(job)
        lanes = lanes_in(job)
        rows = pl.ds(pl.multiple_of(dp * share_rows, share_rows), share_rows)
        total = buffer[base + 2 * core + side, rows, lanes].astype(F32)
        for step in range(1, dp_count):
            copy = dp_copy(job, step)
            copy.wait_send()
            copy.wait_recv()
            total = total + dp_in[job // 2, step - 1, :, lanes].astype(F32)
        fin[job // 2, 2 * core + side, :, lanes] = total.astype(BF16)
        join_copy(job).start()

    def after_join(job):
        copy = join_copy(job)
        copy.wait_send()
        copy.wait_recv()
        last_copy(job).start()

    def fin_copy(job):
        lanes = lanes_in(job)
        return pltpu.make_async_copy(
            fin.at[job // 2, :, :, lanes], fin_hbm.at[job // 2, :, :, lanes], fin_sem.at[job]
        )

    def after_last(job):
        copy = last_copy(job)
        copy.wait_send()
        copy.wait_recv()
        fin_copy(job).start()

    def early_sums():
        sums_of(0)
        sums_of(1)
        after_core(0)
        side_copy(0).start()
        sums_of(2)
        sums_of(3)
        after_core(1)
        side_copy(1).start()

    def one_step(step, carry):
        first_index = jnp.where(step < 4, step, jnp.where(step < 6, 5 - step, step - 4))
        last_index = jnp.where(step < 2, step, jnp.where(step < 4, 3 - step, lax.div(step, 2)))
        first_is = jnp.where(step < 4, 1, 0)
        last_is = jnp.where(step < 2, 1, jnp.where(step < 4, 0, 1 - lax.rem(step, 2)))
        index = jnp.minimum(jnp.where(segment == 0, first_index, last_index), PIECES - 1)
        is_forward = jnp.where(segment == 0, first_is, last_is)
        is_last = jnp.where(step == 2 * PIECES, 1, 0)
        is_split = jnp.where(step >= 2 * PIECES - 1, 1 - segment, 0)

        @pl.when(is_forward * (1 - is_last) == 1)
        def _():
            forward(index)

        @pl.when(is_forward + is_last == 0)
        def _():
            backward(index)

        @pl.when(is_last == 1)
        def _():
            early_sums()

        @pl.when((1 - is_forward) * (1 - is_split) * (1 - is_last) + is_last * is_split == 1)
        def _():
            backward_attention(index)

        return carry

    lax.fori_loop(0, 2 * PIECES + 1, one_step, 0)

    def small_dp_copy(step):
        target = lax.rem(dp + step, dp_count)
        return pltpu.make_async_remote_copy(
            src_ref=small.at[target],
            dst_ref=small_dp.at[step - 1],
            send_sem=sdp_send.at[step - 1],
            recv_sem=sdp_recv.at[step - 1],
            device_id={"dp": target},
            device_id_type=MESH,
        )

    def small_rep_copy(step):
        return pltpu.make_async_remote_copy(
            src_ref=small_rep.at[rep],
            dst_ref=small_rep.at[rep],
            send_sem=srep_send.at[step - 1],
            recv_sem=srep_recv.at[step - 1],
            device_id={"rep": lax.rem(rep + step, 4)},
            device_id_type=MESH,
        )

    sums_of(4)
    sums_of(5)
    after_core(2)
    after_side(0)
    side_copy(2).start()

    rows_of = [jnp.sum(sums[index].T, axis=0, keepdims=True) for index in range(STATS)]
    small[...] = jnp.zeros(small.shape, F32)
    for share_index in range(dp_count):
        for index in range(BIAS_UP):
            start = share_index * share_rows
            small[share_index, index : index + 1, :share_rows] = rows_of[index][
                :, start : start + share_rows
            ]
        for part in range(4):
            start = (share_index * 4 + part) * share_rows
            block, start = start // width, start % width
            small[share_index, BIAS_UP + part : BIAS_UP + part + 1, :share_rows] = rows_of[
                BIAS_UP + block
            ][:, start : start + share_rows]
    for step in range(1, dp_count):
        small_dp_copy(step).start()


    after_core(3)
    after_side(1)
    side_copy(3).start()
    small_total = small[dp]
    for step in range(1, dp_count):
        copy = small_dp_copy(step)
        copy.wait_send()
        copy.wait_recv()
        small_total = small_total + small_dp[step - 1]
    small_rep[rep] = small_total
    for step in range(1, 4):
        small_rep_copy(step).start()
    after_core(4)
    after_dp(0)
    after_side(2)
    side_copy(4).start()
    after_core(5)
    after_dp(1)
    after_join(0)
    after_side(3)
    side_copy(5).start()
    after_last(0)
    after_dp(2)
    after_join(1)
    after_side(4)
    after_last(1)
    after_dp(3)
    after_join(2)
    for step in range(1, 4):
        copy = small_rep_copy(step)
        copy.wait_send()
        copy.wait_recv()
    small_out[...] = (small_rep[0] + small_rep[1]) + (small_rep[2] + small_rep[3])
    small_copy = pltpu.make_async_copy(small_out, small_hbm, load_sem.at[0])
    small_copy.start()
    after_side(5)
    after_last(2)
    after_dp(4)
    after_join(3)
    after_last(3)
    after_dp(5)
    after_join(4)
    after_last(4)
    after_join(5)
    after_last(5)

    for index in range(PIECES):

        @pl.when(segment == 0)
        def _():
            forward_copy(index).wait_send()

        @pl.when(segment == 1)
        def _():
            backward_copy(index).wait_send()

    for index in range(2, PIECES):
        ends_copy(index).wait()
    for job in range(6):
        fin_copy(job).wait()
    small_copy.wait()


def finish_kernel(
    flag_ref,
    ends_in,
    fin,
    small,
    ends,
    grad_qkv,
    grad_out,
    grad_up,
    grad_down,
    grad_up_bias,
    grad_gains,
    grad_biases,
    ends_v,
    fin_v,
    wide_qkv,
    wide_out,
    wide_up,
    wide_down,
    ends_sem,
    in_sem,
    out_sem,
):
    half = ends_in.shape[0] // 2
    share_rows, width = fin.shape[2:]
    start = pl.multiple_of(half * (1 - flag_ref[0, 0]), half)
    ends_copies = [
        pltpu.make_async_copy(
            ends_v.at[pl.ds(0, half)], ends.at[0, pl.ds(start, half)], ends_sem.at[0]
        ),
        pltpu.make_async_copy(
            ends_v.at[pl.ds(half, half)], ends.at[0, pl.ds(half - start, half)], ends_sem.at[1]
        ),
    ]
    ends_loads = [
        pltpu.make_async_copy(
            ends_in.at[pl.ds(part * half, half)],
            ends_v.at[pl.ds(part * half, half)],
            ends_sem.at[2 + part],
        )
        for part in range(2)
    ]
    loads = [
        pltpu.make_async_copy(fin.at[group], fin_v.at[group], in_sem.at[group])
        for group in range(3)
    ]
    stores = [
        pltpu.make_async_copy(wide, target.at[0], out_sem.at[index])
        for index, (wide, target) in enumerate(
            ((wide_down, grad_down), (wide_up, grad_up), (wide_qkv, grad_qkv), (wide_out, grad_out))
        )
    ]
    for copy in loads + ends_loads:
        copy.start()
    for load, copy in zip(ends_loads, ends_copies):
        load.wait()
        copy.start()
    loads[0].wait()
    for position in range(4):
        rows = slice(position * share_rows, (position + 1) * share_rows)
        wide_down[rows, :] = fin_v[0, position].astype(F32)
    stores[0].start()
    loads[1].wait()
    for position in range(4):
        wide_up[:, position * width : (position + 1) * width] = fin_v[1, position].astype(F32)
    stores[1].start()
    loads[2].wait()
    for position in range(3):
        wide_qkv[:, position * width : (position + 1) * width] = fin_v[2, position].astype(F32)
    stores[2].start()
    wide_out[...] = fin_v[2, 3].astype(F32)
    stores[3].start()
    for position in range(4):
        rows = slice(position * share_rows, (position + 1) * share_rows)
        grad_up_bias[:, rows] = small[BIAS_UP + position : BIAS_UP + position + 1, :share_rows]
    grad_gains[0] = small[:2, :share_rows]
    grad_biases[0] = small[2:BIAS_UP, :share_rows]
    for copy in stores + ends_copies:
        copy.wait()


def on_device(
    dp_count,
    block_input,
    cotangent,
    window_group,
    w_qkv,
    w_out,
    w_up,
    w_down,
    up_bias,
    norm_gains,
    biases,
):
    rows, width = block_input.shape
    piece = rows // PIECES
    pairs = width // LANES
    share_rows = width // dp_count
    small_width = max(share_rows, LANES)
    any_spec = pl.BlockSpec(memory_space=pl.ANY)
    vmem_spec = pl.BlockSpec(memory_space=pltpu.VMEM)
    smem_spec = pl.BlockSpec(memory_space=pltpu.SMEM)
    dma = pltpu.SemaphoreType.DMA
    vmem = pltpu.VMEM
    ends_in, fin, small = pl.pallas_call(
        functools.partial(layer_kernel, dp_count),
        out_shape=(
            jax.ShapeDtypeStruct((PIECES, piece, width), F32),
            jax.ShapeDtypeStruct((3, 4, share_rows, width), BF16),
            jax.ShapeDtypeStruct((16, small_width), F32),
        ),
        in_specs=[smem_spec] + [any_spec] * 6 + [vmem_spec] * 3,
        out_specs=(any_spec,) * 3,
        scratch_shapes=[
            vmem((width, 3 * width), BF16),
            vmem((width, width), BF16),
            vmem((width, 4 * width), BF16),
            vmem((4, width, width), BF16),
            vmem((8, width, width), BF16),
            vmem((width, 4 * width), BF16),
            vmem((PIECES, piece, width), BF16),
            vmem((width, rows), BF16),
            vmem((3, pairs, LANES, rows), BF16),
            vmem((PIECES, pairs, piece, LANES), BF16),
            vmem((PIECES, pairs, piece, LANES), BF16),
            vmem((PIECES, pairs, 2, piece, piece), BF16),
            vmem((pairs, 2, piece, piece), BF16),
            vmem((pairs, LANES, rows), BF16),
            vmem((width, rows), F32),
            vmem((width, rows), F32),
            vmem((PIECES, 2, 1, piece), F32),
            vmem((width, rows), BF16),
            vmem((4, width, rows), BF16),
            vmem((4, width, rows), BF16),
            vmem((width, rows), BF16),
            vmem((width, rows), BF16),
            vmem((pairs, LANES, piece), BF16),
            vmem((PIECES, width, piece), BF16),
            vmem((PIECES, width, piece), BF16),
            vmem((STATS, width, LANES), BF16),
            vmem((STATS, width, LANES), F32),
            vmem((2, 2, pairs, LANES, piece), F32),
            vmem((4, piece, piece), BF16),
            vmem((width, piece), F32),
            vmem((width, piece), F32),
            vmem((2, piece, width), F32),
            vmem((3, 2, width, width), BF16),
            vmem((3, width, width), BF16),
            vmem((3, dp_count - 1, share_rows, width), BF16),
            vmem((3, 4, share_rows, width), BF16),
            vmem((dp_count, 16, small_width), F32),
            vmem((dp_count - 1, 16, small_width), F32),
            vmem((4, 16, small_width), F32),
            vmem((16, small_width), F32),
            dma((8,)),
            dma((PIECES,)),
            dma((PIECES,)),
            dma((PIECES,)),
            dma((6,)),
            dma((6,)),
            dma((6,)),
            dma((6,)),
            dma((6, dp_count - 1)),
            dma((6, dp_count - 1)),
            dma((6,)),
            dma((6,)),
            dma((6,)),
            dma((6,)),
            dma((dp_count - 1,)),
            dma((dp_count - 1,)),
            dma((3,)),
            dma((3,)),
            dma((6,)),
        ],
        compiler_params=pltpu.CompilerParams(
            collective_id=0, has_side_effects=True, vmem_limit_bytes=63 * 1024 * 1024
        ),
    )(
        window_group,
        block_input.reshape(PIECES, piece, width),
        cotangent.reshape(PIECES, piece, width),
        w_qkv,
        w_out,
        w_up,
        w_down,
        up_bias,
        norm_gains,
        biases,
    )
    return pl.pallas_call(
        finish_kernel,
        out_shape=(
            jax.ShapeDtypeStruct((1, rows, width), F32),
            jax.ShapeDtypeStruct((1, share_rows, 3 * width), F32),
            jax.ShapeDtypeStruct((1, share_rows, width), F32),
            jax.ShapeDtypeStruct((1, share_rows, 4 * width), F32),
            jax.ShapeDtypeStruct((1, 4 * share_rows, width), F32),
            jax.ShapeDtypeStruct((1, 4 * share_rows), F32),
            jax.ShapeDtypeStruct((1, 2, share_rows), F32),
            jax.ShapeDtypeStruct((1, 4, share_rows), F32),
        ),
        in_specs=[smem_spec, any_spec, any_spec, vmem_spec],
        out_specs=(any_spec,) * 5 + (vmem_spec,) * 3,
        scratch_shapes=[
            vmem((rows, width), F32),
            vmem((3, 4, share_rows, width), BF16),
            vmem((share_rows, 3 * width), F32),
            vmem((share_rows, width), F32),
            vmem((share_rows, 4 * width), F32),
            vmem((4 * share_rows, width), F32),
            dma((4,)),
            dma((3,)),
            dma((4,)),
        ],
        compiler_params=pltpu.CompilerParams(vmem_limit_bytes=63 * 1024 * 1024),
    )(window_group, ends_in.reshape(rows, width), fin, small)


def solution(mesh):
    return jax.shard_map(
        functools.partial(on_device, mesh.shape["dp"]),
        mesh=mesh,
        in_specs=(
            P(("dp", "rep"), None),
            P(("dp", "rep"), None),
            P(("dp", "rep"), None),
            P("segment", None, None),
            P("segment", None, None),
            P("segment", None, None),
            P("segment", None, None),
            P("segment", None),
            P("segment", None, None),
            P("segment", None, None),
        ),
        out_specs=(
            P("segment", ("dp", "rep"), None),
            P("segment", "dp", None),
            P("segment", "dp", None),
            P("segment", "dp", None),
            P("segment", "dp", None),
            P("segment", "dp"),
            P("segment", None, "dp"),
            P("segment", None, "dp"),
        ),
        check_vma=False,
    )
```

```python
import functools
import math

import jax
import jax.numpy as jnp
from jax import lax
from jax.experimental import pallas as pl
from jax.experimental.pallas import tpu as pltpu
from jax.sharding import PartitionSpec as P

MESH = pl.DeviceIdType.MESH
F32 = jnp.float32
BF16 = jnp.bfloat16
HEADS = 8
LANES = 128
PIECES = 4
EPS = 1e-05
GAIN_ONE, GAIN_TWO, BIAS_OUT, BIAS_ONE, BIAS_DOWN, BIAS_TWO, BIAS_UP = range(7)
STATS = 10
CHUNK = 64


def dot_plain(left, right):
    return lax.dot_general(left, right, (((1,), (0,)), ((), ())), preferred_element_type=F32)


def dot_turned(left, right):
    return lax.dot_general(left, right, (((1,), (1,)), ((), ())), preferred_element_type=F32)


def fold(values):
    total = values[:, :LANES]
    for start in range(LANES, values.shape[1], LANES):
        total = total + values[:, start : start + LANES]
    return total


def normal_level(values, bell):
    depth = 1.0 + jnp.abs(values) * (0.3275911 / math.sqrt(2.0))
    near = pl.reciprocal(depth, approx=True)
    near = near * (2.0 - depth * near)
    series = near * (0.5 * 1.061405429) + (0.5 * -1.453152027)
    for factor in (1.421413741, -0.284496736, 0.254829592):
        series = series * near + 0.5 * factor
    upper = series * near * bell
    return jnp.where(values < 0.0, upper, 1.0 - upper)


def pair_blocks(values):
    half = values.shape[0] // 2
    blank = jnp.zeros((half, values.shape[1]), values.dtype)
    first = jnp.concatenate([values[:half], blank], axis=0)
    second = jnp.concatenate([blank, values[half:]], axis=0)
    return jnp.concatenate([first, second], axis=1)


def layer_kernel(
    dp_count,
    flag_ref,
    x_hbm,
    ct_hbm,
    w_qkv_hbm,
    w_out_hbm,
    w_up_hbm,
    w_down_hbm,
    up_bias_ref,
    gains_ref,
    biases_ref,
    ends_hbm,
    fin_hbm,
    small_hbm,
    w_qkv,
    w_out,
    w_up,
    w_down,
    turned,
    down_turned,
    rows_in,
    x_t,
    qkv,
    keys_rm,
    values_rm,
    share,
    share_off,
    mixture,
    norm_one,
    norm_two,
    inverses,
    hidden_low,
    slope,
    active,
    down_grad,
    branch_grad,
    grad_mix,
    outgoing,
    incoming_grad,
    columns,
    sums,
    key_sums,
    score_grad,
    wide_a,
    wide_b,
    ends_v,
    core_in,
    side_in,
    dp_in,
    fin,
    small,
    small_dp,
    small_rep,
    small_out,
    load_sem,
    seg_send,
    seg_recv,
    ends_sem,
    core_send,
    core_recv,
    side_send,
    side_recv,
    dp_send,
    dp_recv,
    join_send,
    join_recv,
    last_send,
    last_recv,
    sdp_send,
    sdp_recv,
    srep_send,
    srep_recv,
    fin_sem,
):
    width = w_out.shape[0]
    piece = x_t.shape[1] // PIECES
    pairs = qkv.shape[1]
    share_rows = width // dp_count
    segment = lax.axis_index("segment")
    dp = lax.axis_index("dp")
    rep = lax.axis_index("rep")
    core = lax.rem(rep, 2)
    side = lax.div(rep, 2)
    other_core = side * 2 + (1 - core)
    other_side = (1 - side) * 2 + core

    loads = [
        (w_qkv_hbm.at[0], w_qkv),
        (w_out_hbm.at[0], w_out),
        (w_up_hbm.at[0], w_up),
    ]
    for block in range(4):
        loads.append((w_down_hbm.at[0, pl.ds(block * width, width), :], w_down.at[block]))
    load_copies = [
        pltpu.make_async_copy(source, target, load_sem.at[index + 1])
        for index, (source, target) in enumerate(loads)
    ]
    first_rows = pltpu.make_async_copy(x_hbm, rows_in, load_sem.at[0])
    last_rows = pltpu.make_async_copy(ct_hbm, rows_in, load_sem.at[0])

    @pl.when(segment == 0)
    def _():
        first_rows.start()

    @pl.when(segment == 1)
    def _():
        last_rows.start()

    for copy in load_copies:
        copy.start()

    barrier = pltpu.get_barrier_semaphore()
    pl.semaphore_signal(
        barrier, inc=1, device_id={"segment": 1 - segment}, device_id_type=MESH
    )
    for step in range(1, 4):
        pl.semaphore_signal(
            barrier, inc=1, device_id={"rep": lax.rem(rep + step, 4)}, device_id_type=MESH
        )
    for step in range(1, dp_count):
        pl.semaphore_signal(
            barrier, inc=1, device_id={"dp": lax.rem(dp + step, dp_count)}, device_id_type=MESH
        )

    params = [gains_ref[0].astype(F32), biases_ref[0].astype(F32)]
    for block in range(4):
        params.append(up_bias_ref[:, block * width : (block + 1) * width].astype(F32))
    params.append(jnp.zeros((16 - STATS, width), F32))
    upright = jnp.concatenate(params, axis=0).T
    for index in range(STATS):
        columns[index] = jnp.broadcast_to(upright[:, index : index + 1], (width, LANES)).astype(BF16)
    for index in range(STATS):
        sums[index] = jnp.zeros((width, LANES), F32)
    key_sums[0] = jnp.zeros(key_sums.shape[1:], F32)

    chunks = [slice(start, start + CHUNK) for start in range(0, width, CHUNK)]

    for copy in load_copies:
        copy.wait()
    first_rows.wait()

    for block in range(3):
        turned[block] = w_qkv[:, block * width : (block + 1) * width].T
    turned[3] = w_out[...].T
    for block in range(4):
        turned[4 + block] = w_up[:, block * width : (block + 1) * width].T
    for block in range(4):
        down_turned[:, block * width : (block + 1) * width] = w_down[block].T

    pl.semaphore_wait(barrier, 4 + dp_count - 1)

    flag = flag_ref[0, 0].astype(F32)

    def lanes_of(index):
        return pl.ds(pl.multiple_of(index * piece, piece), piece)

    def forward_copy(index):
        return pltpu.make_async_remote_copy(
            src_ref=outgoing.at[index],
            dst_ref=x_t.at[:, lanes_of(index)],
            send_sem=seg_send.at[index],
            recv_sem=seg_recv.at[index],
            device_id={"segment": 1 - segment},
            device_id_type=MESH,
        )

    def backward_copy(index):
        return pltpu.make_async_remote_copy(
            src_ref=outgoing.at[index],
            dst_ref=incoming_grad.at[index],
            send_sem=seg_send.at[index],
            recv_sem=seg_recv.at[index],
            device_id={"segment": 1 - segment},
            device_id_type=MESH,
        )

    def ends_copy(index):
        return pltpu.make_async_copy(
            ends_v.at[lax.rem(index, 2)], ends_hbm.at[index], ends_sem.at[index]
        )

    def free_ends(index):
        @pl.when(index >= 2)
        def _():
            ends_copy(index - 2).wait()

    def own_rows(index):
        half = lax.rem(index, 2)
        whole = jnp.where(index < 2, 1.0, 0.0).astype(F32)
        weight = whole * flag + (1.0 - whole) * (1.0 - flag)
        picked = rows_in[half].astype(F32) * weight + rows_in[2 + half].astype(F32) * (1.0 - weight)
        return picked.T

    def attend(index, has_off):
        lanes = lanes_of(index)
        half = LANES // 2
        key_at = lax.broadcasted_iota(jnp.int32, (LANES, LANES), 0)
        query_at = lax.broadcasted_iota(jnp.int32, (LANES, LANES), 1)
        allowed = key_at <= query_at
        blank = jnp.zeros((LANES, LANES), BF16)
        def one_pair(pair, carry):
            queries = pair_blocks(qkv[0, pair, :, lanes])
            scores = dot_plain(keys_rm[index, pair], queries)
            if has_off:
                scores_off = dot_plain(keys_rm[0, pair], queries)
            for head in range(2):
                rows = slice(head * half, (head + 1) * half)
                for part in range(2):
                    start = head * piece + part * LANES
                    span = slice(start, start + LANES)
                    place = slice(part * LANES, (part + 1) * LANES)
                    tiles = [jnp.where(allowed, scores[place, span], -1e30)]
                    if part:
                        tiles.append(scores[:LANES, span])
                    if has_off:
                        tiles.append(scores_off[:LANES, span])
                        tiles.append(scores_off[LANES:, span])
                    top = functools.reduce(jnp.maximum, tiles)
                    top = jnp.max(top, axis=0, keepdims=True)
                    raised = [jnp.exp(tile - top) for tile in tiles]
                    total = functools.reduce(jnp.add, raised)
                    scale = 1.0 / jnp.sum(total, axis=0, keepdims=True)
                    low = [(tile * scale).astype(BF16) for tile in raised]
                    share[index, pair, head, place, place] = low[0]
                    if part:
                        share[index, pair, head, :LANES, place] = low[1]
                    else:
                        share[index, pair, head, LANES:, place] = blank
                    if has_off:
                        share_off[pair, head, :LANES, place] = low[-2]
                        share_off[pair, head, LANES:, place] = low[-1]
                mixed = dot_plain(qkv[2, pair, rows, lanes], share[index, pair, head])
                if has_off:
                    mixed = mixed + dot_plain(qkv[2, pair, rows, :piece], share_off[pair, head])
                mixture[pair, rows, lanes] = mixed.astype(BF16)
            return carry

        lax.fori_loop(0, pairs, one_pair, 0)

    def part_sum(values):
        return jnp.sum(values.reshape(values.shape[0] // 8, 8, values.shape[1]), axis=0)

    def full_mean(parts):
        return jnp.sum(parts, axis=0, keepdims=True) * (1.0 / width)

    def column(index, rows):
        part = columns[index, rows, :].astype(F32)
        return jnp.concatenate([part] * (piece // LANES), axis=1)

    def gather_sum(index, rows, values):
        sums[index, rows, :] = sums[index, rows, :] + fold(values)

    def norm_chunks(index, which, total):
        mean = full_mean(total)
        spread = jnp.zeros((8, piece), F32)
        for rows in chunks:
            centred = wide_a[rows, :] - mean
            spread = spread + part_sum(centred * centred)
        inverse = lax.rsqrt(full_mean(spread) + EPS)
        inverses[index, which] = inverse
        return mean, inverse

    def forward(index):
        lanes = lanes_of(index)

        @pl.when(segment == 0)
        def _():
            x_t[:, lanes] = own_rows(index).astype(BF16)

        @pl.when(segment == 1)
        def _():
            forward_copy(index).wait_recv()

        inputs = x_t[:, lanes]
        score_scale = 1.0 / math.sqrt(width // HEADS)
        for block in range(3):
            result = dot_plain(turned[block], inputs)
            for pair in range(pairs):
                low = result[pair * LANES : (pair + 1) * LANES]
                low = (low * score_scale if block == 0 else low).astype(BF16)
                qkv[block, pair, :, lanes] = low
                if block == 1:
                    keys_rm[index, pair] = low.T
                if block == 2:
                    values_rm[index, pair] = low.T

        @pl.when(index == 1)
        def _():
            attend(index, True)

        @pl.when(index != 1)
        def _():
            attend(index, False)

        branch = dot_plain(turned[3], mixture[:, :, lanes].reshape(width, piece))
        total = jnp.zeros((8, piece), F32)
        for rows in chunks:
            sum_one = x_t[rows, lanes].astype(F32) + (branch[rows] + column(BIAS_OUT, rows))
            wide_a[rows, :] = sum_one
            total = total + part_sum(sum_one)
        mean, inverse = norm_chunks(index, 0, total)
        for rows in chunks:
            normed = (wide_a[rows, :] - mean) * inverse
            norm_one[rows, lanes] = normed
            hidden = normed * column(GAIN_ONE, rows) + column(BIAS_ONE, rows)
            hidden_low[rows, lanes] = hidden.astype(BF16)

        def activate(block, pre_block):
            for rows in chunks:
                pre = pre_block[rows] + column(BIAS_UP + block, rows)
                bell = jnp.exp2(pre * pre * (-0.5 * math.log2(math.e)))
                level = (lax.erf(pre * (1.0 / math.sqrt(2.0))) + 1.0) * 0.5
                active[block, rows, lanes] = (pre * level).astype(BF16)
                slope[block, rows, lanes] = (
                    level + pre * bell * (1.0 / math.sqrt(2.0 * math.pi))
                ).astype(BF16)

        def up_block(block, carry):
            activate(block, dot_plain(turned[4 + block], hidden_low[:, lanes]))
            return carry

        lax.fori_loop(0, 4, up_block, 0)
        branch_two = dot_plain(down_turned[...], active[:, :, lanes].reshape(4 * width, piece))
        total = jnp.zeros((8, piece), F32)
        for rows in chunks:
            hidden = norm_one[rows, lanes] * column(GAIN_ONE, rows) + column(BIAS_ONE, rows)
            sum_two = hidden + (branch_two[rows] + column(BIAS_DOWN, rows))
            wide_a[rows, :] = sum_two
            total = total + part_sum(sum_two)
        mean, inverse = norm_chunks(index, 1, total)

        def outputs(rows):
            normed = (wide_a[rows, :] - mean) * inverse
            norm_two[rows, lanes] = normed
            return normed * column(GAIN_TWO, rows) + column(BIAS_TWO, rows)

        @pl.when(segment == 0)
        def _():
            for rows in chunks:
                outgoing[index, rows, :] = outputs(rows).astype(BF16)
            forward_copy(index).start()

        @pl.when(segment == 1)
        def _():
            free_ends(index)
            for start in range(0, width, LANES):
                rows = slice(start, start + LANES)
                ends_v[lax.rem(index, 2), :, rows] = outputs(rows).T
            ends_copy(index).start()

    def attend_back(index, has_off):
        lanes = lanes_of(index)
        slot = jnp.where(index == 0, 1, 0)
        half = LANES // 2
        score_scale = 1.0 / math.sqrt(width // HEADS)
        blank = jnp.zeros((LANES, LANES), BF16)
        def one_pair(pair, carry):
            grads = grad_mix[pair]
            blocks = pair_blocks(grads)
            back = dot_plain(values_rm[index, pair], blocks)
            if has_off:
                back_off = dot_plain(values_rm[0, pair], blocks)
            for head in range(2):
                rows = slice(head * half, (head + 1) * half)
                for part in range(2):
                    start = head * piece + part * LANES
                    span = slice(start, start + LANES)
                    place = slice(part * LANES, (part + 1) * LANES)
                    shares = [share[index, pair, head, place, place].astype(F32)]
                    backs = [back[place, span]]
                    if part:
                        shares.append(share[index, pair, head, :LANES, place].astype(F32))
                        backs.append(back[:LANES, span])
                    if has_off:
                        for low_half in range(2):
                            keys = slice(low_half * LANES, (low_half + 1) * LANES)
                            shares.append(share_off[pair, head, keys, place].astype(F32))
                            backs.append(back_off[keys, span])
                    products = [left * right for left, right in zip(shares, backs)]
                    inner = jnp.sum(functools.reduce(jnp.add, products), axis=0, keepdims=True)
                    low = [
                        (product - left * inner).astype(BF16)
                        for product, left in zip(products, shares)
                    ]
                    score_grad[head, place, place] = low[0]
                    if part:
                        score_grad[head, :LANES, place] = low[1]
                    else:
                        score_grad[head, LANES:, place] = blank
                    if has_off:
                        score_grad[2 + head, :LANES, place] = low[-2]
                        score_grad[2 + head, LANES:, place] = low[-1]
                queries = qkv[0, pair, rows, lanes]
                grad_scores = score_grad[head]
                grad_query = dot_plain(qkv[1, pair, rows, lanes], grad_scores)
                grad_key = dot_turned(queries, grad_scores) + key_sums[slot, 0, pair, rows]
                grad_value = (
                    dot_turned(grads[rows], share[index, pair, head])
                    + key_sums[slot, 1, pair, rows]
                )
                if has_off:
                    grad_off = score_grad[2 + head]
                    grad_query = grad_query + dot_plain(qkv[1, pair, rows, :piece], grad_off)
                    key_sums[1, 0, pair, rows] = dot_turned(queries, grad_off)
                    key_sums[1, 1, pair, rows] = dot_turned(grads[rows], share_off[pair, head])
                qkv[0, pair, rows, lanes] = (grad_query * score_scale).astype(BF16)
                qkv[1, pair, rows, lanes] = grad_key.astype(BF16)
                qkv[2, pair, rows, lanes] = grad_value.astype(BF16)
            return carry

        lax.fori_loop(0, pairs, one_pair, 0)

    def backward(index):
        lanes = lanes_of(index)

        @pl.when(segment == 1)
        def _():
            incoming_grad[index] = own_rows(index).astype(BF16)

        @pl.when(segment == 0)
        def _():
            backward_copy(index).wait_recv()

        plain = jnp.zeros((8, piece), F32)
        inner = jnp.zeros((8, piece), F32)
        for rows in chunks:
            grad = incoming_grad[index, rows, :].astype(F32)
            product = grad * norm_two[rows, lanes]
            gather_sum(GAIN_TWO, rows, product)
            gather_sum(BIAS_TWO, rows, grad)
            gain = column(GAIN_TWO, rows)
            plain = plain + part_sum(grad * gain)
            inner = inner + part_sum(product * gain)
        plain = full_mean(plain)
        inner = full_mean(inner)
        inverse = inverses[index, 1]
        for rows in chunks:
            scaled = incoming_grad[index, rows, :].astype(F32) * column(GAIN_TWO, rows)
            grad_two = (scaled - plain - norm_two[rows, lanes] * inner) * inverse
            gather_sum(BIAS_DOWN, rows, grad_two)
            wide_a[rows, :] = grad_two
            down_grad[rows, lanes] = grad_two.astype(BF16)

        def down_block(block, carry):
            back = dot_plain(w_down[block], down_grad[:, lanes])
            for rows in chunks:
                grad_pre = back[rows] * slope[block, rows, lanes].astype(F32)
                gather_sum(BIAS_UP + block, rows, grad_pre)
                slope[block, rows, lanes] = grad_pre.astype(BF16)
            return carry

        lax.fori_loop(0, 4, down_block, 0)

        through = dot_plain(w_up[...], slope[:, :, lanes].reshape(4 * width, piece))
        plain = jnp.zeros((8, piece), F32)
        inner = jnp.zeros((8, piece), F32)
        for rows in chunks:
            grad_hidden = wide_a[rows, :] + through[rows]
            wide_a[rows, :] = grad_hidden
            product = grad_hidden * norm_one[rows, lanes]
            gather_sum(GAIN_ONE, rows, product)
            gather_sum(BIAS_ONE, rows, grad_hidden)
            gain = column(GAIN_ONE, rows)
            plain = plain + part_sum(grad_hidden * gain)
            inner = inner + part_sum(product * gain)
        plain = full_mean(plain)
        inner = full_mean(inner)
        inverse = inverses[index, 0]
        for rows in chunks:
            scaled = wide_a[rows, :] * column(GAIN_ONE, rows)
            grad_one = (scaled - plain - norm_one[rows, lanes] * inner) * inverse
            gather_sum(BIAS_OUT, rows, grad_one)
            wide_b[rows, :] = grad_one
            branch_grad[rows, lanes] = grad_one.astype(BF16)
        grad_mix[...] = (
            dot_plain(w_out[...], branch_grad[:, lanes]).astype(BF16).reshape(pairs, LANES, piece)
        )

    def backward_attention(index):
        lanes = lanes_of(index)

        @pl.when(index == 1)
        def _():
            attend_back(index, True)

        @pl.when(index != 1)
        def _():
            attend_back(index, False)

        through = dot_plain(w_qkv[...], qkv[:, :, :, lanes].reshape(3 * width, piece))

        @pl.when(segment == 1)
        def _():
            for rows in chunks:
                outgoing[index, rows, :] = (wide_b[rows, :] + through[rows]).astype(BF16)
            backward_copy(index).start()

        @pl.when(segment == 0)
        def _():
            free_ends(index)
            for start in range(0, width, LANES):
                rows = slice(start, start + LANES)
                ends_v[lax.rem(index, 2), :, rows] = (wide_b[rows, :] + through[rows]).T
            ends_copy(index).start()

    def held(job):
        group = job // 2
        return (w_down, 0) if group == 0 else (turned, 4 if group == 1 else 0)

    def core_copy(job):
        buffer, base = held(job)
        lanes = lanes_in(job)
        return pltpu.make_async_remote_copy(
            src_ref=buffer.at[pl.ds(base + 2 * (1 - core), 2), :, lanes],
            dst_ref=core_in.at[job // 2, :, :, lanes],
            send_sem=core_send.at[job],
            recv_sem=core_recv.at[job],
            device_id={"rep": other_core},
            device_id_type=MESH,
        )

    def side_copy(job):
        buffer, base = held(job)
        lanes = lanes_in(job)
        return pltpu.make_async_remote_copy(
            src_ref=buffer.at[base + 2 * core + (1 - side), :, lanes],
            dst_ref=side_in.at[job // 2, :, lanes],
            send_sem=side_send.at[job],
            recv_sem=side_recv.at[job],
            device_id={"rep": other_side},
            device_id_type=MESH,
        )

    def dp_copy(job, step):
        buffer, base = held(job)
        lanes = lanes_in(job)
        target = lax.rem(dp + step, dp_count)
        rows = pl.ds(pl.multiple_of(target * share_rows, share_rows), share_rows)
        return pltpu.make_async_remote_copy(
            src_ref=buffer.at[base + 2 * core + side, rows, lanes],
            dst_ref=dp_in.at[job // 2, step - 1, :, lanes],
            send_sem=dp_send.at[job, step - 1],
            recv_sem=dp_recv.at[job, step - 1],
            device_id={"dp": target},
            device_id_type=MESH,
        )

    def join_copy(job):
        lanes = lanes_in(job)
        return pltpu.make_async_remote_copy(
            src_ref=fin.at[job // 2, 2 * core + side, :, lanes],
            dst_ref=fin.at[job // 2, 2 * core + side, :, lanes],
            send_sem=join_send.at[job],
            recv_sem=join_recv.at[job],
            device_id={"rep": other_side},
            device_id_type=MESH,
        )

    def last_copy(job):
        lanes = lanes_in(job)
        return pltpu.make_async_remote_copy(
            src_ref=fin.at[job // 2, pl.ds(2 * core, 2), :, lanes],
            dst_ref=fin.at[job // 2, pl.ds(2 * core, 2), :, lanes],
            send_sem=last_send.at[job],
            recv_sem=last_recv.at[job],
            device_id={"rep": other_core},
            device_id_type=MESH,
        )

    def lanes_in(job):
        half = job % 2
        return slice(half * (width // 2), (half + 1) * (width // 2))

    def down_sums(job):
        part = 4 * share_rows
        count = width // part
        lanes = lanes_in(job)

        def one(block, carry):
            result = dot_turned(active[block], down_grad[lanes, :]).astype(BF16)
            for each in range(count):
                for position in range(4):
                    start = each * part + position * share_rows
                    target = pl.multiple_of((block * count + each) * share_rows, share_rows)
                    w_down[position, pl.ds(target, share_rows), lanes] = result[
                        start : start + share_rows
                    ]
            return carry

        lax.fori_loop(0, 4, one, 0)

    def up_sums(job):
        lanes = lanes_in(job)

        def one(block, carry):
            turned[4 + block, :, lanes] = dot_turned(hidden_low[...], slope[block, lanes, :]).astype(
                BF16
            )
            return carry

        lax.fori_loop(0, 4, one, 0)

    def qkv_sums(job):
        lanes = lanes_in(job)
        half_pairs = slice((job % 2) * (pairs // 2), (job % 2 + 1) * (pairs // 2))

        def one(block, carry):
            turned[block, :, lanes] = dot_turned(
                x_t[...], qkv[block, half_pairs].reshape(width // 2, PIECES * piece)
            ).astype(BF16)
            return carry

        lax.fori_loop(0, 3, one, 0)
        turned[3, :, lanes] = dot_turned(
            mixture[...].reshape(width, PIECES * piece), branch_grad[lanes, :]
        ).astype(BF16)

    def sums_of(job):
        (down_sums, up_sums, qkv_sums)[job // 2](job)
        core_copy(job).start()

    def after_core(job):
        buffer, base = held(job)
        lanes = lanes_in(job)
        copy = core_copy(job)
        copy.wait_send()
        copy.wait_recv()
        first = base + 2 * core + (1 - side)
        buffer[first, :, lanes] = (
            buffer[first, :, lanes].astype(F32) + core_in[job // 2, 1 - side, :, lanes].astype(F32)
        ).astype(BF16)

    def after_side(job):
        buffer, base = held(job)
        lanes = lanes_in(job)
        copy = side_copy(job)
        copy.wait_send()
        copy.wait_recv()
        second = base + 2 * core + side
        buffer[second, :, lanes] = (
            buffer[second, :, lanes].astype(F32)
            + core_in[job // 2, side, :, lanes].astype(F32)
            + side_in[job // 2, :, lanes].astype(F32)
        ).astype(BF16)
        for step in range(1, dp_count):
            dp_copy(job, step).start()

    def after_dp(job):
        buffer, base = held(job)
        lanes = lanes_in(job)
        rows = pl.ds(pl.multiple_of(dp * share_rows, share_rows), share_rows)
        total = buffer[base + 2 * core + side, rows, lanes].astype(F32)
        for step in range(1, dp_count):
            copy = dp_copy(job, step)
            copy.wait_send()
            copy.wait_recv()
            total = total + dp_in[job // 2, step - 1, :, lanes].astype(F32)
        fin[job // 2, 2 * core + side, :, lanes] = total.astype(BF16)
        join_copy(job).start()

    def after_join(job):
        copy = join_copy(job)
        copy.wait_send()
        copy.wait_recv()
        last_copy(job).start()

    def fin_copy(job):
        lanes = lanes_in(job)
        return pltpu.make_async_copy(
            fin.at[job // 2, :, :, lanes], fin_hbm.at[job // 2, :, :, lanes], fin_sem.at[job]
        )

    def after_last(job):
        copy = last_copy(job)
        copy.wait_send()
        copy.wait_recv()
        fin_copy(job).start()

    def early_sums():
        sums_of(0)
        sums_of(1)
        after_core(0)
        side_copy(0).start()
        sums_of(2)
        sums_of(3)
        after_core(1)
        side_copy(1).start()

    def one_step(step, carry):
        first_index = jnp.where(step < 4, step, jnp.where(step < 6, 5 - step, step - 4))
        last_index = jnp.where(step < 2, step, jnp.where(step < 4, 3 - step, lax.div(step, 2)))
        first_is = jnp.where(step < 4, 1, 0)
        last_is = jnp.where(step < 2, 1, jnp.where(step < 4, 0, 1 - lax.rem(step, 2)))
        index = jnp.minimum(jnp.where(segment == 0, first_index, last_index), PIECES - 1)
        is_forward = jnp.where(segment == 0, first_is, last_is)
        is_last = jnp.where(step == 2 * PIECES, 1, 0)
        is_split = jnp.where(step >= 2 * PIECES - 1, 1 - segment, 0)

        @pl.when(is_forward * (1 - is_last) == 1)
        def _():
            forward(index)

        @pl.when(is_forward + is_last == 0)
        def _():
            backward(index)

        @pl.when(is_last == 1)
        def _():
            early_sums()

        @pl.when((1 - is_forward) * (1 - is_split) * (1 - is_last) + is_last * is_split == 1)
        def _():
            backward_attention(index)

        return carry

    lax.fori_loop(0, 2 * PIECES + 1, one_step, 0)

    def small_dp_copy(step):
        target = lax.rem(dp + step, dp_count)
        return pltpu.make_async_remote_copy(
            src_ref=small.at[target],
            dst_ref=small_dp.at[step - 1],
            send_sem=sdp_send.at[step - 1],
            recv_sem=sdp_recv.at[step - 1],
            device_id={"dp": target},
            device_id_type=MESH,
        )

    def small_rep_copy(step):
        return pltpu.make_async_remote_copy(
            src_ref=small_rep.at[rep],
            dst_ref=small_rep.at[rep],
            send_sem=srep_send.at[step - 1],
            recv_sem=srep_recv.at[step - 1],
            device_id={"rep": lax.rem(rep + step, 4)},
            device_id_type=MESH,
        )

    sums_of(4)
    sums_of(5)
    after_core(2)
    after_side(0)
    side_copy(2).start()

    rows_of = [jnp.sum(sums[index].T, axis=0, keepdims=True) for index in range(STATS)]
    small[...] = jnp.zeros(small.shape, F32)
    for share_index in range(dp_count):
        for index in range(BIAS_UP):
            start = share_index * share_rows
            small[share_index, index : index + 1, :share_rows] = rows_of[index][
                :, start : start + share_rows
            ]
        for part in range(4):
            start = (share_index * 4 + part) * share_rows
            block, start = start // width, start % width
            small[share_index, BIAS_UP + part : BIAS_UP + part + 1, :share_rows] = rows_of[
                BIAS_UP + block
            ][:, start : start + share_rows]
    for step in range(1, dp_count):
        small_dp_copy(step).start()


    after_core(3)
    after_side(1)
    side_copy(3).start()
    small_total = small[dp]
    for step in range(1, dp_count):
        copy = small_dp_copy(step)
        copy.wait_send()
        copy.wait_recv()
        small_total = small_total + small_dp[step - 1]
    small_rep[rep] = small_total
    for step in range(1, 4):
        small_rep_copy(step).start()
    after_core(4)
    after_dp(0)
    after_side(2)
    side_copy(4).start()
    after_core(5)
    after_dp(1)
    after_join(0)
    after_side(3)
    side_copy(5).start()
    after_last(0)
    after_dp(2)
    after_join(1)
    after_side(4)
    after_last(1)
    after_dp(3)
    after_join(2)
    for step in range(1, 4):
        copy = small_rep_copy(step)
        copy.wait_send()
        copy.wait_recv()
    small_out[...] = (small_rep[0] + small_rep[1]) + (small_rep[2] + small_rep[3])
    small_copy = pltpu.make_async_copy(small_out, small_hbm, load_sem.at[0])
    small_copy.start()
    after_side(5)
    after_last(2)
    after_dp(4)
    after_join(3)
    after_last(3)
    after_dp(5)
    after_join(4)
    after_last(4)
    after_join(5)
    after_last(5)

    for index in range(PIECES):

        @pl.when(segment == 0)
        def _():
            forward_copy(index).wait_send()

        @pl.when(segment == 1)
        def _():
            backward_copy(index).wait_send()

    for index in range(2, PIECES):
        ends_copy(index).wait()
    for job in range(6):
        fin_copy(job).wait()
    small_copy.wait()


def finish_kernel(
    flag_ref,
    ends_in,
    fin,
    small,
    ends,
    grad_qkv,
    grad_out,
    grad_up,
    grad_down,
    grad_up_bias,
    grad_gains,
    grad_biases,
    ends_v,
    fin_v,
    wide_qkv,
    wide_out,
    wide_up,
    wide_down,
    ends_sem,
    in_sem,
    out_sem,
):
    half = ends_in.shape[0] // 2
    share_rows, width = fin.shape[2:]
    start = pl.multiple_of(half * (1 - flag_ref[0, 0]), half)
    ends_copies = [
        pltpu.make_async_copy(
            ends_v.at[pl.ds(0, half)], ends.at[0, pl.ds(start, half)], ends_sem.at[0]
        ),
        pltpu.make_async_copy(
            ends_v.at[pl.ds(half, half)], ends.at[0, pl.ds(half - start, half)], ends_sem.at[1]
        ),
    ]
    ends_loads = [
        pltpu.make_async_copy(
            ends_in.at[pl.ds(part * half, half)],
            ends_v.at[pl.ds(part * half, half)],
            ends_sem.at[2 + part],
        )
        for part in range(2)
    ]
    loads = [
        pltpu.make_async_copy(fin.at[group], fin_v.at[group], in_sem.at[group])
        for group in range(3)
    ]
    stores = [
        pltpu.make_async_copy(wide, target.at[0], out_sem.at[index])
        for index, (wide, target) in enumerate(
            ((wide_down, grad_down), (wide_up, grad_up), (wide_qkv, grad_qkv), (wide_out, grad_out))
        )
    ]
    for copy in loads + ends_loads:
        copy.start()
    for load, copy in zip(ends_loads, ends_copies):
        load.wait()
        copy.start()
    loads[0].wait()
    for position in range(4):
        rows = slice(position * share_rows, (position + 1) * share_rows)
        wide_down[rows, :] = fin_v[0, position].astype(F32)
    stores[0].start()
    loads[1].wait()
    for position in range(4):
        wide_up[:, position * width : (position + 1) * width] = fin_v[1, position].astype(F32)
    stores[1].start()
    loads[2].wait()
    for position in range(3):
        wide_qkv[:, position * width : (position + 1) * width] = fin_v[2, position].astype(F32)
    stores[2].start()
    wide_out[...] = fin_v[2, 3].astype(F32)
    stores[3].start()
    for position in range(4):
        rows = slice(position * share_rows, (position + 1) * share_rows)
        grad_up_bias[:, rows] = small[BIAS_UP + position : BIAS_UP + position + 1, :share_rows]
    grad_gains[0] = small[:2, :share_rows]
    grad_biases[0] = small[2:BIAS_UP, :share_rows]
    for copy in stores + ends_copies:
        copy.wait()


def on_device(
    dp_count,
    block_input,
    cotangent,
    window_group,
    w_qkv,
    w_out,
    w_up,
    w_down,
    up_bias,
    norm_gains,
    biases,
):
    rows, width = block_input.shape
    piece = rows // PIECES
    pairs = width // LANES
    share_rows = width // dp_count
    small_width = max(share_rows, LANES)
    any_spec = pl.BlockSpec(memory_space=pl.ANY)
    vmem_spec = pl.BlockSpec(memory_space=pltpu.VMEM)
    smem_spec = pl.BlockSpec(memory_space=pltpu.SMEM)
    dma = pltpu.SemaphoreType.DMA
    vmem = pltpu.VMEM
    ends_in, fin, small = pl.pallas_call(
        functools.partial(layer_kernel, dp_count),
        out_shape=(
            jax.ShapeDtypeStruct((PIECES, piece, width), F32),
            jax.ShapeDtypeStruct((3, 4, share_rows, width), BF16),
            jax.ShapeDtypeStruct((16, small_width), F32),
        ),
        in_specs=[smem_spec] + [any_spec] * 6 + [vmem_spec] * 3,
        out_specs=(any_spec,) * 3,
        scratch_shapes=[
            vmem((width, 3 * width), BF16),
            vmem((width, width), BF16),
            vmem((width, 4 * width), BF16),
            vmem((4, width, width), BF16),
            vmem((8, width, width), BF16),
            vmem((width, 4 * width), BF16),
            vmem((PIECES, piece, width), BF16),
            vmem((width, rows), BF16),
            vmem((3, pairs, LANES, rows), BF16),
            vmem((PIECES, pairs, piece, LANES), BF16),
            vmem((PIECES, pairs, piece, LANES), BF16),
            vmem((PIECES, pairs, 2, piece, piece), BF16),
            vmem((pairs, 2, piece, piece), BF16),
            vmem((pairs, LANES, rows), BF16),
            vmem((width, rows), F32),
            vmem((width, rows), F32),
            vmem((PIECES, 2, 1, piece), F32),
            vmem((width, rows), BF16),
            vmem((4, width, rows), BF16),
            vmem((4, width, rows), BF16),
            vmem((width, rows), BF16),
            vmem((width, rows), BF16),
            vmem((pairs, LANES, piece), BF16),
            vmem((PIECES, width, piece), BF16),
            vmem((PIECES, width, piece), BF16),
            vmem((STATS, width, LANES), BF16),
            vmem((STATS, width, LANES), F32),
            vmem((2, 2, pairs, LANES, piece), F32),
            vmem((4, piece, piece), BF16),
            vmem((width, piece), F32),
            vmem((width, piece), F32),
            vmem((2, piece, width), F32),
            vmem((3, 2, width, width), BF16),
            vmem((3, width, width), BF16),
            vmem((3, dp_count - 1, share_rows, width), BF16),
            vmem((3, 4, share_rows, width), BF16),
            vmem((dp_count, 16, small_width), F32),
            vmem((dp_count - 1, 16, small_width), F32),
            vmem((4, 16, small_width), F32),
            vmem((16, small_width), F32),
            dma((8,)),
            dma((PIECES,)),
            dma((PIECES,)),
            dma((PIECES,)),
            dma((6,)),
            dma((6,)),
            dma((6,)),
            dma((6,)),
            dma((6, dp_count - 1)),
            dma((6, dp_count - 1)),
            dma((6,)),
            dma((6,)),
            dma((6,)),
            dma((6,)),
            dma((dp_count - 1,)),
            dma((dp_count - 1,)),
            dma((3,)),
            dma((3,)),
            dma((6,)),
        ],
        compiler_params=pltpu.CompilerParams(
            collective_id=0, has_side_effects=True, vmem_limit_bytes=63 * 1024 * 1024
        ),
    )(
        window_group,
        block_input.reshape(PIECES, piece, width),
        cotangent.reshape(PIECES, piece, width),
        w_qkv,
        w_out,
        w_up,
        w_down,
        up_bias,
        norm_gains,
        biases,
    )
    return pl.pallas_call(
        finish_kernel,
        out_shape=(
            jax.ShapeDtypeStruct((1, rows, width), F32),
            jax.ShapeDtypeStruct((1, share_rows, 3 * width), F32),
            jax.ShapeDtypeStruct((1, share_rows, width), F32),
            jax.ShapeDtypeStruct((1, share_rows, 4 * width), F32),
            jax.ShapeDtypeStruct((1, 4 * share_rows, width), F32),
            jax.ShapeDtypeStruct((1, 4 * share_rows), F32),
            jax.ShapeDtypeStruct((1, 2, share_rows), F32),
            jax.ShapeDtypeStruct((1, 4, share_rows), F32),
        ),
        in_specs=[smem_spec, any_spec, any_spec, vmem_spec],
        out_specs=(any_spec,) * 5 + (vmem_spec,) * 3,
        scratch_shapes=[
            vmem((rows, width), F32),
            vmem((3, 4, share_rows, width), BF16),
            vmem((share_rows, 3 * width), F32),
            vmem((share_rows, width), F32),
            vmem((share_rows, 4 * width), F32),
            vmem((4 * share_rows, width), F32),
            dma((4,)),
            dma((3,)),
            dma((4,)),
        ],
        compiler_params=pltpu.CompilerParams(vmem_limit_bytes=63 * 1024 * 1024),
    )(window_group, ends_in.reshape(rows, width), fin, small)


def solution(mesh):
    return jax.shard_map(
        functools.partial(on_device, mesh.shape["dp"]),
        mesh=mesh,
        in_specs=(
            P(("dp", "rep"), None),
            P(("dp", "rep"), None),
            P(("dp", "rep"), None),
            P("segment", None, None),
            P("segment", None, None),
            P("segment", None, None),
            P("segment", None, None),
            P("segment", None),
            P("segment", None, None),
            P("segment", None, None),
        ),
        out_specs=(
            P("segment", ("dp", "rep"), None),
            P("segment", "dp", None),
            P("segment", "dp", None),
            P("segment", "dp", None),
            P("segment", "dp", None),
            P("segment", "dp"),
            P("segment", None, "dp"),
            P("segment", None, "dp"),
        ),
        check_vma=False,
    )
```

```python
import functools
import math

import jax
import jax.numpy as jnp
from jax import lax
from jax.experimental import pallas as pl
from jax.experimental.pallas import tpu as pltpu
from jax.sharding import PartitionSpec as P

MESH = pl.DeviceIdType.MESH
F32 = jnp.float32
BF16 = jnp.bfloat16
HEADS = 8
LANES = 128
PIECES = 4
EPS = 1e-05
GAIN_ONE, GAIN_TWO, BIAS_OUT, BIAS_ONE, BIAS_DOWN, BIAS_TWO, BIAS_UP = range(7)
STATS = 10
CHUNK = 64


def dot_plain(left, right):
    return lax.dot_general(left, right, (((1,), (0,)), ((), ())), preferred_element_type=F32)


def dot_turned(left, right):
    return lax.dot_general(left, right, (((1,), (1,)), ((), ())), preferred_element_type=F32)


def fold(values):
    total = values[:, :LANES]
    for start in range(LANES, values.shape[1], LANES):
        total = total + values[:, start : start + LANES]
    return total


def layer_kernel(
    dp_count,
    flag_ref,
    x_hbm,
    ct_hbm,
    w_qkv_hbm,
    w_out_hbm,
    w_up_hbm,
    w_down_hbm,
    up_bias_ref,
    gains_ref,
    biases_ref,
    ends_hbm,
    fin_hbm,
    small_hbm,
    w_qkv,
    w_out,
    w_up,
    w_down,
    turned,
    down_turned,
    rows_in,
    x_t,
    qkv,
    keys_rm,
    values_rm,
    share,
    share_off,
    mixture,
    norm_one,
    norm_two,
    inverses,
    hidden_low,
    slope,
    active,
    down_grad,
    branch_grad,
    grad_mix,
    outgoing,
    incoming_grad,
    columns,
    sums,
    key_sums,
    wide_a,
    wide_b,
    ends_v,
    core_in,
    side_in,
    dp_in,
    fin,
    small,
    small_dp,
    small_rep,
    small_out,
    load_sem,
    seg_send,
    seg_recv,
    ends_sem,
    core_send,
    core_recv,
    side_send,
    side_recv,
    dp_send,
    dp_recv,
    join_send,
    join_recv,
    last_send,
    last_recv,
    sdp_send,
    sdp_recv,
    srep_send,
    srep_recv,
    fin_sem,
):
    width = w_out.shape[0]
    piece = x_t.shape[1] // PIECES
    pairs = qkv.shape[1]
    share_rows = width // dp_count
    segment = lax.axis_index("segment")
    dp = lax.axis_index("dp")
    rep = lax.axis_index("rep")
    core = lax.rem(rep, 2)
    side = lax.div(rep, 2)
    other_core = side * 2 + (1 - core)
    other_side = (1 - side) * 2 + core

    loads = []
    for block in range(3):
        span = pl.ds(block * width, width)
        loads.append((w_qkv_hbm.at[0, :, span], w_qkv.at[:, span]))
    loads.append((w_out_hbm.at[0], w_out))
    for block in range(4):
        span = pl.ds(block * width, width)
        loads.append((w_up_hbm.at[0, :, span], w_up.at[:, span]))
    for block in range(4):
        span = pl.ds(block * width, width)
        loads.append((w_down_hbm.at[0, span, :], w_down.at[block]))
    load_copies = [
        pltpu.make_async_copy(source, target, load_sem.at[index + 1])
        for index, (source, target) in enumerate(loads)
    ]
    first_rows = pltpu.make_async_copy(x_hbm, rows_in, load_sem.at[0])
    last_rows = pltpu.make_async_copy(ct_hbm, rows_in, load_sem.at[0])

    @pl.when(segment == 0)
    def _():
        first_rows.start()

    @pl.when(segment == 1)
    def _():
        last_rows.start()

    for copy in load_copies:
        copy.start()

    barrier = pltpu.get_barrier_semaphore()
    pl.semaphore_signal(
        barrier, inc=1, device_id={"segment": 1 - segment}, device_id_type=MESH
    )
    for step in range(1, 4):
        pl.semaphore_signal(
            barrier, inc=1, device_id={"rep": lax.rem(rep + step, 4)}, device_id_type=MESH
        )
    for step in range(1, dp_count):
        pl.semaphore_signal(
            barrier, inc=1, device_id={"dp": lax.rem(dp + step, dp_count)}, device_id_type=MESH
        )

    params = [gains_ref[0].astype(F32), biases_ref[0].astype(F32)]
    for block in range(4):
        params.append(up_bias_ref[:, block * width : (block + 1) * width].astype(F32))
    params.append(jnp.zeros((16 - STATS, width), F32))
    upright = jnp.concatenate(params, axis=0).T
    for index in range(STATS):
        columns[index] = jnp.broadcast_to(upright[:, index : index + 1], (width, LANES)).astype(BF16)
    for index in range(STATS):
        sums[index] = jnp.zeros((width, LANES), F32)
    key_sums[0] = jnp.zeros(key_sums.shape[1:], F32)

    chunks = [slice(start, start + CHUNK) for start in range(0, width, CHUNK)]

    for block, copy in enumerate(load_copies):
        copy.wait()
        span = slice(block % 4 * width, (block % 4 + 1) * width)
        if block < 3:
            turned[block] = w_qkv[:, span].T
        elif block == 3:
            turned[block] = w_out[...].T
        elif block < 8:
            turned[block] = w_up[:, span].T
        else:
            down_turned[:, span] = w_down[block - 8].T
    first_rows.wait()

    pl.semaphore_wait(barrier, 4 + dp_count - 1)

    flag = flag_ref[0, 0].astype(F32)

    def lanes_of(index):
        return pl.ds(pl.multiple_of(index * piece, piece), piece)

    def forward_copy(index):
        return pltpu.make_async_remote_copy(
            src_ref=outgoing.at[index],
            dst_ref=x_t.at[:, lanes_of(index)],
            send_sem=seg_send.at[index],
            recv_sem=seg_recv.at[index],
            device_id={"segment": 1 - segment},
            device_id_type=MESH,
        )

    def backward_copy(index):
        return pltpu.make_async_remote_copy(
            src_ref=outgoing.at[index],
            dst_ref=incoming_grad.at[index],
            send_sem=seg_send.at[index],
            recv_sem=seg_recv.at[index],
            device_id={"segment": 1 - segment},
            device_id_type=MESH,
        )

    def ends_copy(index):
        return pltpu.make_async_copy(
            ends_v.at[lax.rem(index, 2)], ends_hbm.at[index], ends_sem.at[index]
        )

    def free_ends(index):
        @pl.when(index >= 2)
        def _():
            ends_copy(index - 2).wait()

    def own_rows(index):
        half = lax.rem(index, 2)
        whole = jnp.where(index < 2, 1.0, 0.0).astype(F32)
        weight = whole * flag + (1.0 - whole) * (1.0 - flag)
        picked = rows_in[half].astype(F32) * weight + rows_in[2 + half].astype(F32) * (1.0 - weight)
        return picked.T

    def by_queries(values):
        half = LANES // 2
        blank = jnp.zeros((half, LANES), values.dtype)
        parts = []
        for part in range(2):
            span = slice(part * LANES, (part + 1) * LANES)
            first = jnp.concatenate([values[:half, span], blank], axis=0)
            second = jnp.concatenate([blank, values[half:, span]], axis=0)
            parts.append(jnp.concatenate([first, second], axis=1))
        return parts

    def against(rows_ref, index, pair, parts, has_off):
        own = rows_ref[index, pair]
        products = [dot_plain(own[:LANES], parts[0]), dot_plain(own, parts[1])]
        if has_off:
            before = rows_ref[0, pair]
            products += [dot_plain(before, parts[0]), dot_plain(before, parts[1])]
        return products

    def tiles_of(products, head, part, has_off):
        lanes = slice(head * LANES, (head + 1) * LANES)
        own = products[part]
        tiles = [own[part * LANES : (part + 1) * LANES, lanes]]
        if part:
            tiles.append(own[:LANES, lanes])
        if has_off:
            off = products[2 + part]
            tiles += [off[:LANES, lanes], off[LANES:, lanes]]
        return tiles

    def joined(lows, has_off):
        blank = jnp.zeros((LANES, LANES), BF16)
        first = jnp.concatenate([lows[0][0], blank], axis=0)
        second = jnp.concatenate([lows[1][1], lows[1][0]], axis=0)
        whole = jnp.concatenate([first, second], axis=1)
        if not has_off:
            return whole, None
        first = jnp.concatenate(lows[0][-2:], axis=0)
        second = jnp.concatenate(lows[1][-2:], axis=0)
        return whole, jnp.concatenate([first, second], axis=1)

    def attend(index, has_off):
        lanes = lanes_of(index)
        half = LANES // 2
        key_at = lax.broadcasted_iota(jnp.int32, (LANES, LANES), 0)
        query_at = lax.broadcasted_iota(jnp.int32, (LANES, LANES), 1)
        allowed = key_at <= query_at

        def scores_of(pair):
            return against(
                keys_rm, index, pair, by_queries(qkv[0, pair, :, lanes]), has_off
            )

        ahead = scores_of(0)
        for pair in range(pairs):
            scores = ahead
            if pair + 1 < pairs:
                ahead = scores_of(pair + 1)
            mixed = []
            for head in range(2):
                rows = slice(head * half, (head + 1) * half)
                lows = []
                for part in range(2):
                    tiles = tiles_of(scores, head, part, has_off)
                    tiles[0] = jnp.where(allowed, tiles[0], -1e30)
                    top = jnp.max(functools.reduce(jnp.maximum, tiles), axis=0, keepdims=True)
                    raised = [jnp.exp(tile - top) for tile in tiles]
                    total = functools.reduce(jnp.add, raised)
                    scale = 1.0 / jnp.sum(total, axis=0, keepdims=True)
                    lows.append([(tile * scale).astype(BF16) for tile in raised])
                low, low_off = joined(lows, has_off)
                share[index, pair, head] = low
                mix = dot_plain(qkv[2, pair, rows, lanes], low)
                if has_off:
                    share_off[pair, head] = low_off
                    mix = mix + dot_plain(qkv[2, pair, rows, :piece], low_off)
                mixed.append(mix.astype(BF16))
            mixture[pair, :, lanes] = jnp.concatenate(mixed, axis=0)

    def part_sum(values):
        return jnp.sum(values.reshape(values.shape[0] // 8, 8, values.shape[1]), axis=0)

    def full_mean(parts):
        return jnp.sum(parts, axis=0, keepdims=True) * (1.0 / width)

    def column(index, rows):
        part = columns[index, rows, :].astype(F32)
        return jnp.concatenate([part] * (piece // LANES), axis=1)

    def gather_sum(index, rows, values):
        sums[index, rows, :] = sums[index, rows, :] + fold(values)

    def norm_chunks(index, which, total):
        mean = full_mean(total)
        spread = jnp.zeros((8, piece), F32)
        for rows in chunks:
            centred = wide_a[rows, :] - mean
            spread = spread + part_sum(centred * centred)
        inverse = lax.rsqrt(full_mean(spread) + EPS)
        inverses[index, which] = inverse
        return mean, inverse

    def forward(index):
        lanes = lanes_of(index)

        @pl.when(segment == 0)
        def _():
            x_t[:, lanes] = own_rows(index).astype(BF16)

        @pl.when(segment == 1)
        def _():
            forward_copy(index).wait_recv()

        inputs = x_t[:, lanes]
        score_scale = 1.0 / math.sqrt(width // HEADS)
        for block in range(3):
            result = dot_plain(turned[block], inputs)
            for pair in range(pairs):
                low = result[pair * LANES : (pair + 1) * LANES]
                low = (low * score_scale if block == 0 else low).astype(BF16)
                qkv[block, pair, :, lanes] = low
                if block == 1:
                    keys_rm[index, pair] = low.T
                if block == 2:
                    values_rm[index, pair] = low.T

        @pl.when(index == 1)
        def _():
            attend(index, True)

        @pl.when(index != 1)
        def _():
            attend(index, False)

        branch = dot_plain(turned[3], mixture[:, :, lanes].reshape(width, piece))
        total = jnp.zeros((8, piece), F32)
        for rows in chunks:
            sum_one = x_t[rows, lanes].astype(F32) + (branch[rows] + column(BIAS_OUT, rows))
            wide_a[rows, :] = sum_one
            total = total + part_sum(sum_one)
        mean, inverse = norm_chunks(index, 0, total)
        for rows in chunks:
            normed = (wide_a[rows, :] - mean) * inverse
            norm_one[rows, lanes] = normed
            hidden = normed * column(GAIN_ONE, rows) + column(BIAS_ONE, rows)
            hidden_low[rows, lanes] = hidden.astype(BF16)

        def activate(block, pre_block):
            for rows in chunks:
                pre = pre_block[rows] + column(BIAS_UP + block, rows)
                bell = jnp.exp2(pre * pre * (-0.5 * math.log2(math.e)))
                level = (lax.erf(pre * (1.0 / math.sqrt(2.0))) + 1.0) * 0.5
                active[block, rows, lanes] = (pre * level).astype(BF16)
                slope[block, rows, lanes] = (
                    level + pre * bell * (1.0 / math.sqrt(2.0 * math.pi))
                ).astype(BF16)

        for block in range(4):
            activate(block, dot_plain(turned[4 + block], hidden_low[:, lanes]))
        branch_two = dot_plain(down_turned[...], active[:, :, lanes].reshape(4 * width, piece))
        total = jnp.zeros((8, piece), F32)
        for rows in chunks:
            hidden = norm_one[rows, lanes] * column(GAIN_ONE, rows) + column(BIAS_ONE, rows)
            sum_two = hidden + (branch_two[rows] + column(BIAS_DOWN, rows))
            wide_a[rows, :] = sum_two
            total = total + part_sum(sum_two)
        mean, inverse = norm_chunks(index, 1, total)

        for rows in chunks:
            norm_two[rows, lanes] = (wide_a[rows, :] - mean) * inverse

        @pl.when(segment == 0)
        def _():
            for rows in chunks:
                outgoing[index, rows, :] = output_rows(rows, lanes).astype(BF16)
            forward_copy(index).start()

    def output_rows(rows, lanes):
        return norm_two[rows, lanes] * column(GAIN_TWO, rows) + column(BIAS_TWO, rows)

    def last_outputs(index, carry):
        free_ends(index)
        for start in range(0, width, LANES):
            rows = slice(start, start + LANES)
            ends_v[lax.rem(index, 2), :, rows] = output_rows(rows, lanes_of(index)).T
        ends_copy(index).start()
        return carry

    def attend_back(index, has_off):
        lanes = lanes_of(index)
        slot = jnp.where(index == 0, 1, 0)
        half = LANES // 2
        score_scale = 1.0 / math.sqrt(width // HEADS)

        def backs_of(pair):
            return against(values_rm, index, pair, by_queries(grad_mix[pair]), has_off)

        ahead = backs_of(0)
        for pair in range(pairs):
            backs = ahead
            if pair + 1 < pairs:
                ahead = backs_of(pair + 1)
            results = ([], [], [])
            for head in range(2):
                rows = slice(head * half, (head + 1) * half)
                low = share[index, pair, head]
                low_off = share_off[pair, head] if has_off else None
                lows = []
                for part in range(2):
                    place = slice(part * LANES, (part + 1) * LANES)
                    wides = [low[place, place]]
                    if part:
                        wides.append(low[:LANES, place])
                    if has_off:
                        wides += [low_off[:LANES, place], low_off[LANES:, place]]
                    wides = [tile.astype(F32) for tile in wides]
                    tiles = tiles_of(backs, head, part, has_off)
                    products = [wide * tile for wide, tile in zip(wides, tiles)]
                    inner = jnp.sum(functools.reduce(jnp.add, products), axis=0, keepdims=True)
                    lows.append(
                        [
                            (product - wide * inner).astype(BF16)
                            for product, wide in zip(products, wides)
                        ]
                    )
                grad_scores, grad_off = joined(lows, has_off)
                queries = qkv[0, pair, rows, lanes]
                grads = grad_mix[pair, rows]
                grad_query = dot_plain(qkv[1, pair, rows, lanes], grad_scores)
                grad_key = dot_turned(queries, grad_scores) + key_sums[slot, 0, pair, rows]
                grad_value = dot_turned(grads, low) + key_sums[slot, 1, pair, rows]
                if has_off:
                    grad_query = grad_query + dot_plain(qkv[1, pair, rows, :piece], grad_off)
                    key_sums[1, 0, pair, rows] = dot_turned(queries, grad_off)
                    key_sums[1, 1, pair, rows] = dot_turned(grads, low_off)
                for kept, grad in zip(results, (grad_query * score_scale, grad_key, grad_value)):
                    kept.append(grad.astype(BF16))
            for block in range(3):
                qkv[block, pair, :, lanes] = jnp.concatenate(results[block], axis=0)

    def backward(index):
        lanes = lanes_of(index)

        @pl.when(segment == 0)
        def _():
            backward_copy(index).wait_recv()

        plain = jnp.zeros((8, piece), F32)
        inner = jnp.zeros((8, piece), F32)
        for rows in chunks:
            grad = incoming_grad[index, rows, :].astype(F32)
            product = grad * norm_two[rows, lanes]
            gather_sum(GAIN_TWO, rows, product)
            gather_sum(BIAS_TWO, rows, grad)
            gain = column(GAIN_TWO, rows)
            plain = plain + part_sum(grad * gain)
            inner = inner + part_sum(product * gain)
        plain = full_mean(plain)
        inner = full_mean(inner)
        inverse = inverses[index, 1]
        for rows in chunks:
            scaled = incoming_grad[index, rows, :].astype(F32) * column(GAIN_TWO, rows)
            grad_two = (scaled - plain - norm_two[rows, lanes] * inner) * inverse
            gather_sum(BIAS_DOWN, rows, grad_two)
            wide_a[rows, :] = grad_two
            down_grad[rows, lanes] = grad_two.astype(BF16)

        for block in range(4):
            back = dot_plain(w_down[block], down_grad[:, lanes])
            for rows in chunks:
                grad_pre = back[rows] * slope[block, rows, lanes].astype(F32)
                gather_sum(BIAS_UP + block, rows, grad_pre)
                slope[block, rows, lanes] = grad_pre.astype(BF16)

        through = dot_plain(w_up[...], slope[:, :, lanes].reshape(4 * width, piece))
        plain = jnp.zeros((8, piece), F32)
        inner = jnp.zeros((8, piece), F32)
        for rows in chunks:
            grad_hidden = wide_a[rows, :] + through[rows]
            wide_a[rows, :] = grad_hidden
            product = grad_hidden * norm_one[rows, lanes]
            gather_sum(GAIN_ONE, rows, product)
            gather_sum(BIAS_ONE, rows, grad_hidden)
            gain = column(GAIN_ONE, rows)
            plain = plain + part_sum(grad_hidden * gain)
            inner = inner + part_sum(product * gain)
        plain = full_mean(plain)
        inner = full_mean(inner)
        inverse = inverses[index, 0]
        for rows in chunks:
            scaled = wide_a[rows, :] * column(GAIN_ONE, rows)
            grad_one = (scaled - plain - norm_one[rows, lanes] * inner) * inverse
            gather_sum(BIAS_OUT, rows, grad_one)
            wide_b[rows, :] = grad_one
            branch_grad[rows, lanes] = grad_one.astype(BF16)
        grad_mix[...] = (
            dot_plain(w_out[...], branch_grad[:, lanes]).astype(BF16).reshape(pairs, LANES, piece)
        )

    def backward_attention(index):
        lanes = lanes_of(index)

        @pl.when(index == 1)
        def _():
            attend_back(index, True)

        @pl.when(index != 1)
        def _():
            attend_back(index, False)

        through = dot_plain(w_qkv[...], qkv[:, :, :, lanes].reshape(3 * width, piece))

        @pl.when(segment == 1)
        def _():
            for rows in chunks:
                outgoing[index, rows, :] = (wide_b[rows, :] + through[rows]).astype(BF16)
            backward_copy(index).start()

        @pl.when(segment == 0)
        def _():
            free_ends(index)
            for start in range(0, width, LANES):
                rows = slice(start, start + LANES)
                ends_v[lax.rem(index, 2), :, rows] = (wide_b[rows, :] + through[rows]).T
            ends_copy(index).start()

    def held(job):
        group = job // 2
        return (w_down, 0) if group == 0 else (turned, 4 if group == 1 else 0)

    def core_copy(job):
        buffer, base = held(job)
        lanes = lanes_in(job)
        return pltpu.make_async_remote_copy(
            src_ref=buffer.at[pl.ds(base + 2 * (1 - core), 2), :, lanes],
            dst_ref=core_in.at[job // 2, :, :, lanes],
            send_sem=core_send.at[job],
            recv_sem=core_recv.at[job],
            device_id={"rep": other_core},
            device_id_type=MESH,
        )

    def side_copy(job):
        buffer, base = held(job)
        lanes = lanes_in(job)
        return pltpu.make_async_remote_copy(
            src_ref=buffer.at[base + 2 * core + (1 - side), :, lanes],
            dst_ref=side_in.at[job // 2, :, lanes],
            send_sem=side_send.at[job],
            recv_sem=side_recv.at[job],
            device_id={"rep": other_side},
            device_id_type=MESH,
        )

    def dp_copy(job, step):
        buffer, base = held(job)
        lanes = lanes_in(job)
        target = lax.rem(dp + step, dp_count)
        rows = pl.ds(pl.multiple_of(target * share_rows, share_rows), share_rows)
        return pltpu.make_async_remote_copy(
            src_ref=buffer.at[base + 2 * core + side, rows, lanes],
            dst_ref=dp_in.at[job // 2, step - 1, :, lanes],
            send_sem=dp_send.at[job, step - 1],
            recv_sem=dp_recv.at[job, step - 1],
            device_id={"dp": target},
            device_id_type=MESH,
        )

    def join_copy(job):
        lanes = lanes_in(job)
        return pltpu.make_async_remote_copy(
            src_ref=fin.at[job // 2, 2 * core + side, :, lanes],
            dst_ref=fin.at[job // 2, 2 * core + side, :, lanes],
            send_sem=join_send.at[job],
            recv_sem=join_recv.at[job],
            device_id={"rep": other_side},
            device_id_type=MESH,
        )

    def last_copy(job):
        lanes = lanes_in(job)
        return pltpu.make_async_remote_copy(
            src_ref=fin.at[job // 2, pl.ds(2 * core, 2), :, lanes],
            dst_ref=fin.at[job // 2, pl.ds(2 * core, 2), :, lanes],
            send_sem=last_send.at[job],
            recv_sem=last_recv.at[job],
            device_id={"rep": other_core},
            device_id_type=MESH,
        )

    def lanes_in(job):
        half = job % 2
        return slice(half * (width // 2), (half + 1) * (width // 2))

    def down_sums(job):
        part = 4 * share_rows
        count = width // part
        lanes = lanes_in(job)

        def one(block, carry):
            result = dot_turned(active[block], down_grad[lanes, :]).astype(BF16)
            for each in range(count):
                for position in range(4):
                    start = each * part + position * share_rows
                    target = pl.multiple_of((block * count + each) * share_rows, share_rows)
                    w_down[position, pl.ds(target, share_rows), lanes] = result[
                        start : start + share_rows
                    ]
            return carry

        lax.fori_loop(0, 4, one, 0)

    def up_sums(job):
        lanes = lanes_in(job)

        def one(block, carry):
            turned[4 + block, :, lanes] = dot_turned(hidden_low[...], slope[block, lanes, :]).astype(
                BF16
            )
            return carry

        lax.fori_loop(0, 4, one, 0)

    def qkv_sums(job):
        lanes = lanes_in(job)
        half_pairs = slice((job % 2) * (pairs // 2), (job % 2 + 1) * (pairs // 2))

        def one(block, carry):
            turned[block, :, lanes] = dot_turned(
                x_t[...], qkv[block, half_pairs].reshape(width // 2, PIECES * piece)
            ).astype(BF16)
            return carry

        lax.fori_loop(0, 3, one, 0)
        turned[3, :, lanes] = dot_turned(
            mixture[...].reshape(width, PIECES * piece), branch_grad[lanes, :]
        ).astype(BF16)

    def sums_of(job):
        (down_sums, up_sums, qkv_sums)[job // 2](job)
        core_copy(job).start()

    def after_core(job):
        buffer, base = held(job)
        lanes = lanes_in(job)
        copy = core_copy(job)
        copy.wait_send()
        copy.wait_recv()
        first = base + 2 * core + (1 - side)
        buffer[first, :, lanes] = (
            buffer[first, :, lanes].astype(F32) + core_in[job // 2, 1 - side, :, lanes].astype(F32)
        ).astype(BF16)

    def after_side(job):
        buffer, base = held(job)
        lanes = lanes_in(job)
        copy = side_copy(job)
        copy.wait_send()
        copy.wait_recv()
        second = base + 2 * core + side
        buffer[second, :, lanes] = (
            buffer[second, :, lanes].astype(F32)
            + core_in[job // 2, side, :, lanes].astype(F32)
            + side_in[job // 2, :, lanes].astype(F32)
        ).astype(BF16)
        for step in range(1, dp_count):
            dp_copy(job, step).start()

    def after_dp(job):
        buffer, base = held(job)
        lanes = lanes_in(job)
        rows = pl.ds(pl.multiple_of(dp * share_rows, share_rows), share_rows)
        total = buffer[base + 2 * core + side, rows, lanes].astype(F32)
        for step in range(1, dp_count):
            copy = dp_copy(job, step)
            copy.wait_send()
            copy.wait_recv()
            total = total + dp_in[job // 2, step - 1, :, lanes].astype(F32)
        fin[job // 2, 2 * core + side, :, lanes] = total.astype(BF16)
        join_copy(job).start()

    def after_join(job):
        copy = join_copy(job)
        copy.wait_send()
        copy.wait_recv()
        last_copy(job).start()

    def fin_copy(job):
        lanes = lanes_in(job)
        return pltpu.make_async_copy(
            fin.at[job // 2, :, :, lanes], fin_hbm.at[job // 2, :, :, lanes], fin_sem.at[job]
        )

    def after_last(job):
        copy = last_copy(job)
        copy.wait_send()
        copy.wait_recv()
        fin_copy(job).start()

    def early_sums():
        sums_of(0)
        sums_of(1)
        after_core(0)
        side_copy(0).start()
        sums_of(2)
        sums_of(3)
        after_core(1)
        side_copy(1).start()

    def one_step(step, carry):
        first_index = jnp.where(step < 4, step, jnp.where(step < 6, 5 - step, step - 4))
        last_index = jnp.where(step < 2, step, jnp.where(step < 4, 3 - step, lax.div(step, 2)))
        first_is = jnp.where(step < 4, 1, 0)
        last_is = jnp.where(step < 2, 1, jnp.where(step < 4, 0, 1 - lax.rem(step, 2)))
        index = jnp.minimum(jnp.where(segment == 0, first_index, last_index), PIECES - 1)
        is_forward = jnp.where(segment == 0, first_is, last_is)
        is_last = jnp.where(step == 2 * PIECES, 1, 0)
        is_split = jnp.where(step >= 2 * PIECES - 1, 1 - segment, 0)

        @pl.when(is_forward * (1 - is_last) == 1)
        def _():
            forward(index)

        @pl.when(is_forward + is_last == 0)
        def _():
            backward(index)

        @pl.when(is_last == 1)
        def _():
            early_sums()

        @pl.when((1 - is_forward) * (1 - is_split) * (1 - is_last) + is_last * is_split == 1)
        def _():
            backward_attention(index)

        return carry

    @pl.when(segment == 1)
    def _():
        for index in range(PIECES):
            incoming_grad[index] = own_rows(index).astype(BF16)

    lax.fori_loop(0, 2 * PIECES + 1, one_step, 0)

    def small_dp_copy(step):
        target = lax.rem(dp + step, dp_count)
        return pltpu.make_async_remote_copy(
            src_ref=small.at[target],
            dst_ref=small_dp.at[step - 1],
            send_sem=sdp_send.at[step - 1],
            recv_sem=sdp_recv.at[step - 1],
            device_id={"dp": target},
            device_id_type=MESH,
        )

    def small_rep_copy(step):
        return pltpu.make_async_remote_copy(
            src_ref=small_rep.at[rep],
            dst_ref=small_rep.at[rep],
            send_sem=srep_send.at[step - 1],
            recv_sem=srep_recv.at[step - 1],
            device_id={"rep": lax.rem(rep + step, 4)},
            device_id_type=MESH,
        )

    sums_of(4)
    sums_of(5)
    after_core(2)
    after_side(0)
    side_copy(2).start()

    @pl.when(segment == 1)
    def _():
        lax.fori_loop(0, PIECES, last_outputs, 0)

    rows_of = [jnp.sum(sums[index].T, axis=0, keepdims=True) for index in range(STATS)]
    small[...] = jnp.zeros(small.shape, F32)
    for share_index in range(dp_count):
        for index in range(BIAS_UP):
            start = share_index * share_rows
            small[share_index, index : index + 1, :share_rows] = rows_of[index][
                :, start : start + share_rows
            ]
        for part in range(4):
            start = (share_index * 4 + part) * share_rows
            block, start = start // width, start % width
            small[share_index, BIAS_UP + part : BIAS_UP + part + 1, :share_rows] = rows_of[
                BIAS_UP + block
            ][:, start : start + share_rows]
    for step in range(1, dp_count):
        small_dp_copy(step).start()


    after_core(3)
    after_side(1)
    side_copy(3).start()
    small_total = small[dp]
    for step in range(1, dp_count):
        copy = small_dp_copy(step)
        copy.wait_send()
        copy.wait_recv()
        small_total = small_total + small_dp[step - 1]
    small_rep[rep] = small_total
    for step in range(1, 4):
        small_rep_copy(step).start()
    after_core(4)
    after_dp(0)
    after_side(2)
    side_copy(4).start()
    after_core(5)
    after_dp(1)
    after_join(0)
    after_side(3)
    side_copy(5).start()
    after_last(0)
    after_dp(2)
    after_join(1)
    after_side(4)
    after_last(1)
    after_dp(3)
    after_join(2)
    for step in range(1, 4):
        copy = small_rep_copy(step)
        copy.wait_send()
        copy.wait_recv()
    small_out[...] = (small_rep[0] + small_rep[1]) + (small_rep[2] + small_rep[3])
    small_copy = pltpu.make_async_copy(small_out, small_hbm, load_sem.at[0])
    small_copy.start()
    after_side(5)
    after_last(2)
    after_dp(4)
    after_join(3)
    after_last(3)
    after_dp(5)
    after_join(4)
    after_last(4)
    after_join(5)
    after_last(5)

    for index in range(PIECES):

        @pl.when(segment == 0)
        def _():
            forward_copy(index).wait_send()

        @pl.when(segment == 1)
        def _():
            backward_copy(index).wait_send()

    for index in range(2, PIECES):
        ends_copy(index).wait()
    for job in range(6):
        fin_copy(job).wait()
    small_copy.wait()


def finish_kernel(
    flag_ref,
    ends_in,
    fin,
    small,
    ends,
    grad_qkv,
    grad_out,
    grad_up,
    grad_down,
    grad_up_bias,
    grad_gains,
    grad_biases,
    ends_v,
    fin_v,
    wide_qkv,
    wide_out,
    wide_up,
    wide_down,
    ends_sem,
    in_sem,
    out_sem,
):
    half = ends_in.shape[0] // 2
    share_rows, width = fin.shape[2:]
    start = pl.multiple_of(half * (1 - flag_ref[0, 0]), half)
    cut = half // 4
    ends_copies = []
    ends_loads = []
    for part in range(8):
        source = pl.ds(part * cut, cut)
        offset = start + part * cut if part < 4 else part * cut - half + (half - start)
        target = pl.ds(pl.multiple_of(offset, cut), cut)
        ends_loads.append(
            pltpu.make_async_copy(ends_in.at[source], ends_v.at[source], ends_sem.at[part])
        )
        ends_copies.append(
            pltpu.make_async_copy(ends_v.at[source], ends.at[0, target], ends_sem.at[8 + part])
        )
    loads = [
        pltpu.make_async_copy(fin.at[group], fin_v.at[group], in_sem.at[group])
        for group in range(3)
    ]
    stores = [
        pltpu.make_async_copy(wide, target.at[0], out_sem.at[index])
        for index, (wide, target) in enumerate(
            ((wide_down, grad_down), (wide_up, grad_up), (wide_qkv, grad_qkv), (wide_out, grad_out))
        )
    ]
    for copy in loads + ends_loads:
        copy.start()
    for load, copy in zip(ends_loads, ends_copies):
        load.wait()
        copy.start()
    loads[0].wait()
    for position in range(4):
        rows = slice(position * share_rows, (position + 1) * share_rows)
        wide_down[rows, :] = fin_v[0, position].astype(F32)
    stores[0].start()
    loads[1].wait()
    for position in range(4):
        wide_up[:, position * width : (position + 1) * width] = fin_v[1, position].astype(F32)
    stores[1].start()
    loads[2].wait()
    for position in range(3):
        wide_qkv[:, position * width : (position + 1) * width] = fin_v[2, position].astype(F32)
    stores[2].start()
    wide_out[...] = fin_v[2, 3].astype(F32)
    stores[3].start()
    for position in range(4):
        rows = slice(position * share_rows, (position + 1) * share_rows)
        grad_up_bias[:, rows] = small[BIAS_UP + position : BIAS_UP + position + 1, :share_rows]
    grad_gains[0] = small[:2, :share_rows]
    grad_biases[0] = small[2:BIAS_UP, :share_rows]
    for copy in stores + ends_copies:
        copy.wait()


def on_device(
    dp_count,
    block_input,
    cotangent,
    window_group,
    w_qkv,
    w_out,
    w_up,
    w_down,
    up_bias,
    norm_gains,
    biases,
):
    rows, width = block_input.shape
    piece = rows // PIECES
    pairs = width // LANES
    share_rows = width // dp_count
    small_width = max(share_rows, LANES)
    any_spec = pl.BlockSpec(memory_space=pl.ANY)
    vmem_spec = pl.BlockSpec(memory_space=pltpu.VMEM)
    smem_spec = pl.BlockSpec(memory_space=pltpu.SMEM)
    dma = pltpu.SemaphoreType.DMA
    vmem = pltpu.VMEM
    ends_in, fin, small = pl.pallas_call(
        functools.partial(layer_kernel, dp_count),
        out_shape=(
            jax.ShapeDtypeStruct((PIECES, piece, width), F32),
            jax.ShapeDtypeStruct((3, 4, share_rows, width), BF16),
            jax.ShapeDtypeStruct((16, small_width), F32),
        ),
        in_specs=[smem_spec] + [any_spec] * 6 + [vmem_spec] * 3,
        out_specs=(any_spec,) * 3,
        scratch_shapes=[
            vmem((width, 3 * width), BF16),
            vmem((width, width), BF16),
            vmem((width, 4 * width), BF16),
            vmem((4, width, width), BF16),
            vmem((8, width, width), BF16),
            vmem((width, 4 * width), BF16),
            vmem((PIECES, piece, width), BF16),
            vmem((width, rows), BF16),
            vmem((3, pairs, LANES, rows), BF16),
            vmem((PIECES, pairs, piece, LANES), BF16),
            vmem((PIECES, pairs, piece, LANES), BF16),
            vmem((PIECES, pairs, 2, piece, piece), BF16),
            vmem((pairs, 2, piece, piece), BF16),
            vmem((pairs, LANES, rows), BF16),
            vmem((width, rows), F32),
            vmem((width, rows), F32),
            vmem((PIECES, 2, 1, piece), F32),
            vmem((width, rows), BF16),
            vmem((4, width, rows), BF16),
            vmem((4, width, rows), BF16),
            vmem((width, rows), BF16),
            vmem((width, rows), BF16),
            vmem((pairs, LANES, piece), BF16),
            vmem((PIECES, width, piece), BF16),
            vmem((PIECES, width, piece), BF16),
            vmem((STATS, width, LANES), BF16),
            vmem((STATS, width, LANES), F32),
            vmem((2, 2, pairs, LANES, piece), F32),
            vmem((width, piece), F32),
            vmem((width, piece), F32),
            vmem((2, piece, width), F32),
            vmem((3, 2, width, width), BF16),
            vmem((3, width, width), BF16),
            vmem((3, dp_count - 1, share_rows, width), BF16),
            vmem((3, 4, share_rows, width), BF16),
            vmem((dp_count, 16, small_width), F32),
            vmem((dp_count - 1, 16, small_width), F32),
            vmem((4, 16, small_width), F32),
            vmem((16, small_width), F32),
            dma((13,)),
            dma((PIECES,)),
            dma((PIECES,)),
            dma((PIECES,)),
            dma((6,)),
            dma((6,)),
            dma((6,)),
            dma((6,)),
            dma((6, dp_count - 1)),
            dma((6, dp_count - 1)),
            dma((6,)),
            dma((6,)),
            dma((6,)),
            dma((6,)),
            dma((dp_count - 1,)),
            dma((dp_count - 1,)),
            dma((3,)),
            dma((3,)),
            dma((6,)),
        ],
        compiler_params=pltpu.CompilerParams(
            collective_id=0, has_side_effects=True, vmem_limit_bytes=63 * 1024 * 1024
        ),
    )(
        window_group,
        block_input.reshape(PIECES, piece, width),
        cotangent.reshape(PIECES, piece, width),
        w_qkv,
        w_out,
        w_up,
        w_down,
        up_bias,
        norm_gains,
        biases,
    )
    return pl.pallas_call(
        finish_kernel,
        out_shape=(
            jax.ShapeDtypeStruct((1, rows, width), F32),
            jax.ShapeDtypeStruct((1, share_rows, 3 * width), F32),
            jax.ShapeDtypeStruct((1, share_rows, width), F32),
            jax.ShapeDtypeStruct((1, share_rows, 4 * width), F32),
            jax.ShapeDtypeStruct((1, 4 * share_rows, width), F32),
            jax.ShapeDtypeStruct((1, 4 * share_rows), F32),
            jax.ShapeDtypeStruct((1, 2, share_rows), F32),
            jax.ShapeDtypeStruct((1, 4, share_rows), F32),
        ),
        in_specs=[smem_spec, any_spec, any_spec, vmem_spec],
        out_specs=(any_spec,) * 5 + (vmem_spec,) * 3,
        scratch_shapes=[
            vmem((rows, width), F32),
            vmem((3, 4, share_rows, width), BF16),
            vmem((share_rows, 3 * width), F32),
            vmem((share_rows, width), F32),
            vmem((share_rows, 4 * width), F32),
            vmem((4 * share_rows, width), F32),
            dma((16,)),
            dma((3,)),
            dma((4,)),
        ],
        compiler_params=pltpu.CompilerParams(vmem_limit_bytes=63 * 1024 * 1024),
    )(window_group, ends_in.reshape(rows, width), fin, small)


def solution(mesh):
    return jax.shard_map(
        functools.partial(on_device, mesh.shape["dp"]),
        mesh=mesh,
        in_specs=(
            P(("dp", "rep"), None),
            P(("dp", "rep"), None),
            P(("dp", "rep"), None),
            P("segment", None, None),
            P("segment", None, None),
            P("segment", None, None),
            P("segment", None, None),
            P("segment", None),
            P("segment", None, None),
            P("segment", None, None),
        ),
        out_specs=(
            P("segment", ("dp", "rep"), None),
            P("segment", "dp", None),
            P("segment", "dp", None),
            P("segment", "dp", None),
            P("segment", "dp", None),
            P("segment", "dp"),
            P("segment", None, "dp"),
            P("segment", None, "dp"),
        ),
        check_vma=False,
    )
```

```python
import functools
import math

import jax
import jax.numpy as jnp
from jax import lax
from jax.experimental import pallas as pl
from jax.experimental.pallas import tpu as pltpu
from jax.sharding import PartitionSpec as P

MESH = pl.DeviceIdType.MESH
F32 = jnp.float32
BF16 = jnp.bfloat16
HEADS = 8
LANES = 128
PIECES = 4
EPS = 1e-05
GAIN_ONE, GAIN_TWO, BIAS_OUT, BIAS_ONE, BIAS_DOWN, BIAS_TWO, BIAS_UP = range(7)
STATS = 10
CHUNK = 64
DP_FIRST = (0, 5)


def dot_plain(left, right):
    return lax.dot_general(left, right, (((1,), (0,)), ((), ())), preferred_element_type=F32)


def dot_turned(left, right):
    return lax.dot_general(left, right, (((1,), (1,)), ((), ())), preferred_element_type=F32)


def fold(values):
    total = values[:, :LANES]
    for start in range(LANES, values.shape[1], LANES):
        total = total + values[:, start : start + LANES]
    return total


def layer_kernel(
    dp_count,
    flag_ref,
    x_hbm,
    ct_hbm,
    w_qkv_hbm,
    w_out_hbm,
    w_up_hbm,
    w_down_hbm,
    up_bias_ref,
    gains_ref,
    biases_ref,
    ends_hbm,
    fin_hbm,
    small_hbm,
    w_qkv,
    w_out,
    w_up,
    w_down,
    turned,
    down_turned,
    rows_in,
    x_t,
    qkv,
    keys_rm,
    values_rm,
    share,
    share_off,
    mixture,
    norm_one,
    norm_two,
    inverses,
    hidden_low,
    slope,
    active,
    down_grad,
    branch_grad,
    grad_mix,
    outgoing,
    incoming_grad,
    columns,
    sums,
    key_sums,
    wide_a,
    wide_b,
    ends_v,
    core_in,
    side_in,
    dp_in,
    fin,
    small,
    small_dp,
    small_rep,
    small_out,
    load_sem,
    seg_send,
    seg_recv,
    ends_sem,
    core_send,
    core_recv,
    side_send,
    side_recv,
    dp_send,
    dp_recv,
    join_send,
    join_recv,
    last_send,
    last_recv,
    sdp_send,
    sdp_recv,
    srep_send,
    srep_recv,
    fin_sem,
):
    width = w_out.shape[0]
    piece = x_t.shape[1] // PIECES
    pairs = qkv.shape[1]
    share_rows = width // dp_count
    dp_steps = dp_count.bit_length() - 1
    segment = lax.axis_index("segment")
    dp = lax.axis_index("dp")
    rep = lax.axis_index("rep")
    core = lax.rem(rep, 2)
    side = lax.div(rep, 2)
    other_core = side * 2 + (1 - core)
    other_side = (1 - side) * 2 + core

    loads = []
    for block in range(3):
        span = pl.ds(block * width, width)
        loads.append((w_qkv_hbm.at[0, :, span], w_qkv.at[:, span]))
    loads.append((w_out_hbm.at[0], w_out))
    for block in range(4):
        span = pl.ds(block * width, width)
        loads.append((w_up_hbm.at[0, :, span], w_up.at[:, span]))
    for block in range(4):
        span = pl.ds(block * width, width)
        loads.append((w_down_hbm.at[0, span, :], w_down.at[block]))
    load_copies = [
        pltpu.make_async_copy(source, target, load_sem.at[index + 1])
        for index, (source, target) in enumerate(loads)
    ]
    first_rows = pltpu.make_async_copy(x_hbm, rows_in, load_sem.at[0])
    last_rows = pltpu.make_async_copy(ct_hbm, rows_in, load_sem.at[0])

    @pl.when(segment == 0)
    def _():
        first_rows.start()

    @pl.when(segment == 1)
    def _():
        last_rows.start()

    for copy in load_copies:
        copy.start()

    barrier = pltpu.get_barrier_semaphore()
    pl.semaphore_signal(
        barrier, inc=1, device_id={"segment": 1 - segment}, device_id_type=MESH
    )
    for step in range(1, 4):
        pl.semaphore_signal(
            barrier, inc=1, device_id={"rep": lax.rem(rep + step, 4)}, device_id_type=MESH
        )
    for step in range(1, dp_count):
        pl.semaphore_signal(
            barrier, inc=1, device_id={"dp": lax.rem(dp + step, dp_count)}, device_id_type=MESH
        )

    params = [gains_ref[0].astype(F32), biases_ref[0].astype(F32)]
    for block in range(4):
        params.append(up_bias_ref[:, block * width : (block + 1) * width].astype(F32))
    params.append(jnp.zeros((16 - STATS, width), F32))
    upright = jnp.concatenate(params, axis=0).T
    for index in range(STATS):
        columns[index] = jnp.broadcast_to(upright[:, index : index + 1], (width, LANES)).astype(BF16)
    for index in range(STATS):
        sums[index] = jnp.zeros((width, LANES), F32)
    key_sums[0] = jnp.zeros(key_sums.shape[1:], F32)

    chunks = [slice(start, start + CHUNK) for start in range(0, width, CHUNK)]

    for block, copy in enumerate(load_copies):
        copy.wait()
        span = slice(block % 4 * width, (block % 4 + 1) * width)
        if block < 3:
            turned[block] = w_qkv[:, span].T
        elif block == 3:
            turned[block] = w_out[...].T
        elif block < 8:
            turned[block] = w_up[:, span].T
        else:
            down_turned[:, span] = w_down[block - 8].T
    first_rows.wait()

    pl.semaphore_wait(barrier, 4 + dp_count - 1)

    flag = flag_ref[0, 0].astype(F32)

    def lanes_of(index):
        return pl.ds(pl.multiple_of(index * piece, piece), piece)

    def forward_copy(index):
        return pltpu.make_async_remote_copy(
            src_ref=outgoing.at[index],
            dst_ref=x_t.at[:, lanes_of(index)],
            send_sem=seg_send.at[index],
            recv_sem=seg_recv.at[index],
            device_id={"segment": 1 - segment},
            device_id_type=MESH,
        )

    def backward_copy(index):
        return pltpu.make_async_remote_copy(
            src_ref=outgoing.at[index],
            dst_ref=incoming_grad.at[index],
            send_sem=seg_send.at[index],
            recv_sem=seg_recv.at[index],
            device_id={"segment": 1 - segment},
            device_id_type=MESH,
        )

    def ends_copy(index):
        return pltpu.make_async_copy(
            ends_v.at[lax.rem(index, 2)], ends_hbm.at[index], ends_sem.at[index]
        )

    def free_ends(index):
        @pl.when(index >= 2)
        def _():
            ends_copy(index - 2).wait()

    def own_rows(index):
        half = lax.rem(index, 2)
        whole = jnp.where(index < 2, 1.0, 0.0).astype(F32)
        weight = whole * flag + (1.0 - whole) * (1.0 - flag)
        picked = rows_in[half].astype(F32) * weight + rows_in[2 + half].astype(F32) * (1.0 - weight)
        return picked.T

    def by_queries(values):
        half = LANES // 2
        blank = jnp.zeros((half, LANES), values.dtype)
        parts = []
        for part in range(2):
            span = slice(part * LANES, (part + 1) * LANES)
            first = jnp.concatenate([values[:half, span], blank], axis=0)
            second = jnp.concatenate([blank, values[half:, span]], axis=0)
            parts.append(jnp.concatenate([first, second], axis=1))
        return parts

    def against(rows_ref, index, pair, parts, has_off):
        own = rows_ref[index, pair]
        products = [dot_plain(own[:LANES], parts[0]), dot_plain(own, parts[1])]
        if has_off:
            before = rows_ref[0, pair]
            products += [dot_plain(before, parts[0]), dot_plain(before, parts[1])]
        return products

    def tiles_of(products, head, part, has_off):
        lanes = slice(head * LANES, (head + 1) * LANES)
        own = products[part]
        tiles = [own[part * LANES : (part + 1) * LANES, lanes]]
        if part:
            tiles.append(own[:LANES, lanes])
        if has_off:
            off = products[2 + part]
            tiles += [off[:LANES, lanes], off[LANES:, lanes]]
        return tiles

    def joined(lows, has_off):
        blank = jnp.zeros((LANES, LANES), BF16)
        first = jnp.concatenate([lows[0][0], blank], axis=0)
        second = jnp.concatenate([lows[1][1], lows[1][0]], axis=0)
        whole = jnp.concatenate([first, second], axis=1)
        if not has_off:
            return whole, None
        first = jnp.concatenate(lows[0][-2:], axis=0)
        second = jnp.concatenate(lows[1][-2:], axis=0)
        return whole, jnp.concatenate([first, second], axis=1)

    def attend(index, has_off):
        lanes = lanes_of(index)
        half = LANES // 2
        key_at = lax.broadcasted_iota(jnp.int32, (LANES, LANES), 0)
        query_at = lax.broadcasted_iota(jnp.int32, (LANES, LANES), 1)
        allowed = key_at <= query_at

        def scores_of(pair):
            return against(
                keys_rm, index, pair, by_queries(qkv[0, pair, :, lanes]), has_off
            )

        ahead = scores_of(0)
        for pair in range(pairs):
            scores = ahead
            if pair + 1 < pairs:
                ahead = scores_of(pair + 1)
            mixed = []
            for head in range(2):
                rows = slice(head * half, (head + 1) * half)
                lows = []
                for part in range(2):
                    tiles = tiles_of(scores, head, part, has_off)
                    tiles[0] = jnp.where(allowed, tiles[0], -1e30)
                    top = jnp.max(functools.reduce(jnp.maximum, tiles), axis=0, keepdims=True)
                    raised = [jnp.exp(tile - top) for tile in tiles]
                    total = functools.reduce(jnp.add, raised)
                    scale = 1.0 / jnp.sum(total, axis=0, keepdims=True)
                    lows.append([(tile * scale).astype(BF16) for tile in raised])
                low, low_off = joined(lows, has_off)
                share[index, pair, head] = low
                mix = dot_plain(qkv[2, pair, rows, lanes], low)
                if has_off:
                    share_off[pair, head] = low_off
                    mix = mix + dot_plain(qkv[2, pair, rows, :piece], low_off)
                mixed.append(mix.astype(BF16))
            mixture[pair, :, lanes] = jnp.concatenate(mixed, axis=0)

    def part_sum(values):
        return jnp.sum(values.reshape(values.shape[0] // 8, 8, values.shape[1]), axis=0)

    def full_mean(parts):
        return jnp.sum(parts, axis=0, keepdims=True) * (1.0 / width)

    def column(index, rows):
        part = columns[index, rows, :].astype(F32)
        return jnp.concatenate([part] * (piece // LANES), axis=1)

    def gather_sum(index, rows, values):
        sums[index, rows, :] = sums[index, rows, :] + fold(values)

    def norm_chunks(index, which, total):
        mean = full_mean(total)
        spread = jnp.zeros((8, piece), F32)
        for rows in chunks:
            centred = wide_a[rows, :] - mean
            spread = spread + part_sum(centred * centred)
        inverse = lax.rsqrt(full_mean(spread) + EPS)
        inverses[index, which] = inverse
        return mean, inverse

    def forward(index):
        lanes = lanes_of(index)

        @pl.when(segment == 0)
        def _():
            x_t[:, lanes] = own_rows(index).astype(BF16)

        @pl.when(segment == 1)
        def _():
            forward_copy(index).wait_recv()

        inputs = x_t[:, lanes]
        score_scale = 1.0 / math.sqrt(width // HEADS)
        for block in range(3):
            result = dot_plain(turned[block], inputs)
            for pair in range(pairs):
                low = result[pair * LANES : (pair + 1) * LANES]
                low = (low * score_scale if block == 0 else low).astype(BF16)
                qkv[block, pair, :, lanes] = low
                if block == 1:
                    keys_rm[index, pair] = low.T
                if block == 2:
                    values_rm[index, pair] = low.T

        @pl.when(index == 1)
        def _():
            attend(index, True)

        @pl.when(index != 1)
        def _():
            attend(index, False)

        branch = dot_plain(turned[3], mixture[:, :, lanes].reshape(width, piece))
        total = jnp.zeros((8, piece), F32)
        for rows in chunks:
            sum_one = x_t[rows, lanes].astype(F32) + (branch[rows] + column(BIAS_OUT, rows))
            wide_a[rows, :] = sum_one
            total = total + part_sum(sum_one)
        mean, inverse = norm_chunks(index, 0, total)
        for rows in chunks:
            normed = (wide_a[rows, :] - mean) * inverse
            norm_one[rows, lanes] = normed
            hidden = normed * column(GAIN_ONE, rows) + column(BIAS_ONE, rows)
            hidden_low[rows, lanes] = hidden.astype(BF16)

        def activate(block, pre_block):
            for rows in chunks:
                pre = pre_block[rows] + column(BIAS_UP + block, rows)
                bell = jnp.exp2(pre * pre * (-0.5 * math.log2(math.e)))
                level = (lax.erf(pre * (1.0 / math.sqrt(2.0))) + 1.0) * 0.5
                active[block, rows, lanes] = (pre * level).astype(BF16)
                slope[block, rows, lanes] = (
                    level + pre * bell * (1.0 / math.sqrt(2.0 * math.pi))
                ).astype(BF16)

        for block in range(4):
            activate(block, dot_plain(turned[4 + block], hidden_low[:, lanes]))
        branch_two = dot_plain(down_turned[...], active[:, :, lanes].reshape(4 * width, piece))
        total = jnp.zeros((8, piece), F32)
        for rows in chunks:
            hidden = norm_one[rows, lanes] * column(GAIN_ONE, rows) + column(BIAS_ONE, rows)
            sum_two = hidden + (branch_two[rows] + column(BIAS_DOWN, rows))
            wide_a[rows, :] = sum_two
            total = total + part_sum(sum_two)
        mean, inverse = norm_chunks(index, 1, total)

        for rows in chunks:
            norm_two[rows, lanes] = (wide_a[rows, :] - mean) * inverse

        @pl.when(segment == 0)
        def _():
            for rows in chunks:
                outgoing[index, rows, :] = output_rows(rows, lanes).astype(BF16)
            forward_copy(index).start()

    def output_rows(rows, lanes):
        return norm_two[rows, lanes] * column(GAIN_TWO, rows) + column(BIAS_TWO, rows)

    def last_outputs(index, carry):
        free_ends(index)
        for start in range(0, width, LANES):
            rows = slice(start, start + LANES)
            ends_v[lax.rem(index, 2), :, rows] = output_rows(rows, lanes_of(index)).T
        ends_copy(index).start()
        return carry

    def attend_back(index, has_off):
        lanes = lanes_of(index)
        slot = jnp.where(index == 0, 1, 0)
        half = LANES // 2
        score_scale = 1.0 / math.sqrt(width // HEADS)

        def backs_of(pair):
            return against(values_rm, index, pair, by_queries(grad_mix[pair]), has_off)

        ahead = backs_of(0)
        for pair in range(pairs):
            backs = ahead
            if pair + 1 < pairs:
                ahead = backs_of(pair + 1)
            results = ([], [], [])
            for head in range(2):
                rows = slice(head * half, (head + 1) * half)
                low = share[index, pair, head]
                low_off = share_off[pair, head] if has_off else None
                lows = []
                for part in range(2):
                    place = slice(part * LANES, (part + 1) * LANES)
                    wides = [low[place, place]]
                    if part:
                        wides.append(low[:LANES, place])
                    if has_off:
                        wides += [low_off[:LANES, place], low_off[LANES:, place]]
                    wides = [tile.astype(F32) for tile in wides]
                    tiles = tiles_of(backs, head, part, has_off)
                    products = [wide * tile for wide, tile in zip(wides, tiles)]
                    inner = jnp.sum(functools.reduce(jnp.add, products), axis=0, keepdims=True)
                    lows.append(
                        [
                            (product - wide * inner).astype(BF16)
                            for product, wide in zip(products, wides)
                        ]
                    )
                grad_scores, grad_off = joined(lows, has_off)
                queries = qkv[0, pair, rows, lanes]
                grads = grad_mix[pair, rows]
                grad_query = dot_plain(qkv[1, pair, rows, lanes], grad_scores)
                grad_key = dot_turned(queries, grad_scores) + key_sums[slot, 0, pair, rows]
                grad_value = dot_turned(grads, low) + key_sums[slot, 1, pair, rows]
                if has_off:
                    grad_query = grad_query + dot_plain(qkv[1, pair, rows, :piece], grad_off)
                    key_sums[1, 0, pair, rows] = dot_turned(queries, grad_off)
                    key_sums[1, 1, pair, rows] = dot_turned(grads, low_off)
                for kept, grad in zip(results, (grad_query * score_scale, grad_key, grad_value)):
                    kept.append(grad.astype(BF16))
            for block in range(3):
                qkv[block, pair, :, lanes] = jnp.concatenate(results[block], axis=0)

    def backward(index):
        lanes = lanes_of(index)

        @pl.when(segment == 0)
        def _():
            backward_copy(index).wait_recv()

        plain = jnp.zeros((8, piece), F32)
        inner = jnp.zeros((8, piece), F32)
        for rows in chunks:
            grad = incoming_grad[index, rows, :].astype(F32)
            product = grad * norm_two[rows, lanes]
            gather_sum(GAIN_TWO, rows, product)
            gather_sum(BIAS_TWO, rows, grad)
            gain = column(GAIN_TWO, rows)
            plain = plain + part_sum(grad * gain)
            inner = inner + part_sum(product * gain)
        plain = full_mean(plain)
        inner = full_mean(inner)
        inverse = inverses[index, 1]
        for rows in chunks:
            scaled = incoming_grad[index, rows, :].astype(F32) * column(GAIN_TWO, rows)
            grad_two = (scaled - plain - norm_two[rows, lanes] * inner) * inverse
            gather_sum(BIAS_DOWN, rows, grad_two)
            wide_a[rows, :] = grad_two
            down_grad[rows, lanes] = grad_two.astype(BF16)

        for block in range(4):
            back = dot_plain(w_down[block], down_grad[:, lanes])
            for rows in chunks:
                grad_pre = back[rows] * slope[block, rows, lanes].astype(F32)
                gather_sum(BIAS_UP + block, rows, grad_pre)
                slope[block, rows, lanes] = grad_pre.astype(BF16)

        through = dot_plain(w_up[...], slope[:, :, lanes].reshape(4 * width, piece))
        plain = jnp.zeros((8, piece), F32)
        inner = jnp.zeros((8, piece), F32)
        for rows in chunks:
            grad_hidden = wide_a[rows, :] + through[rows]
            wide_a[rows, :] = grad_hidden
            product = grad_hidden * norm_one[rows, lanes]
            gather_sum(GAIN_ONE, rows, product)
            gather_sum(BIAS_ONE, rows, grad_hidden)
            gain = column(GAIN_ONE, rows)
            plain = plain + part_sum(grad_hidden * gain)
            inner = inner + part_sum(product * gain)
        plain = full_mean(plain)
        inner = full_mean(inner)
        inverse = inverses[index, 0]
        for rows in chunks:
            scaled = wide_a[rows, :] * column(GAIN_ONE, rows)
            grad_one = (scaled - plain - norm_one[rows, lanes] * inner) * inverse
            gather_sum(BIAS_OUT, rows, grad_one)
            wide_b[rows, :] = grad_one
            branch_grad[rows, lanes] = grad_one.astype(BF16)
        grad_mix[...] = (
            dot_plain(w_out[...], branch_grad[:, lanes]).astype(BF16).reshape(pairs, LANES, piece)
        )

    def backward_attention(index):
        lanes = lanes_of(index)

        @pl.when(index == 1)
        def _():
            attend_back(index, True)

        @pl.when(index != 1)
        def _():
            attend_back(index, False)

        through = dot_plain(w_qkv[...], qkv[:, :, :, lanes].reshape(3 * width, piece))

        @pl.when(segment == 1)
        def _():
            for rows in chunks:
                outgoing[index, rows, :] = (wide_b[rows, :] + through[rows]).astype(BF16)
            backward_copy(index).start()

        @pl.when(segment == 0)
        def _():
            free_ends(index)
            for start in range(0, width, LANES):
                rows = slice(start, start + LANES)
                ends_v[lax.rem(index, 2), :, rows] = (wide_b[rows, :] + through[rows]).T
            ends_copy(index).start()

    def held(job):
        group = job // 2
        return (w_down, 0) if group == 0 else (turned, 4 if group == 1 else 0)

    def core_copy(job):
        buffer, base = held(job)
        lanes = lanes_in(job)
        return pltpu.make_async_remote_copy(
            src_ref=buffer.at[pl.ds(base + 2 * (1 - core), 2), :, lanes],
            dst_ref=core_in.at[job // 2, :, :, lanes],
            send_sem=core_send.at[job],
            recv_sem=core_recv.at[job],
            device_id={"rep": other_core},
            device_id_type=MESH,
        )

    def side_copy(job):
        buffer, base = held(job)
        lanes = lanes_in(job)
        source = buffer.at[base + 2 * core + (1 - side), :, lanes]
        target = side_in.at[job // 2, :, lanes]
        if job in DP_FIRST:
            source = buffer.at[base + 2 * core + (1 - side), dp_rows(dp_steps - 1)[1], lanes]
            target = side_in.at[job // 2, pl.ds(0, share_rows), lanes]
        return pltpu.make_async_remote_copy(
            src_ref=source,
            dst_ref=target,
            send_sem=side_send.at[job],
            recv_sem=side_recv.at[job],
            device_id={"rep": other_side},
            device_id_type=MESH,
        )

    def dp_slot(job):
        return (4, 0, 1, 2, 3, 6)[job]

    def dp_rows(step):
        count = dp_count // 2
        start = 0
        for bit in range(step):
            start = start + lax.rem(lax.div(dp, 2**bit), 2) * count
            count = count // 2
        mine = lax.rem(lax.div(dp, 2**step), 2)
        sent = pl.multiple_of((start + (1 - mine) * count) * share_rows, share_rows)
        kept = pl.multiple_of((start + mine * count) * share_rows, share_rows)
        return pl.ds(sent, count * share_rows), pl.ds(kept, count * share_rows)

    def dp_landing(step):
        count = dp_count // 2 ** (step + 1)
        return pl.ds((dp_count - 2 * count) * share_rows, count * share_rows)

    def dp_copy(job, step):
        buffer, base = held(job)
        lanes = lanes_in(job)
        slot = dp_slot(job)
        mine = lax.rem(lax.div(dp, 2**step), 2)
        if job in DP_FIRST:
            source = buffer.at[pl.ds(base + 2 * core, 2), dp_rows(step)[0], lanes]
            target = dp_in.at[pl.ds(slot, 2), dp_landing(step)]
        else:
            source = buffer.at[base + 2 * core + side, dp_rows(step)[0], lanes]
            target = dp_in.at[slot, dp_landing(step)]
        return pltpu.make_async_remote_copy(
            src_ref=source,
            dst_ref=target,
            send_sem=dp_send.at[job, step],
            recv_sem=dp_recv.at[job, step],
            device_id={"dp": dp + (1 - 2 * mine) * 2**step},
            device_id_type=MESH,
        )

    def join_copy(job):
        lanes = lanes_in(job)
        return pltpu.make_async_remote_copy(
            src_ref=fin.at[job // 2, 2 * core + side, :, lanes],
            dst_ref=fin.at[job // 2, 2 * core + side, :, lanes],
            send_sem=join_send.at[job],
            recv_sem=join_recv.at[job],
            device_id={"rep": other_side},
            device_id_type=MESH,
        )

    def last_copy(job):
        lanes = lanes_in(job)
        return pltpu.make_async_remote_copy(
            src_ref=fin.at[job // 2, pl.ds(2 * core, 2), :, lanes],
            dst_ref=fin.at[job // 2, pl.ds(2 * core, 2), :, lanes],
            send_sem=last_send.at[job],
            recv_sem=last_recv.at[job],
            device_id={"rep": other_core},
            device_id_type=MESH,
        )

    def lanes_in(job):
        half = job % 2
        return slice(half * (width // 2), (half + 1) * (width // 2))

    def turned_bits(value, count):
        place = 0
        while count > 1:
            place = place * 2 + value % 2
            value = value // 2
            count = count // 2
        return place

    def down_sums(job):
        part = 4 * share_rows
        count = width // part
        lanes = lanes_in(job)

        def one(block, carry):
            result = dot_turned(active[block], down_grad[lanes, :]).astype(BF16)
            high = lax.rem(block, 2) * 2 + lax.div(block, 2)
            for each in range(count):
                place = turned_bits(each, count) * 4 + high
                target = pl.multiple_of(place * share_rows, share_rows)
                for position in range(4):
                    start = each * part + position * share_rows
                    w_down[position, pl.ds(target, share_rows), lanes] = result[
                        start : start + share_rows
                    ]
            return carry

        lax.fori_loop(0, 4, one, 0)

    def keep_rows(position, lanes, result):
        for index in range(dp_count):
            start = turned_bits(index, dp_count) * share_rows
            turned[position, start : start + share_rows, lanes] = result[
                index * share_rows : (index + 1) * share_rows
            ]

    def up_sums(job):
        lanes = lanes_in(job)

        def one(block, carry):
            result = dot_turned(hidden_low[...], slope[block, lanes, :]).astype(BF16)
            keep_rows(4 + block, lanes, result)
            return carry

        lax.fori_loop(0, 4, one, 0)

    def qkv_sums(job):
        lanes = lanes_in(job)
        half_pairs = slice((job % 2) * (pairs // 2), (job % 2 + 1) * (pairs // 2))

        def one(block, carry):
            grads = qkv[block, half_pairs].reshape(width // 2, PIECES * piece)
            keep_rows(block, lanes, dot_turned(x_t[...], grads).astype(BF16))
            return carry

        lax.fori_loop(0, 3, one, 0)
        mixed = mixture[...].reshape(width, PIECES * piece)
        keep_rows(3, lanes, dot_turned(mixed, branch_grad[lanes, :]).astype(BF16))

    def sums_of(job):
        (down_sums, up_sums, qkv_sums)[job // 2](job)
        core_copy(job).start()

    def arrived(copy):
        copy.wait_send()
        copy.wait_recv()

    def after_core(job):
        buffer, base = held(job)
        lanes = lanes_in(job)
        arrived(core_copy(job))
        for each in range(2):
            if each == 0 or job in DP_FIRST:
                place = 1 - side if each == 0 else side
                position = base + 2 * core + place
                buffer[position, :, lanes] = (
                    buffer[position, :, lanes].astype(F32)
                    + core_in[job // 2, place, :, lanes].astype(F32)
                ).astype(BF16)
        if job in DP_FIRST:
            dp_copy(job, 0).start()

    def after_side(job):
        buffer, base = held(job)
        lanes = lanes_in(job)
        arrived(side_copy(job))
        second = base + 2 * core + side
        if job in DP_FIRST:
            rows = dp_rows(dp_steps - 1)[1]
            total = buffer[second, rows, lanes].astype(F32) + side_in[
                job // 2, :share_rows, lanes
            ].astype(F32)
            fin[job // 2, 2 * core + side, :, lanes] = total.astype(BF16)
            join_copy(job).start()
            return
        buffer[second, :, lanes] = (
            buffer[second, :, lanes].astype(F32)
            + core_in[job // 2, side, :, lanes].astype(F32)
            + side_in[job // 2, :, lanes].astype(F32)
        ).astype(BF16)
        dp_copy(job, 0).start()

    def dp_total(job, step, each):
        buffer, base = held(job)
        lanes = lanes_in(job)
        position = base + 2 * core + (each if job in DP_FIRST else side)
        kept = buffer[position, dp_rows(step)[1], lanes].astype(F32)
        return position, kept + dp_in[dp_slot(job) + each, dp_landing(step), :].astype(F32)

    def dp_parts(job):
        return range(2) if job in DP_FIRST else range(1)

    def after_dp(job):
        buffer, _ = held(job)
        for step in range(dp_steps - 1):
            arrived(dp_copy(job, step))
            for each in dp_parts(job):
                position, total = dp_total(job, step, each)
                buffer[position, dp_rows(step)[1], lanes_in(job)] = total.astype(BF16)
            dp_copy(job, step + 1).start()

    def after_last_dp(job):
        buffer, _ = held(job)
        lanes = lanes_in(job)
        step = dp_steps - 1
        arrived(dp_copy(job, step))
        for each in dp_parts(job):
            position, total = dp_total(job, step, each)
            if job in DP_FIRST:
                buffer[position, dp_rows(step)[1], lanes] = total.astype(BF16)
            else:
                fin[job // 2, 2 * core + side, :, lanes] = total.astype(BF16)
        if job in DP_FIRST:
            side_copy(job).start()
        else:
            join_copy(job).start()

    def after_join(job):
        arrived(join_copy(job))
        last_copy(job).start()

    def fin_copy(job):
        lanes = lanes_in(job)
        return pltpu.make_async_copy(
            fin.at[job // 2, :, :, lanes], fin_hbm.at[job // 2, :, :, lanes], fin_sem.at[job]
        )

    def after_last(job):
        arrived(last_copy(job))
        fin_copy(job).start()

    def early_sums():
        sums_of(0)
        sums_of(1)
        after_core(0)
        sums_of(2)
        after_core(1)
        side_copy(1).start()
        sums_of(3)
        after_core(2)
        side_copy(2).start()

    def one_step(step, carry):
        first_index = jnp.where(step < 4, step, jnp.where(step < 6, 5 - step, step - 4))
        last_index = jnp.where(step < 2, step, jnp.where(step < 4, 3 - step, lax.div(step, 2)))
        first_is = jnp.where(step < 4, 1, 0)
        last_is = jnp.where(step < 2, 1, jnp.where(step < 4, 0, 1 - lax.rem(step, 2)))
        index = jnp.minimum(jnp.where(segment == 0, first_index, last_index), PIECES - 1)
        is_forward = jnp.where(segment == 0, first_is, last_is)
        is_last = jnp.where(step == 2 * PIECES, 1, 0)
        is_split = jnp.where(step >= 2 * PIECES - 1, 1 - segment, 0)

        @pl.when(is_forward * (1 - is_last) == 1)
        def _():
            forward(index)

        @pl.when(is_forward + is_last == 0)
        def _():
            backward(index)

        @pl.when(is_last == 1)
        def _():
            early_sums()

        @pl.when((1 - is_forward) * (1 - is_split) * (1 - is_last) + is_last * is_split == 1)
        def _():
            backward_attention(index)

        return carry

    @pl.when(segment == 1)
    def _():
        for index in range(PIECES):
            incoming_grad[index] = own_rows(index).astype(BF16)

    lax.fori_loop(0, 2 * PIECES + 1, one_step, 0)

    def small_dp_copy(step):
        target = lax.rem(dp + step, dp_count)
        return pltpu.make_async_remote_copy(
            src_ref=small.at[target],
            dst_ref=small_dp.at[step - 1],
            send_sem=sdp_send.at[step - 1],
            recv_sem=sdp_recv.at[step - 1],
            device_id={"dp": target},
            device_id_type=MESH,
        )

    def small_rep_copy(step):
        return pltpu.make_async_remote_copy(
            src_ref=small_rep.at[rep],
            dst_ref=small_rep.at[rep],
            send_sem=srep_send.at[step - 1],
            recv_sem=srep_recv.at[step - 1],
            device_id={"rep": lax.rem(rep + step, 4)},
            device_id_type=MESH,
        )

    sums_of(4)
    after_dp(0)
    after_core(3)
    sums_of(5)
    after_side(1)
    side_copy(3).start()
    after_core(4)
    after_core(5)

    @pl.when(segment == 1)
    def _():
        lax.fori_loop(0, PIECES, last_outputs, 0)

    rows_of = [jnp.sum(sums[index].T, axis=0, keepdims=True) for index in range(STATS)]
    small[...] = jnp.zeros(small.shape, F32)
    for share_index in range(dp_count):
        for index in range(BIAS_UP):
            start = share_index * share_rows
            small[share_index, index : index + 1, :share_rows] = rows_of[index][
                :, start : start + share_rows
            ]
        for part in range(4):
            start = (share_index * 4 + part) * share_rows
            block, start = start // width, start % width
            small[share_index, BIAS_UP + part : BIAS_UP + part + 1, :share_rows] = rows_of[
                BIAS_UP + block
            ][:, start : start + share_rows]
    for step in range(1, dp_count):
        small_dp_copy(step).start()

    after_last_dp(0)
    after_side(2)
    side_copy(4).start()
    after_dp(1)
    after_side(0)
    small_total = small[dp]
    for step in range(1, dp_count):
        arrived(small_dp_copy(step))
        small_total = small_total + small_dp[step - 1]
    small_rep[rep] = small_total
    for step in range(1, 4):
        small_rep_copy(step).start()
    after_last_dp(1)
    after_dp(2)
    after_dp(5)
    after_join(0)
    after_side(3)
    after_last_dp(2)
    after_last_dp(5)
    after_join(1)
    after_dp(3)
    for step in range(1, 4):
        arrived(small_rep_copy(step))
    small_out[...] = (small_rep[0] + small_rep[1]) + (small_rep[2] + small_rep[3])
    small_copy = pltpu.make_async_copy(small_out, small_hbm, load_sem.at[0])
    small_copy.start()
    after_last(0)
    after_side(4)
    after_join(2)
    after_last_dp(3)
    after_side(5)
    after_last(1)
    after_dp(4)
    after_last(2)
    after_join(3)
    after_join(5)
    after_last_dp(4)
    after_last(3)
    after_last(5)
    after_join(4)
    after_last(4)

    for index in range(PIECES):

        @pl.when(segment == 0)
        def _():
            forward_copy(index).wait_send()

        @pl.when(segment == 1)
        def _():
            backward_copy(index).wait_send()

    for index in range(2, PIECES):
        ends_copy(index).wait()
    for job in range(6):
        fin_copy(job).wait()
    small_copy.wait()


def finish_kernel(
    flag_ref,
    ends_in,
    fin,
    small,
    ends,
    grad_qkv,
    grad_out,
    grad_up,
    grad_down,
    grad_up_bias,
    grad_gains,
    grad_biases,
    ends_v,
    fin_v,
    wide_qkv,
    wide_out,
    wide_up,
    wide_down,
    small_v,
    up_bias_v,
    gains_v,
    biases_v,
    ends_sem,
    in_sem,
    out_sem,
):
    half = ends_in.shape[0] // 2
    share_rows, width = fin.shape[2:]
    start = pl.multiple_of(half * (1 - flag_ref[0, 0]), half)
    cut = half // 4
    ends_copies = []
    ends_loads = []
    for part in range(8):
        source = pl.ds(part * cut, cut)
        offset = start + part * cut if part < 4 else part * cut - half + (half - start)
        target = pl.ds(pl.multiple_of(offset, cut), cut)
        ends_loads.append(
            pltpu.make_async_copy(ends_in.at[source], ends_v.at[source], ends_sem.at[part])
        )
        ends_copies.append(
            pltpu.make_async_copy(ends_v.at[source], ends.at[0, target], ends_sem.at[8 + part])
        )
    loads = [
        pltpu.make_async_copy(fin.at[group], fin_v.at[group], in_sem.at[group])
        for group in range(3)
    ]
    stores = [
        pltpu.make_async_copy(wide, target.at[0], out_sem.at[index])
        for index, (wide, target) in enumerate(
            ((wide_down, grad_down), (wide_up, grad_up), (wide_qkv, grad_qkv), (wide_out, grad_out))
        )
    ]
    small_load = pltpu.make_async_copy(small, small_v, in_sem.at[3])
    small_stores = [
        pltpu.make_async_copy(narrow, target, out_sem.at[4 + index])
        for index, (narrow, target) in enumerate(
            ((up_bias_v, grad_up_bias), (gains_v, grad_gains), (biases_v, grad_biases))
        )
    ]
    small_load.start()
    for copy in loads + ends_loads:
        copy.start()
    for load, copy in zip(ends_loads, ends_copies):
        load.wait()
        copy.start()
    loads[0].wait()
    for position in range(4):
        rows = slice(position * share_rows, (position + 1) * share_rows)
        wide_down[rows, :] = fin_v[0, position].astype(F32)
    stores[0].start()
    loads[1].wait()
    for position in range(4):
        wide_up[:, position * width : (position + 1) * width] = fin_v[1, position].astype(F32)
    stores[1].start()
    loads[2].wait()
    for position in range(3):
        wide_qkv[:, position * width : (position + 1) * width] = fin_v[2, position].astype(F32)
    stores[2].start()
    wide_out[...] = fin_v[2, 3].astype(F32)
    stores[3].start()
    small_load.wait()
    for position in range(4):
        rows = slice(position * share_rows, (position + 1) * share_rows)
        up_bias_v[:, rows] = small_v[BIAS_UP + position : BIAS_UP + position + 1, :share_rows]
    gains_v[0] = small_v[:2, :share_rows]
    biases_v[0] = small_v[2:BIAS_UP, :share_rows]
    for copy in small_stores:
        copy.start()
    for copy in stores + ends_copies + small_stores:
        copy.wait()


def on_device(
    dp_count,
    block_input,
    cotangent,
    window_group,
    w_qkv,
    w_out,
    w_up,
    w_down,
    up_bias,
    norm_gains,
    biases,
):
    rows, width = block_input.shape
    piece = rows // PIECES
    pairs = width // LANES
    share_rows = width // dp_count
    small_width = max(share_rows, LANES)
    dp_steps = dp_count.bit_length() - 1
    any_spec = pl.BlockSpec(memory_space=pl.ANY)
    vmem_spec = pl.BlockSpec(memory_space=pltpu.VMEM)
    smem_spec = pl.BlockSpec(memory_space=pltpu.SMEM)
    dma = pltpu.SemaphoreType.DMA
    vmem = pltpu.VMEM
    ends_in, fin, small = pl.pallas_call(
        functools.partial(layer_kernel, dp_count),
        out_shape=(
            jax.ShapeDtypeStruct((PIECES, piece, width), F32),
            jax.ShapeDtypeStruct((3, 4, share_rows, width), BF16),
            jax.ShapeDtypeStruct((16, small_width), F32),
        ),
        in_specs=[smem_spec] + [any_spec] * 6 + [vmem_spec] * 3,
        out_specs=(any_spec,) * 3,
        scratch_shapes=[
            vmem((width, 3 * width), BF16),
            vmem((width, width), BF16),
            vmem((width, 4 * width), BF16),
            vmem((4, width, width), BF16),
            vmem((8, width, width), BF16),
            vmem((width, 4 * width), BF16),
            vmem((PIECES, piece, width), BF16),
            vmem((width, rows), BF16),
            vmem((3, pairs, LANES, rows), BF16),
            vmem((PIECES, pairs, piece, LANES), BF16),
            vmem((PIECES, pairs, piece, LANES), BF16),
            vmem((PIECES, pairs, 2, piece, piece), BF16),
            vmem((pairs, 2, piece, piece), BF16),
            vmem((pairs, LANES, rows), BF16),
            vmem((width, rows), F32),
            vmem((width, rows), F32),
            vmem((PIECES, 2, 1, piece), F32),
            vmem((width, rows), BF16),
            vmem((4, width, rows), BF16),
            vmem((4, width, rows), BF16),
            vmem((width, rows), BF16),
            vmem((width, rows), BF16),
            vmem((pairs, LANES, piece), BF16),
            vmem((PIECES, width, piece), BF16),
            vmem((PIECES, width, piece), BF16),
            vmem((STATS, width, LANES), BF16),
            vmem((STATS, width, LANES), F32),
            vmem((2, 2, pairs, LANES, piece), F32),
            vmem((width, piece), F32),
            vmem((width, piece), F32),
            vmem((2, piece, width), F32),
            vmem((3, 2, width, width), BF16),
            vmem((3, width, width), BF16),
            vmem((8, width - share_rows, width // 2), BF16),
            vmem((3, 4, share_rows, width), BF16),
            vmem((dp_count, 16, small_width), F32),
            vmem((dp_count - 1, 16, small_width), F32),
            vmem((4, 16, small_width), F32),
            vmem((16, small_width), F32),
            dma((13,)),
            dma((PIECES,)),
            dma((PIECES,)),
            dma((PIECES,)),
            dma((6,)),
            dma((6,)),
            dma((6,)),
            dma((6,)),
            dma((6, dp_steps)),
            dma((6, dp_steps)),
            dma((6,)),
            dma((6,)),
            dma((6,)),
            dma((6,)),
            dma((dp_count - 1,)),
            dma((dp_count - 1,)),
            dma((3,)),
            dma((3,)),
            dma((6,)),
        ],
        compiler_params=pltpu.CompilerParams(
            collective_id=0, has_side_effects=True, vmem_limit_bytes=63 * 1024 * 1024
        ),
    )(
        window_group,
        block_input.reshape(PIECES, piece, width),
        cotangent.reshape(PIECES, piece, width),
        w_qkv,
        w_out,
        w_up,
        w_down,
        up_bias,
        norm_gains,
        biases,
    )
    return pl.pallas_call(
        finish_kernel,
        out_shape=(
            jax.ShapeDtypeStruct((1, rows, width), F32),
            jax.ShapeDtypeStruct((1, share_rows, 3 * width), F32),
            jax.ShapeDtypeStruct((1, share_rows, width), F32),
            jax.ShapeDtypeStruct((1, share_rows, 4 * width), F32),
            jax.ShapeDtypeStruct((1, 4 * share_rows, width), F32),
            jax.ShapeDtypeStruct((1, 4 * share_rows), F32),
            jax.ShapeDtypeStruct((1, 2, share_rows), F32),
            jax.ShapeDtypeStruct((1, 4, share_rows), F32),
        ),
        in_specs=[smem_spec] + [any_spec] * 3,
        out_specs=(any_spec,) * 8,
        scratch_shapes=[
            vmem((rows, width), F32),
            vmem((3, 4, share_rows, width), BF16),
            vmem((share_rows, 3 * width), F32),
            vmem((share_rows, width), F32),
            vmem((share_rows, 4 * width), F32),
            vmem((4 * share_rows, width), F32),
            vmem((16, small_width), F32),
            vmem((1, 4 * share_rows), F32),
            vmem((1, 2, share_rows), F32),
            vmem((1, 4, share_rows), F32),
            dma((16,)),
            dma((4,)),
            dma((7,)),
        ],
        compiler_params=pltpu.CompilerParams(vmem_limit_bytes=63 * 1024 * 1024),
    )(window_group, ends_in.reshape(rows, width), fin, small)


def solution(mesh):
    return jax.shard_map(
        functools.partial(on_device, mesh.shape["dp"]),
        mesh=mesh,
        in_specs=(
            P(("dp", "rep"), None),
            P(("dp", "rep"), None),
            P(("dp", "rep"), None),
            P("segment", None, None),
            P("segment", None, None),
            P("segment", None, None),
            P("segment", None, None),
            P("segment", None),
            P("segment", None, None),
            P("segment", None, None),
        ),
        out_specs=(
            P("segment", ("dp", "rep"), None),
            P("segment", "dp", None),
            P("segment", "dp", None),
            P("segment", "dp", None),
            P("segment", "dp", None),
            P("segment", "dp"),
            P("segment", None, "dp"),
            P("segment", None, "dp"),
        ),
        check_vma=False,
    )
```

```python
import functools
import math

import jax
import jax.numpy as jnp
from jax import lax
from jax.experimental import pallas as pl
from jax.experimental.pallas import tpu as pltpu
from jax.sharding import PartitionSpec as P

MESH = pl.DeviceIdType.MESH
F32 = jnp.float32
BF16 = jnp.bfloat16
HEADS = 8
LANES = 128
PIECES = 4
EPS = 1e-05
GAIN_ONE, GAIN_TWO, BIAS_OUT, BIAS_ONE, BIAS_DOWN, BIAS_TWO, BIAS_UP = range(7)
STATS = 10
CHUNK = 64
DP_FIRST = (0, 5)


def dot_plain(left, right):
    return lax.dot_general(left, right, (((1,), (0,)), ((), ())), preferred_element_type=F32)


def dot_turned(left, right):
    return lax.dot_general(left, right, (((1,), (1,)), ((), ())), preferred_element_type=F32)


def fold(values):
    total = values[:, :LANES]
    for start in range(LANES, values.shape[1], LANES):
        total = total + values[:, start : start + LANES]
    return total


def layer_kernel(
    dp_count,
    flag_ref,
    x_hbm,
    ct_hbm,
    w_qkv_hbm,
    w_out_hbm,
    w_up_hbm,
    w_down_hbm,
    up_bias_ref,
    gains_ref,
    biases_ref,
    ends_hbm,
    fin_hbm,
    small_hbm,
    w_qkv,
    w_out,
    w_up,
    w_down,
    turned,
    down_turned,
    rows_in,
    x_t,
    qkv,
    keys_rm,
    values_rm,
    share,
    share_off,
    mixture,
    norm_one,
    norm_two,
    inverses,
    hidden_low,
    slope,
    active,
    down_grad,
    branch_grad,
    grad_mix,
    outgoing,
    incoming_grad,
    columns,
    sums,
    key_sums,
    wide_a,
    wide_b,
    ends_v,
    core_in,
    side_in,
    dp_in,
    fin,
    small,
    small_dp,
    small_rep,
    small_out,
    load_sem,
    seg_send,
    seg_recv,
    ends_sem,
    core_send,
    core_recv,
    side_send,
    side_recv,
    dp_send,
    dp_recv,
    join_send,
    join_recv,
    last_send,
    last_recv,
    sdp_send,
    sdp_recv,
    srep_send,
    srep_recv,
    fin_sem,
):
    width = w_out.shape[0]
    piece = x_t.shape[1] // PIECES
    pairs = qkv.shape[1]
    share_rows = width // dp_count
    dp_steps = dp_count.bit_length() - 1
    segment = lax.axis_index("segment")
    dp = lax.axis_index("dp")
    rep = lax.axis_index("rep")
    core = lax.rem(rep, 2)
    side = lax.div(rep, 2)
    other_core = side * 2 + (1 - core)
    other_side = (1 - side) * 2 + core

    loads = []
    for block in range(3):
        span = pl.ds(block * width, width)
        loads.append((w_qkv_hbm.at[0, :, span], w_qkv.at[:, span]))
    loads.append((w_out_hbm.at[0], w_out))
    for block in range(4):
        span = pl.ds(block * width, width)
        loads.append((w_up_hbm.at[0, :, span], w_up.at[:, span]))
    for block in range(4):
        span = pl.ds(block * width, width)
        loads.append((w_down_hbm.at[0, span, :], w_down.at[block]))
    load_copies = [
        pltpu.make_async_copy(source, target, load_sem.at[index + 1])
        for index, (source, target) in enumerate(loads)
    ]
    first_rows = pltpu.make_async_copy(x_hbm, rows_in, load_sem.at[0])
    last_rows = pltpu.make_async_copy(ct_hbm, rows_in, load_sem.at[0])

    @pl.when(segment == 0)
    def _():
        first_rows.start()

    @pl.when(segment == 1)
    def _():
        last_rows.start()

    for copy in load_copies:
        copy.start()

    barrier = pltpu.get_barrier_semaphore()
    pl.semaphore_signal(
        barrier, inc=1, device_id={"segment": 1 - segment}, device_id_type=MESH
    )
    for step in range(1, 4):
        pl.semaphore_signal(
            barrier, inc=1, device_id={"rep": lax.rem(rep + step, 4)}, device_id_type=MESH
        )
    for step in range(1, dp_count):
        pl.semaphore_signal(
            barrier, inc=1, device_id={"dp": lax.rem(dp + step, dp_count)}, device_id_type=MESH
        )

    params = [gains_ref[0].astype(F32), biases_ref[0].astype(F32)]
    for block in range(4):
        params.append(up_bias_ref[:, block * width : (block + 1) * width].astype(F32))
    params.append(jnp.zeros((16 - STATS, width), F32))
    upright = jnp.concatenate(params, axis=0).T
    for index in range(STATS):
        columns[index] = jnp.broadcast_to(upright[:, index : index + 1], (width, LANES)).astype(BF16)
    for index in range(STATS):
        sums[index] = jnp.zeros((width, LANES), F32)
    key_sums[0] = jnp.zeros(key_sums.shape[1:], F32)

    chunks = [slice(start, start + CHUNK) for start in range(0, width, CHUNK)]

    for block, copy in enumerate(load_copies):
        copy.wait()
        span = slice(block % 4 * width, (block % 4 + 1) * width)
        if block < 3:
            turned[block] = w_qkv[:, span].T
        elif block == 3:
            turned[block] = w_out[...].T
        elif block < 8:
            turned[block] = w_up[:, span].T
        else:
            down_turned[:, span] = w_down[block - 8].T
    first_rows.wait()

    pl.semaphore_wait(barrier, 4 + dp_count - 1)

    flag = flag_ref[0, 0].astype(F32)

    def lanes_of(index):
        return pl.ds(pl.multiple_of(index * piece, piece), piece)

    def forward_copy(index):
        return pltpu.make_async_remote_copy(
            src_ref=outgoing.at[index],
            dst_ref=x_t.at[:, lanes_of(index)],
            send_sem=seg_send.at[index],
            recv_sem=seg_recv.at[index],
            device_id={"segment": 1 - segment},
            device_id_type=MESH,
        )

    def backward_copy(index):
        return pltpu.make_async_remote_copy(
            src_ref=outgoing.at[index],
            dst_ref=incoming_grad.at[index],
            send_sem=seg_send.at[index],
            recv_sem=seg_recv.at[index],
            device_id={"segment": 1 - segment},
            device_id_type=MESH,
        )

    def ends_copy(index):
        return pltpu.make_async_copy(
            ends_v.at[lax.rem(index, 2)], ends_hbm.at[index], ends_sem.at[index]
        )

    def free_ends(index):
        @pl.when(index >= 2)
        def _():
            ends_copy(index - 2).wait()

    def own_rows(index):
        half = lax.rem(index, 2)
        whole = jnp.where(index < 2, 1.0, 0.0).astype(F32)
        weight = whole * flag + (1.0 - whole) * (1.0 - flag)
        picked = rows_in[half].astype(F32) * weight + rows_in[2 + half].astype(F32) * (1.0 - weight)
        return picked.T

    def by_queries(values):
        half = LANES // 2
        blank = jnp.zeros((half, LANES), values.dtype)
        parts = []
        for part in range(2):
            span = slice(part * LANES, (part + 1) * LANES)
            first = jnp.concatenate([values[:half, span], blank], axis=0)
            second = jnp.concatenate([blank, values[half:, span]], axis=0)
            parts.append(jnp.concatenate([first, second], axis=1))
        return parts

    def against(rows_ref, index, pair, parts, has_off):
        own = rows_ref[index, pair]
        products = [dot_plain(own[:LANES], parts[0]), dot_plain(own, parts[1])]
        if has_off:
            before = rows_ref[0, pair]
            products += [dot_plain(before, parts[0]), dot_plain(before, parts[1])]
        return products

    def tiles_of(products, head, part, has_off):
        lanes = slice(head * LANES, (head + 1) * LANES)
        own = products[part]
        tiles = [own[part * LANES : (part + 1) * LANES, lanes]]
        if part:
            tiles.append(own[:LANES, lanes])
        if has_off:
            off = products[2 + part]
            tiles += [off[:LANES, lanes], off[LANES:, lanes]]
        return tiles

    def joined(lows, has_off):
        blank = jnp.zeros((LANES, LANES), BF16)
        first = jnp.concatenate([lows[0][0], blank], axis=0)
        second = jnp.concatenate([lows[1][1], lows[1][0]], axis=0)
        whole = jnp.concatenate([first, second], axis=1)
        if not has_off:
            return whole, None
        first = jnp.concatenate(lows[0][-2:], axis=0)
        second = jnp.concatenate(lows[1][-2:], axis=0)
        return whole, jnp.concatenate([first, second], axis=1)

    def attend(index, has_off):
        lanes = lanes_of(index)
        half = LANES // 2
        key_at = lax.broadcasted_iota(jnp.int32, (LANES, LANES), 0)
        query_at = lax.broadcasted_iota(jnp.int32, (LANES, LANES), 1)
        allowed = key_at <= query_at

        def scores_of(pair):
            return against(
                keys_rm, index, pair, by_queries(qkv[0, pair, :, lanes]), has_off
            )

        ahead = scores_of(0)
        for pair in range(pairs):
            scores = ahead
            if pair + 1 < pairs:
                ahead = scores_of(pair + 1)
            mixed = []
            for head in range(2):
                rows = slice(head * half, (head + 1) * half)
                lows = []
                for part in range(2):
                    tiles = tiles_of(scores, head, part, has_off)
                    tiles[0] = jnp.where(allowed, tiles[0], -1e30)
                    top = jnp.max(functools.reduce(jnp.maximum, tiles), axis=0, keepdims=True)
                    raised = [jnp.exp(tile - top) for tile in tiles]
                    total = functools.reduce(jnp.add, raised)
                    scale = 1.0 / jnp.sum(total, axis=0, keepdims=True)
                    lows.append([(tile * scale).astype(BF16) for tile in raised])
                low, low_off = joined(lows, has_off)
                share[index, pair, head] = low
                mix = dot_plain(qkv[2, pair, rows, lanes], low)
                if has_off:
                    share_off[pair, head] = low_off
                    mix = mix + dot_plain(qkv[2, pair, rows, :piece], low_off)
                mixed.append(mix.astype(BF16))
            mixture[pair, :, lanes] = jnp.concatenate(mixed, axis=0)

    def part_sum(values):
        return jnp.sum(values.reshape(values.shape[0] // 8, 8, values.shape[1]), axis=0)

    def full_mean(parts):
        return jnp.sum(parts, axis=0, keepdims=True) * (1.0 / width)

    def column(index, rows):
        part = columns[index, rows, :].astype(F32)
        return jnp.concatenate([part] * (piece // LANES), axis=1)

    def gather_sum(index, rows, values):
        sums[index, rows, :] = sums[index, rows, :] + fold(values)

    def norm_chunks(index, which, total):
        mean = full_mean(total)
        spread = jnp.zeros((8, piece), F32)
        for rows in chunks:
            centred = wide_a[rows, :] - mean
            spread = spread + part_sum(centred * centred)
        inverse = lax.rsqrt(full_mean(spread) + EPS)
        inverses[index, which] = inverse
        return mean, inverse

    def forward(index):
        lanes = lanes_of(index)

        @pl.when(segment == 0)
        def _():
            x_t[:, lanes] = own_rows(index).astype(BF16)

        @pl.when(segment == 1)
        def _():
            forward_copy(index).wait_recv()

        inputs = x_t[:, lanes]
        score_scale = 1.0 / math.sqrt(width // HEADS)
        for block in range(3):
            result = dot_plain(turned[block], inputs)
            for pair in range(pairs):
                low = result[pair * LANES : (pair + 1) * LANES]
                low = (low * score_scale if block == 0 else low).astype(BF16)
                qkv[block, pair, :, lanes] = low
                if block == 1:
                    keys_rm[index, pair] = low.T
                if block == 2:
                    values_rm[index, pair] = low.T

        @pl.when(index == 1)
        def _():
            attend(index, True)

        @pl.when(index != 1)
        def _():
            attend(index, False)

        branch = dot_plain(turned[3], mixture[:, :, lanes].reshape(width, piece))
        total = jnp.zeros((8, piece), F32)
        for rows in chunks:
            sum_one = x_t[rows, lanes].astype(F32) + (branch[rows] + column(BIAS_OUT, rows))
            wide_a[rows, :] = sum_one
            total = total + part_sum(sum_one)
        mean, inverse = norm_chunks(index, 0, total)
        for rows in chunks:
            normed = (wide_a[rows, :] - mean) * inverse
            norm_one[rows, lanes] = normed
            hidden = normed * column(GAIN_ONE, rows) + column(BIAS_ONE, rows)
            hidden_low[rows, lanes] = hidden.astype(BF16)

        def activate(block, pre_block):
            for rows in chunks:
                pre = pre_block[rows] + column(BIAS_UP + block, rows)
                bell = jnp.exp2(pre * pre * (-0.5 * math.log2(math.e)))
                level = (lax.erf(pre * (1.0 / math.sqrt(2.0))) + 1.0) * 0.5
                active[block, rows, lanes] = (pre * level).astype(BF16)
                slope[block, rows, lanes] = (
                    level + pre * bell * (1.0 / math.sqrt(2.0 * math.pi))
                ).astype(BF16)

        for block in range(4):
            activate(block, dot_plain(turned[4 + block], hidden_low[:, lanes]))
        branch_two = dot_plain(down_turned[...], active[:, :, lanes].reshape(4 * width, piece))
        total = jnp.zeros((8, piece), F32)
        for rows in chunks:
            hidden = norm_one[rows, lanes] * column(GAIN_ONE, rows) + column(BIAS_ONE, rows)
            sum_two = hidden + (branch_two[rows] + column(BIAS_DOWN, rows))
            wide_a[rows, :] = sum_two
            total = total + part_sum(sum_two)
        mean, inverse = norm_chunks(index, 1, total)

        for rows in chunks:
            norm_two[rows, lanes] = (wide_a[rows, :] - mean) * inverse

        @pl.when(segment == 0)
        def _():
            for rows in chunks:
                outgoing[index, rows, :] = output_rows(rows, lanes).astype(BF16)
            forward_copy(index).start()

    def output_rows(rows, lanes):
        return norm_two[rows, lanes] * column(GAIN_TWO, rows) + column(BIAS_TWO, rows)

    def last_outputs(index, carry):
        free_ends(index)
        for start in range(0, width, LANES):
            rows = slice(start, start + LANES)
            ends_v[lax.rem(index, 2), :, rows] = output_rows(rows, lanes_of(index)).T
        ends_copy(index).start()
        return carry

    def attend_back(index, has_off):
        lanes = lanes_of(index)
        slot = jnp.where(index == 0, 1, 0)
        half = LANES // 2
        score_scale = 1.0 / math.sqrt(width // HEADS)

        def backs_of(pair):
            return against(values_rm, index, pair, by_queries(grad_mix[pair]), has_off)

        ahead = backs_of(0)
        for pair in range(pairs):
            backs = ahead
            if pair + 1 < pairs:
                ahead = backs_of(pair + 1)
            results = ([], [], [])
            for head in range(2):
                rows = slice(head * half, (head + 1) * half)
                low = share[index, pair, head]
                low_off = share_off[pair, head] if has_off else None
                lows = []
                for part in range(2):
                    place = slice(part * LANES, (part + 1) * LANES)
                    wides = [low[place, place]]
                    if part:
                        wides.append(low[:LANES, place])
                    if has_off:
                        wides += [low_off[:LANES, place], low_off[LANES:, place]]
                    wides = [tile.astype(F32) for tile in wides]
                    tiles = tiles_of(backs, head, part, has_off)
                    products = [wide * tile for wide, tile in zip(wides, tiles)]
                    inner = jnp.sum(functools.reduce(jnp.add, products), axis=0, keepdims=True)
                    lows.append(
                        [
                            (product - wide * inner).astype(BF16)
                            for product, wide in zip(products, wides)
                        ]
                    )
                grad_scores, grad_off = joined(lows, has_off)
                queries = qkv[0, pair, rows, lanes]
                grads = grad_mix[pair, rows]
                grad_query = dot_plain(qkv[1, pair, rows, lanes], grad_scores)
                grad_key = dot_turned(queries, grad_scores) + key_sums[slot, 0, pair, rows]
                grad_value = dot_turned(grads, low) + key_sums[slot, 1, pair, rows]
                if has_off:
                    grad_query = grad_query + dot_plain(qkv[1, pair, rows, :piece], grad_off)
                    key_sums[1, 0, pair, rows] = dot_turned(queries, grad_off)
                    key_sums[1, 1, pair, rows] = dot_turned(grads, low_off)
                for kept, grad in zip(results, (grad_query * score_scale, grad_key, grad_value)):
                    kept.append(grad.astype(BF16))
            for block in range(3):
                qkv[block, pair, :, lanes] = jnp.concatenate(results[block], axis=0)

    def backward(index):
        lanes = lanes_of(index)

        @pl.when(segment == 0)
        def _():
            backward_copy(index).wait_recv()

        plain = jnp.zeros((8, piece), F32)
        inner = jnp.zeros((8, piece), F32)
        for rows in chunks:
            grad = incoming_grad[index, rows, :].astype(F32)
            product = grad * norm_two[rows, lanes]
            gather_sum(GAIN_TWO, rows, product)
            gather_sum(BIAS_TWO, rows, grad)
            gain = column(GAIN_TWO, rows)
            plain = plain + part_sum(grad * gain)
            inner = inner + part_sum(product * gain)
        plain = full_mean(plain)
        inner = full_mean(inner)
        inverse = inverses[index, 1]
        for rows in chunks:
            scaled = incoming_grad[index, rows, :].astype(F32) * column(GAIN_TWO, rows)
            grad_two = (scaled - plain - norm_two[rows, lanes] * inner) * inverse
            gather_sum(BIAS_DOWN, rows, grad_two)
            wide_a[rows, :] = grad_two
            down_grad[rows, lanes] = grad_two.astype(BF16)

        for block in range(4):
            back = dot_plain(w_down[block], down_grad[:, lanes])
            for rows in chunks:
                grad_pre = back[rows] * slope[block, rows, lanes].astype(F32)
                gather_sum(BIAS_UP + block, rows, grad_pre)
                slope[block, rows, lanes] = grad_pre.astype(BF16)

        through = dot_plain(w_up[...], slope[:, :, lanes].reshape(4 * width, piece))
        plain = jnp.zeros((8, piece), F32)
        inner = jnp.zeros((8, piece), F32)
        for rows in chunks:
            grad_hidden = wide_a[rows, :] + through[rows]
            wide_a[rows, :] = grad_hidden
            product = grad_hidden * norm_one[rows, lanes]
            gather_sum(GAIN_ONE, rows, product)
            gather_sum(BIAS_ONE, rows, grad_hidden)
            gain = column(GAIN_ONE, rows)
            plain = plain + part_sum(grad_hidden * gain)
            inner = inner + part_sum(product * gain)
        plain = full_mean(plain)
        inner = full_mean(inner)
        inverse = inverses[index, 0]
        for rows in chunks:
            scaled = wide_a[rows, :] * column(GAIN_ONE, rows)
            grad_one = (scaled - plain - norm_one[rows, lanes] * inner) * inverse
            gather_sum(BIAS_OUT, rows, grad_one)
            wide_b[rows, :] = grad_one
            branch_grad[rows, lanes] = grad_one.astype(BF16)
        grad_mix[...] = (
            dot_plain(w_out[...], branch_grad[:, lanes]).astype(BF16).reshape(pairs, LANES, piece)
        )

    def backward_attention(index):
        lanes = lanes_of(index)

        @pl.when(index == 1)
        def _():
            attend_back(index, True)

        @pl.when(index != 1)
        def _():
            attend_back(index, False)

        through = dot_plain(w_qkv[...], qkv[:, :, :, lanes].reshape(3 * width, piece))

        @pl.when(segment == 1)
        def _():
            for rows in chunks:
                outgoing[index, rows, :] = (wide_b[rows, :] + through[rows]).astype(BF16)
            backward_copy(index).start()

        @pl.when(segment == 0)
        def _():
            free_ends(index)
            for start in range(0, width, LANES):
                rows = slice(start, start + LANES)
                ends_v[lax.rem(index, 2), :, rows] = (wide_b[rows, :] + through[rows]).T
            ends_copy(index).start()

    def held(job):
        group = job // 2
        return (w_down, 0) if group == 0 else (turned, 4 if group == 1 else 0)

    class Several:
        def __init__(self, copies):
            self.copies = copies

        def start(self):
            for copy in self.copies:
                copy.start()

        def wait_send(self):
            for copy in self.copies:
                copy.wait_send()

        def wait_recv(self):
            for copy in self.copies:
                copy.wait_recv()

    def core_copy(job):
        buffer, base = held(job)
        lanes = lanes_in(job)
        copies = []
        for part in range(4):
            rows = pl.ds(part % 2 * (width // 2), width // 2)
            copies.append(
                pltpu.make_async_remote_copy(
                    src_ref=buffer.at[base + 2 * (1 - core) + part // 2, rows, lanes],
                    dst_ref=core_in.at[job // 2, part // 2, rows, lanes],
                    send_sem=core_send.at[job, part],
                    recv_sem=core_recv.at[job, part],
                    device_id={"rep": other_core},
                    device_id_type=MESH,
                )
            )
        return Several(copies)

    def side_copy(job):
        buffer, base = held(job)
        lanes = lanes_in(job)
        position = base + 2 * core + (1 - side)
        pairs_of_rows = []
        if job in DP_FIRST:
            pairs_of_rows.append((dp_rows(dp_steps - 1)[1], pl.ds(0, share_rows)))
        else:
            for part in range(4):
                rows = pl.ds(part * (width // 4), width // 4)
                pairs_of_rows.append((rows, rows))
        return Several(
            [
                pltpu.make_async_remote_copy(
                    src_ref=buffer.at[position, rows, lanes],
                    dst_ref=side_in.at[job // 2, target, lanes],
                    send_sem=side_send.at[job, part],
                    recv_sem=side_recv.at[job, part],
                    device_id={"rep": other_side},
                    device_id_type=MESH,
                )
                for part, (rows, target) in enumerate(pairs_of_rows)
            ]
        )

    def dp_slot(job):
        return (4, 0, 1, 2, 3, 6)[job]

    def dp_rows(step):
        count = dp_count // 2
        start = 0
        for bit in range(step):
            start = start + lax.rem(lax.div(dp, 2**bit), 2) * count
            count = count // 2
        mine = lax.rem(lax.div(dp, 2**step), 2)
        sent = pl.multiple_of((start + (1 - mine) * count) * share_rows, share_rows)
        kept = pl.multiple_of((start + mine * count) * share_rows, share_rows)
        return pl.ds(sent, count * share_rows), pl.ds(kept, count * share_rows)

    def dp_landing(step):
        count = dp_count // 2 ** (step + 1)
        return pl.ds((dp_count - 2 * count) * share_rows, count * share_rows)

    def dp_copy(job, step):
        buffer, base = held(job)
        lanes = lanes_in(job)
        mine = lax.rem(lax.div(dp, 2**step), 2)
        return Several(
            [
                pltpu.make_async_remote_copy(
                    src_ref=buffer.at[
                        base + 2 * core + (each if job in DP_FIRST else side),
                        dp_rows(step)[0],
                        lanes,
                    ],
                    dst_ref=dp_in.at[dp_slot(job) + each, dp_landing(step)],
                    send_sem=dp_send.at[job, step, each],
                    recv_sem=dp_recv.at[job, step, each],
                    device_id={"dp": dp + (1 - 2 * mine) * 2**step},
                    device_id_type=MESH,
                )
                for each in dp_parts(job)
            ]
        )

    def dp_parts(job):
        return range(2) if job in DP_FIRST else range(1)

    def join_copy(job):
        lanes = lanes_in(job)
        return pltpu.make_async_remote_copy(
            src_ref=fin.at[job // 2, 2 * core + side, :, lanes],
            dst_ref=fin.at[job // 2, 2 * core + side, :, lanes],
            send_sem=join_send.at[job],
            recv_sem=join_recv.at[job],
            device_id={"rep": other_side},
            device_id_type=MESH,
        )

    def last_copy(job):
        lanes = lanes_in(job)
        return pltpu.make_async_remote_copy(
            src_ref=fin.at[job // 2, pl.ds(2 * core, 2), :, lanes],
            dst_ref=fin.at[job // 2, pl.ds(2 * core, 2), :, lanes],
            send_sem=last_send.at[job],
            recv_sem=last_recv.at[job],
            device_id={"rep": other_core},
            device_id_type=MESH,
        )

    def lanes_in(job):
        half = job % 2
        return slice(half * (width // 2), (half + 1) * (width // 2))

    def turned_bits(value, count):
        place = 0
        while count > 1:
            place = place * 2 + value % 2
            value = value // 2
            count = count // 2
        return place

    def down_sums(job):
        part = 4 * share_rows
        count = width // part
        lanes = lanes_in(job)

        def one(block, carry):
            result = dot_turned(active[block], down_grad[lanes, :]).astype(BF16)
            high = lax.rem(block, 2) * 2 + lax.div(block, 2)
            for each in range(count):
                place = turned_bits(each, count) * 4 + high
                target = pl.multiple_of(place * share_rows, share_rows)
                for position in range(4):
                    start = each * part + position * share_rows
                    w_down[position, pl.ds(target, share_rows), lanes] = result[
                        start : start + share_rows
                    ]
            return carry

        lax.fori_loop(0, 4, one, 0)

    def keep_rows(position, lanes, result):
        for index in range(dp_count):
            start = turned_bits(index, dp_count) * share_rows
            turned[position, start : start + share_rows, lanes] = result[
                index * share_rows : (index + 1) * share_rows
            ]

    def up_sums(job):
        lanes = lanes_in(job)

        def one(block, carry):
            result = dot_turned(hidden_low[...], slope[block, lanes, :]).astype(BF16)
            keep_rows(4 + block, lanes, result)
            return carry

        lax.fori_loop(0, 4, one, 0)

    def qkv_sums(job):
        lanes = lanes_in(job)
        half_pairs = slice((job % 2) * (pairs // 2), (job % 2 + 1) * (pairs // 2))

        def one(block, carry):
            grads = qkv[block, half_pairs].reshape(width // 2, PIECES * piece)
            keep_rows(block, lanes, dot_turned(x_t[...], grads).astype(BF16))
            return carry

        lax.fori_loop(0, 3, one, 0)
        mixed = mixture[...].reshape(width, PIECES * piece)
        keep_rows(3, lanes, dot_turned(mixed, branch_grad[lanes, :]).astype(BF16))

    def sums_of(job):
        (down_sums, up_sums, qkv_sums)[job // 2](job)
        core_copy(job).start()

    def arrived(copy):
        copy.wait_send()
        copy.wait_recv()

    def after_core(job):
        buffer, base = held(job)
        lanes = lanes_in(job)
        arrived(core_copy(job))
        for each in range(2):
            if each == 0 or job in DP_FIRST:
                place = 1 - side if each == 0 else side
                position = base + 2 * core + place
                buffer[position, :, lanes] = (
                    buffer[position, :, lanes].astype(F32)
                    + core_in[job // 2, place, :, lanes].astype(F32)
                ).astype(BF16)
        if job in DP_FIRST:
            dp_copy(job, 0).start()

    def after_side(job):
        buffer, base = held(job)
        lanes = lanes_in(job)
        arrived(side_copy(job))
        second = base + 2 * core + side
        if job in DP_FIRST:
            rows = dp_rows(dp_steps - 1)[1]
            total = buffer[second, rows, lanes].astype(F32) + side_in[
                job // 2, :share_rows, lanes
            ].astype(F32)
            fin[job // 2, 2 * core + side, :, lanes] = total.astype(BF16)
            join_copy(job).start()
            return
        buffer[second, :, lanes] = (
            buffer[second, :, lanes].astype(F32)
            + core_in[job // 2, side, :, lanes].astype(F32)
            + side_in[job // 2, :, lanes].astype(F32)
        ).astype(BF16)
        dp_copy(job, 0).start()

    def dp_total(job, step, each):
        buffer, base = held(job)
        lanes = lanes_in(job)
        position = base + 2 * core + (each if job in DP_FIRST else side)
        kept = buffer[position, dp_rows(step)[1], lanes].astype(F32)
        return position, kept + dp_in[dp_slot(job) + each, dp_landing(step), :].astype(F32)

    def after_dp(job):
        buffer, _ = held(job)
        for step in range(dp_steps - 1):
            arrived(dp_copy(job, step))
            for each in dp_parts(job):
                position, total = dp_total(job, step, each)
                buffer[position, dp_rows(step)[1], lanes_in(job)] = total.astype(BF16)
            dp_copy(job, step + 1).start()

    def after_last_dp(job):
        buffer, _ = held(job)
        lanes = lanes_in(job)
        step = dp_steps - 1
        arrived(dp_copy(job, step))
        for each in dp_parts(job):
            position, total = dp_total(job, step, each)
            if job in DP_FIRST:
                buffer[position, dp_rows(step)[1], lanes] = total.astype(BF16)
            else:
                fin[job // 2, 2 * core + side, :, lanes] = total.astype(BF16)
        if job in DP_FIRST:
            side_copy(job).start()
        else:
            join_copy(job).start()

    def after_join(job):
        arrived(join_copy(job))
        last_copy(job).start()

    def fin_copy(job):
        lanes = lanes_in(job)
        return pltpu.make_async_copy(
            fin.at[job // 2, :, :, lanes], fin_hbm.at[job // 2, :, :, lanes], fin_sem.at[job]
        )

    def after_last(job):
        arrived(last_copy(job))
        fin_copy(job).start()

    def early_sums():
        sums_of(0)
        sums_of(1)
        after_core(0)
        sums_of(2)
        after_core(1)
        side_copy(1).start()
        sums_of(3)
        after_core(2)
        side_copy(2).start()

    def one_step(step, carry):
        first_index = jnp.where(step < 4, step, jnp.where(step < 6, 5 - step, step - 4))
        last_index = jnp.where(step < 2, step, jnp.where(step < 4, 3 - step, lax.div(step, 2)))
        first_is = jnp.where(step < 4, 1, 0)
        last_is = jnp.where(step < 2, 1, jnp.where(step < 4, 0, 1 - lax.rem(step, 2)))
        index = jnp.minimum(jnp.where(segment == 0, first_index, last_index), PIECES - 1)
        is_forward = jnp.where(segment == 0, first_is, last_is)
        is_last = jnp.where(step == 2 * PIECES, 1, 0)
        is_split = jnp.where(step >= 2 * PIECES - 1, 1 - segment, 0)

        @pl.when(is_forward * (1 - is_last) == 1)
        def _():
            forward(index)

        @pl.when(is_forward + is_last == 0)
        def _():
            backward(index)

        @pl.when(is_last == 1)
        def _():
            early_sums()

        @pl.when((1 - is_forward) * (1 - is_split) * (1 - is_last) + is_last * is_split == 1)
        def _():
            backward_attention(index)

        return carry

    @pl.when(segment == 1)
    def _():
        for index in range(PIECES):
            incoming_grad[index] = own_rows(index).astype(BF16)

    lax.fori_loop(0, 2 * PIECES + 1, one_step, 0)

    def small_dp_copy(step):
        target = lax.rem(dp + step, dp_count)
        return pltpu.make_async_remote_copy(
            src_ref=small.at[target],
            dst_ref=small_dp.at[step - 1],
            send_sem=sdp_send.at[step - 1],
            recv_sem=sdp_recv.at[step - 1],
            device_id={"dp": target},
            device_id_type=MESH,
        )

    def small_rep_copy(step):
        return pltpu.make_async_remote_copy(
            src_ref=small_rep.at[rep],
            dst_ref=small_rep.at[rep],
            send_sem=srep_send.at[step - 1],
            recv_sem=srep_recv.at[step - 1],
            device_id={"rep": lax.rem(rep + step, 4)},
            device_id_type=MESH,
        )

    sums_of(4)
    after_dp(0)
    after_core(3)
    sums_of(5)
    after_side(1)
    side_copy(3).start()
    after_core(4)
    after_core(5)

    @pl.when(segment == 1)
    def _():
        lax.fori_loop(0, PIECES, last_outputs, 0)

    rows_of = [jnp.sum(sums[index].T, axis=0, keepdims=True) for index in range(STATS)]
    small[...] = jnp.zeros(small.shape, F32)
    for share_index in range(dp_count):
        for index in range(BIAS_UP):
            start = share_index * share_rows
            small[share_index, index : index + 1, :share_rows] = rows_of[index][
                :, start : start + share_rows
            ]
        for part in range(4):
            start = (share_index * 4 + part) * share_rows
            block, start = start // width, start % width
            small[share_index, BIAS_UP + part : BIAS_UP + part + 1, :share_rows] = rows_of[
                BIAS_UP + block
            ][:, start : start + share_rows]
    for step in range(1, dp_count):
        small_dp_copy(step).start()

    after_last_dp(0)
    after_side(2)
    side_copy(4).start()
    after_dp(1)
    after_side(0)
    small_total = small[dp]
    for step in range(1, dp_count):
        arrived(small_dp_copy(step))
        small_total = small_total + small_dp[step - 1]
    small_rep[rep] = small_total
    for step in range(1, 4):
        small_rep_copy(step).start()
    after_last_dp(1)
    after_dp(2)
    after_dp(5)
    after_join(0)
    after_side(3)
    after_last_dp(2)
    after_last_dp(5)
    after_join(1)
    after_dp(3)
    for step in range(1, 4):
        arrived(small_rep_copy(step))
    small_out[...] = (small_rep[0] + small_rep[1]) + (small_rep[2] + small_rep[3])
    small_copy = pltpu.make_async_copy(small_out, small_hbm, load_sem.at[0])
    small_copy.start()
    after_last(0)
    after_side(4)
    after_join(2)
    after_last_dp(3)
    after_side(5)
    after_last(1)
    after_dp(4)
    after_last(2)
    after_join(3)
    after_join(5)
    after_last_dp(4)
    after_last(3)
    after_last(5)
    after_join(4)
    after_last(4)

    for index in range(PIECES):

        @pl.when(segment == 0)
        def _():
            forward_copy(index).wait_send()

        @pl.when(segment == 1)
        def _():
            backward_copy(index).wait_send()

    for index in range(2, PIECES):
        ends_copy(index).wait()
    for job in range(6):
        fin_copy(job).wait()
    small_copy.wait()


def finish_kernel(
    flag_ref,
    ends_in,
    fin,
    small,
    ends,
    grad_qkv,
    grad_out,
    grad_up,
    grad_down,
    grad_up_bias,
    grad_gains,
    grad_biases,
    ends_v,
    fin_v,
    wide_qkv,
    wide_out,
    wide_up,
    wide_down,
    small_v,
    up_bias_v,
    gains_v,
    biases_v,
    ends_sem,
    in_sem,
    out_sem,
):
    half = ends_in.shape[0] // 2
    share_rows, width = fin.shape[2:]
    start = pl.multiple_of(half * (1 - flag_ref[0, 0]), half)
    cut = half // 4
    ends_copies = []
    ends_loads = []
    for part in range(8):
        source = pl.ds(part * cut, cut)
        offset = start + part * cut if part < 4 else part * cut - half + (half - start)
        target = pl.ds(pl.multiple_of(offset, cut), cut)
        ends_loads.append(
            pltpu.make_async_copy(ends_in.at[source], ends_v.at[source], ends_sem.at[part])
        )
        ends_copies.append(
            pltpu.make_async_copy(ends_v.at[source], ends.at[0, target], ends_sem.at[8 + part])
        )
    loads = [
        pltpu.make_async_copy(fin.at[group], fin_v.at[group], in_sem.at[group])
        for group in range(3)
    ]
    stores = [
        pltpu.make_async_copy(wide, target.at[0], out_sem.at[index])
        for index, (wide, target) in enumerate(
            ((wide_down, grad_down), (wide_up, grad_up), (wide_qkv, grad_qkv), (wide_out, grad_out))
        )
    ]
    small_load = pltpu.make_async_copy(small, small_v, in_sem.at[3])
    small_stores = [
        pltpu.make_async_copy(narrow, target, out_sem.at[4 + index])
        for index, (narrow, target) in enumerate(
            ((up_bias_v, grad_up_bias), (gains_v, grad_gains), (biases_v, grad_biases))
        )
    ]
    small_load.start()
    for copy in loads + ends_loads:
        copy.start()
    for load, copy in zip(ends_loads, ends_copies):
        load.wait()
        copy.start()
    loads[0].wait()
    for position in range(4):
        rows = slice(position * share_rows, (position + 1) * share_rows)
        wide_down[rows, :] = fin_v[0, position].astype(F32)
    stores[0].start()
    loads[1].wait()
    for position in range(4):
        wide_up[:, position * width : (position + 1) * width] = fin_v[1, position].astype(F32)
    stores[1].start()
    loads[2].wait()
    for position in range(3):
        wide_qkv[:, position * width : (position + 1) * width] = fin_v[2, position].astype(F32)
    stores[2].start()
    wide_out[...] = fin_v[2, 3].astype(F32)
    stores[3].start()
    small_load.wait()
    for position in range(4):
        rows = slice(position * share_rows, (position + 1) * share_rows)
        up_bias_v[:, rows] = small_v[BIAS_UP + position : BIAS_UP + position + 1, :share_rows]
    gains_v[0] = small_v[:2, :share_rows]
    biases_v[0] = small_v[2:BIAS_UP, :share_rows]
    for copy in small_stores:
        copy.start()
    for copy in stores + ends_copies + small_stores:
        copy.wait()


def on_device(
    dp_count,
    block_input,
    cotangent,
    window_group,
    w_qkv,
    w_out,
    w_up,
    w_down,
    up_bias,
    norm_gains,
    biases,
):
    rows, width = block_input.shape
    piece = rows // PIECES
    pairs = width // LANES
    share_rows = width // dp_count
    small_width = max(share_rows, LANES)
    dp_steps = dp_count.bit_length() - 1
    any_spec = pl.BlockSpec(memory_space=pl.ANY)
    vmem_spec = pl.BlockSpec(memory_space=pltpu.VMEM)
    smem_spec = pl.BlockSpec(memory_space=pltpu.SMEM)
    dma = pltpu.SemaphoreType.DMA
    vmem = pltpu.VMEM
    ends_in, fin, small = pl.pallas_call(
        functools.partial(layer_kernel, dp_count),
        out_shape=(
            jax.ShapeDtypeStruct((PIECES, piece, width), F32),
            jax.ShapeDtypeStruct((3, 4, share_rows, width), BF16),
            jax.ShapeDtypeStruct((16, small_width), F32),
        ),
        in_specs=[smem_spec] + [any_spec] * 6 + [vmem_spec] * 3,
        out_specs=(any_spec,) * 3,
        scratch_shapes=[
            vmem((width, 3 * width), BF16),
            vmem((width, width), BF16),
            vmem((width, 4 * width), BF16),
            vmem((4, width, width), BF16),
            vmem((8, width, width), BF16),
            vmem((width, 4 * width), BF16),
            vmem((PIECES, piece, width), BF16),
            vmem((width, rows), BF16),
            vmem((3, pairs, LANES, rows), BF16),
            vmem((PIECES, pairs, piece, LANES), BF16),
            vmem((PIECES, pairs, piece, LANES), BF16),
            vmem((PIECES, pairs, 2, piece, piece), BF16),
            vmem((pairs, 2, piece, piece), BF16),
            vmem((pairs, LANES, rows), BF16),
            vmem((width, rows), F32),
            vmem((width, rows), F32),
            vmem((PIECES, 2, 1, piece), F32),
            vmem((width, rows), BF16),
            vmem((4, width, rows), BF16),
            vmem((4, width, rows), BF16),
            vmem((width, rows), BF16),
            vmem((width, rows), BF16),
            vmem((pairs, LANES, piece), BF16),
            vmem((PIECES, width, piece), BF16),
            vmem((PIECES, width, piece), BF16),
            vmem((STATS, width, LANES), BF16),
            vmem((STATS, width, LANES), F32),
            vmem((2, 2, pairs, LANES, piece), F32),
            vmem((width, piece), F32),
            vmem((width, piece), F32),
            vmem((2, piece, width), F32),
            vmem((3, 2, width, width), BF16),
            vmem((3, width, width), BF16),
            vmem((8, width - share_rows, width // 2), BF16),
            vmem((3, 4, share_rows, width), BF16),
            vmem((dp_count, 16, small_width), F32),
            vmem((dp_count - 1, 16, small_width), F32),
            vmem((4, 16, small_width), F32),
            vmem((16, small_width), F32),
            dma((13,)),
            dma((PIECES,)),
            dma((PIECES,)),
            dma((PIECES,)),
            dma((6, 4)),
            dma((6, 4)),
            dma((6, 4)),
            dma((6, 4)),
            dma((6, dp_steps, 2)),
            dma((6, dp_steps, 2)),
            dma((6,)),
            dma((6,)),
            dma((6,)),
            dma((6,)),
            dma((dp_count - 1,)),
            dma((dp_count - 1,)),
            dma((3,)),
            dma((3,)),
            dma((6,)),
        ],
        compiler_params=pltpu.CompilerParams(
            collective_id=0, has_side_effects=True, vmem_limit_bytes=63 * 1024 * 1024
        ),
    )(
        window_group,
        block_input.reshape(PIECES, piece, width),
        cotangent.reshape(PIECES, piece, width),
        w_qkv,
        w_out,
        w_up,
        w_down,
        up_bias,
        norm_gains,
        biases,
    )
    return pl.pallas_call(
        finish_kernel,
        out_shape=(
            jax.ShapeDtypeStruct((1, rows, width), F32),
            jax.ShapeDtypeStruct((1, share_rows, 3 * width), F32),
            jax.ShapeDtypeStruct((1, share_rows, width), F32),
            jax.ShapeDtypeStruct((1, share_rows, 4 * width), F32),
            jax.ShapeDtypeStruct((1, 4 * share_rows, width), F32),
            jax.ShapeDtypeStruct((1, 4 * share_rows), F32),
            jax.ShapeDtypeStruct((1, 2, share_rows), F32),
            jax.ShapeDtypeStruct((1, 4, share_rows), F32),
        ),
        in_specs=[smem_spec] + [any_spec] * 3,
        out_specs=(any_spec,) * 8,
        scratch_shapes=[
            vmem((rows, width), F32),
            vmem((3, 4, share_rows, width), BF16),
            vmem((share_rows, 3 * width), F32),
            vmem((share_rows, width), F32),
            vmem((share_rows, 4 * width), F32),
            vmem((4 * share_rows, width), F32),
            vmem((16, small_width), F32),
            vmem((1, 4 * share_rows), F32),
            vmem((1, 2, share_rows), F32),
            vmem((1, 4, share_rows), F32),
            dma((16,)),
            dma((4,)),
            dma((7,)),
        ],
        compiler_params=pltpu.CompilerParams(vmem_limit_bytes=63 * 1024 * 1024),
    )(window_group, ends_in.reshape(rows, width), fin, small)


def solution(mesh):
    return jax.shard_map(
        functools.partial(on_device, mesh.shape["dp"]),
        mesh=mesh,
        in_specs=(
            P(("dp", "rep"), None),
            P(("dp", "rep"), None),
            P(("dp", "rep"), None),
            P("segment", None, None),
            P("segment", None, None),
            P("segment", None, None),
            P("segment", None, None),
            P("segment", None),
            P("segment", None, None),
            P("segment", None, None),
        ),
        out_specs=(
            P("segment", ("dp", "rep"), None),
            P("segment", "dp", None),
            P("segment", "dp", None),
            P("segment", "dp", None),
            P("segment", "dp", None),
            P("segment", "dp"),
            P("segment", None, "dp"),
            P("segment", None, "dp"),
        ),
        check_vma=False,
    )
```

```python
import functools
import math

import jax
import jax.numpy as jnp
from jax import lax
from jax.experimental import pallas as pl
from jax.experimental.pallas import tpu as pltpu
from jax.sharding import PartitionSpec as P

MESH = pl.DeviceIdType.MESH
F32 = jnp.float32
BF16 = jnp.bfloat16
HEADS = 8
LANES = 128
PIECES = 4
EPS = 1e-05
GAIN_ONE, GAIN_TWO, BIAS_OUT, BIAS_ONE, BIAS_DOWN, BIAS_TWO, BIAS_UP = range(7)
STATS = 10
CHUNK = 64
JOBS = 12
DP_FIRST = (1, 3, 6, 10)
SUM, CORE, SIDE, SIDED, DP, DPED, JOIN, LAST, SMALL = range(9)
ORDER_ONE = (
    (SUM, 0), (SUM, 2),
)
ORDER_TWO = (
    (SUM, 4), (CORE, 1), (CORE, 0), (SIDE, 0), (SUM, 6), (CORE, 2), (SIDE, 2), (CORE, 3),
)
ORDER_THREE = (
    (CORE, 5), (SUM, 8), (SIDE, 5), (CORE, 6), (DP, 3), (CORE, 4), (SUM, 10), (CORE, 7), (SIDE, 4),
    (SIDED, 5), (SIDED, 2), (SIDE, 7), (DP, 1), (CORE, 8), (CORE, 11), (DPED, 3), (DP, 6), (SIDED, 0),
    (DP, 2), (DPED, 1), (SIDED, 4), (SIDE, 11), (JOIN, 3), (SIDED, 7), (CORE, 10), (DP, 0), (DP, 5),
    (CORE, 9), (SMALL, 0), (SIDE, 8), (DP, 4), (SIDE, 9), (SIDED, 11), (DP, 7), (JOIN, 1), (SIDED, 8),
    (SMALL, 1), (LAST, 1), (DPED, 0), (DP, 10), (DPED, 5), (DPED, 2), (LAST, 3), (SIDED, 9), (DPED, 6),
    (DP, 8), (JOIN, 0), (DPED, 4), (DPED, 10), (DP, 11), (JOIN, 4), (JOIN, 5), (DP, 9), (JOIN, 2), (LAST, 0),
    (DPED, 8), (JOIN, 6), (DPED, 7), (DPED, 11), (DPED, 9), (LAST, 4), (JOIN, 10), (JOIN, 7), (JOIN, 11),
    (JOIN, 8), (JOIN, 9), (SMALL, 2), (LAST, 5), (LAST, 8), (LAST, 2), (LAST, 9), (LAST, 10), (LAST, 11),
    (LAST, 7), (LAST, 6),
)


def dot_plain(left, right):
    return lax.dot_general(left, right, (((1,), (0,)), ((), ())), preferred_element_type=F32)


def dot_turned(left, right):
    return lax.dot_general(left, right, (((1,), (1,)), ((), ())), preferred_element_type=F32)


def fold(values):
    total = values[:, :LANES]
    for start in range(LANES, values.shape[1], LANES):
        total = total + values[:, start : start + LANES]
    return total


def layer_kernel(
    dp_count,
    flag_ref,
    x_hbm,
    ct_hbm,
    w_qkv_hbm,
    w_out_hbm,
    w_up_hbm,
    w_down_hbm,
    up_bias_ref,
    gains_ref,
    biases_ref,
    ends_hbm,
    fin_hbm,
    small_hbm,
    w_qkv,
    w_out,
    w_up,
    w_down,
    turned,
    rows_in,
    x_t,
    qkv,
    keys_rm,
    values_rm,
    share,
    share_off,
    mixture,
    norm_one,
    norm_two,
    inverses,
    hidden_low,
    slope,
    active,
    down_grad,
    branch_grad,
    grad_mix,
    outgoing,
    incoming_grad,
    columns,
    sums,
    key_sums,
    wide_a,
    wide_b,
    ends_v,
    core_in,
    side_in,
    dp_in,
    fin,
    small,
    small_dp,
    small_rep,
    small_out,
    load_sem,
    seg_send,
    seg_recv,
    ends_sem,
    core_send,
    core_recv,
    side_send,
    side_recv,
    dp_send,
    dp_recv,
    join_send,
    join_recv,
    last_send,
    last_recv,
    sdp_send,
    sdp_recv,
    srep_send,
    srep_recv,
    fin_sem,
):
    width = w_out.shape[0]
    piece = x_t.shape[1] // PIECES
    pairs = qkv.shape[1]
    share_rows = width // dp_count
    dp_steps = dp_count.bit_length() - 1
    segment = lax.axis_index("segment")
    dp = lax.axis_index("dp")
    rep = lax.axis_index("rep")
    core = lax.rem(rep, 2)
    side = lax.div(rep, 2)
    other_core = side * 2 + (1 - core)
    other_side = (1 - side) * 2 + core

    loads = []
    for block in range(3):
        span = pl.ds(block * width, width)
        loads.append((w_qkv_hbm.at[0, :, span], w_qkv.at[:, span]))
    loads.append((w_out_hbm.at[0], w_out))
    for block in range(4):
        span = pl.ds(block * width, width)
        loads.append((w_up_hbm.at[0, :, span], w_up.at[:, span]))
    for block in range(4):
        span = pl.ds(block * width, width)
        loads.append((w_down_hbm.at[0, span, :], w_down.at[block]))
    load_copies = [
        pltpu.make_async_copy(source, target, load_sem.at[index + 1])
        for index, (source, target) in enumerate(loads)
    ]
    first_rows = pltpu.make_async_copy(x_hbm, rows_in, load_sem.at[0])
    last_rows = pltpu.make_async_copy(ct_hbm, rows_in, load_sem.at[0])

    @pl.when(segment == 0)
    def _():
        first_rows.start()

    @pl.when(segment == 1)
    def _():
        last_rows.start()

    for copy in load_copies:
        copy.start()

    barrier = pltpu.get_barrier_semaphore()
    pl.semaphore_signal(
        barrier, inc=1, device_id={"segment": 1 - segment}, device_id_type=MESH
    )
    for step in range(1, 4):
        pl.semaphore_signal(
            barrier, inc=1, device_id={"rep": lax.rem(rep + step, 4)}, device_id_type=MESH
        )
    for step in range(1, dp_count):
        pl.semaphore_signal(
            barrier, inc=1, device_id={"dp": lax.rem(dp + step, dp_count)}, device_id_type=MESH
        )

    params = [gains_ref[0].astype(F32), biases_ref[0].astype(F32)]
    for block in range(4):
        params.append(up_bias_ref[:, block * width : (block + 1) * width].astype(F32))
    params.append(jnp.zeros((16 - STATS, width), F32))
    upright = jnp.concatenate(params, axis=0).T
    for index in range(STATS):
        columns[index] = jnp.broadcast_to(upright[:, index : index + 1], (width, LANES)).astype(BF16)
    for index in range(STATS):
        sums[index] = jnp.zeros((width, LANES), F32)
    key_sums[0] = jnp.zeros(key_sums.shape[1:], F32)

    chunks = [slice(start, start + CHUNK) for start in range(0, width, CHUNK)]

    for block, copy in enumerate(load_copies):
        copy.wait()
        span = slice(block % 4 * width, (block % 4 + 1) * width)
        if block < 3:
            turned[block] = w_qkv[:, span].T
        elif block == 3:
            turned[block] = w_out[...].T
        elif block < 8:
            turned[block] = w_up[:, span].T
        else:
            turned[block] = w_down[block - 8].T
    first_rows.wait()

    pl.semaphore_wait(barrier, 4 + dp_count - 1)

    flag = flag_ref[0, 0].astype(F32)

    def lanes_of(index):
        return pl.ds(pl.multiple_of(index * piece, piece), piece)

    def forward_copy(index):
        return pltpu.make_async_remote_copy(
            src_ref=outgoing.at[index],
            dst_ref=x_t.at[:, lanes_of(index)],
            send_sem=seg_send.at[index],
            recv_sem=seg_recv.at[index],
            device_id={"segment": 1 - segment},
            device_id_type=MESH,
        )

    def backward_copy(index):
        return pltpu.make_async_remote_copy(
            src_ref=outgoing.at[index],
            dst_ref=incoming_grad.at[index],
            send_sem=seg_send.at[index],
            recv_sem=seg_recv.at[index],
            device_id={"segment": 1 - segment},
            device_id_type=MESH,
        )

    def ends_copy(index):
        return pltpu.make_async_copy(
            ends_v.at[lax.rem(index, 2)], ends_hbm.at[index], ends_sem.at[index]
        )

    def free_ends(index):
        @pl.when(index >= 2)
        def _():
            ends_copy(index - 2).wait()

    def own_rows(index):
        half = lax.rem(index, 2)
        whole = jnp.where(index < 2, 1.0, 0.0).astype(F32)
        weight = whole * flag + (1.0 - whole) * (1.0 - flag)
        picked = rows_in[half].astype(F32) * weight + rows_in[2 + half].astype(F32) * (1.0 - weight)
        return picked.T

    def by_queries(values):
        half = LANES // 2
        blank = jnp.zeros((half, LANES), values.dtype)
        parts = []
        for part in range(2):
            span = slice(part * LANES, (part + 1) * LANES)
            first = jnp.concatenate([values[:half, span], blank], axis=0)
            second = jnp.concatenate([blank, values[half:, span]], axis=0)
            parts.append(jnp.concatenate([first, second], axis=1))
        return parts

    def against(rows_ref, index, pair, parts, has_off):
        own = rows_ref[index, pair]
        products = [dot_plain(own[:LANES], parts[0]), dot_plain(own, parts[1])]
        if has_off:
            before = rows_ref[0, pair]
            products += [dot_plain(before, parts[0]), dot_plain(before, parts[1])]
        return products

    def tiles_of(products, head, part, has_off):
        lanes = slice(head * LANES, (head + 1) * LANES)
        own = products[part]
        tiles = [own[part * LANES : (part + 1) * LANES, lanes]]
        if part:
            tiles.append(own[:LANES, lanes])
        if has_off:
            off = products[2 + part]
            tiles += [off[:LANES, lanes], off[LANES:, lanes]]
        return tiles

    def joined(lows, has_off):
        blank = jnp.zeros((LANES, LANES), BF16)
        first = jnp.concatenate([lows[0][0], blank], axis=0)
        second = jnp.concatenate([lows[1][1], lows[1][0]], axis=0)
        whole = jnp.concatenate([first, second], axis=1)
        if not has_off:
            return whole, None
        first = jnp.concatenate(lows[0][-2:], axis=0)
        second = jnp.concatenate(lows[1][-2:], axis=0)
        return whole, jnp.concatenate([first, second], axis=1)

    def attend(index, has_off):
        lanes = lanes_of(index)
        half = LANES // 2
        key_at = lax.broadcasted_iota(jnp.int32, (LANES, LANES), 0)
        query_at = lax.broadcasted_iota(jnp.int32, (LANES, LANES), 1)
        allowed = key_at <= query_at

        def scores_of(pair):
            return against(
                keys_rm, index, pair, by_queries(qkv[0, pair, :, lanes]), has_off
            )

        ahead = scores_of(0)
        for pair in range(pairs):
            scores = ahead
            if pair + 1 < pairs:
                ahead = scores_of(pair + 1)
            mixed = []
            for head in range(2):
                rows = slice(head * half, (head + 1) * half)
                lows = []
                for part in range(2):
                    tiles = tiles_of(scores, head, part, has_off)
                    tiles[0] = jnp.where(allowed, tiles[0], -1e30)
                    top = jnp.max(functools.reduce(jnp.maximum, tiles), axis=0, keepdims=True)
                    raised = [jnp.exp(tile - top) for tile in tiles]
                    total = functools.reduce(jnp.add, raised)
                    scale = 1.0 / jnp.sum(total, axis=0, keepdims=True)
                    lows.append([(tile * scale).astype(BF16) for tile in raised])
                low, low_off = joined(lows, has_off)
                share[index, pair, head] = low
                mix = dot_plain(qkv[2, pair, rows, lanes], low)
                if has_off:
                    share_off[pair, head] = low_off
                    mix = mix + dot_plain(qkv[2, pair, rows, :piece], low_off)
                mixed.append(mix.astype(BF16))
            mixture[pair, :, lanes] = jnp.concatenate(mixed, axis=0)

    def part_sum(values):
        return jnp.sum(values.reshape(values.shape[0] // 8, 8, values.shape[1]), axis=0)

    def full_mean(parts):
        return jnp.sum(parts, axis=0, keepdims=True) * (1.0 / width)

    def column(index, rows):
        part = columns[index, rows, :].astype(F32)
        return jnp.concatenate([part] * (piece // LANES), axis=1)

    def gather_sum(index, rows, values):
        sums[index, rows, :] = sums[index, rows, :] + fold(values)

    def norm_chunks(index, which, total):
        mean = full_mean(total)
        spread = jnp.zeros((8, piece), F32)
        for rows in chunks:
            centred = wide_a[rows, :] - mean
            spread = spread + part_sum(centred * centred)
        inverse = lax.rsqrt(full_mean(spread) + EPS)
        inverses[index, which] = inverse
        return mean, inverse

    def forward(index):
        lanes = lanes_of(index)

        @pl.when(segment == 0)
        def _():
            x_t[:, lanes] = own_rows(index).astype(BF16)

        @pl.when(segment == 1)
        def _():
            forward_copy(index).wait_recv()

        inputs = x_t[:, lanes]
        score_scale = 1.0 / math.sqrt(width // HEADS)
        for block in range(3):
            result = dot_plain(turned[block], inputs)
            for pair in range(pairs):
                low = result[pair * LANES : (pair + 1) * LANES]
                low = (low * score_scale if block == 0 else low).astype(BF16)
                qkv[block, pair, :, lanes] = low
                if block == 1:
                    keys_rm[index, pair] = low.T
                if block == 2:
                    values_rm[index, pair] = low.T

        @pl.when(index == 1)
        def _():
            attend(index, True)

        @pl.when(index != 1)
        def _():
            attend(index, False)

        branch = dot_plain(turned[3], mixture[:, :, lanes].reshape(width, piece))
        total = jnp.zeros((8, piece), F32)
        for rows in chunks:
            sum_one = x_t[rows, lanes].astype(F32) + (branch[rows] + column(BIAS_OUT, rows))
            wide_a[rows, :] = sum_one
            total = total + part_sum(sum_one)
        mean, inverse = norm_chunks(index, 0, total)
        for rows in chunks:
            normed = (wide_a[rows, :] - mean) * inverse
            norm_one[rows, lanes] = normed
            hidden = normed * column(GAIN_ONE, rows) + column(BIAS_ONE, rows)
            hidden_low[rows, lanes] = hidden.astype(BF16)

        branch_two = None
        for block in range(4):
            pre_block = dot_plain(turned[4 + block], hidden_low[:, lanes])
            lows = []
            for rows in chunks:
                pre = pre_block[rows] + column(BIAS_UP + block, rows)
                level = (lax.erf(pre * (1.0 / math.sqrt(2.0))) + 1.0) * 0.5
                bell = jnp.exp2(pre * pre * (-0.5 * math.log2(math.e)))
                lows.append((pre * level).astype(BF16))
                active[block, rows, lanes] = lows[-1]
                slope[block, rows, lanes] = (
                    level + pre * bell * (1.0 / math.sqrt(2.0 * math.pi))
                ).astype(BF16)
            part = dot_plain(turned[8 + block], jnp.concatenate(lows, axis=0))
            branch_two = part if branch_two is None else branch_two + part
        total = jnp.zeros((8, piece), F32)
        for rows in chunks:
            hidden = norm_one[rows, lanes] * column(GAIN_ONE, rows) + column(BIAS_ONE, rows)
            sum_two = hidden + (branch_two[rows] + column(BIAS_DOWN, rows))
            wide_a[rows, :] = sum_two
            total = total + part_sum(sum_two)
        mean, inverse = norm_chunks(index, 1, total)

        for rows in chunks:
            norm_two[rows, lanes] = (wide_a[rows, :] - mean) * inverse

        @pl.when(segment == 0)
        def _():
            for rows in chunks:
                outgoing[index, rows, :] = output_rows(rows, lanes).astype(BF16)
            forward_copy(index).start()

    def output_rows(rows, lanes):
        return norm_two[rows, lanes] * column(GAIN_TWO, rows) + column(BIAS_TWO, rows)

    def last_outputs(index, carry):
        free_ends(index)
        for start in range(0, width, LANES):
            rows = slice(start, start + LANES)
            ends_v[lax.rem(index, 2), :, rows] = output_rows(rows, lanes_of(index)).T
        ends_copy(index).start()
        return carry

    def attend_back(index, has_off):
        lanes = lanes_of(index)
        slot = jnp.where(index == 0, 1, 0)
        half = LANES // 2
        score_scale = 1.0 / math.sqrt(width // HEADS)

        def backs_of(pair):
            return against(values_rm, index, pair, by_queries(grad_mix[pair]), has_off)

        ahead = backs_of(0)
        for pair in range(pairs):
            backs = ahead
            if pair + 1 < pairs:
                ahead = backs_of(pair + 1)
            results = ([], [], [])
            for head in range(2):
                rows = slice(head * half, (head + 1) * half)
                low = share[index, pair, head]
                low_off = share_off[pair, head] if has_off else None
                lows = []
                for part in range(2):
                    place = slice(part * LANES, (part + 1) * LANES)
                    wides = [low[place, place]]
                    if part:
                        wides.append(low[:LANES, place])
                    if has_off:
                        wides += [low_off[:LANES, place], low_off[LANES:, place]]
                    wides = [tile.astype(F32) for tile in wides]
                    tiles = tiles_of(backs, head, part, has_off)
                    products = [wide * tile for wide, tile in zip(wides, tiles)]
                    inner = jnp.sum(functools.reduce(jnp.add, products), axis=0, keepdims=True)
                    lows.append(
                        [
                            (product - wide * inner).astype(BF16)
                            for product, wide in zip(products, wides)
                        ]
                    )
                grad_scores, grad_off = joined(lows, has_off)
                queries = qkv[0, pair, rows, lanes]
                grads = grad_mix[pair, rows]
                grad_query = dot_plain(qkv[1, pair, rows, lanes], grad_scores)
                grad_key = dot_turned(queries, grad_scores) + key_sums[slot, 0, pair, rows]
                grad_value = dot_turned(grads, low) + key_sums[slot, 1, pair, rows]
                if has_off:
                    grad_query = grad_query + dot_plain(qkv[1, pair, rows, :piece], grad_off)
                    key_sums[1, 0, pair, rows] = dot_turned(queries, grad_off)
                    key_sums[1, 1, pair, rows] = dot_turned(grads, low_off)
                for kept, grad in zip(results, (grad_query * score_scale, grad_key, grad_value)):
                    kept.append(grad.astype(BF16))
            for block in range(3):
                qkv[block, pair, :, lanes] = jnp.concatenate(results[block], axis=0)

    def backward(index):
        lanes = lanes_of(index)

        @pl.when(segment == 0)
        def _():
            backward_copy(index).wait_recv()

        plain = jnp.zeros((8, piece), F32)
        inner = jnp.zeros((8, piece), F32)
        for rows in chunks:
            grad = incoming_grad[index, rows, :].astype(F32)
            product = grad * norm_two[rows, lanes]
            gather_sum(GAIN_TWO, rows, product)
            gather_sum(BIAS_TWO, rows, grad)
            gain = column(GAIN_TWO, rows)
            plain = plain + part_sum(grad * gain)
            inner = inner + part_sum(product * gain)
        plain = full_mean(plain)
        inner = full_mean(inner)
        inverse = inverses[index, 1]
        for rows in chunks:
            scaled = incoming_grad[index, rows, :].astype(F32) * column(GAIN_TWO, rows)
            grad_two = (scaled - plain - norm_two[rows, lanes] * inner) * inverse
            gather_sum(BIAS_DOWN, rows, grad_two)
            wide_a[rows, :] = grad_two
            down_grad[rows, lanes] = grad_two.astype(BF16)

    def backward_feed(index):
        lanes = lanes_of(index)
        for block in range(4):
            back = dot_plain(w_down[block], down_grad[:, lanes])
            for rows in chunks:
                grad_pre = back[rows] * slope[block, rows, lanes].astype(F32)
                gather_sum(BIAS_UP + block, rows, grad_pre)
                slope[block, rows, lanes] = grad_pre.astype(BF16)

        through = dot_plain(w_up[...], slope[:, :, lanes].reshape(4 * width, piece))
        plain = jnp.zeros((8, piece), F32)
        inner = jnp.zeros((8, piece), F32)
        for rows in chunks:
            grad_hidden = wide_a[rows, :] + through[rows]
            wide_a[rows, :] = grad_hidden
            product = grad_hidden * norm_one[rows, lanes]
            gather_sum(GAIN_ONE, rows, product)
            gather_sum(BIAS_ONE, rows, grad_hidden)
            gain = column(GAIN_ONE, rows)
            plain = plain + part_sum(grad_hidden * gain)
            inner = inner + part_sum(product * gain)
        plain = full_mean(plain)
        inner = full_mean(inner)
        inverse = inverses[index, 0]
        for rows in chunks:
            scaled = wide_a[rows, :] * column(GAIN_ONE, rows)
            grad_one = (scaled - plain - norm_one[rows, lanes] * inner) * inverse
            gather_sum(BIAS_OUT, rows, grad_one)
            wide_b[rows, :] = grad_one
            branch_grad[rows, lanes] = grad_one.astype(BF16)
        grad_mix[...] = (
            dot_plain(w_out[...], branch_grad[:, lanes]).astype(BF16).reshape(pairs, LANES, piece)
        )

    def backward_attention(index):
        lanes = lanes_of(index)

        @pl.when(index == 1)
        def _():
            attend_back(index, True)

        @pl.when(index != 1)
        def _():
            attend_back(index, False)

        through = dot_plain(w_qkv[...], qkv[:, :, :, lanes].reshape(3 * width, piece))

        @pl.when(segment == 1)
        def _():
            for rows in chunks:
                outgoing[index, rows, :] = (wide_b[rows, :] + through[rows]).astype(BF16)
            backward_copy(index).start()

        @pl.when(segment == 0)
        def _():
            free_ends(index)
            for start in range(0, width, LANES):
                rows = slice(start, start + LANES)
                ends_v[lax.rem(index, 2), :, rows] = (wide_b[rows, :] + through[rows]).T
            ends_copy(index).start()

    def held(job):
        return turned, (8, 4, 0)[job // 4]

    def lanes_in(job):
        start = job % 4 * (width // 4)
        return slice(start, start + width // 4)

    def parts_of(job):
        return range(2) if job in DP_FIRST else range(1)

    def core_copy(job):
        buffer, base = held(job)
        lanes = lanes_in(job)
        return pltpu.make_async_remote_copy(
            src_ref=buffer.at[pl.ds(base + 2 * (1 - core), 2), :, lanes],
            dst_ref=core_in.at[job // 4, :, :, lanes],
            send_sem=core_send.at[job],
            recv_sem=core_recv.at[job],
            device_id={"rep": other_core},
            device_id_type=MESH,
        )

    def side_copies(job):
        buffer, base = held(job)
        lanes = lanes_in(job)
        copies = []
        for each in parts_of(job):
            if job in DP_FIRST:
                source = buffer.at[base + 2 * core + each, dp_rows(dp_steps - 1)[1], lanes]
                target = side_in.at[job // 4, pl.ds(each * share_rows, share_rows), lanes]
            else:
                source = buffer.at[base + 2 * core + (1 - side), :, lanes]
                target = side_in.at[job // 4, :, lanes]
            copies.append(
                pltpu.make_async_remote_copy(
                    src_ref=source,
                    dst_ref=target,
                    send_sem=side_send.at[job, each],
                    recv_sem=side_recv.at[job, each],
                    device_id={"rep": other_side},
                    device_id_type=MESH,
                )
            )
        return copies

    def dp_slot(job):
        return sum(len(parts_of(before)) for before in range(job))

    def dp_rows(step):
        count = dp_count // 2
        start = 0
        for bit in range(step):
            start = start + lax.rem(lax.div(dp, 2**bit), 2) * count
            count = count // 2
        mine = lax.rem(lax.div(dp, 2**step), 2)
        sent = pl.multiple_of((start + (1 - mine) * count) * share_rows, share_rows)
        kept = pl.multiple_of((start + mine * count) * share_rows, share_rows)
        return pl.ds(sent, count * share_rows), pl.ds(kept, count * share_rows)

    def dp_landing(step):
        count = dp_count // 2 ** (step + 1)
        return pl.ds((dp_count - 2 * count) * share_rows, count * share_rows)

    def dp_copies(job, step):
        buffer, base = held(job)
        lanes = lanes_in(job)
        mine = lax.rem(lax.div(dp, 2**step), 2)
        copies = []
        for each in parts_of(job):
            position = base + 2 * core + (each if job in DP_FIRST else side)
            copies.append(
                pltpu.make_async_remote_copy(
                    src_ref=buffer.at[position, dp_rows(step)[0], lanes],
                    dst_ref=dp_in.at[dp_slot(job) + each, dp_landing(step)],
                    send_sem=dp_send.at[job, step, each],
                    recv_sem=dp_recv.at[job, step, each],
                    device_id={"dp": dp + (1 - 2 * mine) * 2**step},
                    device_id_type=MESH,
                )
            )
        return copies

    def join_copy(job):
        lanes = lanes_in(job)
        return pltpu.make_async_remote_copy(
            src_ref=fin.at[job // 4, 2 * core + side, :, lanes],
            dst_ref=fin.at[job // 4, 2 * core + side, :, lanes],
            send_sem=join_send.at[job],
            recv_sem=join_recv.at[job],
            device_id={"rep": other_side},
            device_id_type=MESH,
        )

    def last_copy(job):
        lanes = lanes_in(job)
        return pltpu.make_async_remote_copy(
            src_ref=fin.at[job // 4, pl.ds(2 * core, 2), :, lanes],
            dst_ref=fin.at[job // 4, pl.ds(2 * core, 2), :, lanes],
            send_sem=last_send.at[job],
            recv_sem=last_recv.at[job],
            device_id={"rep": other_core},
            device_id_type=MESH,
        )

    def fin_copy(job):
        lanes = lanes_in(job)
        return pltpu.make_async_copy(
            fin.at[job // 4, :, :, lanes], fin_hbm.at[job // 4, :, :, lanes], fin_sem.at[job]
        )

    def arrived(*copies):
        for copy in copies:
            copy.wait_send()
        for copy in copies:
            copy.wait_recv()

    def start_all(copies):
        for copy in copies:
            copy.start()

    def turned_bits(value, count):
        place = 0
        while count > 1:
            place = place * 2 + value % 2
            value = value // 2
            count = count // 2
        return place

    def keep_rows(position, lanes, result):
        for index in range(dp_count):
            start = turned_bits(index, dp_count) * share_rows
            turned[position, start : start + share_rows, lanes] = result[
                index * share_rows : (index + 1) * share_rows
            ]

    def down_sums(lanes):
        part = 4 * share_rows
        count = width // part

        def one(block, carry):
            result = dot_turned(active[block], down_grad[lanes, :]).astype(BF16)
            high = lax.rem(block, 2) * 2 + lax.div(block, 2)
            for each in range(count):
                place = turned_bits(each, count) * 4 + high
                target = pl.multiple_of(place * share_rows, share_rows)
                for position in range(4):
                    start = each * part + position * share_rows
                    turned[8 + position, pl.ds(target, share_rows), lanes] = result[
                        start : start + share_rows
                    ]
            return carry

        lax.fori_loop(0, 4, one, 0)

    def up_sums(lanes):
        def one(block, carry):
            result = dot_turned(hidden_low[...], slope[block, lanes, :]).astype(BF16)
            keep_rows(4 + block, lanes, result)
            return carry

        lax.fori_loop(0, 4, one, 0)

    def qkv_sums(lanes):
        span = slice(lanes.start // LANES, lanes.stop // LANES)

        def one(block, carry):
            grads = qkv[block, span].reshape(lanes.stop - lanes.start, PIECES * piece)
            keep_rows(block, lanes, dot_turned(x_t[...], grads).astype(BF16))
            return carry

        lax.fori_loop(0, 3, one, 0)
        mixed = mixture[...].reshape(width, PIECES * piece)
        keep_rows(3, lanes, dot_turned(mixed, branch_grad[lanes, :]).astype(BF16))

    def sums_of(job):
        lanes = slice(lanes_in(job).start, lanes_in(job + 1).stop)
        (down_sums, up_sums, qkv_sums)[job // 4](lanes)
        core_copy(job).start()
        core_copy(job + 1).start()

    def after_core(job):
        buffer, base = held(job)
        lanes = lanes_in(job)
        arrived(core_copy(job))
        for each in parts_of(job):
            place = 1 - side if each == 0 else side
            position = base + 2 * core + place
            buffer[position, :, lanes] = (
                buffer[position, :, lanes].astype(F32)
                + core_in[job // 4, place, :, lanes].astype(F32)
            ).astype(BF16)
        if job in DP_FIRST:
            start_all(dp_copies(job, 0))

    def start_side(job):
        start_all(side_copies(job))

    def after_side(job):
        buffer, base = held(job)
        lanes = lanes_in(job)
        arrived(*side_copies(job))
        second = base + 2 * core + side
        buffer[second, :, lanes] = (
            buffer[second, :, lanes].astype(F32)
            + core_in[job // 4, side, :, lanes].astype(F32)
            + side_in[job // 4, :, lanes].astype(F32)
        ).astype(BF16)
        start_all(dp_copies(job, 0))

    def dp_total(job, step, each):
        buffer, base = held(job)
        position = base + 2 * core + (each if job in DP_FIRST else side)
        kept = buffer[position, dp_rows(step)[1], lanes_in(job)].astype(F32)
        return position, kept + dp_in[dp_slot(job) + each, dp_landing(step), :].astype(F32)

    def after_dp(job):
        buffer, _ = held(job)
        for step in range(dp_steps - 1):
            arrived(*dp_copies(job, step))
            for each in parts_of(job):
                position, total = dp_total(job, step, each)
                buffer[position, dp_rows(step)[1], lanes_in(job)] = total.astype(BF16)
            start_all(dp_copies(job, step + 1))

    def after_last_dp(job):
        buffer, _ = held(job)
        lanes = lanes_in(job)
        step = dp_steps - 1
        arrived(*dp_copies(job, step))
        for each in parts_of(job):
            position, total = dp_total(job, step, each)
            if job in DP_FIRST:
                buffer[position, dp_rows(step)[1], lanes] = total.astype(BF16)
            else:
                fin[job // 4, 2 * core + side, :, lanes] = total.astype(BF16)
        if job in DP_FIRST:
            start_side(job)
        else:
            join_copy(job).start()

    def after_join(job):
        if job in DP_FIRST:
            buffer, base = held(job)
            lanes = lanes_in(job)
            arrived(*side_copies(job))
            for each in range(2):
                rows = slice(each * share_rows, (each + 1) * share_rows)
                own = buffer[base + 2 * core + each, dp_rows(dp_steps - 1)[1], lanes]
                total = own.astype(F32) + side_in[job // 4, rows, lanes].astype(F32)
                fin[job // 4, 2 * core + each, :, lanes] = total.astype(BF16)
        else:
            arrived(join_copy(job))
        last_copy(job).start()

    def after_last(job):
        arrived(last_copy(job))
        fin_copy(job).start()

    def small_dp_copy(step):
        target = lax.rem(dp + step, dp_count)
        return pltpu.make_async_remote_copy(
            src_ref=small.at[target],
            dst_ref=small_dp.at[step - 1],
            send_sem=sdp_send.at[step - 1],
            recv_sem=sdp_recv.at[step - 1],
            device_id={"dp": target},
            device_id_type=MESH,
        )

    def small_rep_copy(step):
        return pltpu.make_async_remote_copy(
            src_ref=small_rep.at[rep],
            dst_ref=small_rep.at[rep],
            send_sem=srep_send.at[step - 1],
            recv_sem=srep_recv.at[step - 1],
            device_id={"rep": lax.rem(rep + step, 4)},
            device_id_type=MESH,
        )

    small_copy = pltpu.make_async_copy(small_out, small_hbm, load_sem.at[0])

    def small_step(stage):
        if stage == 0:
            rows_of = [jnp.sum(sums[index].T, axis=0, keepdims=True) for index in range(STATS)]
            small[...] = jnp.zeros(small.shape, F32)
            for share_index in range(dp_count):
                for index in range(BIAS_UP):
                    start = share_index * share_rows
                    small[share_index, index : index + 1, :share_rows] = rows_of[index][
                        :, start : start + share_rows
                    ]
                for part in range(4):
                    start = (share_index * 4 + part) * share_rows
                    block, start = start // width, start % width
                    small[share_index, BIAS_UP + part : BIAS_UP + part + 1, :share_rows] = rows_of[
                        BIAS_UP + block
                    ][:, start : start + share_rows]
            for step in range(1, dp_count):
                small_dp_copy(step).start()
        elif stage == 1:
            total = small[dp]
            for step in range(1, dp_count):
                arrived(small_dp_copy(step))
                total = total + small_dp[step - 1]
            small_rep[rep] = total
            for step in range(1, 4):
                small_rep_copy(step).start()
        else:
            for step in range(1, 4):
                arrived(small_rep_copy(step))
            small_out[...] = (small_rep[0] + small_rep[1]) + (small_rep[2] + small_rep[3])
            small_copy.start()

    def run(order):
        steps = (
            sums_of,
            after_core,
            start_side,
            after_side,
            after_dp,
            after_last_dp,
            after_join,
            after_last,
            small_step,
        )
        for stage, job in order:
            steps[stage](job)

    def one_step(step, carry):
        first_index = jnp.where(step < 4, step, jnp.where(step < 6, 5 - step, step - 4))
        last_index = jnp.where(step < 2, step, jnp.where(step < 4, 3 - step, lax.div(step, 2)))
        first_is = jnp.where(step < 4, 1, 0)
        last_is = jnp.where(step < 2, 1, jnp.where(step < 4, 0, 1 - lax.rem(step, 2)))
        index = jnp.minimum(jnp.where(segment == 0, first_index, last_index), PIECES - 1)
        is_last = jnp.where(step == 2 * PIECES, 1, 0)
        is_forward = jnp.where(segment == 0, first_is, last_is) * (1 - is_last)
        is_backward = (1 - is_forward) * (1 - is_last)
        is_split = jnp.where(step >= 2 * PIECES - 1, 1 - segment, 0)
        is_rest = is_backward * (1 - is_split) + is_last * is_split

        @pl.when(is_forward == 1)
        def _():
            forward(index)

        @pl.when(is_backward == 1)
        def _():
            backward(index)

        @pl.when(is_last == 1)
        def _():
            run(ORDER_ONE)

        @pl.when(is_rest == 1)
        def _():
            backward_feed(index)

        @pl.when(is_last == 1)
        def _():
            run(ORDER_TWO)

        @pl.when(is_rest == 1)
        def _():
            backward_attention(index)

        return carry

    @pl.when(segment == 1)
    def _():
        for index in range(PIECES):
            incoming_grad[index] = own_rows(index).astype(BF16)

    lax.fori_loop(0, 2 * PIECES + 1, one_step, 0)

    cut = ORDER_THREE.index((SMALL, 0))
    run(ORDER_THREE[:cut])

    @pl.when(segment == 1)
    def _():
        lax.fori_loop(0, PIECES, last_outputs, 0)

    run(ORDER_THREE[cut:])

    for index in range(PIECES):

        @pl.when(segment == 0)
        def _():
            forward_copy(index).wait_send()

        @pl.when(segment == 1)
        def _():
            backward_copy(index).wait_send()

    for index in range(2, PIECES):
        ends_copy(index).wait()
    for job in range(JOBS):
        fin_copy(job).wait()
    small_copy.wait()


def finish_kernel(
    flag_ref,
    ends_in,
    fin,
    small,
    ends,
    grad_qkv,
    grad_out,
    grad_up,
    grad_down,
    grad_up_bias,
    grad_gains,
    grad_biases,
    ends_v,
    fin_v,
    wide_qkv,
    wide_out,
    wide_up,
    wide_down,
    small_v,
    up_bias_v,
    gains_v,
    biases_v,
    ends_sem,
    in_sem,
    out_sem,
):
    half = ends_in.shape[0] // 2
    share_rows, width = fin.shape[2:]
    start = pl.multiple_of(half * (1 - flag_ref[0, 0]), half)
    cut = half // 4
    ends_copies = []
    ends_loads = []
    for part in range(8):
        source = pl.ds(part * cut, cut)
        offset = start + part * cut if part < 4 else part * cut - half + (half - start)
        target = pl.ds(pl.multiple_of(offset, cut), cut)
        ends_loads.append(
            pltpu.make_async_copy(ends_in.at[source], ends_v.at[source], ends_sem.at[part])
        )
        ends_copies.append(
            pltpu.make_async_copy(ends_v.at[source], ends.at[0, target], ends_sem.at[8 + part])
        )
    loads = [
        pltpu.make_async_copy(fin.at[group], fin_v.at[group], in_sem.at[group])
        for group in range(3)
    ]
    stores = [
        pltpu.make_async_copy(wide, target.at[0], out_sem.at[index])
        for index, (wide, target) in enumerate(
            ((wide_down, grad_down), (wide_up, grad_up), (wide_qkv, grad_qkv), (wide_out, grad_out))
        )
    ]
    small_load = pltpu.make_async_copy(small, small_v, in_sem.at[3])
    small_stores = [
        pltpu.make_async_copy(narrow, target, out_sem.at[4 + index])
        for index, (narrow, target) in enumerate(
            ((up_bias_v, grad_up_bias), (gains_v, grad_gains), (biases_v, grad_biases))
        )
    ]
    small_load.start()
    for copy in loads + ends_loads:
        copy.start()
    for load, copy in zip(ends_loads, ends_copies):
        load.wait()
        copy.start()
    loads[0].wait()
    for position in range(4):
        rows = slice(position * share_rows, (position + 1) * share_rows)
        wide_down[rows, :] = fin_v[0, position].astype(F32)
    stores[0].start()
    loads[1].wait()
    for position in range(4):
        wide_up[:, position * width : (position + 1) * width] = fin_v[1, position].astype(F32)
    stores[1].start()
    loads[2].wait()
    for position in range(3):
        wide_qkv[:, position * width : (position + 1) * width] = fin_v[2, position].astype(F32)
    stores[2].start()
    wide_out[...] = fin_v[2, 3].astype(F32)
    stores[3].start()
    small_load.wait()
    for position in range(4):
        rows = slice(position * share_rows, (position + 1) * share_rows)
        up_bias_v[:, rows] = small_v[BIAS_UP + position : BIAS_UP + position + 1, :share_rows]
    gains_v[0] = small_v[:2, :share_rows]
    biases_v[0] = small_v[2:BIAS_UP, :share_rows]
    for copy in small_stores:
        copy.start()
    for copy in stores + ends_copies + small_stores:
        copy.wait()


def on_device(
    dp_count,
    block_input,
    cotangent,
    window_group,
    w_qkv,
    w_out,
    w_up,
    w_down,
    up_bias,
    norm_gains,
    biases,
):
    rows, width = block_input.shape
    piece = rows // PIECES
    pairs = width // LANES
    share_rows = width // dp_count
    small_width = max(share_rows, LANES)
    dp_steps = dp_count.bit_length() - 1
    any_spec = pl.BlockSpec(memory_space=pl.ANY)
    vmem_spec = pl.BlockSpec(memory_space=pltpu.VMEM)
    smem_spec = pl.BlockSpec(memory_space=pltpu.SMEM)
    dma = pltpu.SemaphoreType.DMA
    vmem = pltpu.VMEM
    ends_in, fin, small = pl.pallas_call(
        functools.partial(layer_kernel, dp_count),
        out_shape=(
            jax.ShapeDtypeStruct((PIECES, piece, width), F32),
            jax.ShapeDtypeStruct((3, 4, share_rows, width), BF16),
            jax.ShapeDtypeStruct((16, small_width), F32),
        ),
        in_specs=[smem_spec] + [any_spec] * 6 + [vmem_spec] * 3,
        out_specs=(any_spec,) * 3,
        scratch_shapes=[
            vmem((width, 3 * width), BF16),
            vmem((width, width), BF16),
            vmem((width, 4 * width), BF16),
            vmem((4, width, width), BF16),
            vmem((12, width, width), BF16),
            vmem((PIECES, piece, width), BF16),
            vmem((width, rows), BF16),
            vmem((3, pairs, LANES, rows), BF16),
            vmem((PIECES, pairs, piece, LANES), BF16),
            vmem((PIECES, pairs, piece, LANES), BF16),
            vmem((PIECES, pairs, 2, piece, piece), BF16),
            vmem((pairs, 2, piece, piece), BF16),
            vmem((pairs, LANES, rows), BF16),
            vmem((width, rows), F32),
            vmem((width, rows), F32),
            vmem((PIECES, 2, 1, piece), F32),
            vmem((width, rows), BF16),
            vmem((4, width, rows), BF16),
            vmem((4, width, rows), BF16),
            vmem((width, rows), BF16),
            vmem((width, rows), BF16),
            vmem((pairs, LANES, piece), BF16),
            vmem((PIECES, width, piece), BF16),
            vmem((PIECES, width, piece), BF16),
            vmem((STATS, width, LANES), BF16),
            vmem((STATS, width, LANES), F32),
            vmem((2, 2, pairs, LANES, piece), F32),
            vmem((width, piece), F32),
            vmem((width, piece), F32),
            vmem((2, piece, width), F32),
            vmem((3, 2, width, width), BF16),
            vmem((3, width, width), BF16),
            vmem((JOBS + len(DP_FIRST), width - share_rows, width // 4), BF16),
            vmem((3, 4, share_rows, width), BF16),
            vmem((dp_count, 16, small_width), F32),
            vmem((dp_count - 1, 16, small_width), F32),
            vmem((4, 16, small_width), F32),
            vmem((16, small_width), F32),
            dma((13,)),
            dma((PIECES,)),
            dma((PIECES,)),
            dma((PIECES,)),
            dma((JOBS,)),
            dma((JOBS,)),
            dma((JOBS, 2)),
            dma((JOBS, 2)),
            dma((JOBS, dp_steps, 2)),
            dma((JOBS, dp_steps, 2)),
            dma((JOBS,)),
            dma((JOBS,)),
            dma((JOBS,)),
            dma((JOBS,)),
            dma((dp_count - 1,)),
            dma((dp_count - 1,)),
            dma((3,)),
            dma((3,)),
            dma((JOBS,)),
        ],
        compiler_params=pltpu.CompilerParams(
            collective_id=0, has_side_effects=True, vmem_limit_bytes=63 * 1024 * 1024
        ),
    )(
        window_group,
        block_input.reshape(PIECES, piece, width),
        cotangent.reshape(PIECES, piece, width),
        w_qkv,
        w_out,
        w_up,
        w_down,
        up_bias,
        norm_gains,
        biases,
    )
    return pl.pallas_call(
        finish_kernel,
        out_shape=(
            jax.ShapeDtypeStruct((1, rows, width), F32),
            jax.ShapeDtypeStruct((1, share_rows, 3 * width), F32),
            jax.ShapeDtypeStruct((1, share_rows, width), F32),
            jax.ShapeDtypeStruct((1, share_rows, 4 * width), F32),
            jax.ShapeDtypeStruct((1, 4 * share_rows, width), F32),
            jax.ShapeDtypeStruct((1, 4 * share_rows), F32),
            jax.ShapeDtypeStruct((1, 2, share_rows), F32),
            jax.ShapeDtypeStruct((1, 4, share_rows), F32),
        ),
        in_specs=[smem_spec] + [any_spec] * 3,
        out_specs=(any_spec,) * 8,
        scratch_shapes=[
            vmem((rows, width), F32),
            vmem((3, 4, share_rows, width), BF16),
            vmem((share_rows, 3 * width), F32),
            vmem((share_rows, width), F32),
            vmem((share_rows, 4 * width), F32),
            vmem((4 * share_rows, width), F32),
            vmem((16, small_width), F32),
            vmem((1, 4 * share_rows), F32),
            vmem((1, 2, share_rows), F32),
            vmem((1, 4, share_rows), F32),
            dma((16,)),
            dma((4,)),
            dma((7,)),
        ],
        compiler_params=pltpu.CompilerParams(vmem_limit_bytes=63 * 1024 * 1024),
    )(window_group, ends_in.reshape(rows, width), fin, small)


def solution(mesh):
    return jax.shard_map(
        functools.partial(on_device, mesh.shape["dp"]),
        mesh=mesh,
        in_specs=(
            P(("dp", "rep"), None),
            P(("dp", "rep"), None),
            P(("dp", "rep"), None),
            P("segment", None, None),
            P("segment", None, None),
            P("segment", None, None),
            P("segment", None, None),
            P("segment", None),
            P("segment", None, None),
            P("segment", None, None),
        ),
        out_specs=(
            P("segment", ("dp", "rep"), None),
            P("segment", "dp", None),
            P("segment", "dp", None),
            P("segment", "dp", None),
            P("segment", "dp", None),
            P("segment", "dp"),
            P("segment", None, "dp"),
            P("segment", None, "dp"),
        ),
        check_vma=False,
    )
```

```python
import functools
import math

import jax
import jax.numpy as jnp
from jax import lax
from jax.experimental import pallas as pl
from jax.experimental.pallas import tpu as pltpu
from jax.sharding import PartitionSpec as P

MESH = pl.DeviceIdType.MESH
F32 = jnp.float32
BF16 = jnp.bfloat16
HEADS = 8
LANES = 128
PIECES = 4
EPS = 1e-05
GAIN_ONE, GAIN_TWO, BIAS_OUT, BIAS_ONE, BIAS_DOWN, BIAS_TWO, BIAS_UP = range(7)
STATS = 10
CHUNK = 64
SPLIT = 4
DP_FIRST = (1, 3, 6, 10)
SUM, CORE, SIDE, SIDED, DP, DPED, JOIN, LAST, SMALL = range(9)
ORDER_ONE = (
    (SUM, 0), (SUM, 2),
)
ORDER_TWO = (
    (SUM, 4), (CORE, 1), (CORE, 0), (SIDE, 0), (SUM, 6), (CORE, 2), (SIDE, 2), (CORE, 3),
)
ORDER_THREE = (
    (CORE, 5), (SUM, 8), (SIDE, 5), (CORE, 6), (DP, 3), (CORE, 4), (SUM, 10), (CORE, 7), (SIDE, 4),
    (SIDED, 5), (SIDED, 2), (SIDE, 7), (DP, 1), (CORE, 8), (CORE, 11), (DPED, 3), (DP, 6), (SIDED, 0),
    (DP, 2), (DPED, 1), (SIDED, 4), (SIDE, 11), (JOIN, 3), (SIDED, 7), (CORE, 10), (DP, 0), (DP, 5),
    (CORE, 9), (SMALL, 0), (SIDE, 8), (DP, 4), (SIDE, 9), (SIDED, 11), (DP, 7), (JOIN, 1), (SIDED, 8),
    (SMALL, 1), (LAST, 1), (DPED, 0), (DP, 10), (DPED, 5), (DPED, 2), (LAST, 3), (SIDED, 9), (DPED, 6),
    (DP, 8), (JOIN, 0), (DPED, 4), (DPED, 10), (DP, 11), (JOIN, 4), (JOIN, 5), (DP, 9), (JOIN, 2), (LAST, 0),
    (DPED, 8), (JOIN, 6), (DPED, 7), (DPED, 11), (DPED, 9), (LAST, 4), (JOIN, 10), (JOIN, 7), (JOIN, 11),
    (JOIN, 8), (JOIN, 9), (SMALL, 2), (LAST, 5), (LAST, 8), (LAST, 2), (LAST, 9), (LAST, 10), (LAST, 11),
    (LAST, 7), (LAST, 6),
)


def plain_orders():
    one = ((SUM, 0),)
    two = ((SUM, 1), (CORE, 0), (SIDE, 0))
    three = ((SUM, 2), (CORE, 1), (SIDE, 1), (CORE, 2), (SIDE, 2), (SMALL, 0), (SMALL, 1), (SMALL, 2))
    for stage in (SIDED, DP, DPED, JOIN, LAST):
        three += tuple((stage, job) for job in range(3))
    return one, two, three


def dot_plain(left, right):
    return lax.dot_general(left, right, (((1,), (0,)), ((), ())), preferred_element_type=F32)


def dot_turned(left, right):
    return lax.dot_general(left, right, (((1,), (1,)), ((), ())), preferred_element_type=F32)


def fold(values):
    total = values[:, :LANES]
    for start in range(LANES, values.shape[1], LANES):
        total = total + values[:, start : start + LANES]
    return total


def layer_kernel(
    dp_count,
    flag_ref,
    x_hbm,
    ct_hbm,
    w_qkv_hbm,
    w_out_hbm,
    w_up_hbm,
    w_down_hbm,
    up_bias_ref,
    gains_ref,
    biases_ref,
    ends_hbm,
    fin_hbm,
    small_hbm,
    w_qkv,
    w_out,
    w_up,
    w_down,
    turned,
    rows_in,
    x_t,
    qkv,
    keys_rm,
    values_rm,
    share,
    share_off,
    mixture,
    norm_one,
    norm_two,
    inverses,
    hidden_low,
    slope,
    active,
    down_grad,
    branch_grad,
    grad_mix,
    outgoing,
    incoming_grad,
    columns,
    sums,
    key_sums,
    wide_a,
    wide_b,
    ends_v,
    core_in,
    side_in,
    dp_in,
    fin,
    small,
    small_dp,
    small_rep,
    small_out,
    load_sem,
    seg_send,
    seg_recv,
    ends_sem,
    core_send,
    core_recv,
    side_send,
    side_recv,
    dp_send,
    dp_recv,
    join_send,
    join_recv,
    last_send,
    last_recv,
    sdp_send,
    sdp_recv,
    srep_send,
    srep_recv,
    fin_sem,
):
    width = w_out.shape[0]
    piece = x_t.shape[1] // PIECES
    pairs = qkv.shape[1]
    share_rows = width // dp_count
    dp_steps = dp_count.bit_length() - 1
    segment = lax.axis_index("segment")
    dp = lax.axis_index("dp")
    rep = lax.axis_index("rep")
    core = lax.rem(rep, 2)
    side = lax.div(rep, 2)
    other_core = side * 2 + (1 - core)
    other_side = (1 - side) * 2 + core

    loads = []
    for block in range(3):
        span = pl.ds(block * width, width)
        loads.append((w_qkv_hbm.at[0, :, span], w_qkv.at[:, span]))
    loads.append((w_out_hbm.at[0], w_out))
    for block in range(4):
        span = pl.ds(block * width, width)
        loads.append((w_up_hbm.at[0, :, span], w_up.at[:, span]))
    for block in range(4):
        span = pl.ds(block * width, width)
        loads.append((w_down_hbm.at[0, span, :], w_down.at[block]))
    load_copies = [
        pltpu.make_async_copy(source, target, load_sem.at[index + 1])
        for index, (source, target) in enumerate(loads)
    ]
    first_rows = pltpu.make_async_copy(x_hbm, rows_in, load_sem.at[0])
    last_rows = pltpu.make_async_copy(ct_hbm, rows_in, load_sem.at[0])

    @pl.when(segment == 0)
    def _():
        first_rows.start()

    @pl.when(segment == 1)
    def _():
        last_rows.start()

    for copy in load_copies:
        copy.start()

    barrier = pltpu.get_barrier_semaphore()
    pl.semaphore_signal(
        barrier, inc=1, device_id={"segment": 1 - segment}, device_id_type=MESH
    )
    for step in range(1, 4):
        pl.semaphore_signal(
            barrier, inc=1, device_id={"rep": lax.rem(rep + step, 4)}, device_id_type=MESH
        )
    for step in range(1, dp_count):
        pl.semaphore_signal(
            barrier, inc=1, device_id={"dp": lax.rem(dp + step, dp_count)}, device_id_type=MESH
        )

    params = [gains_ref[0].astype(F32), biases_ref[0].astype(F32)]
    for block in range(4):
        params.append(up_bias_ref[:, block * width : (block + 1) * width].astype(F32))
    params.append(jnp.zeros((16 - STATS, width), F32))
    upright = jnp.concatenate(params, axis=0).T
    for index in range(STATS):
        columns[index] = jnp.broadcast_to(upright[:, index : index + 1], (width, LANES)).astype(BF16)
    for index in range(STATS):
        sums[index] = jnp.zeros((width, LANES), F32)
    key_sums[0] = jnp.zeros(key_sums.shape[1:], F32)

    chunks = [slice(start, start + CHUNK) for start in range(0, width, CHUNK)]

    for block, copy in enumerate(load_copies):
        copy.wait()
        span = slice(block % 4 * width, (block % 4 + 1) * width)
        if block < 3:
            turned[block] = w_qkv[:, span].T
        elif block == 3:
            turned[block] = w_out[...].T
        elif block < 8:
            turned[block] = w_up[:, span].T
        else:
            turned[block] = w_down[block - 8].T
    first_rows.wait()

    pl.semaphore_wait(barrier, 4 + dp_count - 1)

    flag = flag_ref[0, 0].astype(F32)

    def lanes_of(index):
        return pl.ds(pl.multiple_of(index * piece, piece), piece)

    def forward_copy(index):
        return pltpu.make_async_remote_copy(
            src_ref=outgoing.at[index],
            dst_ref=x_t.at[:, lanes_of(index)],
            send_sem=seg_send.at[index],
            recv_sem=seg_recv.at[index],
            device_id={"segment": 1 - segment},
            device_id_type=MESH,
        )

    def backward_copy(index):
        return pltpu.make_async_remote_copy(
            src_ref=outgoing.at[index],
            dst_ref=incoming_grad.at[index],
            send_sem=seg_send.at[index],
            recv_sem=seg_recv.at[index],
            device_id={"segment": 1 - segment},
            device_id_type=MESH,
        )

    def ends_copy(index):
        return pltpu.make_async_copy(
            ends_v.at[lax.rem(index, 2)], ends_hbm.at[index], ends_sem.at[index]
        )

    def free_ends(index):
        @pl.when(index >= 2)
        def _():
            ends_copy(index - 2).wait()

    def own_rows(index):
        half = lax.rem(index, 2)
        whole = jnp.where(index < 2, 1.0, 0.0).astype(F32)
        weight = whole * flag + (1.0 - whole) * (1.0 - flag)
        picked = rows_in[half].astype(F32) * weight + rows_in[2 + half].astype(F32) * (1.0 - weight)
        return picked.T

    def by_queries(values):
        half = LANES // 2
        blank = jnp.zeros((half, LANES), values.dtype)
        parts = []
        for part in range(2):
            span = slice(part * LANES, (part + 1) * LANES)
            first = jnp.concatenate([values[:half, span], blank], axis=0)
            second = jnp.concatenate([blank, values[half:, span]], axis=0)
            parts.append(jnp.concatenate([first, second], axis=1))
        return parts

    def against(rows_ref, index, pair, parts, has_off):
        own = rows_ref[index, pair]
        products = [dot_plain(own[:LANES], parts[0]), dot_plain(own, parts[1])]
        if has_off:
            before = rows_ref[0, pair]
            products += [dot_plain(before, parts[0]), dot_plain(before, parts[1])]
        return products

    def tiles_of(products, head, part, has_off):
        lanes = slice(head * LANES, (head + 1) * LANES)
        own = products[part]
        tiles = [own[part * LANES : (part + 1) * LANES, lanes]]
        if part:
            tiles.append(own[:LANES, lanes])
        if has_off:
            off = products[2 + part]
            tiles += [off[:LANES, lanes], off[LANES:, lanes]]
        return tiles

    def joined(lows, has_off):
        blank = jnp.zeros((LANES, LANES), BF16)
        first = jnp.concatenate([lows[0][0], blank], axis=0)
        second = jnp.concatenate([lows[1][1], lows[1][0]], axis=0)
        whole = jnp.concatenate([first, second], axis=1)
        if not has_off:
            return whole, None
        first = jnp.concatenate(lows[0][-2:], axis=0)
        second = jnp.concatenate(lows[1][-2:], axis=0)
        return whole, jnp.concatenate([first, second], axis=1)

    def attend(index, has_off):
        lanes = lanes_of(index)
        half = LANES // 2
        key_at = lax.broadcasted_iota(jnp.int32, (LANES, LANES), 0)
        query_at = lax.broadcasted_iota(jnp.int32, (LANES, LANES), 1)
        allowed = key_at <= query_at

        def scores_of(pair):
            return against(
                keys_rm, index, pair, by_queries(qkv[0, pair, :, lanes]), has_off
            )

        ahead = scores_of(0)
        for pair in range(pairs):
            scores = ahead
            if pair + 1 < pairs:
                ahead = scores_of(pair + 1)
            mixed = []
            for head in range(2):
                rows = slice(head * half, (head + 1) * half)
                lows = []
                for part in range(2):
                    tiles = tiles_of(scores, head, part, has_off)
                    tiles[0] = jnp.where(allowed, tiles[0], -1e30)
                    top = jnp.max(functools.reduce(jnp.maximum, tiles), axis=0, keepdims=True)
                    raised = [jnp.exp(tile - top) for tile in tiles]
                    total = functools.reduce(jnp.add, raised)
                    scale = 1.0 / jnp.sum(total, axis=0, keepdims=True)
                    lows.append([(tile * scale).astype(BF16) for tile in raised])
                low, low_off = joined(lows, has_off)
                share[index, pair, head] = low
                mix = dot_plain(qkv[2, pair, rows, lanes], low)
                if has_off:
                    share_off[pair, head] = low_off
                    mix = mix + dot_plain(qkv[2, pair, rows, :piece], low_off)
                mixed.append(mix.astype(BF16))
            mixture[pair, :, lanes] = jnp.concatenate(mixed, axis=0)

    def part_sum(values):
        return jnp.sum(values.reshape(values.shape[0] // 8, 8, values.shape[1]), axis=0)

    def full_mean(parts):
        return jnp.sum(parts, axis=0, keepdims=True) * (1.0 / width)

    def column(index, rows):
        part = columns[index, rows, :].astype(F32)
        return jnp.concatenate([part] * (piece // LANES), axis=1)

    def gather_sum(index, rows, values):
        sums[index, rows, :] = sums[index, rows, :] + fold(values)

    def norm_chunks(index, which, total):
        mean = full_mean(total)
        spread = jnp.zeros((8, piece), F32)
        for rows in chunks:
            centred = wide_a[rows, :] - mean
            spread = spread + part_sum(centred * centred)
        inverse = lax.rsqrt(full_mean(spread) + EPS)
        inverses[index, which] = inverse
        return mean, inverse

    def forward(index):
        lanes = lanes_of(index)

        @pl.when(segment == 0)
        def _():
            x_t[:, lanes] = own_rows(index).astype(BF16)

        @pl.when(segment == 1)
        def _():
            forward_copy(index).wait_recv()

        inputs = x_t[:, lanes]
        score_scale = 1.0 / math.sqrt(width // HEADS)
        for block in range(3):
            result = dot_plain(turned[block], inputs)
            for pair in range(pairs):
                low = result[pair * LANES : (pair + 1) * LANES]
                low = (low * score_scale if block == 0 else low).astype(BF16)
                qkv[block, pair, :, lanes] = low
                if block == 1:
                    keys_rm[index, pair] = low.T
                if block == 2:
                    values_rm[index, pair] = low.T

        @pl.when(index == 1)
        def _():
            attend(index, True)

        @pl.when(index != 1)
        def _():
            attend(index, False)

        branch = dot_plain(turned[3], mixture[:, :, lanes].reshape(width, piece))
        total = jnp.zeros((8, piece), F32)
        for rows in chunks:
            sum_one = x_t[rows, lanes].astype(F32) + (branch[rows] + column(BIAS_OUT, rows))
            wide_a[rows, :] = sum_one
            total = total + part_sum(sum_one)
        mean, inverse = norm_chunks(index, 0, total)
        for rows in chunks:
            normed = (wide_a[rows, :] - mean) * inverse
            norm_one[rows, lanes] = normed
            hidden = normed * column(GAIN_ONE, rows) + column(BIAS_ONE, rows)
            hidden_low[rows, lanes] = hidden.astype(BF16)

        branch_two = None
        for block in range(4):
            pre_block = dot_plain(turned[4 + block], hidden_low[:, lanes])
            lows = []
            for rows in chunks:
                pre = pre_block[rows] + column(BIAS_UP + block, rows)
                level = (lax.erf(pre * (1.0 / math.sqrt(2.0))) + 1.0) * 0.5
                bell = jnp.exp2(pre * pre * (-0.5 * math.log2(math.e)))
                lows.append((pre * level).astype(BF16))
                active[block, rows, lanes] = lows[-1]
                slope[block, rows, lanes] = (
                    level + pre * bell * (1.0 / math.sqrt(2.0 * math.pi))
                ).astype(BF16)
            part = dot_plain(turned[8 + block], jnp.concatenate(lows, axis=0))
            branch_two = part if branch_two is None else branch_two + part
        total = jnp.zeros((8, piece), F32)
        for rows in chunks:
            hidden = norm_one[rows, lanes] * column(GAIN_ONE, rows) + column(BIAS_ONE, rows)
            sum_two = hidden + (branch_two[rows] + column(BIAS_DOWN, rows))
            wide_a[rows, :] = sum_two
            total = total + part_sum(sum_two)
        mean, inverse = norm_chunks(index, 1, total)

        for rows in chunks:
            norm_two[rows, lanes] = (wide_a[rows, :] - mean) * inverse

        @pl.when(segment == 0)
        def _():
            for rows in chunks:
                outgoing[index, rows, :] = output_rows(rows, lanes).astype(BF16)
            forward_copy(index).start()

    def output_rows(rows, lanes):
        return norm_two[rows, lanes] * column(GAIN_TWO, rows) + column(BIAS_TWO, rows)

    def last_outputs(index, carry):
        free_ends(index)
        for start in range(0, width, LANES):
            rows = slice(start, start + LANES)
            ends_v[lax.rem(index, 2), :, rows] = output_rows(rows, lanes_of(index)).T
        ends_copy(index).start()
        return carry

    def attend_back(index, has_off):
        lanes = lanes_of(index)
        slot = jnp.where(index == 0, 1, 0)
        half = LANES // 2
        score_scale = 1.0 / math.sqrt(width // HEADS)

        def backs_of(pair):
            return against(values_rm, index, pair, by_queries(grad_mix[pair]), has_off)

        ahead = backs_of(0)
        for pair in range(pairs):
            backs = ahead
            if pair + 1 < pairs:
                ahead = backs_of(pair + 1)
            results = ([], [], [])
            for head in range(2):
                rows = slice(head * half, (head + 1) * half)
                low = share[index, pair, head]
                low_off = share_off[pair, head] if has_off else None
                lows = []
                for part in range(2):
                    place = slice(part * LANES, (part + 1) * LANES)
                    wides = [low[place, place]]
                    if part:
                        wides.append(low[:LANES, place])
                    if has_off:
                        wides += [low_off[:LANES, place], low_off[LANES:, place]]
                    wides = [tile.astype(F32) for tile in wides]
                    tiles = tiles_of(backs, head, part, has_off)
                    products = [wide * tile for wide, tile in zip(wides, tiles)]
                    inner = jnp.sum(functools.reduce(jnp.add, products), axis=0, keepdims=True)
                    lows.append(
                        [
                            (product - wide * inner).astype(BF16)
                            for product, wide in zip(products, wides)
                        ]
                    )
                grad_scores, grad_off = joined(lows, has_off)
                queries = qkv[0, pair, rows, lanes]
                grads = grad_mix[pair, rows]
                grad_query = dot_plain(qkv[1, pair, rows, lanes], grad_scores)
                grad_key = dot_turned(queries, grad_scores) + key_sums[slot, 0, pair, rows]
                grad_value = dot_turned(grads, low) + key_sums[slot, 1, pair, rows]
                if has_off:
                    grad_query = grad_query + dot_plain(qkv[1, pair, rows, :piece], grad_off)
                    key_sums[1, 0, pair, rows] = dot_turned(queries, grad_off)
                    key_sums[1, 1, pair, rows] = dot_turned(grads, low_off)
                for kept, grad in zip(results, (grad_query * score_scale, grad_key, grad_value)):
                    kept.append(grad.astype(BF16))
            for block in range(3):
                qkv[block, pair, :, lanes] = jnp.concatenate(results[block], axis=0)

    def backward(index):
        lanes = lanes_of(index)

        @pl.when(segment == 0)
        def _():
            backward_copy(index).wait_recv()

        plain = jnp.zeros((8, piece), F32)
        inner = jnp.zeros((8, piece), F32)
        for rows in chunks:
            grad = incoming_grad[index, rows, :].astype(F32)
            product = grad * norm_two[rows, lanes]
            gather_sum(GAIN_TWO, rows, product)
            gather_sum(BIAS_TWO, rows, grad)
            gain = column(GAIN_TWO, rows)
            plain = plain + part_sum(grad * gain)
            inner = inner + part_sum(product * gain)
        plain = full_mean(plain)
        inner = full_mean(inner)
        inverse = inverses[index, 1]
        for rows in chunks:
            scaled = incoming_grad[index, rows, :].astype(F32) * column(GAIN_TWO, rows)
            grad_two = (scaled - plain - norm_two[rows, lanes] * inner) * inverse
            gather_sum(BIAS_DOWN, rows, grad_two)
            wide_a[rows, :] = grad_two
            down_grad[rows, lanes] = grad_two.astype(BF16)

    def backward_feed(index):
        lanes = lanes_of(index)
        for block in range(4):
            back = dot_plain(w_down[block], down_grad[:, lanes])
            for rows in chunks:
                grad_pre = back[rows] * slope[block, rows, lanes].astype(F32)
                gather_sum(BIAS_UP + block, rows, grad_pre)
                slope[block, rows, lanes] = grad_pre.astype(BF16)

        through = dot_plain(w_up[...], slope[:, :, lanes].reshape(4 * width, piece))
        plain = jnp.zeros((8, piece), F32)
        inner = jnp.zeros((8, piece), F32)
        for rows in chunks:
            grad_hidden = wide_a[rows, :] + through[rows]
            wide_a[rows, :] = grad_hidden
            product = grad_hidden * norm_one[rows, lanes]
            gather_sum(GAIN_ONE, rows, product)
            gather_sum(BIAS_ONE, rows, grad_hidden)
            gain = column(GAIN_ONE, rows)
            plain = plain + part_sum(grad_hidden * gain)
            inner = inner + part_sum(product * gain)
        plain = full_mean(plain)
        inner = full_mean(inner)
        inverse = inverses[index, 0]
        for rows in chunks:
            scaled = wide_a[rows, :] * column(GAIN_ONE, rows)
            grad_one = (scaled - plain - norm_one[rows, lanes] * inner) * inverse
            gather_sum(BIAS_OUT, rows, grad_one)
            wide_b[rows, :] = grad_one
            branch_grad[rows, lanes] = grad_one.astype(BF16)
        grad_mix[...] = (
            dot_plain(w_out[...], branch_grad[:, lanes]).astype(BF16).reshape(pairs, LANES, piece)
        )

    def backward_attention(index):
        lanes = lanes_of(index)

        @pl.when(index == 1)
        def _():
            attend_back(index, True)

        @pl.when(index != 1)
        def _():
            attend_back(index, False)

        through = dot_plain(w_qkv[...], qkv[:, :, :, lanes].reshape(3 * width, piece))

        @pl.when(segment == 1)
        def _():
            for rows in chunks:
                outgoing[index, rows, :] = (wide_b[rows, :] + through[rows]).astype(BF16)
            backward_copy(index).start()

        @pl.when(segment == 0)
        def _():
            free_ends(index)
            for start in range(0, width, LANES):
                rows = slice(start, start + LANES)
                ends_v[lax.rem(index, 2), :, rows] = (wide_b[rows, :] + through[rows]).T
            ends_copy(index).start()

    split = SPLIT if share_rows % (16 * SPLIT) == 0 else 1
    dp_first = DP_FIRST if split == SPLIT else ()
    orders = (ORDER_ONE, ORDER_TWO, ORDER_THREE) if split == SPLIT else plain_orders()
    jobs = 3 * split
    cut_rows = share_rows // split
    job_rows = width // split

    def base_of(job):
        return (8, 4, 0)[job // split]

    def job_span(job):
        return pl.ds(job % split * job_rows, job_rows)

    def fin_rows(job):
        return pl.ds(job % split * cut_rows, cut_rows)

    def parts_of(job):
        return range(2) if job in dp_first else range(1)

    def core_copies(job):
        return [
            pltpu.make_async_remote_copy(
                src_ref=turned.at[base_of(job) + 2 * (1 - core) + each, job_span(job)],
                dst_ref=core_in.at[job // split, each, job_span(job)],
                send_sem=core_send.at[job, each],
                recv_sem=core_recv.at[job, each],
                device_id={"rep": other_core},
                device_id_type=MESH,
            )
            for each in range(2)
        ]

    def side_copies(job):
        base = base_of(job)
        copies = []
        for each in parts_of(job):
            if job in dp_first:
                source = turned.at[base + 2 * core + each, dp_rows(job, dp_steps - 1)[1]]
                target = side_in.at[
                    job // split, pl.ds(job % split * job_rows + each * cut_rows, cut_rows)
                ]
            else:
                source = turned.at[base + 2 * core + (1 - side), job_span(job)]
                target = side_in.at[job // split, job_span(job)]
            copies.append(
                pltpu.make_async_remote_copy(
                    src_ref=source,
                    dst_ref=target,
                    send_sem=side_send.at[job, each],
                    recv_sem=side_recv.at[job, each],
                    device_id={"rep": other_side},
                    device_id_type=MESH,
                )
            )
        return copies

    def dp_slot(job):
        return sum(len(parts_of(before)) for before in range(job))

    def dp_rows(job, step):
        count = dp_count // 2
        start = 0
        for bit in range(step):
            start = start + lax.rem(lax.div(dp, 2**bit), 2) * count
            count = count // 2
        mine = lax.rem(lax.div(dp, 2**step), 2)
        first = job % split * job_rows
        sent = pl.multiple_of(first + (start + (1 - mine) * count) * cut_rows, cut_rows)
        kept = pl.multiple_of(first + (start + mine * count) * cut_rows, cut_rows)
        return pl.ds(sent, count * cut_rows), pl.ds(kept, count * cut_rows)

    def dp_landing(step):
        count = dp_count // 2 ** (step + 1)
        return pl.ds((dp_count - 2 * count) * cut_rows, count * cut_rows)

    def dp_copies(job, step):
        mine = lax.rem(lax.div(dp, 2**step), 2)
        copies = []
        for each in parts_of(job):
            position = base_of(job) + 2 * core + (each if job in dp_first else side)
            copies.append(
                pltpu.make_async_remote_copy(
                    src_ref=turned.at[position, dp_rows(job, step)[0]],
                    dst_ref=dp_in.at[dp_slot(job) + each, dp_landing(step)],
                    send_sem=dp_send.at[job, step, each],
                    recv_sem=dp_recv.at[job, step, each],
                    device_id={"dp": dp + (1 - 2 * mine) * 2**step},
                    device_id_type=MESH,
                )
            )
        return copies

    def join_copy(job):
        part = fin.at[job // split, 2 * core + side, fin_rows(job)]
        return pltpu.make_async_remote_copy(
            src_ref=part,
            dst_ref=part,
            send_sem=join_send.at[job],
            recv_sem=join_recv.at[job],
            device_id={"rep": other_side},
            device_id_type=MESH,
        )

    def last_copies(job):
        copies = []
        for each in range(2):
            part = fin.at[job // split, 2 * core + each, fin_rows(job)]
            copies.append(
                pltpu.make_async_remote_copy(
                    src_ref=part,
                    dst_ref=part,
                    send_sem=last_send.at[job, each],
                    recv_sem=last_recv.at[job, each],
                    device_id={"rep": other_core},
                    device_id_type=MESH,
                )
            )
        return copies

    def fin_copy(job):
        return pltpu.make_async_copy(
            fin.at[job // split, :, fin_rows(job)],
            fin_hbm.at[job // split, :, fin_rows(job)],
            fin_sem.at[job],
        )

    def arrived(*copies):
        for copy in copies:
            copy.wait_send()
        for copy in copies:
            copy.wait_recv()

    def start_all(copies):
        for copy in copies:
            copy.start()

    def turned_bits(value, count):
        place = 0
        while count > 1:
            place = place * 2 + value % 2
            value = value // 2
            count = count // 2
        return place

    pack = min(2, split)

    def left_rows(source, part):
        count = pack * cut_rows
        start = part * pack * cut_rows
        return jnp.concatenate(
            [source(index * share_rows + start, count) for index in range(dp_count)], axis=0
        )

    def keep_rows(block, part, result):
        for index in range(dp_count):
            for each in range(pack):
                target = (part * pack + each) * job_rows + turned_bits(index, dp_count) * cut_rows
                start = (index * pack + each) * cut_rows
                turned[block, target : target + cut_rows, :] = result[start : start + cut_rows]

    def down_sums(part):
        count = width // (4 * share_rows)

        def one(block, carry):
            pieces = []
            for each in range(4 * count):
                start = each * share_rows + part * pack * cut_rows
                pieces.append(active[block, start : start + pack * cut_rows, :])
            result = dot_turned(jnp.concatenate(pieces, axis=0), down_grad[...]).astype(BF16)
            high = lax.rem(block, 2) * 2 + lax.div(block, 2)
            for each in range(count):
                place = turned_bits(each, count) * 4 + high
                for position in range(4):
                    for job in range(pack):
                        target = (part * pack + job) * job_rows + place * cut_rows
                        start = ((each * 4 + position) * pack + job) * cut_rows
                        turned[
                            8 + position, pl.ds(pl.multiple_of(target, cut_rows), cut_rows), :
                        ] = result[start : start + cut_rows]
            return carry

        lax.fori_loop(0, 4, one, 0)

    def up_sums(part):
        def one(block, carry):
            left = left_rows(lambda start, count: hidden_low[start : start + count, :], part)
            keep_rows(4 + block, part, dot_turned(left, slope[block]).astype(BF16))
            return carry

        lax.fori_loop(0, 4, one, 0)

    def qkv_sums(part):
        def one(block, carry):
            left = left_rows(lambda start, count: x_t[start : start + count, :], part)
            grads = qkv[block].reshape(width, PIECES * piece)
            keep_rows(block, part, dot_turned(left, grads).astype(BF16))
            return carry

        lax.fori_loop(0, 3, one, 0)
        left = left_rows(
            lambda start, count: mixture[start // LANES, start % LANES : start % LANES + count, :], part
        )
        keep_rows(3, part, dot_turned(left, branch_grad[...]).astype(BF16))

    def sums_of(job):
        (down_sums, up_sums, qkv_sums)[job // split](job % split // pack)
        for each in range(pack):
            start_all(core_copies(job + each))

    def after_core(job):
        arrived(*core_copies(job))
        rows = job_span(job)
        for each in parts_of(job):
            place = 1 - side if each == 0 else side
            position = base_of(job) + 2 * core + place
            turned[position, rows, :] = (
                turned[position, rows, :].astype(F32)
                + core_in[job // split, place, rows, :].astype(F32)
            ).astype(BF16)
        if job in dp_first:
            start_all(dp_copies(job, 0))

    def start_side(job):
        start_all(side_copies(job))

    def after_side(job):
        arrived(*side_copies(job))
        rows = job_span(job)
        position = base_of(job) + 2 * core + side
        turned[position, rows, :] = (
            turned[position, rows, :].astype(F32)
            + core_in[job // split, side, rows, :].astype(F32)
            + side_in[job // split, rows, :].astype(F32)
        ).astype(BF16)
        start_all(dp_copies(job, 0))

    def dp_total(job, step, each):
        position = base_of(job) + 2 * core + (each if job in dp_first else side)
        kept = turned[position, dp_rows(job, step)[1], :].astype(F32)
        return position, kept + dp_in[dp_slot(job) + each, dp_landing(step), :].astype(F32)

    def after_dp(job):
        for step in range(dp_steps - 1):
            arrived(*dp_copies(job, step))
            for each in parts_of(job):
                position, total = dp_total(job, step, each)
                turned[position, dp_rows(job, step)[1], :] = total.astype(BF16)
            start_all(dp_copies(job, step + 1))

    def after_last_dp(job):
        step = dp_steps - 1
        arrived(*dp_copies(job, step))
        for each in parts_of(job):
            position, total = dp_total(job, step, each)
            if job in dp_first:
                turned[position, dp_rows(job, step)[1], :] = total.astype(BF16)
            else:
                fin[job // split, 2 * core + side, fin_rows(job), :] = total.astype(BF16)
        if job in dp_first:
            start_side(job)
        else:
            join_copy(job).start()

    def after_join(job):
        if job in dp_first:
            arrived(*side_copies(job))
            for each in range(2):
                rows = pl.ds(job % split * job_rows + each * cut_rows, cut_rows)
                own = turned[base_of(job) + 2 * core + each, dp_rows(job, dp_steps - 1)[1], :]
                total = own.astype(F32) + side_in[job // split, rows, :].astype(F32)
                fin[job // split, 2 * core + each, fin_rows(job), :] = total.astype(BF16)
        else:
            arrived(join_copy(job))
        start_all(last_copies(job))

    def after_last(job):
        arrived(*last_copies(job))
        fin_copy(job).start()

    def small_dp_copy(step):
        target = lax.rem(dp + step, dp_count)
        return pltpu.make_async_remote_copy(
            src_ref=small.at[target],
            dst_ref=small_dp.at[step - 1],
            send_sem=sdp_send.at[step - 1],
            recv_sem=sdp_recv.at[step - 1],
            device_id={"dp": target},
            device_id_type=MESH,
        )

    def small_rep_copy(step):
        return pltpu.make_async_remote_copy(
            src_ref=small_rep.at[rep],
            dst_ref=small_rep.at[rep],
            send_sem=srep_send.at[step - 1],
            recv_sem=srep_recv.at[step - 1],
            device_id={"rep": lax.rem(rep + step, 4)},
            device_id_type=MESH,
        )

    small_copy = pltpu.make_async_copy(small_out, small_hbm, load_sem.at[0])

    def small_step(stage):
        if stage == 0:
            rows_of = [jnp.sum(sums[index].T, axis=0, keepdims=True) for index in range(STATS)]
            small[...] = jnp.zeros(small.shape, F32)
            for share_index in range(dp_count):
                for index in range(BIAS_UP):
                    start = share_index * share_rows
                    small[share_index, index : index + 1, :share_rows] = rows_of[index][
                        :, start : start + share_rows
                    ]
                for part in range(4):
                    start = (share_index * 4 + part) * share_rows
                    block, start = start // width, start % width
                    small[share_index, BIAS_UP + part : BIAS_UP + part + 1, :share_rows] = rows_of[
                        BIAS_UP + block
                    ][:, start : start + share_rows]
            for step in range(1, dp_count):
                small_dp_copy(step).start()
        elif stage == 1:
            total = small[dp]
            for step in range(1, dp_count):
                arrived(small_dp_copy(step))
                total = total + small_dp[step - 1]
            small_rep[rep] = total
            for step in range(1, 4):
                small_rep_copy(step).start()
        else:
            for step in range(1, 4):
                arrived(small_rep_copy(step))
            small_out[...] = (small_rep[0] + small_rep[1]) + (small_rep[2] + small_rep[3])
            small_copy.start()

    def run(order):
        steps = (
            sums_of,
            after_core,
            start_side,
            after_side,
            after_dp,
            after_last_dp,
            after_join,
            after_last,
            small_step,
        )
        for stage, job in order:
            steps[stage](job)

    def one_step(step, carry):
        first_index = jnp.where(step < 4, step, jnp.where(step < 6, 5 - step, step - 4))
        last_index = jnp.where(step < 2, step, jnp.where(step < 4, 3 - step, lax.div(step, 2)))
        first_is = jnp.where(step < 4, 1, 0)
        last_is = jnp.where(step < 2, 1, jnp.where(step < 4, 0, 1 - lax.rem(step, 2)))
        index = jnp.minimum(jnp.where(segment == 0, first_index, last_index), PIECES - 1)
        is_last = jnp.where(step == 2 * PIECES, 1, 0)
        is_forward = jnp.where(segment == 0, first_is, last_is) * (1 - is_last)
        is_backward = (1 - is_forward) * (1 - is_last)
        is_split = jnp.where(step >= 2 * PIECES - 1, 1 - segment, 0)
        is_rest = is_backward * (1 - is_split) + is_last * is_split

        @pl.when(is_forward == 1)
        def _():
            forward(index)

        @pl.when(is_backward == 1)
        def _():
            backward(index)

        @pl.when(is_last == 1)
        def _():
            run(orders[0])

        @pl.when(is_rest == 1)
        def _():
            backward_feed(index)

        @pl.when(is_last == 1)
        def _():
            run(orders[1])

        @pl.when(is_rest == 1)
        def _():
            backward_attention(index)

        return carry

    @pl.when(segment == 1)
    def _():
        for index in range(PIECES):
            incoming_grad[index] = own_rows(index).astype(BF16)

    lax.fori_loop(0, 2 * PIECES + 1, one_step, 0)

    cut = orders[2].index((SMALL, 0))
    run(orders[2][:cut])

    @pl.when(segment == 1)
    def _():
        lax.fori_loop(0, PIECES, last_outputs, 0)

    run(orders[2][cut:])

    for index in range(PIECES):

        @pl.when(segment == 0)
        def _():
            forward_copy(index).wait_send()

        @pl.when(segment == 1)
        def _():
            backward_copy(index).wait_send()

    for index in range(2, PIECES):
        ends_copy(index).wait()
    for job in range(jobs):
        fin_copy(job).wait()
    small_copy.wait()


def finish_kernel(
    flag_ref,
    ends_in,
    fin,
    small,
    ends,
    grad_qkv,
    grad_out,
    grad_up,
    grad_down,
    grad_up_bias,
    grad_gains,
    grad_biases,
    ends_v,
    fin_v,
    wide_qkv,
    wide_out,
    wide_up,
    wide_down,
    small_v,
    up_bias_v,
    gains_v,
    biases_v,
    ends_sem,
    in_sem,
    out_sem,
):
    half = ends_in.shape[0] // 2
    share_rows, width = fin.shape[2:]
    start = pl.multiple_of(half * (1 - flag_ref[0, 0]), half)
    cut = half // 4
    ends_copies = []
    ends_loads = []
    for part in range(8):
        source = pl.ds(part * cut, cut)
        offset = start + part * cut if part < 4 else part * cut - half + (half - start)
        target = pl.ds(pl.multiple_of(offset, cut), cut)
        ends_loads.append(
            pltpu.make_async_copy(ends_in.at[source], ends_v.at[source], ends_sem.at[part])
        )
        ends_copies.append(
            pltpu.make_async_copy(ends_v.at[source], ends.at[0, target], ends_sem.at[8 + part])
        )
    loads = [
        pltpu.make_async_copy(fin.at[group], fin_v.at[group], in_sem.at[group])
        for group in range(3)
    ]
    stores = [
        pltpu.make_async_copy(wide, target.at[0], out_sem.at[index])
        for index, (wide, target) in enumerate(
            ((wide_down, grad_down), (wide_up, grad_up), (wide_qkv, grad_qkv), (wide_out, grad_out))
        )
    ]
    small_load = pltpu.make_async_copy(small, small_v, in_sem.at[3])
    small_stores = [
        pltpu.make_async_copy(narrow, target, out_sem.at[4 + index])
        for index, (narrow, target) in enumerate(
            ((up_bias_v, grad_up_bias), (gains_v, grad_gains), (biases_v, grad_biases))
        )
    ]
    small_load.start()
    for copy in loads + ends_loads:
        copy.start()
    for load, copy in zip(ends_loads, ends_copies):
        load.wait()
        copy.start()
    loads[0].wait()
    for position in range(4):
        rows = slice(position * share_rows, (position + 1) * share_rows)
        wide_down[rows, :] = fin_v[0, position].astype(F32)
    stores[0].start()
    loads[1].wait()
    for position in range(4):
        wide_up[:, position * width : (position + 1) * width] = fin_v[1, position].astype(F32)
    stores[1].start()
    loads[2].wait()
    for position in range(3):
        wide_qkv[:, position * width : (position + 1) * width] = fin_v[2, position].astype(F32)
    stores[2].start()
    wide_out[...] = fin_v[2, 3].astype(F32)
    stores[3].start()
    small_load.wait()
    for position in range(4):
        rows = slice(position * share_rows, (position + 1) * share_rows)
        up_bias_v[:, rows] = small_v[BIAS_UP + position : BIAS_UP + position + 1, :share_rows]
    gains_v[0] = small_v[:2, :share_rows]
    biases_v[0] = small_v[2:BIAS_UP, :share_rows]
    for copy in small_stores:
        copy.start()
    for copy in stores + ends_copies + small_stores:
        copy.wait()


def on_device(
    dp_count,
    block_input,
    cotangent,
    window_group,
    w_qkv,
    w_out,
    w_up,
    w_down,
    up_bias,
    norm_gains,
    biases,
):
    rows, width = block_input.shape
    piece = rows // PIECES
    pairs = width // LANES
    share_rows = width // dp_count
    small_width = max(share_rows, LANES)
    dp_steps = dp_count.bit_length() - 1
    split = SPLIT if share_rows % (16 * SPLIT) == 0 else 1
    jobs = 3 * split
    slots = jobs + (len(DP_FIRST) if split == SPLIT else 0)
    any_spec = pl.BlockSpec(memory_space=pl.ANY)
    vmem_spec = pl.BlockSpec(memory_space=pltpu.VMEM)
    smem_spec = pl.BlockSpec(memory_space=pltpu.SMEM)
    dma = pltpu.SemaphoreType.DMA
    vmem = pltpu.VMEM
    ends_in, fin, small = pl.pallas_call(
        functools.partial(layer_kernel, dp_count),
        out_shape=(
            jax.ShapeDtypeStruct((PIECES, piece, width), F32),
            jax.ShapeDtypeStruct((3, 4, share_rows, width), BF16),
            jax.ShapeDtypeStruct((16, small_width), F32),
        ),
        in_specs=[smem_spec] + [any_spec] * 6 + [vmem_spec] * 3,
        out_specs=(any_spec,) * 3,
        scratch_shapes=[
            vmem((width, 3 * width), BF16),
            vmem((width, width), BF16),
            vmem((width, 4 * width), BF16),
            vmem((4, width, width), BF16),
            vmem((12, width, width), BF16),
            vmem((PIECES, piece, width), BF16),
            vmem((width, rows), BF16),
            vmem((3, pairs, LANES, rows), BF16),
            vmem((PIECES, pairs, piece, LANES), BF16),
            vmem((PIECES, pairs, piece, LANES), BF16),
            vmem((PIECES, pairs, 2, piece, piece), BF16),
            vmem((pairs, 2, piece, piece), BF16),
            vmem((pairs, LANES, rows), BF16),
            vmem((width, rows), F32),
            vmem((width, rows), F32),
            vmem((PIECES, 2, 1, piece), F32),
            vmem((width, rows), BF16),
            vmem((4, width, rows), BF16),
            vmem((4, width, rows), BF16),
            vmem((width, rows), BF16),
            vmem((width, rows), BF16),
            vmem((pairs, LANES, piece), BF16),
            vmem((PIECES, width, piece), BF16),
            vmem((PIECES, width, piece), BF16),
            vmem((STATS, width, LANES), BF16),
            vmem((STATS, width, LANES), F32),
            vmem((2, 2, pairs, LANES, piece), F32),
            vmem((width, piece), F32),
            vmem((width, piece), F32),
            vmem((2, piece, width), F32),
            vmem((3, 2, width, width), BF16),
            vmem((3, width, width), BF16),
            vmem((slots, (width - share_rows) // split, width), BF16),
            vmem((3, 4, share_rows, width), BF16),
            vmem((dp_count, 16, small_width), F32),
            vmem((dp_count - 1, 16, small_width), F32),
            vmem((4, 16, small_width), F32),
            vmem((16, small_width), F32),
            dma((13,)),
            dma((PIECES,)),
            dma((PIECES,)),
            dma((PIECES,)),
            dma((jobs, 2)),
            dma((jobs, 2)),
            dma((jobs, 2)),
            dma((jobs, 2)),
            dma((jobs, dp_steps, 2)),
            dma((jobs, dp_steps, 2)),
            dma((jobs,)),
            dma((jobs,)),
            dma((jobs, 2)),
            dma((jobs, 2)),
            dma((dp_count - 1,)),
            dma((dp_count - 1,)),
            dma((3,)),
            dma((3,)),
            dma((jobs,)),
        ],
        compiler_params=pltpu.CompilerParams(
            collective_id=0, has_side_effects=True, vmem_limit_bytes=63 * 1024 * 1024
        ),
    )(
        window_group,
        block_input.reshape(PIECES, piece, width),
        cotangent.reshape(PIECES, piece, width),
        w_qkv,
        w_out,
        w_up,
        w_down,
        up_bias,
        norm_gains,
        biases,
    )
    return pl.pallas_call(
        finish_kernel,
        out_shape=(
            jax.ShapeDtypeStruct((1, rows, width), F32),
            jax.ShapeDtypeStruct((1, share_rows, 3 * width), F32),
            jax.ShapeDtypeStruct((1, share_rows, width), F32),
            jax.ShapeDtypeStruct((1, share_rows, 4 * width), F32),
            jax.ShapeDtypeStruct((1, 4 * share_rows, width), F32),
            jax.ShapeDtypeStruct((1, 4 * share_rows), F32),
            jax.ShapeDtypeStruct((1, 2, share_rows), F32),
            jax.ShapeDtypeStruct((1, 4, share_rows), F32),
        ),
        in_specs=[smem_spec] + [any_spec] * 3,
        out_specs=(any_spec,) * 8,
        scratch_shapes=[
            vmem((rows, width), F32),
            vmem((3, 4, share_rows, width), BF16),
            vmem((share_rows, 3 * width), F32),
            vmem((share_rows, width), F32),
            vmem((share_rows, 4 * width), F32),
            vmem((4 * share_rows, width), F32),
            vmem((16, small_width), F32),
            vmem((1, 4 * share_rows), F32),
            vmem((1, 2, share_rows), F32),
            vmem((1, 4, share_rows), F32),
            dma((16,)),
            dma((4,)),
            dma((7,)),
        ],
        compiler_params=pltpu.CompilerParams(vmem_limit_bytes=63 * 1024 * 1024),
    )(window_group, ends_in.reshape(rows, width), fin, small)


def solution(mesh):
    return jax.shard_map(
        functools.partial(on_device, mesh.shape["dp"]),
        mesh=mesh,
        in_specs=(
            P(("dp", "rep"), None),
            P(("dp", "rep"), None),
            P(("dp", "rep"), None),
            P("segment", None, None),
            P("segment", None, None),
            P("segment", None, None),
            P("segment", None, None),
            P("segment", None),
            P("segment", None, None),
            P("segment", None, None),
        ),
        out_specs=(
            P("segment", ("dp", "rep"), None),
            P("segment", "dp", None),
            P("segment", "dp", None),
            P("segment", "dp", None),
            P("segment", "dp", None),
            P("segment", "dp"),
            P("segment", None, "dp"),
            P("segment", None, "dp"),
        ),
        check_vma=False,
    )
```

```python
import functools
import math

import jax
import jax.numpy as jnp
from jax import lax
from jax.experimental import pallas as pl
from jax.experimental.pallas import tpu as pltpu
from jax.sharding import PartitionSpec as P

MESH = pl.DeviceIdType.MESH
F32 = jnp.float32
BF16 = jnp.bfloat16
HEADS = 8
LANES = 128
PIECES = 4
EPS = 1e-05
GAIN_ONE, GAIN_TWO, BIAS_OUT, BIAS_ONE, BIAS_DOWN, BIAS_TWO, BIAS_UP = range(7)
STATS = 10
CHUNK = 64
SPLIT = 4
DP_FIRST = (1, 3, 6, 10)
SUM, CORE, SIDE, SIDED, DP, DPED, JOIN, LAST, SMALL = range(9)
ORDER_ONE = (
    (SUM, 0), (SUM, 2),
)
ORDER_TWO = (
    (SUM, 4), (CORE, 1), (CORE, 0), (SIDE, 0), (SUM, 6), (CORE, 2), (SIDE, 2), (CORE, 3),
)
ORDER_THREE = (
    (CORE, 5), (SUM, 8), (SIDE, 5), (CORE, 6), (DP, 3), (CORE, 4), (SUM, 10), (CORE, 7), (SIDE, 4),
    (SIDED, 5), (SIDED, 2), (SIDE, 7), (DP, 1), (CORE, 8), (CORE, 11), (DPED, 3), (DP, 6), (SIDED, 0),
    (DP, 2), (DPED, 1), (SIDED, 4), (SIDE, 11), (JOIN, 3), (SIDED, 7), (CORE, 10), (DP, 0), (DP, 5),
    (CORE, 9), (SMALL, 0), (SIDE, 8), (DP, 4), (SIDE, 9), (SIDED, 11), (DP, 7), (JOIN, 1), (SIDED, 8),
    (SMALL, 1), (LAST, 1), (DPED, 0), (DP, 10), (DPED, 5), (DPED, 2), (LAST, 3), (SIDED, 9), (DPED, 6),
    (DP, 8), (JOIN, 0), (DPED, 4), (DPED, 10), (DP, 11), (JOIN, 4), (JOIN, 5), (DP, 9), (JOIN, 2), (LAST, 0),
    (DPED, 8), (JOIN, 6), (DPED, 7), (DPED, 11), (DPED, 9), (LAST, 4), (JOIN, 10), (JOIN, 7), (JOIN, 11),
    (JOIN, 8), (JOIN, 9), (SMALL, 2), (LAST, 5), (LAST, 8), (LAST, 2), (LAST, 9), (LAST, 10), (LAST, 11),
    (LAST, 7), (LAST, 6),
)


def plain_orders():
    one = ((SUM, 0),)
    two = ((SUM, 1), (CORE, 0), (SIDE, 0))
    three = ((SUM, 2), (CORE, 1), (SIDE, 1), (CORE, 2), (SIDE, 2), (SMALL, 0), (SMALL, 1), (SMALL, 2))
    for stage in (SIDED, DP, DPED, JOIN, LAST):
        three += tuple((stage, job) for job in range(3))
    return one, two, three


def dot_plain(left, right):
    return lax.dot_general(left, right, (((1,), (0,)), ((), ())), preferred_element_type=F32)


def drain(parts):
    for _ in parts:
        pass


def side_by_side(one, two):
    spent = [0, 300]
    live = [one, two]
    while live[0] or live[1]:
        which = 0 if live[0] and (not live[1] or spent[0] <= spent[1]) else 1
        cost = next(live[which], None)
        if cost is None:
            live[which] = None
        else:
            spent[which] += cost


def dot_turned(left, right):
    return lax.dot_general(left, right, (((1,), (1,)), ((), ())), preferred_element_type=F32)


def fold(values):
    total = values[:, :LANES]
    for start in range(LANES, values.shape[1], LANES):
        total = total + values[:, start : start + LANES]
    return total


def layer_kernel(
    dp_count,
    flag_ref,
    x_hbm,
    ct_hbm,
    w_qkv_hbm,
    w_out_hbm,
    w_up_hbm,
    w_down_hbm,
    up_bias_ref,
    gains_ref,
    biases_ref,
    ends_hbm,
    fin_hbm,
    small_hbm,
    w_qkv,
    w_out,
    w_up,
    w_down,
    turned,
    rows_in,
    x_t,
    qkv,
    keys_rm,
    values_rm,
    share,
    share_off,
    mixture,
    norm_one,
    norm_two,
    inverses,
    hidden_low,
    slope,
    active,
    down_grad,
    branch_grad,
    grad_mix,
    outgoing,
    incoming_grad,
    columns,
    sums,
    key_sums,
    wide_a,
    wide_b,
    wide_c,
    ends_v,
    core_in,
    side_in,
    dp_in,
    fin,
    small,
    small_dp,
    small_rep,
    small_out,
    load_sem,
    seg_send,
    seg_recv,
    ends_sem,
    core_send,
    core_recv,
    side_send,
    side_recv,
    dp_send,
    dp_recv,
    join_send,
    join_recv,
    last_send,
    last_recv,
    sdp_send,
    sdp_recv,
    srep_send,
    srep_recv,
    fin_sem,
):
    width = w_out.shape[0]
    piece = x_t.shape[1] // PIECES
    pairs = qkv.shape[1]
    share_rows = width // dp_count
    dp_steps = dp_count.bit_length() - 1
    segment = lax.axis_index("segment")
    dp = lax.axis_index("dp")
    rep = lax.axis_index("rep")
    core = lax.rem(rep, 2)
    side = lax.div(rep, 2)
    other_core = side * 2 + (1 - core)
    other_side = (1 - side) * 2 + core

    loads = []
    for block in range(3):
        span = pl.ds(block * width, width)
        loads.append((w_qkv_hbm.at[0, :, span], w_qkv.at[:, span]))
    loads.append((w_out_hbm.at[0], w_out))
    for block in range(4):
        span = pl.ds(block * width, width)
        loads.append((w_up_hbm.at[0, :, span], w_up.at[:, span]))
    for block in range(4):
        span = pl.ds(block * width, width)
        loads.append((w_down_hbm.at[0, span, :], w_down.at[block]))
    load_copies = [
        pltpu.make_async_copy(source, target, load_sem.at[index + 1])
        for index, (source, target) in enumerate(loads)
    ]
    first_rows = pltpu.make_async_copy(x_hbm, rows_in, load_sem.at[0])
    last_rows = pltpu.make_async_copy(ct_hbm, rows_in, load_sem.at[0])

    @pl.when(segment == 0)
    def _():
        first_rows.start()

    @pl.when(segment == 1)
    def _():
        last_rows.start()

    for copy in load_copies:
        copy.start()

    barrier = pltpu.get_barrier_semaphore()
    pl.semaphore_signal(
        barrier, inc=1, device_id={"segment": 1 - segment}, device_id_type=MESH
    )
    for step in range(1, 4):
        pl.semaphore_signal(
            barrier, inc=1, device_id={"rep": lax.rem(rep + step, 4)}, device_id_type=MESH
        )
    for step in range(1, dp_count):
        pl.semaphore_signal(
            barrier, inc=1, device_id={"dp": lax.rem(dp + step, dp_count)}, device_id_type=MESH
        )

    params = [gains_ref[0].astype(F32), biases_ref[0].astype(F32)]
    for block in range(4):
        params.append(up_bias_ref[:, block * width : (block + 1) * width].astype(F32))
    params.append(jnp.zeros((16 - STATS, width), F32))
    upright = jnp.concatenate(params, axis=0).T
    for index in range(STATS):
        columns[index] = jnp.broadcast_to(upright[:, index : index + 1], (width, LANES)).astype(BF16)
    for index in range(STATS):
        sums[index] = jnp.zeros((width, LANES), F32)
    key_sums[0] = jnp.zeros(key_sums.shape[1:], F32)

    chunks = [slice(start, start + CHUNK) for start in range(0, width, CHUNK)]

    for block, copy in enumerate(load_copies):
        copy.wait()
        span = slice(block % 4 * width, (block % 4 + 1) * width)
        if block < 3:
            turned[block] = w_qkv[:, span].T
        elif block == 3:
            turned[block] = w_out[...].T
        elif block < 8:
            turned[block] = w_up[:, span].T
        else:
            turned[block] = w_down[block - 8].T
    first_rows.wait()

    pl.semaphore_wait(barrier, 4 + dp_count - 1)

    flag = flag_ref[0, 0].astype(F32)

    def lanes_of(index):
        if isinstance(index, int):
            return pl.ds(index * piece, piece)
        return pl.ds(pl.multiple_of(index * piece, piece), piece)

    def forward_copy(index):
        return pltpu.make_async_remote_copy(
            src_ref=outgoing.at[index],
            dst_ref=x_t.at[:, lanes_of(index)],
            send_sem=seg_send.at[index],
            recv_sem=seg_recv.at[index],
            device_id={"segment": 1 - segment},
            device_id_type=MESH,
        )

    def backward_copy(index):
        return pltpu.make_async_remote_copy(
            src_ref=outgoing.at[index],
            dst_ref=incoming_grad.at[index],
            send_sem=seg_send.at[index],
            recv_sem=seg_recv.at[index],
            device_id={"segment": 1 - segment},
            device_id_type=MESH,
        )

    def ends_copy(index):
        return pltpu.make_async_copy(
            ends_v.at[lax.rem(index, 2)], ends_hbm.at[index], ends_sem.at[index]
        )

    def free_ends(index):
        @pl.when(index >= 2)
        def _():
            ends_copy(index - 2).wait()

    def own_rows(index):
        half = lax.rem(index, 2)
        whole = jnp.where(index < 2, 1.0, 0.0).astype(F32)
        weight = whole * flag + (1.0 - whole) * (1.0 - flag)
        picked = rows_in[half].astype(F32) * weight + rows_in[2 + half].astype(F32) * (1.0 - weight)
        return picked.T

    def by_queries(values):
        half = LANES // 2
        blank = jnp.zeros((half, LANES), values.dtype)
        parts = []
        for part in range(2):
            span = slice(part * LANES, (part + 1) * LANES)
            first = jnp.concatenate([values[:half, span], blank], axis=0)
            second = jnp.concatenate([blank, values[half:, span]], axis=0)
            parts.append(jnp.concatenate([first, second], axis=1))
        return parts

    def against(rows_ref, index, pair, parts, has_off):
        own = rows_ref[index, pair]
        products = [dot_plain(own[:LANES], parts[0]), dot_plain(own, parts[1])]
        if has_off:
            before = rows_ref[0, pair]
            products += [dot_plain(before, parts[0]), dot_plain(before, parts[1])]
        return products

    def tiles_of(products, head, part, has_off):
        lanes = slice(head * LANES, (head + 1) * LANES)
        own = products[part]
        tiles = [own[part * LANES : (part + 1) * LANES, lanes]]
        if part:
            tiles.append(own[:LANES, lanes])
        if has_off:
            off = products[2 + part]
            tiles += [off[:LANES, lanes], off[LANES:, lanes]]
        return tiles

    def joined(lows, has_off):
        blank = jnp.zeros((LANES, LANES), BF16)
        first = jnp.concatenate([lows[0][0], blank], axis=0)
        second = jnp.concatenate([lows[1][1], lows[1][0]], axis=0)
        whole = jnp.concatenate([first, second], axis=1)
        if not has_off:
            return whole, None
        first = jnp.concatenate(lows[0][-2:], axis=0)
        second = jnp.concatenate(lows[1][-2:], axis=0)
        return whole, jnp.concatenate([first, second], axis=1)

    def attend(index, has_off):
        lanes = lanes_of(index)
        half = LANES // 2
        key_at = lax.broadcasted_iota(jnp.int32, (LANES, LANES), 0)
        query_at = lax.broadcasted_iota(jnp.int32, (LANES, LANES), 1)
        allowed = key_at <= query_at

        def scores_of(pair):
            return against(
                keys_rm, index, pair, by_queries(qkv[0, pair, :, lanes]), has_off
            )

        ahead = scores_of(0)
        for pair in range(pairs):
            scores = ahead
            if pair + 1 < pairs:
                ahead = scores_of(pair + 1)
            mixed = []
            for head in range(2):
                rows = slice(head * half, (head + 1) * half)
                lows = []
                for part in range(2):
                    tiles = tiles_of(scores, head, part, has_off)
                    tiles[0] = jnp.where(allowed, tiles[0], -1e30)
                    top = jnp.max(functools.reduce(jnp.maximum, tiles), axis=0, keepdims=True)
                    raised = [jnp.exp(tile - top) for tile in tiles]
                    total = functools.reduce(jnp.add, raised)
                    scale = 1.0 / jnp.sum(total, axis=0, keepdims=True)
                    lows.append([(tile * scale).astype(BF16) for tile in raised])
                low, low_off = joined(lows, has_off)
                share[index, pair, head] = low
                mix = dot_plain(qkv[2, pair, rows, lanes], low)
                if has_off:
                    share_off[pair, head] = low_off
                    mix = mix + dot_plain(qkv[2, pair, rows, :piece], low_off)
                mixed.append(mix.astype(BF16))
            mixture[pair, :, lanes] = jnp.concatenate(mixed, axis=0)
            yield 280

    def part_sum(values):
        return jnp.sum(values.reshape(values.shape[0] // 8, 8, values.shape[1]), axis=0)

    def full_mean(parts):
        return jnp.sum(parts, axis=0, keepdims=True) * (1.0 / width)

    def column(index, rows):
        part = columns[index, rows, :].astype(F32)
        return jnp.concatenate([part] * (piece // LANES), axis=1)

    def gather_sum(index, rows, values):
        sums[index, rows, :] = sums[index, rows, :] + fold(values)

    def norm_chunks(index, which, wide_a, total):
        mean = full_mean(total)
        spread = jnp.zeros((8, piece), F32)
        for rows in chunks:
            centred = wide_a[rows, :] - mean
            spread = spread + part_sum(centred * centred)
        inverse = lax.rsqrt(full_mean(spread) + EPS)
        inverses[index, which] = inverse
        return mean, inverse

    def forward_start(index):
        @pl.when(segment == 0)
        def _():
            x_t[:, lanes_of(index)] = own_rows(index).astype(BF16)

        @pl.when(segment == 1)
        def _():
            forward_copy(index).wait_recv()

    def forward_first(index):
        lanes = lanes_of(index)
        inputs = x_t[:, lanes]
        score_scale = 1.0 / math.sqrt(width // HEADS)
        for block in range(3):
            result = dot_plain(turned[block], inputs)
            for pair in range(pairs):
                low = result[pair * LANES : (pair + 1) * LANES]
                low = (low * score_scale if block == 0 else low).astype(BF16)
                qkv[block, pair, :, lanes] = low
                if block == 1:
                    keys_rm[index, pair] = low.T
                if block == 2:
                    values_rm[index, pair] = low.T
            yield 270

    def forward_rest(index, wide_a):
        lanes = lanes_of(index)
        branch = dot_plain(turned[3], mixture[:, :, lanes].reshape(width, piece))
        yield 250
        total = jnp.zeros((8, piece), F32)
        for rows in chunks:
            sum_one = x_t[rows, lanes].astype(F32) + (branch[rows] + column(BIAS_OUT, rows))
            wide_a[rows, :] = sum_one
            total = total + part_sum(sum_one)
            yield 25
        mean, inverse = norm_chunks(index, 0, wide_a, total)
        yield 150
        for rows in chunks:
            normed = (wide_a[rows, :] - mean) * inverse
            norm_one[rows, lanes] = normed
            hidden = normed * column(GAIN_ONE, rows) + column(BIAS_ONE, rows)
            hidden_low[rows, lanes] = hidden.astype(BF16)
            yield 30

        branch_two = None
        for block in range(4):
            pre_block = dot_plain(turned[4 + block], hidden_low[:, lanes])
            yield 50
            lows = []
            for rows in chunks:
                pre = pre_block[rows] + column(BIAS_UP + block, rows)
                level = (lax.erf(pre * (1.0 / math.sqrt(2.0))) + 1.0) * 0.5
                bell = jnp.exp2(pre * pre * (-0.5 * math.log2(math.e)))
                lows.append((pre * level).astype(BF16))
                active[block, rows, lanes] = lows[-1]
                slope[block, rows, lanes] = (
                    level + pre * bell * (1.0 / math.sqrt(2.0 * math.pi))
                ).astype(BF16)
                yield 65
            part = dot_plain(turned[8 + block], jnp.concatenate(lows, axis=0))
            branch_two = part if branch_two is None else branch_two + part
            yield 100
        total = jnp.zeros((8, piece), F32)
        for rows in chunks:
            hidden = norm_one[rows, lanes] * column(GAIN_ONE, rows) + column(BIAS_ONE, rows)
            sum_two = hidden + (branch_two[rows] + column(BIAS_DOWN, rows))
            wide_a[rows, :] = sum_two
            total = total + part_sum(sum_two)
            yield 25
        mean, inverse = norm_chunks(index, 1, wide_a, total)
        yield 150
        for rows in chunks:
            norm_two[rows, lanes] = (wide_a[rows, :] - mean) * inverse
            yield 20

    def forward_end(index):
        @pl.when(segment == 0)
        def _():
            for rows in chunks:
                outgoing[index, rows, :] = output_rows(rows, lanes_of(index)).astype(BF16)
            forward_copy(index).start()

    def off_or_not(index, run):
        @pl.when(index == 1)
        def _():
            drain(run(index, True))

        @pl.when(index != 1)
        def _():
            drain(run(index, False))

    def forward(index):
        forward_start(index)
        drain(forward_first(index))
        off_or_not(index, attend)
        drain(forward_rest(index, wide_a))
        forward_end(index)

    def output_rows(rows, lanes):
        return norm_two[rows, lanes] * column(GAIN_TWO, rows) + column(BIAS_TWO, rows)

    def last_outputs(index, carry):
        free_ends(index)
        for start in range(0, width, LANES):
            rows = slice(start, start + LANES)
            ends_v[lax.rem(index, 2), :, rows] = output_rows(rows, lanes_of(index)).T
        ends_copy(index).start()
        return carry

    def attend_back(index, has_off):
        lanes = lanes_of(index)
        slot = (1 if index == 0 else 0) if isinstance(index, int) else jnp.where(index == 0, 1, 0)
        half = LANES // 2
        score_scale = 1.0 / math.sqrt(width // HEADS)

        def backs_of(pair):
            return against(values_rm, index, pair, by_queries(grad_mix[pair]), has_off)

        ahead = backs_of(0)
        for pair in range(pairs):
            backs = ahead
            if pair + 1 < pairs:
                ahead = backs_of(pair + 1)
            results = ([], [], [])
            for head in range(2):
                rows = slice(head * half, (head + 1) * half)
                low = share[index, pair, head]
                low_off = share_off[pair, head] if has_off else None
                lows = []
                for part in range(2):
                    place = slice(part * LANES, (part + 1) * LANES)
                    wides = [low[place, place]]
                    if part:
                        wides.append(low[:LANES, place])
                    if has_off:
                        wides += [low_off[:LANES, place], low_off[LANES:, place]]
                    wides = [tile.astype(F32) for tile in wides]
                    tiles = tiles_of(backs, head, part, has_off)
                    products = [wide * tile for wide, tile in zip(wides, tiles)]
                    inner = jnp.sum(functools.reduce(jnp.add, products), axis=0, keepdims=True)
                    lows.append(
                        [
                            (product - wide * inner).astype(BF16)
                            for product, wide in zip(products, wides)
                        ]
                    )
                grad_scores, grad_off = joined(lows, has_off)
                queries = qkv[0, pair, rows, lanes]
                grads = grad_mix[pair, rows]
                grad_query = dot_plain(qkv[1, pair, rows, lanes], grad_scores)
                grad_key = dot_turned(queries, grad_scores) + key_sums[slot, 0, pair, rows]
                grad_value = dot_turned(grads, low) + key_sums[slot, 1, pair, rows]
                if has_off:
                    grad_query = grad_query + dot_plain(qkv[1, pair, rows, :piece], grad_off)
                    key_sums[1, 0, pair, rows] = dot_turned(queries, grad_off)
                    key_sums[1, 1, pair, rows] = dot_turned(grads, low_off)
                for kept, grad in zip(results, (grad_query * score_scale, grad_key, grad_value)):
                    kept.append(grad.astype(BF16))
            for block in range(3):
                qkv[block, pair, :, lanes] = jnp.concatenate(results[block], axis=0)
            yield 440

    def backward_start(index):
        @pl.when(segment == 0)
        def _():
            backward_copy(index).wait_recv()

    def backward_norm(index):
        lanes = lanes_of(index)
        plain = jnp.zeros((8, piece), F32)
        inner = jnp.zeros((8, piece), F32)
        for rows in chunks:
            grad = incoming_grad[index, rows, :].astype(F32)
            product = grad * norm_two[rows, lanes]
            gather_sum(GAIN_TWO, rows, product)
            gather_sum(BIAS_TWO, rows, grad)
            gain = column(GAIN_TWO, rows)
            plain = plain + part_sum(grad * gain)
            inner = inner + part_sum(product * gain)
            yield 40
        plain = full_mean(plain)
        inner = full_mean(inner)
        inverse = inverses[index, 1]
        for rows in chunks:
            scaled = incoming_grad[index, rows, :].astype(F32) * column(GAIN_TWO, rows)
            grad_two = (scaled - plain - norm_two[rows, lanes] * inner) * inverse
            gather_sum(BIAS_DOWN, rows, grad_two)
            wide_a[rows, :] = grad_two
            down_grad[rows, lanes] = grad_two.astype(BF16)
            yield 40

    def backward_feed(index):
        lanes = lanes_of(index)
        for block in range(4):
            back = dot_plain(w_down[block], down_grad[:, lanes])
            for rows in chunks:
                grad_pre = back[rows] * slope[block, rows, lanes].astype(F32)
                gather_sum(BIAS_UP + block, rows, grad_pre)
                slope[block, rows, lanes] = grad_pre.astype(BF16)
            yield 250

        through = dot_plain(w_up[...], slope[:, :, lanes].reshape(4 * width, piece))
        plain = jnp.zeros((8, piece), F32)
        inner = jnp.zeros((8, piece), F32)
        for rows in chunks:
            grad_hidden = wide_a[rows, :] + through[rows]
            wide_a[rows, :] = grad_hidden
            product = grad_hidden * norm_one[rows, lanes]
            gather_sum(GAIN_ONE, rows, product)
            gather_sum(BIAS_ONE, rows, grad_hidden)
            gain = column(GAIN_ONE, rows)
            plain = plain + part_sum(grad_hidden * gain)
            inner = inner + part_sum(product * gain)
            yield 120 if rows.start == 0 else 45
        plain = full_mean(plain)
        inner = full_mean(inner)
        inverse = inverses[index, 0]
        for rows in chunks:
            scaled = wide_a[rows, :] * column(GAIN_ONE, rows)
            grad_one = (scaled - plain - norm_one[rows, lanes] * inner) * inverse
            gather_sum(BIAS_OUT, rows, grad_one)
            wide_b[rows, :] = grad_one
            branch_grad[rows, lanes] = grad_one.astype(BF16)
            yield 40
        grad_mix[...] = (
            dot_plain(w_out[...], branch_grad[:, lanes]).astype(BF16).reshape(pairs, LANES, piece)
        )
        yield 300

    def backward_attention(index):
        off_or_not(index, attend_back)
        through = dot_plain(w_qkv[...], qkv[:, :, :, lanes_of(index)].reshape(3 * width, piece))

        @pl.when(segment == 1)
        def _():
            for rows in chunks:
                outgoing[index, rows, :] = (wide_b[rows, :] + through[rows]).astype(BF16)
            backward_copy(index).start()

        @pl.when(segment == 0)
        def _():
            free_ends(index)
            for start in range(0, width, LANES):
                rows = slice(start, start + LANES)
                ends_v[lax.rem(index, 2), :, rows] = (wide_b[rows, :] + through[rows]).T
            ends_copy(index).start()

    def backward_both(index, forward_index):
        forward_copy(forward_index).wait_recv()

        def back():
            yield from backward_norm(index)
            yield from backward_feed(index)
            yield from attend_back(index, False)
            through = dot_plain(w_qkv[...], qkv[:, :, :, lanes_of(index)].reshape(3 * width, piece))
            for rows in chunks:
                outgoing[index, rows, :] = (wide_b[rows, :] + through[rows]).astype(BF16)
                yield 90

        def ahead():
            yield from forward_first(forward_index)
            yield from attend(forward_index, False)
            yield from forward_rest(forward_index, wide_c)

        side_by_side(back(), ahead())
        backward_copy(index).start()

    split = SPLIT if share_rows % (16 * SPLIT) == 0 else 1
    dp_first = DP_FIRST if split == SPLIT else ()
    orders = (ORDER_ONE, ORDER_TWO, ORDER_THREE) if split == SPLIT else plain_orders()
    jobs = 3 * split
    cut_rows = share_rows // split
    job_rows = width // split

    def base_of(job):
        return (8, 4, 0)[job // split]

    def job_span(job):
        return pl.ds(job % split * job_rows, job_rows)

    def fin_rows(job):
        return pl.ds(job % split * cut_rows, cut_rows)

    def parts_of(job):
        return range(2) if job in dp_first else range(1)

    def core_copies(job):
        return [
            pltpu.make_async_remote_copy(
                src_ref=turned.at[base_of(job) + 2 * (1 - core) + each, job_span(job)],
                dst_ref=core_in.at[job // split, each, job_span(job)],
                send_sem=core_send.at[job, each],
                recv_sem=core_recv.at[job, each],
                device_id={"rep": other_core},
                device_id_type=MESH,
            )
            for each in range(2)
        ]

    def side_copies(job):
        base = base_of(job)
        copies = []
        for each in parts_of(job):
            if job in dp_first:
                source = turned.at[base + 2 * core + each, dp_rows(job, dp_steps - 1)[1]]
                target = side_in.at[
                    job // split, pl.ds(job % split * job_rows + each * cut_rows, cut_rows)
                ]
            else:
                source = turned.at[base + 2 * core + (1 - side), job_span(job)]
                target = side_in.at[job // split, job_span(job)]
            copies.append(
                pltpu.make_async_remote_copy(
                    src_ref=source,
                    dst_ref=target,
                    send_sem=side_send.at[job, each],
                    recv_sem=side_recv.at[job, each],
                    device_id={"rep": other_side},
                    device_id_type=MESH,
                )
            )
        return copies

    def dp_slot(job):
        return sum(len(parts_of(before)) for before in range(job))

    def dp_rows(job, step):
        count = dp_count // 2
        start = 0
        for bit in range(step):
            start = start + lax.rem(lax.div(dp, 2**bit), 2) * count
            count = count // 2
        mine = lax.rem(lax.div(dp, 2**step), 2)
        first = job % split * job_rows
        sent = pl.multiple_of(first + (start + (1 - mine) * count) * cut_rows, cut_rows)
        kept = pl.multiple_of(first + (start + mine * count) * cut_rows, cut_rows)
        return pl.ds(sent, count * cut_rows), pl.ds(kept, count * cut_rows)

    def dp_landing(step):
        count = dp_count // 2 ** (step + 1)
        return pl.ds((dp_count - 2 * count) * cut_rows, count * cut_rows)

    def dp_copies(job, step):
        mine = lax.rem(lax.div(dp, 2**step), 2)
        copies = []
        for each in parts_of(job):
            position = base_of(job) + 2 * core + (each if job in dp_first else side)
            copies.append(
                pltpu.make_async_remote_copy(
                    src_ref=turned.at[position, dp_rows(job, step)[0]],
                    dst_ref=dp_in.at[dp_slot(job) + each, dp_landing(step)],
                    send_sem=dp_send.at[job, step, each],
                    recv_sem=dp_recv.at[job, step, each],
                    device_id={"dp": dp + (1 - 2 * mine) * 2**step},
                    device_id_type=MESH,
                )
            )
        return copies

    def join_copy(job):
        part = fin.at[job // split, 2 * core + side, fin_rows(job)]
        return pltpu.make_async_remote_copy(
            src_ref=part,
            dst_ref=part,
            send_sem=join_send.at[job],
            recv_sem=join_recv.at[job],
            device_id={"rep": other_side},
            device_id_type=MESH,
        )

    def last_copies(job):
        copies = []
        for each in range(2):
            part = fin.at[job // split, 2 * core + each, fin_rows(job)]
            copies.append(
                pltpu.make_async_remote_copy(
                    src_ref=part,
                    dst_ref=part,
                    send_sem=last_send.at[job, each],
                    recv_sem=last_recv.at[job, each],
                    device_id={"rep": other_core},
                    device_id_type=MESH,
                )
            )
        return copies

    def fin_copy(job):
        return pltpu.make_async_copy(
            fin.at[job // split, :, fin_rows(job)],
            fin_hbm.at[job // split, :, fin_rows(job)],
            fin_sem.at[job],
        )

    def arrived(*copies):
        for copy in copies:
            copy.wait_send()
        for copy in copies:
            copy.wait_recv()

    def start_all(copies):
        for copy in copies:
            copy.start()

    def turned_bits(value, count):
        place = 0
        while count > 1:
            place = place * 2 + value % 2
            value = value // 2
            count = count // 2
        return place

    pack = min(2, split)

    def left_rows(source, part):
        count = pack * cut_rows
        start = part * pack * cut_rows
        return jnp.concatenate(
            [source(index * share_rows + start, count) for index in range(dp_count)], axis=0
        )

    def keep_rows(block, part, result):
        for index in range(dp_count):
            for each in range(pack):
                target = (part * pack + each) * job_rows + turned_bits(index, dp_count) * cut_rows
                start = (index * pack + each) * cut_rows
                turned[block, target : target + cut_rows, :] = result[start : start + cut_rows]

    def down_sums(part):
        count = width // (4 * share_rows)

        def one(block, carry):
            pieces = []
            for each in range(4 * count):
                start = each * share_rows + part * pack * cut_rows
                pieces.append(active[block, start : start + pack * cut_rows, :])
            result = dot_turned(jnp.concatenate(pieces, axis=0), down_grad[...]).astype(BF16)
            high = lax.rem(block, 2) * 2 + lax.div(block, 2)
            for each in range(count):
                place = turned_bits(each, count) * 4 + high
                for position in range(4):
                    for job in range(pack):
                        target = (part * pack + job) * job_rows + place * cut_rows
                        start = ((each * 4 + position) * pack + job) * cut_rows
                        turned[
                            8 + position, pl.ds(pl.multiple_of(target, cut_rows), cut_rows), :
                        ] = result[start : start + cut_rows]
            return carry

        lax.fori_loop(0, 4, one, 0)

    def up_sums(part):
        def one(block, carry):
            left = left_rows(lambda start, count: hidden_low[start : start + count, :], part)
            keep_rows(4 + block, part, dot_turned(left, slope[block]).astype(BF16))
            return carry

        lax.fori_loop(0, 4, one, 0)

    def qkv_sums(part):
        def one(block, carry):
            left = left_rows(lambda start, count: x_t[start : start + count, :], part)
            grads = qkv[block].reshape(width, PIECES * piece)
            keep_rows(block, part, dot_turned(left, grads).astype(BF16))
            return carry

        lax.fori_loop(0, 3, one, 0)
        left = left_rows(
            lambda start, count: mixture[start // LANES, start % LANES : start % LANES + count, :], part
        )
        keep_rows(3, part, dot_turned(left, branch_grad[...]).astype(BF16))

    def sums_of(job):
        (down_sums, up_sums, qkv_sums)[job // split](job % split // pack)
        for each in range(pack):
            start_all(core_copies(job + each))

    def after_core(job):
        arrived(*core_copies(job))
        rows = job_span(job)
        for each in parts_of(job):
            place = 1 - side if each == 0 else side
            position = base_of(job) + 2 * core + place
            turned[position, rows, :] = (
                turned[position, rows, :].astype(F32)
                + core_in[job // split, place, rows, :].astype(F32)
            ).astype(BF16)
        if job in dp_first:
            start_all(dp_copies(job, 0))

    def start_side(job):
        start_all(side_copies(job))

    def after_side(job):
        arrived(*side_copies(job))
        rows = job_span(job)
        position = base_of(job) + 2 * core + side
        turned[position, rows, :] = (
            turned[position, rows, :].astype(F32)
            + core_in[job // split, side, rows, :].astype(F32)
            + side_in[job // split, rows, :].astype(F32)
        ).astype(BF16)
        start_all(dp_copies(job, 0))

    def dp_total(job, step, each):
        position = base_of(job) + 2 * core + (each if job in dp_first else side)
        kept = turned[position, dp_rows(job, step)[1], :].astype(F32)
        return position, kept + dp_in[dp_slot(job) + each, dp_landing(step), :].astype(F32)

    def after_dp(job):
        for step in range(dp_steps - 1):
            arrived(*dp_copies(job, step))
            for each in parts_of(job):
                position, total = dp_total(job, step, each)
                turned[position, dp_rows(job, step)[1], :] = total.astype(BF16)
            start_all(dp_copies(job, step + 1))

    def after_last_dp(job):
        step = dp_steps - 1
        arrived(*dp_copies(job, step))
        for each in parts_of(job):
            position, total = dp_total(job, step, each)
            if job in dp_first:
                turned[position, dp_rows(job, step)[1], :] = total.astype(BF16)
            else:
                fin[job // split, 2 * core + side, fin_rows(job), :] = total.astype(BF16)
        if job in dp_first:
            start_side(job)
        else:
            join_copy(job).start()

    def after_join(job):
        if job in dp_first:
            arrived(*side_copies(job))
            for each in range(2):
                rows = pl.ds(job % split * job_rows + each * cut_rows, cut_rows)
                own = turned[base_of(job) + 2 * core + each, dp_rows(job, dp_steps - 1)[1], :]
                total = own.astype(F32) + side_in[job // split, rows, :].astype(F32)
                fin[job // split, 2 * core + each, fin_rows(job), :] = total.astype(BF16)
        else:
            arrived(join_copy(job))
        start_all(last_copies(job))

    def after_last(job):
        arrived(*last_copies(job))
        fin_copy(job).start()

    def small_dp_copy(step):
        target = lax.rem(dp + step, dp_count)
        return pltpu.make_async_remote_copy(
            src_ref=small.at[target],
            dst_ref=small_dp.at[step - 1],
            send_sem=sdp_send.at[step - 1],
            recv_sem=sdp_recv.at[step - 1],
            device_id={"dp": target},
            device_id_type=MESH,
        )

    def small_rep_copy(step):
        return pltpu.make_async_remote_copy(
            src_ref=small_rep.at[rep],
            dst_ref=small_rep.at[rep],
            send_sem=srep_send.at[step - 1],
            recv_sem=srep_recv.at[step - 1],
            device_id={"rep": lax.rem(rep + step, 4)},
            device_id_type=MESH,
        )

    small_copy = pltpu.make_async_copy(small_out, small_hbm, load_sem.at[0])

    def small_step(stage):
        if stage == 0:
            rows_of = [jnp.sum(sums[index].T, axis=0, keepdims=True) for index in range(STATS)]
            small[...] = jnp.zeros(small.shape, F32)
            for share_index in range(dp_count):
                for index in range(BIAS_UP):
                    start = share_index * share_rows
                    small[share_index, index : index + 1, :share_rows] = rows_of[index][
                        :, start : start + share_rows
                    ]
                for part in range(4):
                    start = (share_index * 4 + part) * share_rows
                    block, start = start // width, start % width
                    small[share_index, BIAS_UP + part : BIAS_UP + part + 1, :share_rows] = rows_of[
                        BIAS_UP + block
                    ][:, start : start + share_rows]
            for step in range(1, dp_count):
                small_dp_copy(step).start()
        elif stage == 1:
            total = small[dp]
            for step in range(1, dp_count):
                arrived(small_dp_copy(step))
                total = total + small_dp[step - 1]
            small_rep[rep] = total
            for step in range(1, 4):
                small_rep_copy(step).start()
        else:
            for step in range(1, 4):
                arrived(small_rep_copy(step))
            small_out[...] = (small_rep[0] + small_rep[1]) + (small_rep[2] + small_rep[3])
            small_copy.start()

    def run(order):
        steps = (
            sums_of,
            after_core,
            start_side,
            after_side,
            after_dp,
            after_last_dp,
            after_join,
            after_last,
            small_step,
        )
        for stage, job in order:
            steps[stage](job)

    def one_step(step, carry):
        first_index = jnp.where(step < 4, step, jnp.where(step < 6, 5 - step, step - 4))
        last_index = jnp.where(step < 2, step, jnp.where(step == 2, 1, 3))
        index = jnp.minimum(jnp.where(segment == 0, first_index, last_index), PIECES - 1)
        is_last = jnp.where(step == 2 * PIECES, 1, 0)
        is_forward = jnp.where(step < jnp.where(segment == 0, 4, 2), 1, 0)
        last_backward = jnp.where(step == 2, 1, 0) + jnp.where(step == 5, 1, 0)
        is_backward = jnp.where(segment == 0, (1 - is_forward) * (1 - is_last), last_backward)
        is_split = jnp.where(step >= 2 * PIECES - 1, 1 - segment, 0)
        is_rest = is_backward * (1 - is_split) + is_last * is_split

        @pl.when(is_forward == 1)
        def _():
            forward(index)

        @pl.when(is_backward == 1)
        def _():
            backward_start(index)
            drain(backward_norm(index))

        @pl.when(segment * step == 3)
        def _():
            backward_both(0, 2)

        @pl.when(segment * step == 4)
        def _():
            backward_both(2, 3)

        @pl.when(is_last == 1)
        def _():
            run(orders[0])

        @pl.when(is_rest == 1)
        def _():
            drain(backward_feed(index))

        @pl.when(is_last == 1)
        def _():
            run(orders[1])

        @pl.when(is_rest == 1)
        def _():
            backward_attention(index)

        return carry

    @pl.when(segment == 1)
    def _():
        for index in range(PIECES):
            incoming_grad[index] = own_rows(index).astype(BF16)

    lax.fori_loop(0, 2 * PIECES + 1, one_step, 0)

    cut = orders[2].index((SMALL, 0))
    run(orders[2][:cut])

    @pl.when(segment == 1)
    def _():
        lax.fori_loop(0, PIECES, last_outputs, 0)

    run(orders[2][cut:])

    for index in range(PIECES):

        @pl.when(segment == 0)
        def _():
            forward_copy(index).wait_send()

        @pl.when(segment == 1)
        def _():
            backward_copy(index).wait_send()

    for index in range(2, PIECES):
        ends_copy(index).wait()
    for job in range(jobs):
        fin_copy(job).wait()
    small_copy.wait()


def finish_kernel(
    flag_ref,
    ends_in,
    fin,
    small,
    ends,
    grad_qkv,
    grad_out,
    grad_up,
    grad_down,
    grad_up_bias,
    grad_gains,
    grad_biases,
    ends_v,
    fin_v,
    wide_qkv,
    wide_out,
    wide_up,
    wide_down,
    small_v,
    up_bias_v,
    gains_v,
    biases_v,
    ends_sem,
    in_sem,
    out_sem,
):
    half = ends_in.shape[0] // 2
    share_rows, width = fin.shape[2:]
    start = pl.multiple_of(half * (1 - flag_ref[0, 0]), half)
    cut = half // 4
    ends_copies = []
    ends_loads = []
    for part in range(8):
        source = pl.ds(part * cut, cut)
        offset = start + part * cut if part < 4 else part * cut - half + (half - start)
        target = pl.ds(pl.multiple_of(offset, cut), cut)
        ends_loads.append(
            pltpu.make_async_copy(ends_in.at[source], ends_v.at[source], ends_sem.at[part])
        )
        ends_copies.append(
            pltpu.make_async_copy(ends_v.at[source], ends.at[0, target], ends_sem.at[8 + part])
        )
    loads = [
        pltpu.make_async_copy(fin.at[group], fin_v.at[group], in_sem.at[group])
        for group in range(3)
    ]
    stores = [
        pltpu.make_async_copy(wide, target.at[0], out_sem.at[index])
        for index, (wide, target) in enumerate(
            ((wide_down, grad_down), (wide_up, grad_up), (wide_qkv, grad_qkv), (wide_out, grad_out))
        )
    ]
    small_load = pltpu.make_async_copy(small, small_v, in_sem.at[3])
    small_stores = [
        pltpu.make_async_copy(narrow, target, out_sem.at[4 + index])
        for index, (narrow, target) in enumerate(
            ((up_bias_v, grad_up_bias), (gains_v, grad_gains), (biases_v, grad_biases))
        )
    ]
    small_load.start()
    for copy in loads + ends_loads:
        copy.start()
    for load, copy in zip(ends_loads, ends_copies):
        load.wait()
        copy.start()
    loads[0].wait()
    for position in range(4):
        rows = slice(position * share_rows, (position + 1) * share_rows)
        wide_down[rows, :] = fin_v[0, position].astype(F32)
    stores[0].start()
    loads[1].wait()
    for position in range(4):
        wide_up[:, position * width : (position + 1) * width] = fin_v[1, position].astype(F32)
    stores[1].start()
    loads[2].wait()
    for position in range(3):
        wide_qkv[:, position * width : (position + 1) * width] = fin_v[2, position].astype(F32)
    stores[2].start()
    wide_out[...] = fin_v[2, 3].astype(F32)
    stores[3].start()
    small_load.wait()
    for position in range(4):
        rows = slice(position * share_rows, (position + 1) * share_rows)
        up_bias_v[:, rows] = small_v[BIAS_UP + position : BIAS_UP + position + 1, :share_rows]
    gains_v[0] = small_v[:2, :share_rows]
    biases_v[0] = small_v[2:BIAS_UP, :share_rows]
    for copy in small_stores:
        copy.start()
    for copy in stores + ends_copies + small_stores:
        copy.wait()


def on_device(
    dp_count,
    block_input,
    cotangent,
    window_group,
    w_qkv,
    w_out,
    w_up,
    w_down,
    up_bias,
    norm_gains,
    biases,
):
    rows, width = block_input.shape
    piece = rows // PIECES
    pairs = width // LANES
    share_rows = width // dp_count
    small_width = max(share_rows, LANES)
    dp_steps = dp_count.bit_length() - 1
    split = SPLIT if share_rows % (16 * SPLIT) == 0 else 1
    jobs = 3 * split
    slots = jobs + (len(DP_FIRST) if split == SPLIT else 0)
    any_spec = pl.BlockSpec(memory_space=pl.ANY)
    vmem_spec = pl.BlockSpec(memory_space=pltpu.VMEM)
    smem_spec = pl.BlockSpec(memory_space=pltpu.SMEM)
    dma = pltpu.SemaphoreType.DMA
    vmem = pltpu.VMEM
    ends_in, fin, small = pl.pallas_call(
        functools.partial(layer_kernel, dp_count),
        out_shape=(
            jax.ShapeDtypeStruct((PIECES, piece, width), F32),
            jax.ShapeDtypeStruct((3, 4, share_rows, width), BF16),
            jax.ShapeDtypeStruct((16, small_width), F32),
        ),
        in_specs=[smem_spec] + [any_spec] * 6 + [vmem_spec] * 3,
        out_specs=(any_spec,) * 3,
        scratch_shapes=[
            vmem((width, 3 * width), BF16),
            vmem((width, width), BF16),
            vmem((width, 4 * width), BF16),
            vmem((4, width, width), BF16),
            vmem((12, width, width), BF16),
            vmem((PIECES, piece, width), BF16),
            vmem((width, rows), BF16),
            vmem((3, pairs, LANES, rows), BF16),
            vmem((PIECES, pairs, piece, LANES), BF16),
            vmem((PIECES, pairs, piece, LANES), BF16),
            vmem((PIECES, pairs, 2, piece, piece), BF16),
            vmem((pairs, 2, piece, piece), BF16),
            vmem((pairs, LANES, rows), BF16),
            vmem((width, rows), F32),
            vmem((width, rows), F32),
            vmem((PIECES, 2, 1, piece), F32),
            vmem((width, rows), BF16),
            vmem((4, width, rows), BF16),
            vmem((4, width, rows), BF16),
            vmem((width, rows), BF16),
            vmem((width, rows), BF16),
            vmem((pairs, LANES, piece), BF16),
            vmem((PIECES, width, piece), BF16),
            vmem((PIECES, width, piece), BF16),
            vmem((STATS, width, LANES), BF16),
            vmem((STATS, width, LANES), F32),
            vmem((2, 2, pairs, LANES, piece), F32),
            vmem((width, piece), F32),
            vmem((width, piece), F32),
            vmem((width, piece), F32),
            vmem((2, piece, width), F32),
            vmem((3, 2, width, width), BF16),
            vmem((3, width, width), BF16),
            vmem((slots, (width - share_rows) // split, width), BF16),
            vmem((3, 4, share_rows, width), BF16),
            vmem((dp_count, 16, small_width), F32),
            vmem((dp_count - 1, 16, small_width), F32),
            vmem((4, 16, small_width), F32),
            vmem((16, small_width), F32),
            dma((13,)),
            dma((PIECES,)),
            dma((PIECES,)),
            dma((PIECES,)),
            dma((jobs, 2)),
            dma((jobs, 2)),
            dma((jobs, 2)),
            dma((jobs, 2)),
            dma((jobs, dp_steps, 2)),
            dma((jobs, dp_steps, 2)),
            dma((jobs,)),
            dma((jobs,)),
            dma((jobs, 2)),
            dma((jobs, 2)),
            dma((dp_count - 1,)),
            dma((dp_count - 1,)),
            dma((3,)),
            dma((3,)),
            dma((jobs,)),
        ],
        compiler_params=pltpu.CompilerParams(
            collective_id=0, has_side_effects=True, vmem_limit_bytes=63 * 1024 * 1024
        ),
    )(
        window_group,
        block_input.reshape(PIECES, piece, width),
        cotangent.reshape(PIECES, piece, width),
        w_qkv,
        w_out,
        w_up,
        w_down,
        up_bias,
        norm_gains,
        biases,
    )
    return pl.pallas_call(
        finish_kernel,
        out_shape=(
            jax.ShapeDtypeStruct((1, rows, width), F32),
            jax.ShapeDtypeStruct((1, share_rows, 3 * width), F32),
            jax.ShapeDtypeStruct((1, share_rows, width), F32),
            jax.ShapeDtypeStruct((1, share_rows, 4 * width), F32),
            jax.ShapeDtypeStruct((1, 4 * share_rows, width), F32),
            jax.ShapeDtypeStruct((1, 4 * share_rows), F32),
            jax.ShapeDtypeStruct((1, 2, share_rows), F32),
            jax.ShapeDtypeStruct((1, 4, share_rows), F32),
        ),
        in_specs=[smem_spec] + [any_spec] * 3,
        out_specs=(any_spec,) * 8,
        scratch_shapes=[
            vmem((rows, width), F32),
            vmem((3, 4, share_rows, width), BF16),
            vmem((share_rows, 3 * width), F32),
            vmem((share_rows, width), F32),
            vmem((share_rows, 4 * width), F32),
            vmem((4 * share_rows, width), F32),
            vmem((16, small_width), F32),
            vmem((1, 4 * share_rows), F32),
            vmem((1, 2, share_rows), F32),
            vmem((1, 4, share_rows), F32),
            dma((16,)),
            dma((4,)),
            dma((7,)),
        ],
        compiler_params=pltpu.CompilerParams(vmem_limit_bytes=63 * 1024 * 1024),
    )(window_group, ends_in.reshape(rows, width), fin, small)


def solution(mesh):
    return jax.shard_map(
        functools.partial(on_device, mesh.shape["dp"]),
        mesh=mesh,
        in_specs=(
            P(("dp", "rep"), None),
            P(("dp", "rep"), None),
            P(("dp", "rep"), None),
            P("segment", None, None),
            P("segment", None, None),
            P("segment", None, None),
            P("segment", None, None),
            P("segment", None),
            P("segment", None, None),
            P("segment", None, None),
        ),
        out_specs=(
            P("segment", ("dp", "rep"), None),
            P("segment", "dp", None),
            P("segment", "dp", None),
            P("segment", "dp", None),
            P("segment", "dp", None),
            P("segment", "dp"),
            P("segment", None, "dp"),
            P("segment", None, "dp"),
        ),
        check_vma=False,
    )
```

```python
import functools
import math

import jax
import jax.numpy as jnp
from jax import lax
from jax.experimental import pallas as pl
from jax.experimental.pallas import tpu as pltpu
from jax.sharding import PartitionSpec as P

MESH = pl.DeviceIdType.MESH
F32 = jnp.float32
BF16 = jnp.bfloat16
HEADS = 8
LANES = 128
PIECES = 4
EPS = 1e-05
GAIN_ONE, GAIN_TWO, BIAS_OUT, BIAS_ONE, BIAS_DOWN, BIAS_TWO, BIAS_UP = range(7)
STATS = 10
CHUNK = 64
SPLIT = 4
DP_FIRST = (1, 3, 6, 10)
SUM, CORE, SIDE, SIDED, DP, DPED, JOIN, LAST, SMALL = range(9)
ORDER_ONE = (
    (SUM, 0), (SUM, 2),
)
ORDER_TWO = (
    (SUM, 4), (CORE, 1), (CORE, 0), (SIDE, 0), (SUM, 6), (CORE, 2), (SIDE, 2), (CORE, 3),
)
ORDER_THREE = (
    (CORE, 5), (SUM, 8), (SIDE, 5), (CORE, 6), (DP, 3), (CORE, 4), (SUM, 10), (CORE, 7), (SIDE, 4),
    (SIDED, 5), (SIDED, 2), (SIDE, 7), (DP, 1), (CORE, 8), (CORE, 11), (DPED, 3), (DP, 6), (SIDED, 0),
    (DP, 2), (DPED, 1), (SIDED, 4), (SIDE, 11), (JOIN, 3), (SIDED, 7), (CORE, 10), (DP, 0), (DP, 5),
    (CORE, 9), (SMALL, 0), (SIDE, 8), (DP, 4), (SIDE, 9), (SIDED, 11), (DP, 7), (JOIN, 1), (SIDED, 8),
    (SMALL, 1), (LAST, 1), (DPED, 0), (DP, 10), (DPED, 5), (DPED, 2), (LAST, 3), (SIDED, 9), (DPED, 6),
    (DP, 8), (JOIN, 0), (DPED, 4), (DPED, 10), (DP, 11), (JOIN, 4), (JOIN, 5), (DP, 9), (JOIN, 2), (LAST, 0),
    (DPED, 8), (JOIN, 6), (DPED, 7), (DPED, 11), (DPED, 9), (LAST, 4), (JOIN, 10), (JOIN, 7), (JOIN, 11),
    (JOIN, 8), (JOIN, 9), (SMALL, 2), (LAST, 5), (LAST, 8), (LAST, 2), (LAST, 9), (LAST, 10), (LAST, 11),
    (LAST, 7), (LAST, 6),
)


def plain_orders():
    one = ((SUM, 0),)
    two = ((SUM, 1), (CORE, 0), (SIDE, 0))
    three = ((SUM, 2), (CORE, 1), (SIDE, 1), (CORE, 2), (SIDE, 2), (SMALL, 0), (SMALL, 1), (SMALL, 2))
    for stage in (SIDED, DP, DPED, JOIN, LAST):
        three += tuple((stage, job) for job in range(3))
    return one, two, three


def dot_plain(left, right):
    return lax.dot_general(left, right, (((1,), (0,)), ((), ())), preferred_element_type=F32)


def drain(parts):
    for _ in parts:
        pass


def side_by_side(one, two):
    spent = [0, 300]
    live = [one, two]
    while live[0] or live[1]:
        which = 0 if live[0] and (not live[1] or spent[0] <= spent[1]) else 1
        cost = next(live[which], None)
        if cost is None:
            live[which] = None
        else:
            spent[which] += cost


def dot_turned(left, right):
    return lax.dot_general(left, right, (((1,), (1,)), ((), ())), preferred_element_type=F32)


def fold(values):
    total = values[:, :LANES]
    for start in range(LANES, values.shape[1], LANES):
        total = total + values[:, start : start + LANES]
    return total


def layer_kernel(
    dp_count,
    flag_ref,
    x_hbm,
    ct_hbm,
    w_qkv_hbm,
    w_out_hbm,
    w_up_hbm,
    w_down_hbm,
    up_bias_ref,
    gains_ref,
    biases_ref,
    ends_hbm,
    fin_hbm,
    small_hbm,
    w_qkv,
    w_out,
    w_up,
    w_down,
    turned,
    rows_in,
    x_t,
    qkv,
    keys_rm,
    values_rm,
    share,
    share_off,
    mixture,
    norm_one,
    norm_two,
    inverses,
    hidden_low,
    slope,
    active,
    down_grad,
    branch_grad,
    grad_mix,
    outgoing,
    incoming_grad,
    columns,
    sums,
    key_sums,
    wide_a,
    wide_b,
    wide_c,
    ends_v,
    core_in,
    side_in,
    dp_in,
    fin,
    small,
    small_dp,
    small_rep,
    small_out,
    load_sem,
    seg_send,
    seg_recv,
    ends_sem,
    core_send,
    core_recv,
    side_send,
    side_recv,
    dp_send,
    dp_recv,
    join_send,
    join_recv,
    last_send,
    last_recv,
    sdp_send,
    sdp_recv,
    srep_send,
    srep_recv,
    fin_sem,
):
    width = w_out.shape[0]
    piece = x_t.shape[1] // PIECES
    pairs = qkv.shape[1]
    share_rows = width // dp_count
    dp_steps = dp_count.bit_length() - 1
    segment = lax.axis_index("segment")
    dp = lax.axis_index("dp")
    rep = lax.axis_index("rep")
    core = lax.rem(rep, 2)
    side = lax.div(rep, 2)
    other_core = side * 2 + (1 - core)
    other_side = (1 - side) * 2 + core

    def load_copy(block):
        def span(first):
            return pl.ds(pl.multiple_of((block - first) * width, width), width)

        def copy_of(source, target):
            return pltpu.make_async_copy(source, target, load_sem.at[1 + block])

        return (
            lambda: copy_of(w_qkv_hbm.at[0, :, span(0)], w_qkv.at[:, span(0)]),
            lambda: copy_of(w_out_hbm.at[0], w_out),
            lambda: copy_of(w_up_hbm.at[0, :, span(4)], w_up.at[:, span(4)]),
            lambda: copy_of(w_down_hbm.at[0, span(8), :], w_down.at[block - 8]),
        )

    parts_of_load = ((0, 3), (3, 4), (4, 8), (8, 12))
    first_rows = pltpu.make_async_copy(x_hbm, rows_in, load_sem.at[0])
    last_rows = pltpu.make_async_copy(ct_hbm, rows_in, load_sem.at[0])

    @pl.when(segment == 0)
    def _():
        first_rows.start()

    @pl.when(segment == 1)
    def _():
        last_rows.start()

    for part, (first, after) in enumerate(parts_of_load):
        for block in range(first, after):
            load_copy(block)[part]().start()

    barrier = pltpu.get_barrier_semaphore()
    pl.semaphore_signal(
        barrier, inc=1, device_id={"segment": 1 - segment}, device_id_type=MESH
    )
    for step in range(1, 4):
        pl.semaphore_signal(
            barrier, inc=1, device_id={"rep": lax.rem(rep + step, 4)}, device_id_type=MESH
        )
    for step in range(1, dp_count):
        pl.semaphore_signal(
            barrier, inc=1, device_id={"dp": lax.rem(dp + step, dp_count)}, device_id_type=MESH
        )

    params = [gains_ref[0].astype(F32), biases_ref[0].astype(F32)]
    for block in range(4):
        params.append(up_bias_ref[:, block * width : (block + 1) * width].astype(F32))
    params.append(jnp.zeros((16 - STATS, width), F32))
    upright = jnp.concatenate(params, axis=0).T
    for index in range(STATS):
        columns[index] = jnp.broadcast_to(upright[:, index : index + 1], (width, LANES)).astype(BF16)
    for index in range(STATS):
        sums[index] = jnp.zeros((width, LANES), F32)
    key_sums[0] = jnp.zeros(key_sums.shape[1:], F32)

    chunks = [slice(start, start + CHUNK) for start in range(0, width, CHUNK)]

    def turn(part):
        def one(block, carry):
            load_copy(block)[part]().wait()
            if part == 3:
                turned[block] = w_down[block - 8].T
            elif part == 1:
                turned[block] = w_out[...].T
            else:
                first = parts_of_load[part][0]
                span = pl.ds(pl.multiple_of((block - first) * width, width), width)
                turned[block] = (w_qkv if part == 0 else w_up)[:, span].T
            return carry

        lax.fori_loop(*parts_of_load[part], one, 0)

    for part in range(4):
        turn(part)
    first_rows.wait()

    pl.semaphore_wait(barrier, 4 + dp_count - 1)

    flag = flag_ref[0, 0].astype(F32)

    def lanes_of(index):
        if isinstance(index, int):
            return pl.ds(index * piece, piece)
        return pl.ds(pl.multiple_of(index * piece, piece), piece)

    def forward_copy(index):
        return pltpu.make_async_remote_copy(
            src_ref=outgoing.at[index],
            dst_ref=x_t.at[:, lanes_of(index)],
            send_sem=seg_send.at[index],
            recv_sem=seg_recv.at[index],
            device_id={"segment": 1 - segment},
            device_id_type=MESH,
        )

    def backward_copy(index):
        return pltpu.make_async_remote_copy(
            src_ref=outgoing.at[index],
            dst_ref=incoming_grad.at[index],
            send_sem=seg_send.at[index],
            recv_sem=seg_recv.at[index],
            device_id={"segment": 1 - segment},
            device_id_type=MESH,
        )

    def ends_copy(index):
        return pltpu.make_async_copy(
            ends_v.at[lax.rem(index, 2)], ends_hbm.at[index], ends_sem.at[index]
        )

    def free_ends(index):
        if isinstance(index, int):
            ends_copy(index - 2).wait()
            return

        @pl.when(index >= 2)
        def _():
            ends_copy(index - 2).wait()

    def own_rows(index):
        half = lax.rem(index, 2)
        whole = jnp.where(index < 2, 1.0, 0.0).astype(F32)
        weight = whole * flag + (1.0 - whole) * (1.0 - flag)
        picked = rows_in[half].astype(F32) * weight + rows_in[2 + half].astype(F32) * (1.0 - weight)
        return picked.T

    def by_queries(values):
        half = LANES // 2
        blank = jnp.zeros((half, LANES), values.dtype)
        parts = []
        for part in range(2):
            span = slice(part * LANES, (part + 1) * LANES)
            first = jnp.concatenate([values[:half, span], blank], axis=0)
            second = jnp.concatenate([blank, values[half:, span]], axis=0)
            parts.append(jnp.concatenate([first, second], axis=1))
        return parts

    def against(rows_ref, index, pair, parts, has_off):
        own = rows_ref[index, pair]
        products = [dot_plain(own[:LANES], parts[0]), dot_plain(own, parts[1])]
        if has_off:
            before = rows_ref[0, pair]
            products += [dot_plain(before, parts[0]), dot_plain(before, parts[1])]
        return products

    def tiles_of(products, head, part, has_off):
        lanes = slice(head * LANES, (head + 1) * LANES)
        own = products[part]
        tiles = [own[part * LANES : (part + 1) * LANES, lanes]]
        if part:
            tiles.append(own[:LANES, lanes])
        if has_off:
            off = products[2 + part]
            tiles += [off[:LANES, lanes], off[LANES:, lanes]]
        return tiles

    def joined(lows, has_off):
        blank = jnp.zeros((LANES, LANES), BF16)
        first = jnp.concatenate([lows[0][0], blank], axis=0)
        second = jnp.concatenate([lows[1][1], lows[1][0]], axis=0)
        whole = jnp.concatenate([first, second], axis=1)
        if not has_off:
            return whole, None
        first = jnp.concatenate(lows[0][-2:], axis=0)
        second = jnp.concatenate(lows[1][-2:], axis=0)
        return whole, jnp.concatenate([first, second], axis=1)

    def attend(index, has_off):
        lanes = lanes_of(index)
        half = LANES // 2
        key_at = lax.broadcasted_iota(jnp.int32, (LANES, LANES), 0)
        query_at = lax.broadcasted_iota(jnp.int32, (LANES, LANES), 1)
        allowed = key_at <= query_at

        def scores_of(pair):
            return against(
                keys_rm, index, pair, by_queries(qkv[0, pair, :, lanes]), has_off
            )

        ahead = scores_of(0)
        for pair in range(pairs):
            scores = ahead
            if pair + 1 < pairs:
                ahead = scores_of(pair + 1)
            mixed = []
            for head in range(2):
                rows = slice(head * half, (head + 1) * half)
                lows = []
                for part in range(2):
                    tiles = tiles_of(scores, head, part, has_off)
                    tiles[0] = jnp.where(allowed, tiles[0], -1e30)
                    top = jnp.max(functools.reduce(jnp.maximum, tiles), axis=0, keepdims=True)
                    raised = [jnp.exp(tile - top) for tile in tiles]
                    total = functools.reduce(jnp.add, raised)
                    scale = 1.0 / jnp.sum(total, axis=0, keepdims=True)
                    lows.append([(tile * scale).astype(BF16) for tile in raised])
                low, low_off = joined(lows, has_off)
                share[index, pair, head] = low
                mix = dot_plain(qkv[2, pair, rows, lanes], low)
                if has_off:
                    share_off[pair, head] = low_off
                    mix = mix + dot_plain(qkv[2, pair, rows, :piece], low_off)
                mixed.append(mix.astype(BF16))
            mixture[pair, :, lanes] = jnp.concatenate(mixed, axis=0)
            yield 280

    def part_sum(values):
        return jnp.sum(values.reshape(values.shape[0] // 8, 8, values.shape[1]), axis=0)

    def full_mean(parts):
        return jnp.sum(parts, axis=0, keepdims=True) * (1.0 / width)

    def column(index, rows):
        part = columns[index, rows, :].astype(F32)
        return jnp.concatenate([part] * (piece // LANES), axis=1)

    def gather_sum(index, rows, values):
        sums[index, rows, :] = sums[index, rows, :] + fold(values)

    def norm_chunks(index, which, wide_a, total):
        mean = full_mean(total)
        spread = jnp.zeros((8, piece), F32)
        for rows in chunks:
            centred = wide_a[rows, :] - mean
            spread = spread + part_sum(centred * centred)
        inverse = lax.rsqrt(full_mean(spread) + EPS)
        inverses[index, which] = inverse
        return mean, inverse

    def forward_first(index):
        lanes = lanes_of(index)
        inputs = x_t[:, lanes]
        score_scale = 1.0 / math.sqrt(width // HEADS)
        for block in range(3):
            result = dot_plain(turned[block], inputs)
            for pair in range(pairs):
                low = result[pair * LANES : (pair + 1) * LANES]
                low = (low * score_scale if block == 0 else low).astype(BF16)
                qkv[block, pair, :, lanes] = low
                if block == 1:
                    keys_rm[index, pair] = low.T
                if block == 2:
                    values_rm[index, pair] = low.T
            yield 270

    def forward_rest(index, wide_a):
        lanes = lanes_of(index)
        branch = dot_plain(turned[3], mixture[:, :, lanes].reshape(width, piece))
        yield 250
        total = jnp.zeros((8, piece), F32)
        for rows in chunks:
            sum_one = x_t[rows, lanes].astype(F32) + (branch[rows] + column(BIAS_OUT, rows))
            wide_a[rows, :] = sum_one
            total = total + part_sum(sum_one)
            yield 25
        mean, inverse = norm_chunks(index, 0, wide_a, total)
        yield 150
        for rows in chunks:
            normed = (wide_a[rows, :] - mean) * inverse
            norm_one[rows, lanes] = normed
            hidden = normed * column(GAIN_ONE, rows) + column(BIAS_ONE, rows)
            hidden_low[rows, lanes] = hidden.astype(BF16)
            yield 30

        branch_two = None
        for block in range(4):
            pre_block = dot_plain(turned[4 + block], hidden_low[:, lanes])
            yield 50
            lows = []
            for rows in chunks:
                pre = pre_block[rows] + column(BIAS_UP + block, rows)
                level = (lax.erf(pre * (1.0 / math.sqrt(2.0))) + 1.0) * 0.5
                bell = jnp.exp2(pre * pre * (-0.5 * math.log2(math.e)))
                lows.append((pre * level).astype(BF16))
                active[block, rows, lanes] = lows[-1]
                slope[block, rows, lanes] = (
                    level + pre * bell * (1.0 / math.sqrt(2.0 * math.pi))
                ).astype(BF16)
                yield 65
            part = dot_plain(turned[8 + block], jnp.concatenate(lows, axis=0))
            branch_two = part if branch_two is None else branch_two + part
            yield 100
        total = jnp.zeros((8, piece), F32)
        for rows in chunks:
            hidden = norm_one[rows, lanes] * column(GAIN_ONE, rows) + column(BIAS_ONE, rows)
            sum_two = hidden + (branch_two[rows] + column(BIAS_DOWN, rows))
            wide_a[rows, :] = sum_two
            total = total + part_sum(sum_two)
            yield 25
        mean, inverse = norm_chunks(index, 1, wide_a, total)
        yield 150
        for rows in chunks:
            norm_two[rows, lanes] = (wide_a[rows, :] - mean) * inverse
            yield 20

    def off_or_not(index, run):
        @pl.when(index == 1)
        def _():
            drain(run(index, True))

        @pl.when(index != 1)
        def _():
            drain(run(index, False))

    def forward(index):
        x_t[:, lanes_of(index)] = own_rows(index).astype(BF16)
        drain(forward_first(index))
        off_or_not(index, attend)
        drain(forward_rest(index, wide_a))
        for rows in chunks:
            outgoing[index, rows, :] = output_rows(rows, lanes_of(index)).astype(BF16)
        forward_copy(index).start()

    def output_rows(rows, lanes):
        return norm_two[rows, lanes] * column(GAIN_TWO, rows) + column(BIAS_TWO, rows)

    def last_outputs(index, carry):
        free_ends(index)
        for start in range(0, width, LANES):
            rows = slice(start, start + LANES)
            ends_v[lax.rem(index, 2), :, rows] = output_rows(rows, lanes_of(index)).T
        ends_copy(index).start()
        return carry

    def attend_back(index, has_off):
        lanes = lanes_of(index)
        slot = (1 if index == 0 else 0) if isinstance(index, int) else jnp.where(index == 0, 1, 0)
        half = LANES // 2
        score_scale = 1.0 / math.sqrt(width // HEADS)

        def backs_of(pair):
            return against(values_rm, index, pair, by_queries(grad_mix[pair]), has_off)

        ahead = backs_of(0)
        for pair in range(pairs):
            backs = ahead
            if pair + 1 < pairs:
                ahead = backs_of(pair + 1)
            results = ([], [], [])
            for head in range(2):
                rows = slice(head * half, (head + 1) * half)
                low = share[index, pair, head]
                low_off = share_off[pair, head] if has_off else None
                lows = []
                for part in range(2):
                    place = slice(part * LANES, (part + 1) * LANES)
                    wides = [low[place, place]]
                    if part:
                        wides.append(low[:LANES, place])
                    if has_off:
                        wides += [low_off[:LANES, place], low_off[LANES:, place]]
                    wides = [tile.astype(F32) for tile in wides]
                    tiles = tiles_of(backs, head, part, has_off)
                    products = [wide * tile for wide, tile in zip(wides, tiles)]
                    inner = jnp.sum(functools.reduce(jnp.add, products), axis=0, keepdims=True)
                    lows.append(
                        [
                            (product - wide * inner).astype(BF16)
                            for product, wide in zip(products, wides)
                        ]
                    )
                grad_scores, grad_off = joined(lows, has_off)
                queries = qkv[0, pair, rows, lanes]
                grads = grad_mix[pair, rows]
                grad_query = dot_plain(qkv[1, pair, rows, lanes], grad_scores)
                grad_key = dot_turned(queries, grad_scores) + key_sums[slot, 0, pair, rows]
                grad_value = dot_turned(grads, low) + key_sums[slot, 1, pair, rows]
                if has_off:
                    grad_query = grad_query + dot_plain(qkv[1, pair, rows, :piece], grad_off)
                    key_sums[1, 0, pair, rows] = dot_turned(queries, grad_off)
                    key_sums[1, 1, pair, rows] = dot_turned(grads, low_off)
                for kept, grad in zip(results, (grad_query * score_scale, grad_key, grad_value)):
                    kept.append(grad.astype(BF16))
            for block in range(3):
                qkv[block, pair, :, lanes] = jnp.concatenate(results[block], axis=0)
            yield 440

    def backward_start(index):
        backward_copy(index).wait_recv()

    def backward_norm(index):
        lanes = lanes_of(index)
        plain = jnp.zeros((8, piece), F32)
        inner = jnp.zeros((8, piece), F32)
        for rows in chunks:
            grad = incoming_grad[index, rows, :].astype(F32)
            product = grad * norm_two[rows, lanes]
            gather_sum(GAIN_TWO, rows, product)
            gather_sum(BIAS_TWO, rows, grad)
            gain = column(GAIN_TWO, rows)
            plain = plain + part_sum(grad * gain)
            inner = inner + part_sum(product * gain)
            yield 40
        plain = full_mean(plain)
        inner = full_mean(inner)
        inverse = inverses[index, 1]
        for rows in chunks:
            scaled = incoming_grad[index, rows, :].astype(F32) * column(GAIN_TWO, rows)
            grad_two = (scaled - plain - norm_two[rows, lanes] * inner) * inverse
            gather_sum(BIAS_DOWN, rows, grad_two)
            wide_a[rows, :] = grad_two
            down_grad[rows, lanes] = grad_two.astype(BF16)
            yield 40

    def backward_feed(index):
        lanes = lanes_of(index)
        for block in range(4):
            back = dot_plain(w_down[block], down_grad[:, lanes])
            for rows in chunks:
                grad_pre = back[rows] * slope[block, rows, lanes].astype(F32)
                gather_sum(BIAS_UP + block, rows, grad_pre)
                slope[block, rows, lanes] = grad_pre.astype(BF16)
            yield 250

        through = dot_plain(w_up[...], slope[:, :, lanes].reshape(4 * width, piece))
        plain = jnp.zeros((8, piece), F32)
        inner = jnp.zeros((8, piece), F32)
        for rows in chunks:
            grad_hidden = wide_a[rows, :] + through[rows]
            wide_a[rows, :] = grad_hidden
            product = grad_hidden * norm_one[rows, lanes]
            gather_sum(GAIN_ONE, rows, product)
            gather_sum(BIAS_ONE, rows, grad_hidden)
            gain = column(GAIN_ONE, rows)
            plain = plain + part_sum(grad_hidden * gain)
            inner = inner + part_sum(product * gain)
            yield 120 if rows.start == 0 else 45
        plain = full_mean(plain)
        inner = full_mean(inner)
        inverse = inverses[index, 0]
        for rows in chunks:
            scaled = wide_a[rows, :] * column(GAIN_ONE, rows)
            grad_one = (scaled - plain - norm_one[rows, lanes] * inner) * inverse
            gather_sum(BIAS_OUT, rows, grad_one)
            wide_b[rows, :] = grad_one
            branch_grad[rows, lanes] = grad_one.astype(BF16)
            yield 40
        grad_mix[...] = (
            dot_plain(w_out[...], branch_grad[:, lanes]).astype(BF16).reshape(pairs, LANES, piece)
        )
        yield 300

    def finish_rows(index):
        through = dot_plain(w_qkv[...], qkv[:, :, :, lanes_of(index)].reshape(3 * width, piece))
        free_ends(index)
        for start in range(0, width, LANES):
            rows = slice(start, start + LANES)
            ends_v[lax.rem(index, 2), :, rows] = (wide_b[rows, :] + through[rows]).T
        ends_copy(index).start()

    def backward_attention(index):
        off_or_not(index, attend_back)
        finish_rows(index)

    def backward_end(index):
        through = dot_plain(w_qkv[...], qkv[:, :, :, lanes_of(index)].reshape(3 * width, piece))
        for rows in chunks:
            outgoing[index, rows, :] = (wide_b[rows, :] + through[rows]).astype(BF16)
            yield 90

    def backward_both(index, forward_index):
        forward_copy(forward_index).wait_recv()

        def back():
            yield from backward_norm(index)
            yield from backward_feed(index)
            yield from attend_back(index, False)
            yield from backward_end(index)

        def ahead():
            yield from forward_first(forward_index)
            yield from attend(forward_index, False)
            yield from forward_rest(forward_index, wide_c)

        side_by_side(back(), ahead())
        backward_copy(index).start()

    split = SPLIT if share_rows % (16 * SPLIT) == 0 else 1
    dp_first = DP_FIRST if split == SPLIT else ()
    orders = (ORDER_ONE, ORDER_TWO, ORDER_THREE) if split == SPLIT else plain_orders()
    jobs = 3 * split
    cut_rows = share_rows // split
    job_rows = width // split

    def base_of(job):
        return (8, 4, 0)[job // split]

    def job_span(job):
        return pl.ds(job % split * job_rows, job_rows)

    def fin_rows(job):
        return pl.ds(job % split * cut_rows, cut_rows)

    def parts_of(job):
        return range(2) if job in dp_first else range(1)

    def core_copies(job):
        return [
            pltpu.make_async_remote_copy(
                src_ref=turned.at[base_of(job) + 2 * (1 - core) + each, job_span(job)],
                dst_ref=core_in.at[job // split, each, job_span(job)],
                send_sem=core_send.at[job, each],
                recv_sem=core_recv.at[job, each],
                device_id={"rep": other_core},
                device_id_type=MESH,
            )
            for each in range(2)
        ]

    def side_copies(job):
        base = base_of(job)
        copies = []
        for each in parts_of(job):
            if job in dp_first:
                source = turned.at[base + 2 * core + each, dp_rows(job, dp_steps - 1)[1]]
                target = side_in.at[
                    job // split, pl.ds(job % split * job_rows + each * cut_rows, cut_rows)
                ]
            else:
                source = turned.at[base + 2 * core + (1 - side), job_span(job)]
                target = side_in.at[job // split, job_span(job)]
            copies.append(
                pltpu.make_async_remote_copy(
                    src_ref=source,
                    dst_ref=target,
                    send_sem=side_send.at[job, each],
                    recv_sem=side_recv.at[job, each],
                    device_id={"rep": other_side},
                    device_id_type=MESH,
                )
            )
        return copies

    def dp_slot(job):
        return sum(len(parts_of(before)) for before in range(job))

    def dp_rows(job, step):
        count = dp_count // 2
        start = 0
        for bit in range(step):
            start = start + lax.rem(lax.div(dp, 2**bit), 2) * count
            count = count // 2
        mine = lax.rem(lax.div(dp, 2**step), 2)
        first = job % split * job_rows
        sent = pl.multiple_of(first + (start + (1 - mine) * count) * cut_rows, cut_rows)
        kept = pl.multiple_of(first + (start + mine * count) * cut_rows, cut_rows)
        return pl.ds(sent, count * cut_rows), pl.ds(kept, count * cut_rows)

    def dp_landing(step):
        count = dp_count // 2 ** (step + 1)
        return pl.ds((dp_count - 2 * count) * cut_rows, count * cut_rows)

    def dp_copies(job, step):
        mine = lax.rem(lax.div(dp, 2**step), 2)
        copies = []
        for each in parts_of(job):
            position = base_of(job) + 2 * core + (each if job in dp_first else side)
            copies.append(
                pltpu.make_async_remote_copy(
                    src_ref=turned.at[position, dp_rows(job, step)[0]],
                    dst_ref=dp_in.at[dp_slot(job) + each, dp_landing(step)],
                    send_sem=dp_send.at[job, step, each],
                    recv_sem=dp_recv.at[job, step, each],
                    device_id={"dp": dp + (1 - 2 * mine) * 2**step},
                    device_id_type=MESH,
                )
            )
        return copies

    def join_copy(job):
        part = fin.at[job // split, 2 * core + side, fin_rows(job)]
        return pltpu.make_async_remote_copy(
            src_ref=part,
            dst_ref=part,
            send_sem=join_send.at[job],
            recv_sem=join_recv.at[job],
            device_id={"rep": other_side},
            device_id_type=MESH,
        )

    def last_copies(job):
        copies = []
        for each in range(2):
            part = fin.at[job // split, 2 * core + each, fin_rows(job)]
            copies.append(
                pltpu.make_async_remote_copy(
                    src_ref=part,
                    dst_ref=part,
                    send_sem=last_send.at[job, each],
                    recv_sem=last_recv.at[job, each],
                    device_id={"rep": other_core},
                    device_id_type=MESH,
                )
            )
        return copies

    def fin_copy(job):
        return pltpu.make_async_copy(
            fin.at[job // split, :, fin_rows(job)],
            fin_hbm.at[job // split, :, fin_rows(job)],
            fin_sem.at[job],
        )

    def arrived(*copies):
        for copy in copies:
            copy.wait_send()
        for copy in copies:
            copy.wait_recv()

    def start_all(copies):
        for copy in copies:
            copy.start()

    def turned_bits(value, count):
        place = 0
        while count > 1:
            place = place * 2 + value % 2
            value = value // 2
            count = count // 2
        return place

    pack = min(2, split)

    def left_rows(source, part):
        count = pack * cut_rows
        start = part * pack * cut_rows
        return jnp.concatenate(
            [source(index * share_rows + start, count) for index in range(dp_count)], axis=0
        )

    def keep_rows(block, part, result):
        for index in range(dp_count):
            for each in range(pack):
                target = (part * pack + each) * job_rows + turned_bits(index, dp_count) * cut_rows
                start = (index * pack + each) * cut_rows
                turned[block, target : target + cut_rows, :] = result[start : start + cut_rows]

    def down_sums(part):
        count = width // (4 * share_rows)

        def one(block, carry):
            pieces = []
            for each in range(4 * count):
                start = each * share_rows + part * pack * cut_rows
                pieces.append(active[block, start : start + pack * cut_rows, :])
            result = dot_turned(jnp.concatenate(pieces, axis=0), down_grad[...]).astype(BF16)
            high = lax.rem(block, 2) * 2 + lax.div(block, 2)
            for each in range(count):
                place = turned_bits(each, count) * 4 + high
                for position in range(4):
                    for job in range(pack):
                        target = (part * pack + job) * job_rows + place * cut_rows
                        start = ((each * 4 + position) * pack + job) * cut_rows
                        turned[
                            8 + position, pl.ds(pl.multiple_of(target, cut_rows), cut_rows), :
                        ] = result[start : start + cut_rows]
            return carry

        lax.fori_loop(0, 4, one, 0)

    def up_sums(part):
        def one(block, carry):
            left = left_rows(lambda start, count: hidden_low[start : start + count, :], part)
            keep_rows(4 + block, part, dot_turned(left, slope[block]).astype(BF16))
            return carry

        lax.fori_loop(0, 4, one, 0)

    def qkv_sums(part):
        def one(block, carry):
            left = left_rows(lambda start, count: x_t[start : start + count, :], part)
            grads = qkv[block].reshape(width, PIECES * piece)
            keep_rows(block, part, dot_turned(left, grads).astype(BF16))
            return carry

        lax.fori_loop(0, 3, one, 0)
        left = left_rows(
            lambda start, count: mixture[start // LANES, start % LANES : start % LANES + count, :], part
        )
        keep_rows(3, part, dot_turned(left, branch_grad[...]).astype(BF16))

    def sums_of(job):
        (down_sums, up_sums, qkv_sums)[job // split](job % split // pack)
        for each in range(pack):
            start_all(core_copies(job + each))

    def after_core(job):
        arrived(*core_copies(job))
        rows = job_span(job)
        for each in parts_of(job):
            place = 1 - side if each == 0 else side
            position = base_of(job) + 2 * core + place
            turned[position, rows, :] = (
                turned[position, rows, :].astype(F32)
                + core_in[job // split, place, rows, :].astype(F32)
            ).astype(BF16)
        if job in dp_first:
            start_all(dp_copies(job, 0))

    def start_side(job):
        start_all(side_copies(job))

    def after_side(job):
        arrived(*side_copies(job))
        rows = job_span(job)
        position = base_of(job) + 2 * core + side
        turned[position, rows, :] = (
            turned[position, rows, :].astype(F32)
            + core_in[job // split, side, rows, :].astype(F32)
            + side_in[job // split, rows, :].astype(F32)
        ).astype(BF16)
        start_all(dp_copies(job, 0))

    def dp_total(job, step, each):
        position = base_of(job) + 2 * core + (each if job in dp_first else side)
        kept = turned[position, dp_rows(job, step)[1], :].astype(F32)
        return position, kept + dp_in[dp_slot(job) + each, dp_landing(step), :].astype(F32)

    def after_dp(job):
        for step in range(dp_steps - 1):
            arrived(*dp_copies(job, step))
            for each in parts_of(job):
                position, total = dp_total(job, step, each)
                turned[position, dp_rows(job, step)[1], :] = total.astype(BF16)
            start_all(dp_copies(job, step + 1))

    def after_last_dp(job):
        step = dp_steps - 1
        arrived(*dp_copies(job, step))
        for each in parts_of(job):
            position, total = dp_total(job, step, each)
            if job in dp_first:
                turned[position, dp_rows(job, step)[1], :] = total.astype(BF16)
            else:
                fin[job // split, 2 * core + side, fin_rows(job), :] = total.astype(BF16)
        if job in dp_first:
            start_side(job)
        else:
            join_copy(job).start()

    def after_join(job):
        if job in dp_first:
            arrived(*side_copies(job))
            for each in range(2):
                rows = pl.ds(job % split * job_rows + each * cut_rows, cut_rows)
                own = turned[base_of(job) + 2 * core + each, dp_rows(job, dp_steps - 1)[1], :]
                total = own.astype(F32) + side_in[job // split, rows, :].astype(F32)
                fin[job // split, 2 * core + each, fin_rows(job), :] = total.astype(BF16)
        else:
            arrived(join_copy(job))
        start_all(last_copies(job))

    def after_last(job):
        arrived(*last_copies(job))
        fin_copy(job).start()

    def small_dp_copy(step):
        target = lax.rem(dp + step, dp_count)
        return pltpu.make_async_remote_copy(
            src_ref=small.at[target],
            dst_ref=small_dp.at[step - 1],
            send_sem=sdp_send.at[step - 1],
            recv_sem=sdp_recv.at[step - 1],
            device_id={"dp": target},
            device_id_type=MESH,
        )

    def small_rep_copy(step):
        return pltpu.make_async_remote_copy(
            src_ref=small_rep.at[rep],
            dst_ref=small_rep.at[rep],
            send_sem=srep_send.at[step - 1],
            recv_sem=srep_recv.at[step - 1],
            device_id={"rep": lax.rem(rep + step, 4)},
            device_id_type=MESH,
        )

    small_copy = pltpu.make_async_copy(small_out, small_hbm, load_sem.at[0])

    def small_step(stage):
        if stage == 0:
            rows_of = [jnp.sum(sums[index].T, axis=0, keepdims=True) for index in range(STATS)]
            small[...] = jnp.zeros(small.shape, F32)
            for share_index in range(dp_count):
                for index in range(BIAS_UP):
                    start = share_index * share_rows
                    small[share_index, index : index + 1, :share_rows] = rows_of[index][
                        :, start : start + share_rows
                    ]
                for part in range(4):
                    start = (share_index * 4 + part) * share_rows
                    block, start = start // width, start % width
                    small[share_index, BIAS_UP + part : BIAS_UP + part + 1, :share_rows] = rows_of[
                        BIAS_UP + block
                    ][:, start : start + share_rows]
            for step in range(1, dp_count):
                small_dp_copy(step).start()
        elif stage == 1:
            total = small[dp]
            for step in range(1, dp_count):
                arrived(small_dp_copy(step))
                total = total + small_dp[step - 1]
            small_rep[rep] = total
            for step in range(1, 4):
                small_rep_copy(step).start()
        else:
            for step in range(1, 4):
                arrived(small_rep_copy(step))
            small_out[...] = (small_rep[0] + small_rep[1]) + (small_rep[2] + small_rep[3])
            small_copy.start()

    def run(order):
        steps = (
            sums_of,
            after_core,
            start_side,
            after_side,
            after_dp,
            after_last_dp,
            after_join,
            after_last,
            small_step,
        )
        for stage, job in order:
            steps[stage](job)

    def first_step(step, carry):
        index = jnp.where(step < 4, step, jnp.where(step < 6, 5 - step, step - 4))

        @pl.when(step < 4)
        def _():
            forward(index)

        @pl.when(step >= 4)
        def _():
            backward_start(index)
            drain(backward_norm(index))
            drain(backward_feed(index))
            backward_attention(index)

        return carry

    def forward_alone(index):
        forward_copy(index).wait_recv()
        drain(forward_first(index))
        drain(attend(index, index == 1))
        drain(forward_rest(index, wide_a))

    def backward_alone(index):
        drain(backward_norm(index))
        drain(backward_feed(index))
        drain(attend_back(index, index == 1))
        drain(backward_end(index))
        backward_copy(index).start()

    @pl.when(segment == 1)
    def _():
        for index in range(PIECES):
            incoming_grad[index] = own_rows(index).astype(BF16)
        forward_alone(0)
        forward_alone(1)
        backward_alone(1)
        backward_both(0, 2)
        backward_both(2, 3)
        backward_alone(3)

    @pl.when(segment == 0)
    def _():
        lax.fori_loop(0, 2 * PIECES - 1, first_step, 0)
        backward_start(PIECES - 1)
        drain(backward_norm(PIECES - 1))

    run(orders[0])

    @pl.when(segment == 0)
    def _():
        drain(backward_feed(PIECES - 1))

    run(orders[1])

    @pl.when(segment == 0)
    def _():
        drain(attend_back(PIECES - 1, False))
        finish_rows(PIECES - 1)

    cut = orders[2].index((SMALL, 0))
    run(orders[2][:cut])

    @pl.when(segment == 1)
    def _():
        lax.fori_loop(0, PIECES, last_outputs, 0)

    run(orders[2][cut:])

    for index in range(PIECES):

        @pl.when(segment == 0)
        def _():
            forward_copy(index).wait_send()

        @pl.when(segment == 1)
        def _():
            backward_copy(index).wait_send()

    for index in range(2, PIECES):
        ends_copy(index).wait()
    for job in range(jobs):
        fin_copy(job).wait()
    small_copy.wait()


def finish_kernel(
    flag_ref,
    ends_in,
    fin,
    small,
    ends,
    grad_qkv,
    grad_out,
    grad_up,
    grad_down,
    grad_up_bias,
    grad_gains,
    grad_biases,
    ends_v,
    fin_v,
    wide_qkv,
    wide_out,
    wide_up,
    wide_down,
    small_v,
    up_bias_v,
    gains_v,
    biases_v,
    ends_sem,
    in_sem,
    out_sem,
):
    half = ends_in.shape[0] // 2
    share_rows, width = fin.shape[2:]
    start = pl.multiple_of(half * (1 - flag_ref[0, 0]), half)
    cut = half // 4
    ends_copies = []
    ends_loads = []
    for part in range(8):
        source = pl.ds(part * cut, cut)
        offset = start + part * cut if part < 4 else part * cut - half + (half - start)
        target = pl.ds(pl.multiple_of(offset, cut), cut)
        ends_loads.append(
            pltpu.make_async_copy(ends_in.at[source], ends_v.at[source], ends_sem.at[part])
        )
        ends_copies.append(
            pltpu.make_async_copy(ends_v.at[source], ends.at[0, target], ends_sem.at[8 + part])
        )
    loads = [
        pltpu.make_async_copy(fin.at[group], fin_v.at[group], in_sem.at[group])
        for group in range(3)
    ]
    stores = [
        pltpu.make_async_copy(wide, target.at[0], out_sem.at[index])
        for index, (wide, target) in enumerate(
            ((wide_down, grad_down), (wide_up, grad_up), (wide_qkv, grad_qkv), (wide_out, grad_out))
        )
    ]
    small_load = pltpu.make_async_copy(small, small_v, in_sem.at[3])
    small_stores = [
        pltpu.make_async_copy(narrow, target, out_sem.at[4 + index])
        for index, (narrow, target) in enumerate(
            ((up_bias_v, grad_up_bias), (gains_v, grad_gains), (biases_v, grad_biases))
        )
    ]
    small_load.start()
    for copy in loads + ends_loads:
        copy.start()
    for load, copy in zip(ends_loads, ends_copies):
        load.wait()
        copy.start()
    loads[0].wait()
    for position in range(4):
        rows = slice(position * share_rows, (position + 1) * share_rows)
        wide_down[rows, :] = fin_v[0, position].astype(F32)
    stores[0].start()
    loads[1].wait()
    for position in range(4):
        wide_up[:, position * width : (position + 1) * width] = fin_v[1, position].astype(F32)
    stores[1].start()
    loads[2].wait()
    for position in range(3):
        wide_qkv[:, position * width : (position + 1) * width] = fin_v[2, position].astype(F32)
    stores[2].start()
    wide_out[...] = fin_v[2, 3].astype(F32)
    stores[3].start()
    small_load.wait()
    for position in range(4):
        rows = slice(position * share_rows, (position + 1) * share_rows)
        up_bias_v[:, rows] = small_v[BIAS_UP + position : BIAS_UP + position + 1, :share_rows]
    gains_v[0] = small_v[:2, :share_rows]
    biases_v[0] = small_v[2:BIAS_UP, :share_rows]
    for copy in small_stores:
        copy.start()
    for copy in stores + ends_copies + small_stores:
        copy.wait()


def on_device(
    dp_count,
    block_input,
    cotangent,
    window_group,
    w_qkv,
    w_out,
    w_up,
    w_down,
    up_bias,
    norm_gains,
    biases,
):
    rows, width = block_input.shape
    piece = rows // PIECES
    pairs = width // LANES
    share_rows = width // dp_count
    small_width = max(share_rows, LANES)
    dp_steps = dp_count.bit_length() - 1
    split = SPLIT if share_rows % (16 * SPLIT) == 0 else 1
    jobs = 3 * split
    slots = jobs + (len(DP_FIRST) if split == SPLIT else 0)
    any_spec = pl.BlockSpec(memory_space=pl.ANY)
    vmem_spec = pl.BlockSpec(memory_space=pltpu.VMEM)
    smem_spec = pl.BlockSpec(memory_space=pltpu.SMEM)
    dma = pltpu.SemaphoreType.DMA
    vmem = pltpu.VMEM
    ends_in, fin, small = pl.pallas_call(
        functools.partial(layer_kernel, dp_count),
        out_shape=(
            jax.ShapeDtypeStruct((PIECES, piece, width), F32),
            jax.ShapeDtypeStruct((3, 4, share_rows, width), BF16),
            jax.ShapeDtypeStruct((16, small_width), F32),
        ),
        in_specs=[smem_spec] + [any_spec] * 6 + [vmem_spec] * 3,
        out_specs=(any_spec,) * 3,
        scratch_shapes=[
            vmem((width, 3 * width), BF16),
            vmem((width, width), BF16),
            vmem((width, 4 * width), BF16),
            vmem((4, width, width), BF16),
            vmem((12, width, width), BF16),
            vmem((PIECES, piece, width), BF16),
            vmem((width, rows), BF16),
            vmem((3, pairs, LANES, rows), BF16),
            vmem((PIECES, pairs, piece, LANES), BF16),
            vmem((PIECES, pairs, piece, LANES), BF16),
            vmem((PIECES, pairs, 2, piece, piece), BF16),
            vmem((pairs, 2, piece, piece), BF16),
            vmem((pairs, LANES, rows), BF16),
            vmem((width, rows), F32),
            vmem((width, rows), F32),
            vmem((PIECES, 2, 1, piece), F32),
            vmem((width, rows), BF16),
            vmem((4, width, rows), BF16),
            vmem((4, width, rows), BF16),
            vmem((width, rows), BF16),
            vmem((width, rows), BF16),
            vmem((pairs, LANES, piece), BF16),
            vmem((PIECES, width, piece), BF16),
            vmem((PIECES, width, piece), BF16),
            vmem((STATS, width, LANES), BF16),
            vmem((STATS, width, LANES), F32),
            vmem((2, 2, pairs, LANES, piece), F32),
            vmem((width, piece), F32),
            vmem((width, piece), F32),
            vmem((width, piece), F32),
            vmem((2, piece, width), F32),
            vmem((3, 2, width, width), BF16),
            vmem((3, width, width), BF16),
            vmem((slots, (width - share_rows) // split, width), BF16),
            vmem((3, 4, share_rows, width), BF16),
            vmem((dp_count, 16, small_width), F32),
            vmem((dp_count - 1, 16, small_width), F32),
            vmem((4, 16, small_width), F32),
            vmem((16, small_width), F32),
            dma((13,)),
            dma((PIECES,)),
            dma((PIECES,)),
            dma((PIECES,)),
            dma((jobs, 2)),
            dma((jobs, 2)),
            dma((jobs, 2)),
            dma((jobs, 2)),
            dma((jobs, dp_steps, 2)),
            dma((jobs, dp_steps, 2)),
            dma((jobs,)),
            dma((jobs,)),
            dma((jobs, 2)),
            dma((jobs, 2)),
            dma((dp_count - 1,)),
            dma((dp_count - 1,)),
            dma((3,)),
            dma((3,)),
            dma((jobs,)),
        ],
        compiler_params=pltpu.CompilerParams(
            collective_id=0, has_side_effects=True, vmem_limit_bytes=63 * 1024 * 1024
        ),
    )(
        window_group,
        block_input.reshape(PIECES, piece, width),
        cotangent.reshape(PIECES, piece, width),
        w_qkv,
        w_out,
        w_up,
        w_down,
        up_bias,
        norm_gains,
        biases,
    )
    return pl.pallas_call(
        finish_kernel,
        out_shape=(
            jax.ShapeDtypeStruct((1, rows, width), F32),
            jax.ShapeDtypeStruct((1, share_rows, 3 * width), F32),
            jax.ShapeDtypeStruct((1, share_rows, width), F32),
            jax.ShapeDtypeStruct((1, share_rows, 4 * width), F32),
            jax.ShapeDtypeStruct((1, 4 * share_rows, width), F32),
            jax.ShapeDtypeStruct((1, 4 * share_rows), F32),
            jax.ShapeDtypeStruct((1, 2, share_rows), F32),
            jax.ShapeDtypeStruct((1, 4, share_rows), F32),
        ),
        in_specs=[smem_spec] + [any_spec] * 3,
        out_specs=(any_spec,) * 8,
        scratch_shapes=[
            vmem((rows, width), F32),
            vmem((3, 4, share_rows, width), BF16),
            vmem((share_rows, 3 * width), F32),
            vmem((share_rows, width), F32),
            vmem((share_rows, 4 * width), F32),
            vmem((4 * share_rows, width), F32),
            vmem((16, small_width), F32),
            vmem((1, 4 * share_rows), F32),
            vmem((1, 2, share_rows), F32),
            vmem((1, 4, share_rows), F32),
            dma((16,)),
            dma((4,)),
            dma((7,)),
        ],
        compiler_params=pltpu.CompilerParams(vmem_limit_bytes=63 * 1024 * 1024),
    )(window_group, ends_in.reshape(rows, width), fin, small)


def solution(mesh):
    return jax.shard_map(
        functools.partial(on_device, mesh.shape["dp"]),
        mesh=mesh,
        in_specs=(
            P(("dp", "rep"), None),
            P(("dp", "rep"), None),
            P(("dp", "rep"), None),
            P("segment", None, None),
            P("segment", None, None),
            P("segment", None, None),
            P("segment", None, None),
            P("segment", None),
            P("segment", None, None),
            P("segment", None, None),
        ),
        out_specs=(
            P("segment", ("dp", "rep"), None),
            P("segment", "dp", None),
            P("segment", "dp", None),
            P("segment", "dp", None),
            P("segment", "dp", None),
            P("segment", "dp"),
            P("segment", None, "dp"),
            P("segment", None, "dp"),
        ),
        check_vma=False,
    )
```

```python
import functools
import math

import jax
import jax.numpy as jnp
from jax import lax
from jax.experimental import pallas as pl
from jax.experimental.pallas import tpu as pltpu
from jax.sharding import PartitionSpec as P

MESH = pl.DeviceIdType.MESH
F32 = jnp.float32
BF16 = jnp.bfloat16
HEADS = 8
LANES = 128
PIECES = 4
EPS = 1e-05
GAIN_ONE, GAIN_TWO, BIAS_OUT, BIAS_ONE, BIAS_DOWN, BIAS_TWO, BIAS_UP = range(7)
STATS = 10
CHUNK = 64
SPLIT = 4
DP_FIRST = (1, 3, 6, 10)
SUM, CORE, SIDE, SIDED, DP, DPED, JOIN, LAST, SMALL = range(9)
ORDER_ONE = (
    (SUM, 0), (SUM, 2),
)
ORDER_TWO = (
    (SUM, 4), (CORE, 1), (CORE, 0), (SIDE, 0), (SUM, 6), (CORE, 2), (SIDE, 2), (CORE, 3),
)
ORDER_THREE = (
    (CORE, 5), (SUM, 8), (SIDE, 5), (CORE, 6), (DP, 3), (CORE, 4), (SUM, 10), (CORE, 7), (SIDE, 4),
    (SIDED, 5), (SIDED, 2), (SIDE, 7), (DP, 1), (CORE, 8), (CORE, 11), (DPED, 3), (DP, 6), (SIDED, 0),
    (DP, 2), (DPED, 1), (SIDED, 4), (SIDE, 11), (JOIN, 3), (SIDED, 7), (CORE, 10), (DP, 0), (DP, 5),
    (CORE, 9), (SMALL, 0), (SIDE, 8), (DP, 4), (SIDE, 9), (SIDED, 11), (DP, 7), (JOIN, 1), (SIDED, 8),
    (SMALL, 1), (LAST, 1), (DPED, 0), (DP, 10), (DPED, 5), (DPED, 2), (LAST, 3), (SIDED, 9), (DPED, 6),
    (DP, 8), (JOIN, 0), (DPED, 4), (DPED, 10), (DP, 11), (JOIN, 4), (JOIN, 5), (DP, 9), (JOIN, 2), (LAST, 0),
    (DPED, 8), (JOIN, 6), (DPED, 7), (DPED, 11), (DPED, 9), (LAST, 4), (JOIN, 10), (JOIN, 7), (JOIN, 11),
    (JOIN, 8), (JOIN, 9), (SMALL, 2), (LAST, 5), (LAST, 8), (LAST, 2), (LAST, 9), (LAST, 10), (LAST, 11),
    (LAST, 7), (LAST, 6),
)


def plain_orders():
    one = ((SUM, 0),)
    two = ((SUM, 1), (CORE, 0), (SIDE, 0))
    three = ((SUM, 2), (CORE, 1), (SIDE, 1), (CORE, 2), (SIDE, 2), (SMALL, 0), (SMALL, 1), (SMALL, 2))
    for stage in (SIDED, DP, DPED, JOIN, LAST):
        three += tuple((stage, job) for job in range(3))
    return one, two, three


def dot_plain(left, right):
    return lax.dot_general(left, right, (((1,), (0,)), ((), ())), preferred_element_type=F32)


def drain(parts):
    for _ in parts:
        pass


def side_by_side(one, two):
    spent = [0, 300]
    live = [one, two]
    while live[0] or live[1]:
        which = 0 if live[0] and (not live[1] or spent[0] <= spent[1]) else 1
        cost = next(live[which], None)
        if cost is None:
            live[which] = None
        else:
            spent[which] += cost


def dot_turned(left, right):
    return lax.dot_general(left, right, (((1,), (1,)), ((), ())), preferred_element_type=F32)


def fold(values):
    total = values[:, :LANES]
    for start in range(LANES, values.shape[1], LANES):
        total = total + values[:, start : start + LANES]
    return total


def layer_kernel(
    dp_count,
    flag_ref,
    x_hbm,
    ct_hbm,
    w_qkv_hbm,
    w_out_hbm,
    w_up_hbm,
    w_down_hbm,
    up_bias_ref,
    gains_ref,
    biases_ref,
    ends_hbm,
    fin_hbm,
    small_hbm,
    w_qkv,
    w_out,
    w_up,
    w_down,
    turned,
    rows_in,
    x_t,
    qkv,
    keys_rm,
    values_rm,
    share,
    share_off,
    mixture,
    norm_one,
    norm_two,
    inverses,
    hidden_low,
    slope,
    active,
    down_grad,
    branch_grad,
    grad_mix,
    outgoing,
    incoming_grad,
    columns,
    sums,
    key_sums,
    wide_a,
    wide_b,
    wide_c,
    ends_v,
    core_in,
    side_in,
    dp_in,
    fin,
    small,
    small_dp,
    small_rep,
    small_out,
    load_sem,
    seg_send,
    seg_recv,
    ends_sem,
    core_send,
    core_recv,
    side_send,
    side_recv,
    dp_send,
    dp_recv,
    join_send,
    join_recv,
    last_send,
    last_recv,
    sdp_send,
    sdp_recv,
    srep_send,
    srep_recv,
    fin_sem,
):
    width = w_out.shape[0]
    piece = x_t.shape[1] // PIECES
    pairs = qkv.shape[1]
    share_rows = width // dp_count
    dp_steps = dp_count.bit_length() - 1
    segment = lax.axis_index("segment")
    dp = lax.axis_index("dp")
    rep = lax.axis_index("rep")
    core = lax.rem(rep, 2)
    side = lax.div(rep, 2)
    other_core = side * 2 + (1 - core)
    other_side = (1 - side) * 2 + core

    def load_copy(block):
        def span(first):
            return pl.ds(pl.multiple_of((block - first) * width, width), width)

        def copy_of(source, target):
            return pltpu.make_async_copy(source, target, load_sem.at[1 + block])

        return (
            lambda: copy_of(w_qkv_hbm.at[0, :, span(0)], w_qkv.at[:, span(0)]),
            lambda: copy_of(w_out_hbm.at[0], w_out),
            lambda: copy_of(w_up_hbm.at[0, :, span(4)], w_up.at[:, span(4)]),
            lambda: copy_of(w_down_hbm.at[0, span(8), :], w_down.at[block - 8]),
        )

    parts_of_load = ((0, 3), (3, 4), (4, 8), (8, 12))
    first_rows = pltpu.make_async_copy(x_hbm, rows_in, load_sem.at[0])
    last_rows = pltpu.make_async_copy(ct_hbm, rows_in, load_sem.at[0])

    @pl.when(segment == 0)
    def _():
        first_rows.start()

    @pl.when(segment == 1)
    def _():
        last_rows.start()

    for part, (first, after) in enumerate(parts_of_load):
        for block in range(first, after):
            load_copy(block)[part]().start()

    barrier = pltpu.get_barrier_semaphore()
    pl.semaphore_signal(
        barrier, inc=1, device_id={"segment": 1 - segment}, device_id_type=MESH
    )
    for step in range(1, 4):
        pl.semaphore_signal(
            barrier, inc=1, device_id={"rep": lax.rem(rep + step, 4)}, device_id_type=MESH
        )
    for step in range(1, dp_count):
        pl.semaphore_signal(
            barrier, inc=1, device_id={"dp": lax.rem(dp + step, dp_count)}, device_id_type=MESH
        )

    params = [gains_ref[0].astype(F32), biases_ref[0].astype(F32)]
    for block in range(4):
        params.append(up_bias_ref[:, block * width : (block + 1) * width].astype(F32))
    params.append(jnp.zeros((16 - STATS, width), F32))
    upright = jnp.concatenate(params, axis=0).T
    for index in range(STATS):
        columns[index] = jnp.broadcast_to(upright[:, index : index + 1], (width, LANES)).astype(BF16)
    for index in range(STATS):
        sums[index] = jnp.zeros((width, LANES), F32)
    key_sums[0] = jnp.zeros(key_sums.shape[1:], F32)

    chunks = [slice(start, start + CHUNK) for start in range(0, width, CHUNK)]

    def turn(part):
        def one(block, carry):
            load_copy(block)[part]().wait()
            if part == 3:
                turned[block] = w_down[block - 8].T
            elif part == 1:
                turned[block] = w_out[...].T
            else:
                first = parts_of_load[part][0]
                span = pl.ds(pl.multiple_of((block - first) * width, width), width)
                turned[block] = (w_qkv if part == 0 else w_up)[:, span].T
            return carry

        lax.fori_loop(*parts_of_load[part], one, 0)

    for part in range(4):
        turn(part)
    first_rows.wait()

    pl.semaphore_wait(barrier, 4 + dp_count - 1)

    flag = flag_ref[0, 0].astype(F32)

    def lanes_of(index):
        if isinstance(index, int):
            return pl.ds(index * piece, piece)
        return pl.ds(pl.multiple_of(index * piece, piece), piece)

    def forward_copy(index):
        return pltpu.make_async_remote_copy(
            src_ref=outgoing.at[index],
            dst_ref=x_t.at[:, lanes_of(index)],
            send_sem=seg_send.at[index],
            recv_sem=seg_recv.at[index],
            device_id={"segment": 1 - segment},
            device_id_type=MESH,
        )

    def backward_copy(index):
        return pltpu.make_async_remote_copy(
            src_ref=outgoing.at[index],
            dst_ref=incoming_grad.at[index],
            send_sem=seg_send.at[index],
            recv_sem=seg_recv.at[index],
            device_id={"segment": 1 - segment},
            device_id_type=MESH,
        )

    def ends_copy(index):
        return pltpu.make_async_copy(
            ends_v.at[lax.rem(index, 2)], ends_hbm.at[index], ends_sem.at[index]
        )

    def free_ends(index):
        @pl.when(index >= 2)
        def _():
            ends_copy(index - 2).wait()

    def own_rows(index):
        half = lax.rem(index, 2)
        whole = jnp.where(index < 2, 1.0, 0.0).astype(F32)
        weight = whole * flag + (1.0 - whole) * (1.0 - flag)
        picked = rows_in[half].astype(F32) * weight + rows_in[2 + half].astype(F32) * (1.0 - weight)
        return picked.T

    def by_queries(values):
        half = LANES // 2
        blank = jnp.zeros((half, LANES), values.dtype)
        parts = []
        for part in range(2):
            span = slice(part * LANES, (part + 1) * LANES)
            first = jnp.concatenate([values[:half, span], blank], axis=0)
            second = jnp.concatenate([blank, values[half:, span]], axis=0)
            parts.append(jnp.concatenate([first, second], axis=1))
        return parts

    def against(rows_ref, index, pair, parts, has_off):
        own = rows_ref[index, pair]
        products = [dot_plain(own[:LANES], parts[0]), dot_plain(own, parts[1])]
        if has_off:
            before = rows_ref[0, pair]
            products += [dot_plain(before, parts[0]), dot_plain(before, parts[1])]
        return products

    def tiles_of(products, head, part, has_off):
        lanes = slice(head * LANES, (head + 1) * LANES)
        own = products[part]
        tiles = [own[part * LANES : (part + 1) * LANES, lanes]]
        if part:
            tiles.append(own[:LANES, lanes])
        if has_off:
            off = products[2 + part]
            tiles += [off[:LANES, lanes], off[LANES:, lanes]]
        return tiles

    def joined(lows, has_off):
        blank = jnp.zeros((LANES, LANES), BF16)
        first = jnp.concatenate([lows[0][0], blank], axis=0)
        second = jnp.concatenate([lows[1][1], lows[1][0]], axis=0)
        whole = jnp.concatenate([first, second], axis=1)
        if not has_off:
            return whole, None
        first = jnp.concatenate(lows[0][-2:], axis=0)
        second = jnp.concatenate(lows[1][-2:], axis=0)
        return whole, jnp.concatenate([first, second], axis=1)

    def attend(index, has_off):
        lanes = lanes_of(index)
        half = LANES // 2
        key_at = lax.broadcasted_iota(jnp.int32, (LANES, LANES), 0)
        query_at = lax.broadcasted_iota(jnp.int32, (LANES, LANES), 1)
        allowed = key_at <= query_at

        def scores_of(pair):
            return against(
                keys_rm, index, pair, by_queries(qkv[0, pair, :, lanes]), has_off
            )

        ahead = scores_of(0)
        for pair in range(pairs):
            scores = ahead
            if pair + 1 < pairs:
                ahead = scores_of(pair + 1)
            mixed = []
            for head in range(2):
                rows = slice(head * half, (head + 1) * half)
                lows = []
                for part in range(2):
                    tiles = tiles_of(scores, head, part, has_off)
                    tiles[0] = jnp.where(allowed, tiles[0], -1e30)
                    top = jnp.max(functools.reduce(jnp.maximum, tiles), axis=0, keepdims=True)
                    raised = [jnp.exp(tile - top) for tile in tiles]
                    total = functools.reduce(jnp.add, raised)
                    scale = 1.0 / jnp.sum(total, axis=0, keepdims=True)
                    lows.append([(tile * scale).astype(BF16) for tile in raised])
                low, low_off = joined(lows, has_off)
                share[index, pair, head] = low
                mix = dot_plain(qkv[2, pair, rows, lanes], low)
                if has_off:
                    share_off[pair, head] = low_off
                    mix = mix + dot_plain(qkv[2, pair, rows, :piece], low_off)
                mixed.append(mix.astype(BF16))
            mixture[pair, :, lanes] = jnp.concatenate(mixed, axis=0)
            yield 280

    def part_sum(values):
        return jnp.sum(values.reshape(values.shape[0] // 8, 8, values.shape[1]), axis=0)

    def full_mean(parts):
        return jnp.sum(parts, axis=0, keepdims=True) * (1.0 / width)

    def column(index, rows):
        part = columns[index, rows, :].astype(F32)
        return jnp.concatenate([part] * (piece // LANES), axis=1)

    def gather_sum(index, rows, values):
        sums[index, rows, :] = sums[index, rows, :] + fold(values)

    def norm_chunks(index, which, wide_a, total):
        mean = full_mean(total)
        spread = jnp.zeros((8, piece), F32)
        for rows in chunks:
            centred = wide_a[rows, :] - mean
            spread = spread + part_sum(centred * centred)
        inverse = lax.rsqrt(full_mean(spread) + EPS)
        inverses[index, which] = inverse
        return mean, inverse

    def forward_start(index):
        @pl.when(segment == 0)
        def _():
            x_t[:, lanes_of(index)] = own_rows(index).astype(BF16)

        @pl.when(segment == 1)
        def _():
            forward_copy(index).wait_recv()

    def forward_first(index):
        lanes = lanes_of(index)
        inputs = x_t[:, lanes]
        score_scale = 1.0 / math.sqrt(width // HEADS)
        for block in range(3):
            result = dot_plain(turned[block], inputs)
            for pair in range(pairs):
                low = result[pair * LANES : (pair + 1) * LANES]
                low = (low * score_scale if block == 0 else low).astype(BF16)
                qkv[block, pair, :, lanes] = low
                if block == 1:
                    keys_rm[index, pair] = low.T
                if block == 2:
                    values_rm[index, pair] = low.T
            yield 270

    def forward_rest(index, wide_a):
        lanes = lanes_of(index)
        branch = dot_plain(turned[3], mixture[:, :, lanes].reshape(width, piece))
        yield 250
        total = jnp.zeros((8, piece), F32)
        for rows in chunks:
            sum_one = x_t[rows, lanes].astype(F32) + (branch[rows] + column(BIAS_OUT, rows))
            wide_a[rows, :] = sum_one
            total = total + part_sum(sum_one)
            yield 25
        mean, inverse = norm_chunks(index, 0, wide_a, total)
        yield 150
        for rows in chunks:
            normed = (wide_a[rows, :] - mean) * inverse
            norm_one[rows, lanes] = normed
            hidden = normed * column(GAIN_ONE, rows) + column(BIAS_ONE, rows)
            hidden_low[rows, lanes] = hidden.astype(BF16)
            yield 30

        branch_two = None
        for block in range(4):
            pre_block = dot_plain(turned[4 + block], hidden_low[:, lanes])
            yield 50
            lows = []
            for rows in chunks:
                pre = pre_block[rows] + column(BIAS_UP + block, rows)
                level = (lax.erf(pre * (1.0 / math.sqrt(2.0))) + 1.0) * 0.5
                bell = jnp.exp2(pre * pre * (-0.5 * math.log2(math.e)))
                lows.append((pre * level).astype(BF16))
                active[block, rows, lanes] = lows[-1]
                slope[block, rows, lanes] = (
                    level + pre * bell * (1.0 / math.sqrt(2.0 * math.pi))
                ).astype(BF16)
                yield 65
            part = dot_plain(turned[8 + block], jnp.concatenate(lows, axis=0))
            branch_two = part if branch_two is None else branch_two + part
            yield 100
        total = jnp.zeros((8, piece), F32)
        for rows in chunks:
            hidden = norm_one[rows, lanes] * column(GAIN_ONE, rows) + column(BIAS_ONE, rows)
            sum_two = hidden + (branch_two[rows] + column(BIAS_DOWN, rows))
            wide_a[rows, :] = sum_two
            total = total + part_sum(sum_two)
            yield 25
        mean, inverse = norm_chunks(index, 1, wide_a, total)
        yield 150
        for rows in chunks:
            norm_two[rows, lanes] = (wide_a[rows, :] - mean) * inverse
            yield 20

    def forward_end(index):
        @pl.when(segment == 0)
        def _():
            for rows in chunks:
                outgoing[index, rows, :] = output_rows(rows, lanes_of(index)).astype(BF16)
            forward_copy(index).start()

    def off_or_not(index, run):
        @pl.when(index == 1)
        def _():
            drain(run(index, True))

        @pl.when(index != 1)
        def _():
            drain(run(index, False))

    def forward(index):
        forward_start(index)
        drain(forward_first(index))
        off_or_not(index, attend)
        drain(forward_rest(index, wide_a))
        forward_end(index)

    def output_rows(rows, lanes):
        return norm_two[rows, lanes] * column(GAIN_TWO, rows) + column(BIAS_TWO, rows)

    def last_outputs(index, carry):
        free_ends(index)
        for start in range(0, width, LANES):
            rows = slice(start, start + LANES)
            ends_v[lax.rem(index, 2), :, rows] = output_rows(rows, lanes_of(index)).T
        ends_copy(index).start()
        return carry

    def attend_back(index, has_off):
        lanes = lanes_of(index)
        slot = (1 if index == 0 else 0) if isinstance(index, int) else jnp.where(index == 0, 1, 0)
        half = LANES // 2
        score_scale = 1.0 / math.sqrt(width // HEADS)

        def backs_of(pair):
            return against(values_rm, index, pair, by_queries(grad_mix[pair]), has_off)

        ahead = backs_of(0)
        for pair in range(pairs):
            backs = ahead
            if pair + 1 < pairs:
                ahead = backs_of(pair + 1)
            results = ([], [], [])
            for head in range(2):
                rows = slice(head * half, (head + 1) * half)
                low = share[index, pair, head]
                low_off = share_off[pair, head] if has_off else None
                lows = []
                for part in range(2):
                    place = slice(part * LANES, (part + 1) * LANES)
                    wides = [low[place, place]]
                    if part:
                        wides.append(low[:LANES, place])
                    if has_off:
                        wides += [low_off[:LANES, place], low_off[LANES:, place]]
                    wides = [tile.astype(F32) for tile in wides]
                    tiles = tiles_of(backs, head, part, has_off)
                    products = [wide * tile for wide, tile in zip(wides, tiles)]
                    inner = jnp.sum(functools.reduce(jnp.add, products), axis=0, keepdims=True)
                    lows.append(
                        [
                            (product - wide * inner).astype(BF16)
                            for product, wide in zip(products, wides)
                        ]
                    )
                grad_scores, grad_off = joined(lows, has_off)
                queries = qkv[0, pair, rows, lanes]
                grads = grad_mix[pair, rows]
                grad_query = dot_plain(qkv[1, pair, rows, lanes], grad_scores)
                grad_key = dot_turned(queries, grad_scores) + key_sums[slot, 0, pair, rows]
                grad_value = dot_turned(grads, low) + key_sums[slot, 1, pair, rows]
                if has_off:
                    grad_query = grad_query + dot_plain(qkv[1, pair, rows, :piece], grad_off)
                    key_sums[1, 0, pair, rows] = dot_turned(queries, grad_off)
                    key_sums[1, 1, pair, rows] = dot_turned(grads, low_off)
                for kept, grad in zip(results, (grad_query * score_scale, grad_key, grad_value)):
                    kept.append(grad.astype(BF16))
            for block in range(3):
                qkv[block, pair, :, lanes] = jnp.concatenate(results[block], axis=0)
            yield 440

    def backward_start(index):
        @pl.when(segment == 0)
        def _():
            backward_copy(index).wait_recv()

    def backward_norm(index):
        lanes = lanes_of(index)
        plain = jnp.zeros((8, piece), F32)
        inner = jnp.zeros((8, piece), F32)
        for rows in chunks:
            grad = incoming_grad[index, rows, :].astype(F32)
            product = grad * norm_two[rows, lanes]
            gather_sum(GAIN_TWO, rows, product)
            gather_sum(BIAS_TWO, rows, grad)
            gain = column(GAIN_TWO, rows)
            plain = plain + part_sum(grad * gain)
            inner = inner + part_sum(product * gain)
            yield 40
        plain = full_mean(plain)
        inner = full_mean(inner)
        inverse = inverses[index, 1]
        for rows in chunks:
            scaled = incoming_grad[index, rows, :].astype(F32) * column(GAIN_TWO, rows)
            grad_two = (scaled - plain - norm_two[rows, lanes] * inner) * inverse
            gather_sum(BIAS_DOWN, rows, grad_two)
            wide_a[rows, :] = grad_two
            down_grad[rows, lanes] = grad_two.astype(BF16)
            yield 40

    def backward_feed(index):
        lanes = lanes_of(index)
        for block in range(4):
            back = dot_plain(w_down[block], down_grad[:, lanes])
            for rows in chunks:
                grad_pre = back[rows] * slope[block, rows, lanes].astype(F32)
                gather_sum(BIAS_UP + block, rows, grad_pre)
                slope[block, rows, lanes] = grad_pre.astype(BF16)
            yield 250

        through = dot_plain(w_up[...], slope[:, :, lanes].reshape(4 * width, piece))
        plain = jnp.zeros((8, piece), F32)
        inner = jnp.zeros((8, piece), F32)
        for rows in chunks:
            grad_hidden = wide_a[rows, :] + through[rows]
            wide_a[rows, :] = grad_hidden
            product = grad_hidden * norm_one[rows, lanes]
            gather_sum(GAIN_ONE, rows, product)
            gather_sum(BIAS_ONE, rows, grad_hidden)
            gain = column(GAIN_ONE, rows)
            plain = plain + part_sum(grad_hidden * gain)
            inner = inner + part_sum(product * gain)
            yield 120 if rows.start == 0 else 45
        plain = full_mean(plain)
        inner = full_mean(inner)
        inverse = inverses[index, 0]
        for rows in chunks:
            scaled = wide_a[rows, :] * column(GAIN_ONE, rows)
            grad_one = (scaled - plain - norm_one[rows, lanes] * inner) * inverse
            gather_sum(BIAS_OUT, rows, grad_one)
            wide_b[rows, :] = grad_one
            branch_grad[rows, lanes] = grad_one.astype(BF16)
            yield 40
        grad_mix[...] = (
            dot_plain(w_out[...], branch_grad[:, lanes]).astype(BF16).reshape(pairs, LANES, piece)
        )
        yield 300

    def backward_attention(index):
        off_or_not(index, attend_back)
        through = dot_plain(w_qkv[...], qkv[:, :, :, lanes_of(index)].reshape(3 * width, piece))

        @pl.when(segment == 1)
        def _():
            for rows in chunks:
                outgoing[index, rows, :] = (wide_b[rows, :] + through[rows]).astype(BF16)
            backward_copy(index).start()

        @pl.when(segment == 0)
        def _():
            free_ends(index)
            for start in range(0, width, LANES):
                rows = slice(start, start + LANES)
                ends_v[lax.rem(index, 2), :, rows] = (wide_b[rows, :] + through[rows]).T
            ends_copy(index).start()

    def backward_both(index, forward_index):
        forward_copy(forward_index).wait_recv()

        def back():
            yield from backward_norm(index)
            yield from backward_feed(index)
            yield from attend_back(index, False)
            through = dot_plain(w_qkv[...], qkv[:, :, :, lanes_of(index)].reshape(3 * width, piece))
            for rows in chunks:
                outgoing[index, rows, :] = (wide_b[rows, :] + through[rows]).astype(BF16)
                yield 90

        def ahead():
            yield from forward_first(forward_index)
            yield from attend(forward_index, False)
            yield from forward_rest(forward_index, wide_c)

        side_by_side(back(), ahead())
        backward_copy(index).start()

    split = SPLIT if share_rows % (16 * SPLIT) == 0 else 1
    dp_first = DP_FIRST if split == SPLIT else ()
    orders = (ORDER_ONE, ORDER_TWO, ORDER_THREE) if split == SPLIT else plain_orders()
    jobs = 3 * split
    cut_rows = share_rows // split
    job_rows = width // split

    def base_of(job):
        return (8, 4, 0)[job // split]

    def job_span(job):
        return pl.ds(job % split * job_rows, job_rows)

    def fin_rows(job):
        return pl.ds(job % split * cut_rows, cut_rows)

    def parts_of(job):
        return range(2) if job in dp_first else range(1)

    def core_copies(job):
        return [
            pltpu.make_async_remote_copy(
                src_ref=turned.at[base_of(job) + 2 * (1 - core) + each, job_span(job)],
                dst_ref=core_in.at[job // split, each, job_span(job)],
                send_sem=core_send.at[job, each],
                recv_sem=core_recv.at[job, each],
                device_id={"rep": other_core},
                device_id_type=MESH,
            )
            for each in range(2)
        ]

    def side_copies(job):
        base = base_of(job)
        copies = []
        for each in parts_of(job):
            if job in dp_first:
                source = turned.at[base + 2 * core + each, dp_rows(job, dp_steps - 1)[1]]
                target = side_in.at[
                    job // split, pl.ds(job % split * job_rows + each * cut_rows, cut_rows)
                ]
            else:
                source = turned.at[base + 2 * core + (1 - side), job_span(job)]
                target = side_in.at[job // split, job_span(job)]
            copies.append(
                pltpu.make_async_remote_copy(
                    src_ref=source,
                    dst_ref=target,
                    send_sem=side_send.at[job, each],
                    recv_sem=side_recv.at[job, each],
                    device_id={"rep": other_side},
                    device_id_type=MESH,
                )
            )
        return copies

    def dp_slot(job):
        return sum(len(parts_of(before)) for before in range(job))

    def dp_rows(job, step):
        count = dp_count // 2
        start = 0
        for bit in range(step):
            start = start + lax.rem(lax.div(dp, 2**bit), 2) * count
            count = count // 2
        mine = lax.rem(lax.div(dp, 2**step), 2)
        first = job % split * job_rows
        sent = pl.multiple_of(first + (start + (1 - mine) * count) * cut_rows, cut_rows)
        kept = pl.multiple_of(first + (start + mine * count) * cut_rows, cut_rows)
        return pl.ds(sent, count * cut_rows), pl.ds(kept, count * cut_rows)

    def dp_landing(step):
        count = dp_count // 2 ** (step + 1)
        return pl.ds((dp_count - 2 * count) * cut_rows, count * cut_rows)

    def dp_copies(job, step):
        mine = lax.rem(lax.div(dp, 2**step), 2)
        copies = []
        for each in parts_of(job):
            position = base_of(job) + 2 * core + (each if job in dp_first else side)
            copies.append(
                pltpu.make_async_remote_copy(
                    src_ref=turned.at[position, dp_rows(job, step)[0]],
                    dst_ref=dp_in.at[dp_slot(job) + each, dp_landing(step)],
                    send_sem=dp_send.at[job, step, each],
                    recv_sem=dp_recv.at[job, step, each],
                    device_id={"dp": dp + (1 - 2 * mine) * 2**step},
                    device_id_type=MESH,
                )
            )
        return copies

    def join_copy(job):
        part = fin.at[job // split, 2 * core + side, fin_rows(job)]
        return pltpu.make_async_remote_copy(
            src_ref=part,
            dst_ref=part,
            send_sem=join_send.at[job],
            recv_sem=join_recv.at[job],
            device_id={"rep": other_side},
            device_id_type=MESH,
        )

    def last_copies(job):
        copies = []
        for each in range(2):
            part = fin.at[job // split, 2 * core + each, fin_rows(job)]
            copies.append(
                pltpu.make_async_remote_copy(
                    src_ref=part,
                    dst_ref=part,
                    send_sem=last_send.at[job, each],
                    recv_sem=last_recv.at[job, each],
                    device_id={"rep": other_core},
                    device_id_type=MESH,
                )
            )
        return copies

    def fin_copy(job):
        return pltpu.make_async_copy(
            fin.at[job // split, :, fin_rows(job)],
            fin_hbm.at[job // split, :, fin_rows(job)],
            fin_sem.at[job],
        )

    def arrived(*copies):
        for copy in copies:
            copy.wait_send()
        for copy in copies:
            copy.wait_recv()

    def start_all(copies):
        for copy in copies:
            copy.start()

    def turned_bits(value, count):
        place = 0
        while count > 1:
            place = place * 2 + value % 2
            value = value // 2
            count = count // 2
        return place

    pack = min(2, split)

    def left_rows(source, part):
        count = pack * cut_rows
        start = part * pack * cut_rows
        return jnp.concatenate(
            [source(index * share_rows + start, count) for index in range(dp_count)], axis=0
        )

    def keep_rows(block, part, result):
        for index in range(dp_count):
            for each in range(pack):
                target = (part * pack + each) * job_rows + turned_bits(index, dp_count) * cut_rows
                start = (index * pack + each) * cut_rows
                turned[block, target : target + cut_rows, :] = result[start : start + cut_rows]

    def down_sums(part):
        count = width // (4 * share_rows)

        def one(block, carry):
            pieces = []
            for each in range(4 * count):
                start = each * share_rows + part * pack * cut_rows
                pieces.append(active[block, start : start + pack * cut_rows, :])
            result = dot_turned(jnp.concatenate(pieces, axis=0), down_grad[...]).astype(BF16)
            high = lax.rem(block, 2) * 2 + lax.div(block, 2)
            for each in range(count):
                place = turned_bits(each, count) * 4 + high
                for position in range(4):
                    for job in range(pack):
                        target = (part * pack + job) * job_rows + place * cut_rows
                        start = ((each * 4 + position) * pack + job) * cut_rows
                        turned[
                            8 + position, pl.ds(pl.multiple_of(target, cut_rows), cut_rows), :
                        ] = result[start : start + cut_rows]
            return carry

        lax.fori_loop(0, 4, one, 0)

    def up_sums(part):
        def one(block, carry):
            left = left_rows(lambda start, count: hidden_low[start : start + count, :], part)
            keep_rows(4 + block, part, dot_turned(left, slope[block]).astype(BF16))
            return carry

        lax.fori_loop(0, 4, one, 0)

    def qkv_sums(part):
        def one(block, carry):
            left = left_rows(lambda start, count: x_t[start : start + count, :], part)
            grads = qkv[block].reshape(width, PIECES * piece)
            keep_rows(block, part, dot_turned(left, grads).astype(BF16))
            return carry

        lax.fori_loop(0, 3, one, 0)
        left = left_rows(
            lambda start, count: mixture[start // LANES, start % LANES : start % LANES + count, :], part
        )
        keep_rows(3, part, dot_turned(left, branch_grad[...]).astype(BF16))

    def sums_of(job):
        (down_sums, up_sums, qkv_sums)[job // split](job % split // pack)
        for each in range(pack):
            start_all(core_copies(job + each))

    def after_core(job):
        arrived(*core_copies(job))
        rows = job_span(job)
        for each in parts_of(job):
            place = 1 - side if each == 0 else side
            position = base_of(job) + 2 * core + place
            turned[position, rows, :] = (
                turned[position, rows, :].astype(F32)
                + core_in[job // split, place, rows, :].astype(F32)
            ).astype(BF16)
        if job in dp_first:
            start_all(dp_copies(job, 0))

    def start_side(job):
        start_all(side_copies(job))

    def after_side(job):
        arrived(*side_copies(job))
        rows = job_span(job)
        position = base_of(job) + 2 * core + side
        turned[position, rows, :] = (
            turned[position, rows, :].astype(F32)
            + core_in[job // split, side, rows, :].astype(F32)
            + side_in[job // split, rows, :].astype(F32)
        ).astype(BF16)
        start_all(dp_copies(job, 0))

    def dp_total(job, step, each):
        position = base_of(job) + 2 * core + (each if job in dp_first else side)
        kept = turned[position, dp_rows(job, step)[1], :].astype(F32)
        return position, kept + dp_in[dp_slot(job) + each, dp_landing(step), :].astype(F32)

    def after_dp(job):
        for step in range(dp_steps - 1):
            arrived(*dp_copies(job, step))
            for each in parts_of(job):
                position, total = dp_total(job, step, each)
                turned[position, dp_rows(job, step)[1], :] = total.astype(BF16)
            start_all(dp_copies(job, step + 1))

    def after_last_dp(job):
        step = dp_steps - 1
        arrived(*dp_copies(job, step))
        for each in parts_of(job):
            position, total = dp_total(job, step, each)
            if job in dp_first:
                turned[position, dp_rows(job, step)[1], :] = total.astype(BF16)
            else:
                fin[job // split, 2 * core + side, fin_rows(job), :] = total.astype(BF16)
        if job in dp_first:
            start_side(job)
        else:
            join_copy(job).start()

    def after_join(job):
        if job in dp_first:
            arrived(*side_copies(job))
            for each in range(2):
                rows = pl.ds(job % split * job_rows + each * cut_rows, cut_rows)
                own = turned[base_of(job) + 2 * core + each, dp_rows(job, dp_steps - 1)[1], :]
                total = own.astype(F32) + side_in[job // split, rows, :].astype(F32)
                fin[job // split, 2 * core + each, fin_rows(job), :] = total.astype(BF16)
        else:
            arrived(join_copy(job))
        start_all(last_copies(job))

    def after_last(job):
        arrived(*last_copies(job))
        fin_copy(job).start()

    def small_dp_copy(step):
        target = lax.rem(dp + step, dp_count)
        return pltpu.make_async_remote_copy(
            src_ref=small.at[target],
            dst_ref=small_dp.at[step - 1],
            send_sem=sdp_send.at[step - 1],
            recv_sem=sdp_recv.at[step - 1],
            device_id={"dp": target},
            device_id_type=MESH,
        )

    def small_rep_copy(step):
        return pltpu.make_async_remote_copy(
            src_ref=small_rep.at[rep],
            dst_ref=small_rep.at[rep],
            send_sem=srep_send.at[step - 1],
            recv_sem=srep_recv.at[step - 1],
            device_id={"rep": lax.rem(rep + step, 4)},
            device_id_type=MESH,
        )

    small_copy = pltpu.make_async_copy(small_out, small_hbm, load_sem.at[0])

    def small_step(stage):
        if stage == 0:
            rows_of = [jnp.sum(sums[index].T, axis=0, keepdims=True) for index in range(STATS)]
            small[...] = jnp.zeros(small.shape, F32)
            for share_index in range(dp_count):
                for index in range(BIAS_UP):
                    start = share_index * share_rows
                    small[share_index, index : index + 1, :share_rows] = rows_of[index][
                        :, start : start + share_rows
                    ]
                for part in range(4):
                    start = (share_index * 4 + part) * share_rows
                    block, start = start // width, start % width
                    small[share_index, BIAS_UP + part : BIAS_UP + part + 1, :share_rows] = rows_of[
                        BIAS_UP + block
                    ][:, start : start + share_rows]
            for step in range(1, dp_count):
                small_dp_copy(step).start()
        elif stage == 1:
            total = small[dp]
            for step in range(1, dp_count):
                arrived(small_dp_copy(step))
                total = total + small_dp[step - 1]
            small_rep[rep] = total
            for step in range(1, 4):
                small_rep_copy(step).start()
        else:
            for step in range(1, 4):
                arrived(small_rep_copy(step))
            small_out[...] = (small_rep[0] + small_rep[1]) + (small_rep[2] + small_rep[3])
            small_copy.start()

    def run(order):
        steps = (
            sums_of,
            after_core,
            start_side,
            after_side,
            after_dp,
            after_last_dp,
            after_join,
            after_last,
            small_step,
        )
        for stage, job in order:
            steps[stage](job)

    def one_step(step, carry):
        first_index = jnp.where(step < 4, step, jnp.where(step < 6, 5 - step, step - 4))
        last_index = jnp.where(step < 2, step, jnp.where(step == 2, 1, 3))
        index = jnp.minimum(jnp.where(segment == 0, first_index, last_index), PIECES - 1)
        is_last = jnp.where(step == 2 * PIECES, 1, 0)
        is_forward = jnp.where(step < jnp.where(segment == 0, 4, 2), 1, 0)
        last_backward = jnp.where(step == 2, 1, 0) + jnp.where(step == 5, 1, 0)
        is_backward = jnp.where(segment == 0, (1 - is_forward) * (1 - is_last), last_backward)
        is_split = jnp.where(step >= 2 * PIECES - 1, 1 - segment, 0)
        is_rest = is_backward * (1 - is_split) + is_last * is_split

        @pl.when(is_forward == 1)
        def _():
            forward(index)

        @pl.when(is_backward == 1)
        def _():
            backward_start(index)
            drain(backward_norm(index))

        @pl.when(segment * lax.div(step, 3) * (5 - jnp.minimum(step, 5)) >= 1)
        def _():
            backward_both(2 * step - 6, step - 1)

        @pl.when(is_last == 1)
        def _():
            run(orders[0])

        @pl.when(is_rest == 1)
        def _():
            drain(backward_feed(index))

        @pl.when(is_last == 1)
        def _():
            run(orders[1])

        @pl.when(is_rest == 1)
        def _():
            backward_attention(index)

        return carry

    @pl.when(segment == 1)
    def _():
        for index in range(PIECES):
            incoming_grad[index] = own_rows(index).astype(BF16)

    lax.fori_loop(0, 2 * PIECES + 1, one_step, 0)

    cut = orders[2].index((SMALL, 0))
    run(orders[2][:cut])

    @pl.when(segment == 1)
    def _():
        lax.fori_loop(0, PIECES, last_outputs, 0)

    run(orders[2][cut:])

    for index in range(PIECES):

        @pl.when(segment == 0)
        def _():
            forward_copy(index).wait_send()

        @pl.when(segment == 1)
        def _():
            backward_copy(index).wait_send()

    for index in range(2, PIECES):
        ends_copy(index).wait()
    for job in range(jobs):
        fin_copy(job).wait()
    small_copy.wait()


def finish_kernel(
    flag_ref,
    ends_in,
    fin,
    small,
    ends,
    grad_qkv,
    grad_out,
    grad_up,
    grad_down,
    grad_up_bias,
    grad_gains,
    grad_biases,
    ends_v,
    fin_v,
    wide_qkv,
    wide_out,
    wide_up,
    wide_down,
    small_v,
    up_bias_v,
    gains_v,
    biases_v,
    ends_sem,
    in_sem,
    out_sem,
):
    half = ends_in.shape[0] // 2
    share_rows, width = fin.shape[2:]
    start = pl.multiple_of(half * (1 - flag_ref[0, 0]), half)
    cut = half // 4
    ends_copies = []
    ends_loads = []
    for part in range(8):
        source = pl.ds(part * cut, cut)
        offset = start + part * cut if part < 4 else part * cut - half + (half - start)
        target = pl.ds(pl.multiple_of(offset, cut), cut)
        ends_loads.append(
            pltpu.make_async_copy(ends_in.at[source], ends_v.at[source], ends_sem.at[part])
        )
        ends_copies.append(
            pltpu.make_async_copy(ends_v.at[source], ends.at[0, target], ends_sem.at[8 + part])
        )
    loads = [
        pltpu.make_async_copy(fin.at[group], fin_v.at[group], in_sem.at[group])
        for group in range(3)
    ]
    stores = [
        pltpu.make_async_copy(wide, target.at[0], out_sem.at[index])
        for index, (wide, target) in enumerate(
            ((wide_down, grad_down), (wide_up, grad_up), (wide_qkv, grad_qkv), (wide_out, grad_out))
        )
    ]
    small_load = pltpu.make_async_copy(small, small_v, in_sem.at[3])
    small_stores = [
        pltpu.make_async_copy(narrow, target, out_sem.at[4 + index])
        for index, (narrow, target) in enumerate(
            ((up_bias_v, grad_up_bias), (gains_v, grad_gains), (biases_v, grad_biases))
        )
    ]
    small_load.start()
    for copy in loads + ends_loads:
        copy.start()
    for load, copy in zip(ends_loads, ends_copies):
        load.wait()
        copy.start()
    loads[0].wait()
    for position in range(4):
        rows = slice(position * share_rows, (position + 1) * share_rows)
        wide_down[rows, :] = fin_v[0, position].astype(F32)
    stores[0].start()
    loads[1].wait()
    for position in range(4):
        wide_up[:, position * width : (position + 1) * width] = fin_v[1, position].astype(F32)
    stores[1].start()
    loads[2].wait()
    for position in range(3):
        wide_qkv[:, position * width : (position + 1) * width] = fin_v[2, position].astype(F32)
    stores[2].start()
    wide_out[...] = fin_v[2, 3].astype(F32)
    stores[3].start()
    small_load.wait()
    for position in range(4):
        rows = slice(position * share_rows, (position + 1) * share_rows)
        up_bias_v[:, rows] = small_v[BIAS_UP + position : BIAS_UP + position + 1, :share_rows]
    gains_v[0] = small_v[:2, :share_rows]
    biases_v[0] = small_v[2:BIAS_UP, :share_rows]
    for copy in small_stores:
        copy.start()
    for copy in stores + ends_copies + small_stores:
        copy.wait()


def on_device(
    dp_count,
    block_input,
    cotangent,
    window_group,
    w_qkv,
    w_out,
    w_up,
    w_down,
    up_bias,
    norm_gains,
    biases,
):
    rows, width = block_input.shape
    piece = rows // PIECES
    pairs = width // LANES
    share_rows = width // dp_count
    small_width = max(share_rows, LANES)
    dp_steps = dp_count.bit_length() - 1
    split = SPLIT if share_rows % (16 * SPLIT) == 0 else 1
    jobs = 3 * split
    slots = jobs + (len(DP_FIRST) if split == SPLIT else 0)
    any_spec = pl.BlockSpec(memory_space=pl.ANY)
    vmem_spec = pl.BlockSpec(memory_space=pltpu.VMEM)
    smem_spec = pl.BlockSpec(memory_space=pltpu.SMEM)
    dma = pltpu.SemaphoreType.DMA
    vmem = pltpu.VMEM
    ends_in, fin, small = pl.pallas_call(
        functools.partial(layer_kernel, dp_count),
        out_shape=(
            jax.ShapeDtypeStruct((PIECES, piece, width), F32),
            jax.ShapeDtypeStruct((3, 4, share_rows, width), BF16),
            jax.ShapeDtypeStruct((16, small_width), F32),
        ),
        in_specs=[smem_spec] + [any_spec] * 6 + [vmem_spec] * 3,
        out_specs=(any_spec,) * 3,
        scratch_shapes=[
            vmem((width, 3 * width), BF16),
            vmem((width, width), BF16),
            vmem((width, 4 * width), BF16),
            vmem((4, width, width), BF16),
            vmem((12, width, width), BF16),
            vmem((PIECES, piece, width), BF16),
            vmem((width, rows), BF16),
            vmem((3, pairs, LANES, rows), BF16),
            vmem((PIECES, pairs, piece, LANES), BF16),
            vmem((PIECES, pairs, piece, LANES), BF16),
            vmem((PIECES, pairs, 2, piece, piece), BF16),
            vmem((pairs, 2, piece, piece), BF16),
            vmem((pairs, LANES, rows), BF16),
            vmem((width, rows), F32),
            vmem((width, rows), F32),
            vmem((PIECES, 2, 1, piece), F32),
            vmem((width, rows), BF16),
            vmem((4, width, rows), BF16),
            vmem((4, width, rows), BF16),
            vmem((width, rows), BF16),
            vmem((width, rows), BF16),
            vmem((pairs, LANES, piece), BF16),
            vmem((PIECES, width, piece), BF16),
            vmem((PIECES, width, piece), BF16),
            vmem((STATS, width, LANES), BF16),
            vmem((STATS, width, LANES), F32),
            vmem((2, 2, pairs, LANES, piece), F32),
            vmem((width, piece), F32),
            vmem((width, piece), F32),
            vmem((width, piece), F32),
            vmem((2, piece, width), F32),
            vmem((3, 2, width, width), BF16),
            vmem((3, width, width), BF16),
            vmem((slots, (width - share_rows) // split, width), BF16),
            vmem((3, 4, share_rows, width), BF16),
            vmem((dp_count, 16, small_width), F32),
            vmem((dp_count - 1, 16, small_width), F32),
            vmem((4, 16, small_width), F32),
            vmem((16, small_width), F32),
            dma((13,)),
            dma((PIECES,)),
            dma((PIECES,)),
            dma((PIECES,)),
            dma((jobs, 2)),
            dma((jobs, 2)),
            dma((jobs, 2)),
            dma((jobs, 2)),
            dma((jobs, dp_steps, 2)),
            dma((jobs, dp_steps, 2)),
            dma((jobs,)),
            dma((jobs,)),
            dma((jobs, 2)),
            dma((jobs, 2)),
            dma((dp_count - 1,)),
            dma((dp_count - 1,)),
            dma((3,)),
            dma((3,)),
            dma((jobs,)),
        ],
        compiler_params=pltpu.CompilerParams(
            collective_id=0, has_side_effects=True, vmem_limit_bytes=63 * 1024 * 1024
        ),
    )(
        window_group,
        block_input.reshape(PIECES, piece, width),
        cotangent.reshape(PIECES, piece, width),
        w_qkv,
        w_out,
        w_up,
        w_down,
        up_bias,
        norm_gains,
        biases,
    )
    return pl.pallas_call(
        finish_kernel,
        out_shape=(
            jax.ShapeDtypeStruct((1, rows, width), F32),
            jax.ShapeDtypeStruct((1, share_rows, 3 * width), F32),
            jax.ShapeDtypeStruct((1, share_rows, width), F32),
            jax.ShapeDtypeStruct((1, share_rows, 4 * width), F32),
            jax.ShapeDtypeStruct((1, 4 * share_rows, width), F32),
            jax.ShapeDtypeStruct((1, 4 * share_rows), F32),
            jax.ShapeDtypeStruct((1, 2, share_rows), F32),
            jax.ShapeDtypeStruct((1, 4, share_rows), F32),
        ),
        in_specs=[smem_spec] + [any_spec] * 3,
        out_specs=(any_spec,) * 8,
        scratch_shapes=[
            vmem((rows, width), F32),
            vmem((3, 4, share_rows, width), BF16),
            vmem((share_rows, 3 * width), F32),
            vmem((share_rows, width), F32),
            vmem((share_rows, 4 * width), F32),
            vmem((4 * share_rows, width), F32),
            vmem((16, small_width), F32),
            vmem((1, 4 * share_rows), F32),
            vmem((1, 2, share_rows), F32),
            vmem((1, 4, share_rows), F32),
            dma((16,)),
            dma((4,)),
            dma((7,)),
        ],
        compiler_params=pltpu.CompilerParams(vmem_limit_bytes=63 * 1024 * 1024),
    )(window_group, ends_in.reshape(rows, width), fin, small)


def solution(mesh):
    return jax.shard_map(
        functools.partial(on_device, mesh.shape["dp"]),
        mesh=mesh,
        in_specs=(
            P(("dp", "rep"), None),
            P(("dp", "rep"), None),
            P(("dp", "rep"), None),
            P("segment", None, None),
            P("segment", None, None),
            P("segment", None, None),
            P("segment", None, None),
            P("segment", None),
            P("segment", None, None),
            P("segment", None, None),
        ),
        out_specs=(
            P("segment", ("dp", "rep"), None),
            P("segment", "dp", None),
            P("segment", "dp", None),
            P("segment", "dp", None),
            P("segment", "dp", None),
            P("segment", "dp"),
            P("segment", None, "dp"),
            P("segment", None, "dp"),
        ),
        check_vma=False,
    )
```

```python
import functools
import math

import jax
import jax.numpy as jnp
from jax import lax
from jax.experimental import pallas as pl
from jax.experimental.pallas import tpu as pltpu
from jax.sharding import PartitionSpec as P

MESH = pl.DeviceIdType.MESH
F32 = jnp.float32
BF16 = jnp.bfloat16
HEADS = 8
LANES = 128
PIECES = 4
EPS = 1e-05
GAIN_ONE, GAIN_TWO, BIAS_OUT, BIAS_ONE, BIAS_DOWN, BIAS_TWO, BIAS_UP = range(7)
STATS = 10
CHUNK = 64
SPLIT = 4
DP_FIRST = (1, 5, 9)
SUM, CORE, SIDE, SIDED, DP, DPED, JOIN, LAST, SMALL = range(9)
ORDER_ONE = (
    (SUM, 0), (SUM, 2),
)
ORDER_TWO = (
    (CORE, 0), (SIDE, 0), (SUM, 4), (CORE, 3), (CORE, 2), (CORE, 1), (SIDE, 3), (SUM, 6), (SIDED, 0),
    (SIDE, 2),
)
ORDER_THREE = (
    (CORE, 4), (SIDED, 3), (CORE, 6), (SIDE, 6), (CORE, 5), (DP, 0), (SIDE, 4), (SUM, 8), (DPED, 0), (DP, 1),
    (SIDED, 2), (CORE, 7), (SIDE, 7), (SUM, 10), (DP, 3), (SIDED, 6), (CORE, 8), (SIDE, 8), (SIDED, 4),
    (DPED, 1), (DP, 2), (CORE, 9), (DP, 6), (DPED, 3), (CORE, 11), (SIDE, 11), (SIDED, 8), (DP, 4),
    (CORE, 10), (SMALL, 0), (DP, 5), (DPED, 6), (JOIN, 1), (JOIN, 3), (SIDED, 7), (DP, 9), (SIDE, 10),
    (SIDED, 11), (DP, 8), (DPED, 4), (DPED, 2), (SIDED, 10), (DP, 7), (DPED, 9), (DP, 11), (JOIN, 6),
    (JOIN, 4), (DPED, 5), (DPED, 8), (DP, 10), (DPED, 7), (SMALL, 1), (LAST, 6), (LAST, 1), (JOIN, 2),
    (DPED, 11), (LAST, 3), (JOIN, 0), (DPED, 10), (JOIN, 7), (JOIN, 8), (JOIN, 11), (JOIN, 9), (JOIN, 5),
    (LAST, 4), (SMALL, 2), (LAST, 0), (JOIN, 10), (LAST, 9), (LAST, 11), (LAST, 5), (LAST, 7), (LAST, 8),
    (LAST, 2), (LAST, 10),
)


def plain_orders():
    one = ((SUM, 0),)
    two = ((SUM, 1), (CORE, 0), (SIDE, 0))
    three = ((SUM, 2), (CORE, 1), (SIDE, 1), (CORE, 2), (SIDE, 2), (SMALL, 0), (SMALL, 1), (SMALL, 2))
    for stage in (SIDED, DP, DPED, JOIN, LAST):
        three += tuple((stage, job) for job in range(3))
    return one, two, three


def dot_plain(left, right):
    return lax.dot_general(left, right, (((1,), (0,)), ((), ())), preferred_element_type=F32)


def drain(parts):
    for _ in parts:
        pass


def side_by_side(one, two):
    spent = [0, 300]
    live = [one, two]
    while live[0] or live[1]:
        which = 0 if live[0] and (not live[1] or spent[0] <= spent[1]) else 1
        cost = next(live[which], None)
        if cost is None:
            live[which] = None
        else:
            spent[which] += cost


def dot_turned(left, right):
    return lax.dot_general(left, right, (((1,), (1,)), ((), ())), preferred_element_type=F32)


def fold(values):
    total = values[:, :LANES]
    for start in range(LANES, values.shape[1], LANES):
        total = total + values[:, start : start + LANES]
    return total


def layer_kernel(
    dp_count,
    flag_ref,
    x_hbm,
    ct_hbm,
    w_qkv_hbm,
    w_out_hbm,
    w_up_hbm,
    w_down_hbm,
    up_bias_ref,
    gains_ref,
    biases_ref,
    ends_hbm,
    fin_hbm,
    small_hbm,
    w_qkv,
    w_out,
    w_up,
    w_down,
    turned,
    rows_in,
    x_t,
    qkv,
    keys_rm,
    values_rm,
    share,
    share_off,
    mixture,
    norm_one,
    norm_two,
    inverses,
    hidden_low,
    slope,
    active,
    down_grad,
    branch_grad,
    grad_mix,
    outgoing,
    incoming_grad,
    columns,
    sums,
    key_sums,
    wide_a,
    wide_b,
    wide_c,
    ends_v,
    core_in,
    side_in,
    dp_in,
    fin,
    small,
    small_dp,
    small_rep,
    small_out,
    load_sem,
    seg_send,
    seg_recv,
    ends_sem,
    core_send,
    core_recv,
    side_send,
    side_recv,
    dp_send,
    dp_recv,
    join_send,
    join_recv,
    last_send,
    last_recv,
    sdp_send,
    sdp_recv,
    srep_send,
    srep_recv,
    fin_sem,
):
    width = w_out.shape[0]
    piece = x_t.shape[1] // PIECES
    pairs = qkv.shape[1]
    share_rows = width // dp_count
    dp_steps = dp_count.bit_length() - 1
    segment = lax.axis_index("segment")
    dp = lax.axis_index("dp")
    rep = lax.axis_index("rep")
    core = lax.rem(rep, 2)
    side = lax.div(rep, 2)
    other_core = side * 2 + (1 - core)
    other_side = (1 - side) * 2 + core

    def load_copy(block):
        def span(first):
            return pl.ds(pl.multiple_of((block - first) * width, width), width)

        def copy_of(source, target):
            return pltpu.make_async_copy(source, target, load_sem.at[1 + block])

        return (
            lambda: copy_of(w_qkv_hbm.at[0, :, span(0)], w_qkv.at[:, span(0)]),
            lambda: copy_of(w_out_hbm.at[0], w_out),
            lambda: copy_of(w_up_hbm.at[0, :, span(4)], w_up.at[:, span(4)]),
            lambda: copy_of(w_down_hbm.at[0, span(8), :], w_down.at[block - 8]),
        )

    parts_of_load = ((0, 3), (3, 4), (4, 8), (8, 12))
    first_rows = pltpu.make_async_copy(x_hbm, rows_in, load_sem.at[0])
    last_rows = pltpu.make_async_copy(ct_hbm, rows_in, load_sem.at[0])

    @pl.when(segment == 0)
    def _():
        first_rows.start()

    @pl.when(segment == 1)
    def _():
        last_rows.start()

    for part, (first, after) in enumerate(parts_of_load):
        for block in range(first, after):
            load_copy(block)[part]().start()

    barrier = pltpu.get_barrier_semaphore()
    pl.semaphore_signal(
        barrier, inc=1, device_id={"segment": 1 - segment}, device_id_type=MESH
    )
    for step in range(1, 4):
        pl.semaphore_signal(
            barrier, inc=1, device_id={"rep": lax.rem(rep + step, 4)}, device_id_type=MESH
        )
    for step in range(1, dp_count):
        pl.semaphore_signal(
            barrier, inc=1, device_id={"dp": lax.rem(dp + step, dp_count)}, device_id_type=MESH
        )

    params = [gains_ref[0].astype(F32), biases_ref[0].astype(F32)]
    for block in range(4):
        params.append(up_bias_ref[:, block * width : (block + 1) * width].astype(F32))
    params.append(jnp.zeros((16 - STATS, width), F32))
    upright = jnp.concatenate(params, axis=0).T
    for index in range(STATS):
        columns[index] = jnp.broadcast_to(upright[:, index : index + 1], (width, LANES)).astype(BF16)
    for index in range(STATS):
        sums[index] = jnp.zeros((width, LANES), F32)
    key_sums[0] = jnp.zeros(key_sums.shape[1:], F32)

    chunks = [slice(start, start + CHUNK) for start in range(0, width, CHUNK)]

    def turn(part):
        def one(block, carry):
            load_copy(block)[part]().wait()
            if part == 3:
                turned[block] = w_down[block - 8].T
            elif part == 1:
                turned[block] = w_out[...].T
            else:
                first = parts_of_load[part][0]
                span = pl.ds(pl.multiple_of((block - first) * width, width), width)
                turned[block] = (w_qkv if part == 0 else w_up)[:, span].T
            return carry

        lax.fori_loop(*parts_of_load[part], one, 0)

    def turn_apart(first, after):
        for block in range(first, after):
            part = (0, 0, 0, 1, 2, 2, 2, 2, 3, 3, 3, 3)[block]
            load_copy(block)[part]().wait()
            span = slice(block % 4 * width, (block % 4 + 1) * width)
            if part == 0:
                turned[block] = w_qkv[:, span].T
            elif part == 1:
                turned[block] = w_out[...].T
            elif part == 2:
                turned[block] = w_up[:, span].T
            else:
                turned[block] = w_down[block - 8].T
            yield 230

    first_rows.wait()

    flag = flag_ref[0, 0].astype(F32)

    def lanes_of(index):
        if isinstance(index, int):
            return pl.ds(index * piece, piece)
        return pl.ds(pl.multiple_of(index * piece, piece), piece)

    def forward_copy(index):
        return pltpu.make_async_remote_copy(
            src_ref=outgoing.at[index],
            dst_ref=x_t.at[:, lanes_of(index)],
            send_sem=seg_send.at[index],
            recv_sem=seg_recv.at[index],
            device_id={"segment": 1 - segment},
            device_id_type=MESH,
        )

    def backward_copy(index):
        return pltpu.make_async_remote_copy(
            src_ref=outgoing.at[index],
            dst_ref=incoming_grad.at[index],
            send_sem=seg_send.at[index],
            recv_sem=seg_recv.at[index],
            device_id={"segment": 1 - segment},
            device_id_type=MESH,
        )

    def ends_copy(index):
        return pltpu.make_async_copy(
            ends_v.at[lax.rem(index, 2)], ends_hbm.at[index], ends_sem.at[index]
        )

    def free_ends(index):
        @pl.when(index >= 2)
        def _():
            ends_copy(index - 2).wait()

    def own_rows(index):
        half = lax.rem(index, 2)
        whole = jnp.where(index < 2, 1.0, 0.0).astype(F32)
        weight = whole * flag + (1.0 - whole) * (1.0 - flag)
        picked = rows_in[half].astype(F32) * weight + rows_in[2 + half].astype(F32) * (1.0 - weight)
        return picked.T

    def by_queries(values):
        half = LANES // 2
        blank = jnp.zeros((half, LANES), values.dtype)
        parts = []
        for part in range(2):
            span = slice(part * LANES, (part + 1) * LANES)
            first = jnp.concatenate([values[:half, span], blank], axis=0)
            second = jnp.concatenate([blank, values[half:, span]], axis=0)
            parts.append(jnp.concatenate([first, second], axis=1))
        return parts

    def against(rows_ref, index, pair, parts, has_off):
        own = rows_ref[index, pair]
        products = [dot_plain(own[:LANES], parts[0]), dot_plain(own, parts[1])]
        if has_off:
            before = rows_ref[0, pair]
            products += [dot_plain(before, parts[0]), dot_plain(before, parts[1])]
        return products

    def tiles_of(products, head, part, has_off):
        lanes = slice(head * LANES, (head + 1) * LANES)
        own = products[part]
        tiles = [own[part * LANES : (part + 1) * LANES, lanes]]
        if part:
            tiles.append(own[:LANES, lanes])
        if has_off:
            off = products[2 + part]
            tiles += [off[:LANES, lanes], off[LANES:, lanes]]
        return tiles

    def joined(lows, has_off):
        blank = jnp.zeros((LANES, LANES), BF16)
        first = jnp.concatenate([lows[0][0], blank], axis=0)
        second = jnp.concatenate([lows[1][1], lows[1][0]], axis=0)
        whole = jnp.concatenate([first, second], axis=1)
        if not has_off:
            return whole, None
        first = jnp.concatenate(lows[0][-2:], axis=0)
        second = jnp.concatenate(lows[1][-2:], axis=0)
        return whole, jnp.concatenate([first, second], axis=1)

    def attend(index, has_off):
        lanes = lanes_of(index)
        half = LANES // 2
        key_at = lax.broadcasted_iota(jnp.int32, (LANES, LANES), 0)
        query_at = lax.broadcasted_iota(jnp.int32, (LANES, LANES), 1)
        allowed = key_at <= query_at

        def scores_of(pair):
            return against(
                keys_rm, index, pair, by_queries(qkv[0, pair, :, lanes]), has_off
            )

        ahead = scores_of(0)
        for pair in range(pairs):
            scores = ahead
            if pair + 1 < pairs:
                ahead = scores_of(pair + 1)
            mixed = []
            for head in range(2):
                rows = slice(head * half, (head + 1) * half)
                lows = []
                for part in range(2):
                    tiles = tiles_of(scores, head, part, has_off)
                    tiles[0] = jnp.where(allowed, tiles[0], -1e30)
                    top = jnp.max(functools.reduce(jnp.maximum, tiles), axis=0, keepdims=True)
                    raised = [jnp.exp(tile - top) for tile in tiles]
                    total = functools.reduce(jnp.add, raised)
                    scale = 1.0 / jnp.sum(total, axis=0, keepdims=True)
                    lows.append([(tile * scale).astype(BF16) for tile in raised])
                low, low_off = joined(lows, has_off)
                share[index, pair, head] = low
                mix = dot_plain(qkv[2, pair, rows, lanes], low)
                if has_off:
                    share_off[pair, head] = low_off
                    mix = mix + dot_plain(qkv[2, pair, rows, :piece], low_off)
                mixed.append(mix.astype(BF16))
            mixture[pair, :, lanes] = jnp.concatenate(mixed, axis=0)
            yield 280

    def part_sum(values):
        return jnp.sum(values.reshape(values.shape[0] // 8, 8, values.shape[1]), axis=0)

    def full_mean(parts):
        return jnp.sum(parts, axis=0, keepdims=True) * (1.0 / width)

    def column(index, rows):
        part = columns[index, rows, :].astype(F32)
        return jnp.concatenate([part] * (piece // LANES), axis=1)

    def gather_sum(index, rows, values):
        sums[index, rows, :] = sums[index, rows, :] + fold(values)

    def norm_chunks(index, which, wide_a, total):
        mean = full_mean(total)
        spread = jnp.zeros((8, piece), F32)
        for rows in chunks:
            centred = wide_a[rows, :] - mean
            spread = spread + part_sum(centred * centred)
        inverse = lax.rsqrt(full_mean(spread) + EPS)
        inverses[index, which] = inverse
        return mean, inverse

    def forward_start(index):
        @pl.when(segment == 0)
        def _():
            x_t[:, lanes_of(index)] = own_rows(index).astype(BF16)

        @pl.when(segment == 1)
        def _():
            forward_copy(index).wait_recv()

    def forward_first(index):
        lanes = lanes_of(index)
        inputs = x_t[:, lanes]
        score_scale = 1.0 / math.sqrt(width // HEADS)
        for block in range(3):
            result = dot_plain(turned[block], inputs)
            for pair in range(pairs):
                low = result[pair * LANES : (pair + 1) * LANES]
                low = (low * score_scale if block == 0 else low).astype(BF16)
                qkv[block, pair, :, lanes] = low
                if block == 1:
                    keys_rm[index, pair] = low.T
                if block == 2:
                    values_rm[index, pair] = low.T
            yield 270

    def forward_rest(index, wide_a):
        lanes = lanes_of(index)
        branch = dot_plain(turned[3], mixture[:, :, lanes].reshape(width, piece))
        yield 250
        total = jnp.zeros((8, piece), F32)
        for rows in chunks:
            sum_one = x_t[rows, lanes].astype(F32) + (branch[rows] + column(BIAS_OUT, rows))
            wide_a[rows, :] = sum_one
            total = total + part_sum(sum_one)
            yield 25
        mean, inverse = norm_chunks(index, 0, wide_a, total)
        yield 150
        for rows in chunks:
            normed = (wide_a[rows, :] - mean) * inverse
            norm_one[rows, lanes] = normed
            hidden = normed * column(GAIN_ONE, rows) + column(BIAS_ONE, rows)
            hidden_low[rows, lanes] = hidden.astype(BF16)
            yield 30

        branch_two = None
        for block in range(4):
            pre_block = dot_plain(turned[4 + block], hidden_low[:, lanes])
            yield 50
            lows = []
            for rows in chunks:
                pre = pre_block[rows] + column(BIAS_UP + block, rows)
                level = (lax.erf(pre * (1.0 / math.sqrt(2.0))) + 1.0) * 0.5
                bell = jnp.exp2(pre * pre * (-0.5 * math.log2(math.e)))
                lows.append((pre * level).astype(BF16))
                active[block, rows, lanes] = lows[-1]
                slope[block, rows, lanes] = (
                    level + pre * bell * (1.0 / math.sqrt(2.0 * math.pi))
                ).astype(BF16)
                yield 65
            part = dot_plain(turned[8 + block], jnp.concatenate(lows, axis=0))
            branch_two = part if branch_two is None else branch_two + part
            yield 100
        total = jnp.zeros((8, piece), F32)
        for rows in chunks:
            hidden = norm_one[rows, lanes] * column(GAIN_ONE, rows) + column(BIAS_ONE, rows)
            sum_two = hidden + (branch_two[rows] + column(BIAS_DOWN, rows))
            wide_a[rows, :] = sum_two
            total = total + part_sum(sum_two)
            yield 25
        mean, inverse = norm_chunks(index, 1, wide_a, total)
        yield 150
        for rows in chunks:
            norm_two[rows, lanes] = (wide_a[rows, :] - mean) * inverse
            yield 20

    def forward_end(index):
        for rows in chunks:
            outgoing[index, rows, :] = output_rows(rows, lanes_of(index)).astype(BF16)
        forward_copy(index).start()

    def off_or_not(index, run):
        @pl.when(index == 1)
        def _():
            drain(run(index, True))

        @pl.when(index != 1)
        def _():
            drain(run(index, False))

    def forward(index):
        forward_start(index)
        drain(forward_first(index))
        off_or_not(index, attend)
        drain(forward_rest(index, wide_a))

        @pl.when(segment == 0)
        def _():
            forward_end(index)

    def output_rows(rows, lanes):
        return norm_two[rows, lanes] * column(GAIN_TWO, rows) + column(BIAS_TWO, rows)

    def last_outputs(index, carry):
        free_ends(index)
        for start in range(0, width, LANES):
            rows = slice(start, start + LANES)
            ends_v[lax.rem(index, 2), :, rows] = output_rows(rows, lanes_of(index)).T
        ends_copy(index).start()
        return carry

    def attend_back(index, has_off):
        lanes = lanes_of(index)
        slot = (1 if index == 0 else 0) if isinstance(index, int) else jnp.where(index == 0, 1, 0)
        half = LANES // 2
        score_scale = 1.0 / math.sqrt(width // HEADS)

        def backs_of(pair):
            return against(values_rm, index, pair, by_queries(grad_mix[pair]), has_off)

        ahead = backs_of(0)
        for pair in range(pairs):
            backs = ahead
            if pair + 1 < pairs:
                ahead = backs_of(pair + 1)
            results = ([], [], [])
            for head in range(2):
                rows = slice(head * half, (head + 1) * half)
                low = share[index, pair, head]
                low_off = share_off[pair, head] if has_off else None
                lows = []
                for part in range(2):
                    place = slice(part * LANES, (part + 1) * LANES)
                    wides = [low[place, place]]
                    if part:
                        wides.append(low[:LANES, place])
                    if has_off:
                        wides += [low_off[:LANES, place], low_off[LANES:, place]]
                    wides = [tile.astype(F32) for tile in wides]
                    tiles = tiles_of(backs, head, part, has_off)
                    products = [wide * tile for wide, tile in zip(wides, tiles)]
                    inner = jnp.sum(functools.reduce(jnp.add, products), axis=0, keepdims=True)
                    lows.append(
                        [
                            (product - wide * inner).astype(BF16)
                            for product, wide in zip(products, wides)
                        ]
                    )
                grad_scores, grad_off = joined(lows, has_off)
                queries = qkv[0, pair, rows, lanes]
                grads = grad_mix[pair, rows]
                grad_query = dot_plain(qkv[1, pair, rows, lanes], grad_scores)
                grad_key = dot_turned(queries, grad_scores) + key_sums[slot, 0, pair, rows]
                grad_value = dot_turned(grads, low) + key_sums[slot, 1, pair, rows]
                if has_off:
                    grad_query = grad_query + dot_plain(qkv[1, pair, rows, :piece], grad_off)
                    key_sums[1, 0, pair, rows] = dot_turned(queries, grad_off)
                    key_sums[1, 1, pair, rows] = dot_turned(grads, low_off)
                for kept, grad in zip(results, (grad_query * score_scale, grad_key, grad_value)):
                    kept.append(grad.astype(BF16))
            for block in range(3):
                qkv[block, pair, :, lanes] = jnp.concatenate(results[block], axis=0)
            yield 440

    def backward_start(index):
        @pl.when(segment == 0)
        def _():
            backward_copy(index).wait_recv()

    def backward_norm(index):
        lanes = lanes_of(index)
        plain = jnp.zeros((8, piece), F32)
        inner = jnp.zeros((8, piece), F32)
        for rows in chunks:
            grad = incoming_grad[index, rows, :].astype(F32)
            product = grad * norm_two[rows, lanes]
            gather_sum(GAIN_TWO, rows, product)
            gather_sum(BIAS_TWO, rows, grad)
            gain = column(GAIN_TWO, rows)
            plain = plain + part_sum(grad * gain)
            inner = inner + part_sum(product * gain)
            yield 40
        plain = full_mean(plain)
        inner = full_mean(inner)
        inverse = inverses[index, 1]
        for rows in chunks:
            scaled = incoming_grad[index, rows, :].astype(F32) * column(GAIN_TWO, rows)
            grad_two = (scaled - plain - norm_two[rows, lanes] * inner) * inverse
            gather_sum(BIAS_DOWN, rows, grad_two)
            wide_a[rows, :] = grad_two
            down_grad[rows, lanes] = grad_two.astype(BF16)
            yield 40

    def backward_feed(index):
        lanes = lanes_of(index)
        for block in range(4):
            back = dot_plain(w_down[block], down_grad[:, lanes])
            for rows in chunks:
                grad_pre = back[rows] * slope[block, rows, lanes].astype(F32)
                gather_sum(BIAS_UP + block, rows, grad_pre)
                slope[block, rows, lanes] = grad_pre.astype(BF16)
            yield 250

        through = dot_plain(w_up[...], slope[:, :, lanes].reshape(4 * width, piece))
        plain = jnp.zeros((8, piece), F32)
        inner = jnp.zeros((8, piece), F32)
        for rows in chunks:
            grad_hidden = wide_a[rows, :] + through[rows]
            wide_a[rows, :] = grad_hidden
            product = grad_hidden * norm_one[rows, lanes]
            gather_sum(GAIN_ONE, rows, product)
            gather_sum(BIAS_ONE, rows, grad_hidden)
            gain = column(GAIN_ONE, rows)
            plain = plain + part_sum(grad_hidden * gain)
            inner = inner + part_sum(product * gain)
            yield 120 if rows.start == 0 else 45
        plain = full_mean(plain)
        inner = full_mean(inner)
        inverse = inverses[index, 0]
        for rows in chunks:
            scaled = wide_a[rows, :] * column(GAIN_ONE, rows)
            grad_one = (scaled - plain - norm_one[rows, lanes] * inner) * inverse
            gather_sum(BIAS_OUT, rows, grad_one)
            wide_b[rows, :] = grad_one
            branch_grad[rows, lanes] = grad_one.astype(BF16)
            yield 40
        grad_mix[...] = (
            dot_plain(w_out[...], branch_grad[:, lanes]).astype(BF16).reshape(pairs, LANES, piece)
        )
        yield 300

    def backward_attention(index):
        off_or_not(index, attend_back)
        through = dot_plain(w_qkv[...], qkv[:, :, :, lanes_of(index)].reshape(3 * width, piece))

        @pl.when(segment == 1)
        def _():
            for rows in chunks:
                outgoing[index, rows, :] = (wide_b[rows, :] + through[rows]).astype(BF16)
            backward_copy(index).start()

        @pl.when(segment == 0)
        def _():
            free_ends(index)
            for start in range(0, width, LANES):
                rows = slice(start, start + LANES)
                ends_v[lax.rem(index, 2), :, rows] = (wide_b[rows, :] + through[rows]).T
            ends_copy(index).start()

    def backward_both(index, forward_index):
        forward_copy(forward_index).wait_recv()

        def back():
            yield from backward_norm(index)
            yield from backward_feed(index)
            yield from attend_back(index, False)
            through = dot_plain(w_qkv[...], qkv[:, :, :, lanes_of(index)].reshape(3 * width, piece))
            for rows in chunks:
                outgoing[index, rows, :] = (wide_b[rows, :] + through[rows]).astype(BF16)
                yield 90

        def ahead():
            yield from forward_first(forward_index)
            yield from attend(forward_index, False)
            yield from forward_rest(forward_index, wide_c)

        side_by_side(back(), ahead())
        backward_copy(index).start()

    split = SPLIT if share_rows % (16 * SPLIT) == 0 else 1
    dp_first = DP_FIRST if split == SPLIT else ()
    orders = (ORDER_ONE, ORDER_TWO, ORDER_THREE) if split == SPLIT else plain_orders()
    jobs = 3 * split
    cut_rows = share_rows // split
    job_rows = width // split

    def base_of(job):
        return (8, 4, 0)[job // split]

    def job_span(job):
        return pl.ds(job % split * job_rows, job_rows)

    def fin_rows(job):
        return pl.ds(job % split * cut_rows, cut_rows)

    def parts_of(job):
        return range(2) if job in dp_first else range(1)

    def core_copies(job):
        return [
            pltpu.make_async_remote_copy(
                src_ref=turned.at[base_of(job) + 2 * (1 - core) + each, job_span(job)],
                dst_ref=core_in.at[job // split, each, job_span(job)],
                send_sem=core_send.at[job, each],
                recv_sem=core_recv.at[job, each],
                device_id={"rep": other_core},
                device_id_type=MESH,
            )
            for each in range(2)
        ]

    def side_copies(job):
        base = base_of(job)
        copies = []
        for each in parts_of(job):
            if job in dp_first:
                source = turned.at[base + 2 * core + each, dp_rows(job, dp_steps - 1)[1]]
                target = side_in.at[
                    job // split, pl.ds(job % split * job_rows + each * cut_rows, cut_rows)
                ]
            else:
                source = turned.at[base + 2 * core + (1 - side), job_span(job)]
                target = side_in.at[job // split, job_span(job)]
            copies.append(
                pltpu.make_async_remote_copy(
                    src_ref=source,
                    dst_ref=target,
                    send_sem=side_send.at[job, each],
                    recv_sem=side_recv.at[job, each],
                    device_id={"rep": other_side},
                    device_id_type=MESH,
                )
            )
        return copies

    def dp_slot(job):
        return sum(len(parts_of(before)) for before in range(job))

    def dp_rows(job, step):
        count = dp_count // 2
        start = 0
        for bit in range(step):
            start = start + lax.rem(lax.div(dp, 2**bit), 2) * count
            count = count // 2
        mine = lax.rem(lax.div(dp, 2**step), 2)
        first = job % split * job_rows
        sent = pl.multiple_of(first + (start + (1 - mine) * count) * cut_rows, cut_rows)
        kept = pl.multiple_of(first + (start + mine * count) * cut_rows, cut_rows)
        return pl.ds(sent, count * cut_rows), pl.ds(kept, count * cut_rows)

    def dp_landing(step):
        count = dp_count // 2 ** (step + 1)
        return pl.ds((dp_count - 2 * count) * cut_rows, count * cut_rows)

    def dp_copies(job, step):
        mine = lax.rem(lax.div(dp, 2**step), 2)
        copies = []
        for each in parts_of(job):
            position = base_of(job) + 2 * core + (each if job in dp_first else side)
            copies.append(
                pltpu.make_async_remote_copy(
                    src_ref=turned.at[position, dp_rows(job, step)[0]],
                    dst_ref=dp_in.at[dp_slot(job) + each, dp_landing(step)],
                    send_sem=dp_send.at[job, step, each],
                    recv_sem=dp_recv.at[job, step, each],
                    device_id={"dp": dp + (1 - 2 * mine) * 2**step},
                    device_id_type=MESH,
                )
            )
        return copies

    def join_copy(job):
        part = fin.at[job // split, 2 * core + side, fin_rows(job)]
        return pltpu.make_async_remote_copy(
            src_ref=part,
            dst_ref=part,
            send_sem=join_send.at[job],
            recv_sem=join_recv.at[job],
            device_id={"rep": other_side},
            device_id_type=MESH,
        )

    def last_copies(job):
        copies = []
        for each in range(2):
            part = fin.at[job // split, 2 * core + each, fin_rows(job)]
            copies.append(
                pltpu.make_async_remote_copy(
                    src_ref=part,
                    dst_ref=part,
                    send_sem=last_send.at[job, each],
                    recv_sem=last_recv.at[job, each],
                    device_id={"rep": other_core},
                    device_id_type=MESH,
                )
            )
        return copies

    def fin_copy(job):
        return pltpu.make_async_copy(
            fin.at[job // split, :, fin_rows(job)],
            fin_hbm.at[job // split, :, fin_rows(job)],
            fin_sem.at[job],
        )

    def arrived(*copies):
        for copy in copies:
            copy.wait_send()
        for copy in copies:
            copy.wait_recv()

    def start_all(copies):
        for copy in copies:
            copy.start()

    def turned_bits(value, count):
        place = 0
        while count > 1:
            place = place * 2 + value % 2
            value = value // 2
            count = count // 2
        return place

    pack = min(2, split)

    def left_rows(source, part):
        count = pack * cut_rows
        start = part * pack * cut_rows
        return jnp.concatenate(
            [source(index * share_rows + start, count) for index in range(dp_count)], axis=0
        )

    def keep_rows(block, part, result):
        for index in range(dp_count):
            for each in range(pack):
                target = (part * pack + each) * job_rows + turned_bits(index, dp_count) * cut_rows
                start = (index * pack + each) * cut_rows
                turned[block, target : target + cut_rows, :] = result[start : start + cut_rows]

    def down_sums(part):
        count = width // (4 * share_rows)

        def one(block, carry):
            pieces = []
            for each in range(4 * count):
                start = each * share_rows + part * pack * cut_rows
                pieces.append(active[block, start : start + pack * cut_rows, :])
            result = dot_turned(jnp.concatenate(pieces, axis=0), down_grad[...]).astype(BF16)
            high = lax.rem(block, 2) * 2 + lax.div(block, 2)
            for each in range(count):
                place = turned_bits(each, count) * 4 + high
                for position in range(4):
                    for job in range(pack):
                        target = (part * pack + job) * job_rows + place * cut_rows
                        start = ((each * 4 + position) * pack + job) * cut_rows
                        turned[
                            8 + position, pl.ds(pl.multiple_of(target, cut_rows), cut_rows), :
                        ] = result[start : start + cut_rows]
            return carry

        lax.fori_loop(0, 4, one, 0)

    def up_sums(part):
        def one(block, carry):
            left = left_rows(lambda start, count: hidden_low[start : start + count, :], part)
            keep_rows(4 + block, part, dot_turned(left, slope[block]).astype(BF16))
            return carry

        lax.fori_loop(0, 4, one, 0)

    def qkv_sums(part):
        def one(block, carry):
            left = left_rows(lambda start, count: x_t[start : start + count, :], part)
            grads = qkv[block].reshape(width, PIECES * piece)
            keep_rows(block, part, dot_turned(left, grads).astype(BF16))
            return carry

        lax.fori_loop(0, 3, one, 0)
        left = left_rows(
            lambda start, count: mixture[start // LANES, start % LANES : start % LANES + count, :], part
        )
        keep_rows(3, part, dot_turned(left, branch_grad[...]).astype(BF16))

    def sums_of(job):
        (down_sums, up_sums, qkv_sums)[job // split](job % split // pack)
        for each in range(pack):
            start_all(core_copies(job + each))

    def after_core(job):
        arrived(*core_copies(job))
        rows = job_span(job)
        for each in parts_of(job):
            place = 1 - side if each == 0 else side
            position = base_of(job) + 2 * core + place
            turned[position, rows, :] = (
                turned[position, rows, :].astype(F32)
                + core_in[job // split, place, rows, :].astype(F32)
            ).astype(BF16)
        if job in dp_first:
            start_all(dp_copies(job, 0))

    def start_side(job):
        start_all(side_copies(job))

    def after_side(job):
        arrived(*side_copies(job))
        rows = job_span(job)
        position = base_of(job) + 2 * core + side
        turned[position, rows, :] = (
            turned[position, rows, :].astype(F32)
            + core_in[job // split, side, rows, :].astype(F32)
            + side_in[job // split, rows, :].astype(F32)
        ).astype(BF16)
        start_all(dp_copies(job, 0))

    def dp_total(job, step, each):
        position = base_of(job) + 2 * core + (each if job in dp_first else side)
        kept = turned[position, dp_rows(job, step)[1], :].astype(F32)
        return position, kept + dp_in[dp_slot(job) + each, dp_landing(step), :].astype(F32)

    def after_dp(job):
        for step in range(dp_steps - 1):
            arrived(*dp_copies(job, step))
            for each in parts_of(job):
                position, total = dp_total(job, step, each)
                turned[position, dp_rows(job, step)[1], :] = total.astype(BF16)
            start_all(dp_copies(job, step + 1))

    def after_last_dp(job):
        step = dp_steps - 1
        arrived(*dp_copies(job, step))
        for each in parts_of(job):
            position, total = dp_total(job, step, each)
            if job in dp_first:
                turned[position, dp_rows(job, step)[1], :] = total.astype(BF16)
            else:
                fin[job // split, 2 * core + side, fin_rows(job), :] = total.astype(BF16)
        if job in dp_first:
            start_side(job)
        else:
            join_copy(job).start()

    def after_join(job):
        if job in dp_first:
            arrived(*side_copies(job))
            for each in range(2):
                rows = pl.ds(job % split * job_rows + each * cut_rows, cut_rows)
                own = turned[base_of(job) + 2 * core + each, dp_rows(job, dp_steps - 1)[1], :]
                total = own.astype(F32) + side_in[job // split, rows, :].astype(F32)
                fin[job // split, 2 * core + each, fin_rows(job), :] = total.astype(BF16)
        else:
            arrived(join_copy(job))
        start_all(last_copies(job))

    def after_last(job):
        arrived(*last_copies(job))
        fin_copy(job).start()

    def small_dp_copy(step):
        target = lax.rem(dp + step, dp_count)
        return pltpu.make_async_remote_copy(
            src_ref=small.at[target],
            dst_ref=small_dp.at[step - 1],
            send_sem=sdp_send.at[step - 1],
            recv_sem=sdp_recv.at[step - 1],
            device_id={"dp": target},
            device_id_type=MESH,
        )

    def small_rep_copy(step):
        return pltpu.make_async_remote_copy(
            src_ref=small_rep.at[rep],
            dst_ref=small_rep.at[rep],
            send_sem=srep_send.at[step - 1],
            recv_sem=srep_recv.at[step - 1],
            device_id={"rep": lax.rem(rep + step, 4)},
            device_id_type=MESH,
        )

    small_copy = pltpu.make_async_copy(small_out, small_hbm, load_sem.at[0])

    def small_step(stage):
        if stage == 0:
            rows_of = [jnp.sum(sums[index].T, axis=0, keepdims=True) for index in range(STATS)]
            small[...] = jnp.zeros(small.shape, F32)
            for share_index in range(dp_count):
                for index in range(BIAS_UP):
                    start = share_index * share_rows
                    small[share_index, index : index + 1, :share_rows] = rows_of[index][
                        :, start : start + share_rows
                    ]
                for part in range(4):
                    start = (share_index * 4 + part) * share_rows
                    block, start = start // width, start % width
                    small[share_index, BIAS_UP + part : BIAS_UP + part + 1, :share_rows] = rows_of[
                        BIAS_UP + block
                    ][:, start : start + share_rows]
            for step in range(1, dp_count):
                small_dp_copy(step).start()
        elif stage == 1:
            total = small[dp]
            for step in range(1, dp_count):
                arrived(small_dp_copy(step))
                total = total + small_dp[step - 1]
            small_rep[rep] = total
            for step in range(1, 4):
                small_rep_copy(step).start()
        else:
            for step in range(1, 4):
                arrived(small_rep_copy(step))
            small_out[...] = (small_rep[0] + small_rep[1]) + (small_rep[2] + small_rep[3])
            small_copy.start()

    def run(order):
        steps = (
            sums_of,
            after_core,
            start_side,
            after_side,
            after_dp,
            after_last_dp,
            after_join,
            after_last,
            small_step,
        )
        for stage, job in order:
            steps[stage](job)

    def one_step(step, carry):
        first_index = jnp.where(step < 4, step, jnp.where(step < 6, 5 - step, step - 4))
        last_index = jnp.where(step < 2, step, jnp.where(step == 2, 1, 3))
        index = jnp.minimum(jnp.where(segment == 0, first_index, last_index), PIECES - 1)
        is_last = jnp.where(step == 2 * PIECES, 1, 0)
        begun = jnp.where(step + segment == 0, 0, 1)
        is_forward = jnp.where(step < jnp.where(segment == 0, 4, 2), begun, 0)
        last_backward = jnp.where(step == 2, 1, 0) + jnp.where(step == 5, 1, 0)
        is_backward = jnp.where(segment == 0, begun * (1 - is_forward) * (1 - is_last), last_backward)
        is_split = jnp.where(step >= 2 * PIECES - 1, 1 - segment, 0)
        is_rest = is_backward * (1 - is_split) + is_last * is_split

        @pl.when(is_forward == 1)
        def _():
            forward(index)

        @pl.when(is_backward == 1)
        def _():
            backward_start(index)
            drain(backward_norm(index))

        @pl.when(segment * lax.div(step, 3) * (5 - jnp.minimum(step, 5)) >= 1)
        def _():
            backward_both(2 * step - 6, step - 1)

        @pl.when(is_last == 1)
        def _():
            run(orders[0])

        @pl.when(is_rest == 1)
        def _():
            drain(backward_feed(index))

        @pl.when(is_last == 1)
        def _():
            run(orders[1])

        @pl.when(is_rest == 1)
        def _():
            backward_attention(index)

        return carry

    @pl.when(segment == 1)
    def _():
        for part in range(4):
            turn(part)
        for index in range(PIECES):
            incoming_grad[index] = own_rows(index).astype(BF16)

    @pl.when(segment == 0)
    def _():
        def ahead():
            x_t[:, lanes_of(0)] = own_rows(0).astype(BF16)
            yield from forward_first(0)
            yield from attend(0, False)
            yield from forward_rest(0, wide_a)

        drain(turn_apart(0, 4))
        side_by_side(ahead(), turn_apart(4, 12))

    pl.semaphore_wait(barrier, 4 + dp_count - 1)

    @pl.when(segment == 0)
    def _():
        forward_end(0)

    lax.fori_loop(0, 2 * PIECES + 1, one_step, 0)

    cut = orders[2].index((SMALL, 0))
    run(orders[2][:cut])

    @pl.when(segment == 1)
    def _():
        lax.fori_loop(0, PIECES, last_outputs, 0)

    run(orders[2][cut:])

    for index in range(PIECES):

        @pl.when(segment == 0)
        def _():
            forward_copy(index).wait_send()

        @pl.when(segment == 1)
        def _():
            backward_copy(index).wait_send()

    for index in range(2, PIECES):
        ends_copy(index).wait()
    for job in range(jobs):
        fin_copy(job).wait()
    small_copy.wait()


def finish_kernel(
    flag_ref,
    ends_in,
    fin,
    small,
    ends,
    grad_qkv,
    grad_out,
    grad_up,
    grad_down,
    grad_up_bias,
    grad_gains,
    grad_biases,
    ends_v,
    fin_v,
    wide_qkv,
    wide_out,
    wide_up,
    wide_down,
    small_v,
    up_bias_v,
    gains_v,
    biases_v,
    ends_sem,
    in_sem,
    out_sem,
):
    half = ends_in.shape[0] // 2
    share_rows, width = fin.shape[2:]
    start = pl.multiple_of(half * (1 - flag_ref[0, 0]), half)
    cut = half // 4
    ends_copies = []
    ends_loads = []
    for part in range(8):
        source = pl.ds(part * cut, cut)
        offset = start + part * cut if part < 4 else part * cut - half + (half - start)
        target = pl.ds(pl.multiple_of(offset, cut), cut)
        ends_loads.append(
            pltpu.make_async_copy(ends_in.at[source], ends_v.at[source], ends_sem.at[part])
        )
        ends_copies.append(
            pltpu.make_async_copy(ends_v.at[source], ends.at[0, target], ends_sem.at[8 + part])
        )
    loads = [
        pltpu.make_async_copy(fin.at[group], fin_v.at[group], in_sem.at[group])
        for group in range(3)
    ]
    stores = [
        pltpu.make_async_copy(wide, target.at[0], out_sem.at[index])
        for index, (wide, target) in enumerate(
            ((wide_down, grad_down), (wide_up, grad_up), (wide_qkv, grad_qkv), (wide_out, grad_out))
        )
    ]
    small_load = pltpu.make_async_copy(small, small_v, in_sem.at[3])
    small_stores = [
        pltpu.make_async_copy(narrow, target, out_sem.at[4 + index])
        for index, (narrow, target) in enumerate(
            ((up_bias_v, grad_up_bias), (gains_v, grad_gains), (biases_v, grad_biases))
        )
    ]
    small_load.start()
    for copy in loads + ends_loads:
        copy.start()
    for load, copy in zip(ends_loads, ends_copies):
        load.wait()
        copy.start()
    loads[0].wait()
    for position in range(4):
        rows = slice(position * share_rows, (position + 1) * share_rows)
        wide_down[rows, :] = fin_v[0, position].astype(F32)
    stores[0].start()
    loads[1].wait()
    for position in range(4):
        wide_up[:, position * width : (position + 1) * width] = fin_v[1, position].astype(F32)
    stores[1].start()
    loads[2].wait()
    for position in range(3):
        wide_qkv[:, position * width : (position + 1) * width] = fin_v[2, position].astype(F32)
    stores[2].start()
    wide_out[...] = fin_v[2, 3].astype(F32)
    stores[3].start()
    small_load.wait()
    for position in range(4):
        rows = slice(position * share_rows, (position + 1) * share_rows)
        up_bias_v[:, rows] = small_v[BIAS_UP + position : BIAS_UP + position + 1, :share_rows]
    gains_v[0] = small_v[:2, :share_rows]
    biases_v[0] = small_v[2:BIAS_UP, :share_rows]
    for copy in small_stores:
        copy.start()
    for copy in stores + ends_copies + small_stores:
        copy.wait()


def on_device(
    dp_count,
    block_input,
    cotangent,
    window_group,
    w_qkv,
    w_out,
    w_up,
    w_down,
    up_bias,
    norm_gains,
    biases,
):
    rows, width = block_input.shape
    piece = rows // PIECES
    pairs = width // LANES
    share_rows = width // dp_count
    small_width = max(share_rows, LANES)
    dp_steps = dp_count.bit_length() - 1
    split = SPLIT if share_rows % (16 * SPLIT) == 0 else 1
    jobs = 3 * split
    slots = jobs + (len(DP_FIRST) if split == SPLIT else 0)
    any_spec = pl.BlockSpec(memory_space=pl.ANY)
    vmem_spec = pl.BlockSpec(memory_space=pltpu.VMEM)
    smem_spec = pl.BlockSpec(memory_space=pltpu.SMEM)
    dma = pltpu.SemaphoreType.DMA
    vmem = pltpu.VMEM
    ends_in, fin, small = pl.pallas_call(
        functools.partial(layer_kernel, dp_count),
        out_shape=(
            jax.ShapeDtypeStruct((PIECES, piece, width), F32),
            jax.ShapeDtypeStruct((3, 4, share_rows, width), BF16),
            jax.ShapeDtypeStruct((16, small_width), F32),
        ),
        in_specs=[smem_spec] + [any_spec] * 6 + [vmem_spec] * 3,
        out_specs=(any_spec,) * 3,
        scratch_shapes=[
            vmem((width, 3 * width), BF16),
            vmem((width, width), BF16),
            vmem((width, 4 * width), BF16),
            vmem((4, width, width), BF16),
            vmem((12, width, width), BF16),
            vmem((PIECES, piece, width), BF16),
            vmem((width, rows), BF16),
            vmem((3, pairs, LANES, rows), BF16),
            vmem((PIECES, pairs, piece, LANES), BF16),
            vmem((PIECES, pairs, piece, LANES), BF16),
            vmem((PIECES, pairs, 2, piece, piece), BF16),
            vmem((pairs, 2, piece, piece), BF16),
            vmem((pairs, LANES, rows), BF16),
            vmem((width, rows), F32),
            vmem((width, rows), F32),
            vmem((PIECES, 2, 1, piece), F32),
            vmem((width, rows), BF16),
            vmem((4, width, rows), BF16),
            vmem((4, width, rows), BF16),
            vmem((width, rows), BF16),
            vmem((width, rows), BF16),
            vmem((pairs, LANES, piece), BF16),
            vmem((PIECES, width, piece), BF16),
            vmem((PIECES, width, piece), BF16),
            vmem((STATS, width, LANES), BF16),
            vmem((STATS, width, LANES), F32),
            vmem((2, 2, pairs, LANES, piece), F32),
            vmem((width, piece), F32),
            vmem((width, piece), F32),
            vmem((width, piece), F32),
            vmem((2, piece, width), F32),
            vmem((3, 2, width, width), BF16),
            vmem((3, width, width), BF16),
            vmem((slots, (width - share_rows) // split, width), BF16),
            vmem((3, 4, share_rows, width), BF16),
            vmem((dp_count, 16, small_width), F32),
            vmem((dp_count - 1, 16, small_width), F32),
            vmem((4, 16, small_width), F32),
            vmem((16, small_width), F32),
            dma((13,)),
            dma((PIECES,)),
            dma((PIECES,)),
            dma((PIECES,)),
            dma((jobs, 2)),
            dma((jobs, 2)),
            dma((jobs, 2)),
            dma((jobs, 2)),
            dma((jobs, dp_steps, 2)),
            dma((jobs, dp_steps, 2)),
            dma((jobs,)),
            dma((jobs,)),
            dma((jobs, 2)),
            dma((jobs, 2)),
            dma((dp_count - 1,)),
            dma((dp_count - 1,)),
            dma((3,)),
            dma((3,)),
            dma((jobs,)),
        ],
        compiler_params=pltpu.CompilerParams(
            collective_id=0, has_side_effects=True, vmem_limit_bytes=63 * 1024 * 1024
        ),
    )(
        window_group,
        block_input.reshape(PIECES, piece, width),
        cotangent.reshape(PIECES, piece, width),
        w_qkv,
        w_out,
        w_up,
        w_down,
        up_bias,
        norm_gains,
        biases,
    )
    return pl.pallas_call(
        finish_kernel,
        out_shape=(
            jax.ShapeDtypeStruct((1, rows, width), F32),
            jax.ShapeDtypeStruct((1, share_rows, 3 * width), F32),
            jax.ShapeDtypeStruct((1, share_rows, width), F32),
            jax.ShapeDtypeStruct((1, share_rows, 4 * width), F32),
            jax.ShapeDtypeStruct((1, 4 * share_rows, width), F32),
            jax.ShapeDtypeStruct((1, 4 * share_rows), F32),
            jax.ShapeDtypeStruct((1, 2, share_rows), F32),
            jax.ShapeDtypeStruct((1, 4, share_rows), F32),
        ),
        in_specs=[smem_spec] + [any_spec] * 3,
        out_specs=(any_spec,) * 8,
        scratch_shapes=[
            vmem((rows, width), F32),
            vmem((3, 4, share_rows, width), BF16),
            vmem((share_rows, 3 * width), F32),
            vmem((share_rows, width), F32),
            vmem((share_rows, 4 * width), F32),
            vmem((4 * share_rows, width), F32),
            vmem((16, small_width), F32),
            vmem((1, 4 * share_rows), F32),
            vmem((1, 2, share_rows), F32),
            vmem((1, 4, share_rows), F32),
            dma((16,)),
            dma((4,)),
            dma((7,)),
        ],
        compiler_params=pltpu.CompilerParams(vmem_limit_bytes=63 * 1024 * 1024),
    )(window_group, ends_in.reshape(rows, width), fin, small)


def solution(mesh):
    return jax.shard_map(
        functools.partial(on_device, mesh.shape["dp"]),
        mesh=mesh,
        in_specs=(
            P(("dp", "rep"), None),
            P(("dp", "rep"), None),
            P(("dp", "rep"), None),
            P("segment", None, None),
            P("segment", None, None),
            P("segment", None, None),
            P("segment", None, None),
            P("segment", None),
            P("segment", None, None),
            P("segment", None, None),
        ),
        out_specs=(
            P("segment", ("dp", "rep"), None),
            P("segment", "dp", None),
            P("segment", "dp", None),
            P("segment", "dp", None),
            P("segment", "dp", None),
            P("segment", "dp"),
            P("segment", None, "dp"),
            P("segment", None, "dp"),
        ),
        check_vma=False,
    )
```

```python
import functools
import math

import jax
import jax.numpy as jnp
from jax import lax
from jax.experimental import pallas as pl
from jax.experimental.pallas import tpu as pltpu
from jax.sharding import PartitionSpec as P

MESH = pl.DeviceIdType.MESH
F32 = jnp.float32
BF16 = jnp.bfloat16
HEADS = 8
LANES = 128
PIECES = 4
EPS = 1e-05
GAIN_ONE, GAIN_TWO, BIAS_OUT, BIAS_ONE, BIAS_DOWN, BIAS_TWO, BIAS_UP = range(7)
STATS = 10
CHUNK = 64
SPLIT = 4
DP_FIRST = (1, 5, 9)
SUM, CORE, SIDE, SIDED, DP, DPED, JOIN, LAST, SMALL = range(9)
ORDER_ONE = (
    (SUM, 0), (SUM, 2),
)
ORDER_TWO = (
    (CORE, 0), (SIDE, 0), (SUM, 4), (CORE, 3), (CORE, 2), (CORE, 1), (SIDE, 3), (SUM, 6), (SIDED, 0),
    (SIDE, 2),
)
ORDER_THREE = (
    (CORE, 4), (SIDED, 3), (CORE, 6), (SIDE, 6), (CORE, 5), (DP, 0), (SIDE, 4), (SUM, 8), (DPED, 0), (DP, 1),
    (SIDED, 2), (CORE, 7), (SIDE, 7), (SUM, 10), (DP, 3), (SIDED, 6), (CORE, 8), (SIDE, 8), (SIDED, 4),
    (DPED, 1), (DP, 2), (CORE, 9), (DP, 6), (DPED, 3), (CORE, 11), (SIDE, 11), (SIDED, 8), (DP, 4),
    (CORE, 10), (SMALL, 0), (DP, 5), (DPED, 6), (JOIN, 1), (JOIN, 3), (SIDED, 7), (DP, 9), (SIDE, 10),
    (SIDED, 11), (DP, 8), (DPED, 4), (DPED, 2), (SIDED, 10), (DP, 7), (DPED, 9), (DP, 11), (JOIN, 6),
    (JOIN, 4), (DPED, 5), (DPED, 8), (DP, 10), (DPED, 7), (SMALL, 1), (LAST, 6), (LAST, 1), (JOIN, 2),
    (DPED, 11), (LAST, 3), (JOIN, 0), (DPED, 10), (JOIN, 7), (JOIN, 8), (JOIN, 11), (JOIN, 9), (JOIN, 5),
    (LAST, 4), (SMALL, 2), (LAST, 0), (JOIN, 10), (LAST, 9), (LAST, 11), (LAST, 5), (LAST, 7), (LAST, 8),
    (LAST, 2), (LAST, 10),
)


def plain_orders():
    one = ((SUM, 0),)
    two = ((SUM, 1), (CORE, 0), (SIDE, 0))
    three = ((SUM, 2), (CORE, 1), (SIDE, 1), (CORE, 2), (SIDE, 2), (SMALL, 0), (SMALL, 1), (SMALL, 2))
    for stage in (SIDED, DP, DPED, JOIN, LAST):
        three += tuple((stage, job) for job in range(3))
    return one, two, three


def dot_plain(left, right):
    return lax.dot_general(left, right, (((1,), (0,)), ((), ())), preferred_element_type=F32)


def drain(parts):
    for _ in parts:
        pass


def side_by_side(one, two):
    spent = [0, 300]
    live = [one, two]
    while live[0] or live[1]:
        which = 0 if live[0] and (not live[1] or spent[0] <= spent[1]) else 1
        cost = next(live[which], None)
        if cost is None:
            live[which] = None
        else:
            spent[which] += cost


def dot_turned(left, right):
    return lax.dot_general(left, right, (((1,), (1,)), ((), ())), preferred_element_type=F32)


def fold(values):
    total = values[:, :LANES]
    for start in range(LANES, values.shape[1], LANES):
        total = total + values[:, start : start + LANES]
    return total


def layer_kernel(
    dp_count,
    flag_ref,
    x_hbm,
    ct_hbm,
    w_qkv_hbm,
    w_out_hbm,
    w_up_hbm,
    w_down_hbm,
    up_bias_ref,
    gains_ref,
    biases_ref,
    ends_hbm,
    fin_hbm,
    small_hbm,
    w_qkv,
    w_out,
    w_up,
    w_down,
    turned,
    rows_in,
    x_t,
    qkv,
    keys_rm,
    values_rm,
    share,
    share_off,
    mixture,
    norm_one,
    norm_two,
    inverses,
    hidden_low,
    slope,
    active,
    down_grad,
    branch_grad,
    grad_mix,
    outgoing,
    incoming_grad,
    columns,
    sums,
    key_sums,
    wide_a,
    wide_b,
    wide_c,
    ends_v,
    core_in,
    side_in,
    dp_in,
    fin,
    small,
    small_dp,
    small_rep,
    small_out,
    load_sem,
    seg_send,
    seg_recv,
    ends_sem,
    core_send,
    core_recv,
    side_send,
    side_recv,
    dp_send,
    dp_recv,
    join_send,
    join_recv,
    last_send,
    last_recv,
    sdp_send,
    sdp_recv,
    srep_send,
    srep_recv,
    fin_sem,
):
    width = w_out.shape[0]
    piece = x_t.shape[1] // PIECES
    pairs = qkv.shape[1]
    share_rows = width // dp_count
    dp_steps = dp_count.bit_length() - 1
    segment = lax.axis_index("segment")
    dp = lax.axis_index("dp")
    rep = lax.axis_index("rep")
    core = lax.rem(rep, 2)
    side = lax.div(rep, 2)
    other_core = side * 2 + (1 - core)
    other_side = (1 - side) * 2 + core

    def load_copy(block):
        def span(first):
            return pl.ds(pl.multiple_of((block - first) * width, width), width)

        def copy_of(source, target):
            return pltpu.make_async_copy(source, target, load_sem.at[1 + block])

        return (
            lambda: copy_of(w_qkv_hbm.at[0, :, span(0)], w_qkv.at[:, span(0)]),
            lambda: copy_of(w_out_hbm.at[0], w_out),
            lambda: copy_of(w_up_hbm.at[0, :, span(4)], w_up.at[:, span(4)]),
            lambda: copy_of(w_down_hbm.at[0, span(8), :], w_down.at[block - 8]),
        )

    parts_of_load = ((0, 3), (3, 4), (4, 8), (8, 12))
    first_rows = pltpu.make_async_copy(x_hbm, rows_in, load_sem.at[0])
    last_rows = pltpu.make_async_copy(ct_hbm, rows_in, load_sem.at[0])

    @pl.when(segment == 0)
    def _():
        first_rows.start()

    @pl.when(segment == 1)
    def _():
        last_rows.start()

    for part, (first, after) in enumerate(parts_of_load):
        for block in range(first, after):
            load_copy(block)[part]().start()

    barrier = pltpu.get_barrier_semaphore()
    pl.semaphore_signal(
        barrier, inc=1, device_id={"segment": 1 - segment}, device_id_type=MESH
    )
    for step in range(1, 4):
        pl.semaphore_signal(
            barrier, inc=1, device_id={"rep": lax.rem(rep + step, 4)}, device_id_type=MESH
        )
    for step in range(1, dp_count):
        pl.semaphore_signal(
            barrier, inc=1, device_id={"dp": lax.rem(dp + step, dp_count)}, device_id_type=MESH
        )

    params = [gains_ref[0].astype(F32), biases_ref[0].astype(F32)]
    for block in range(4):
        params.append(up_bias_ref[:, block * width : (block + 1) * width].astype(F32))
    params.append(jnp.zeros((16 - STATS, width), F32))
    upright = jnp.concatenate(params, axis=0).T
    for index in range(STATS):
        columns[index] = jnp.broadcast_to(upright[:, index : index + 1], (width, LANES)).astype(BF16)
    for index in range(STATS):
        sums[index] = jnp.zeros((width, LANES), F32)
    key_sums[0] = jnp.zeros(key_sums.shape[1:], F32)

    chunks = [slice(start, start + CHUNK) for start in range(0, width, CHUNK)]

    def turn(part):
        def one(block, carry):
            load_copy(block)[part]().wait()
            if part == 3:
                turned[block] = w_down[block - 8].T
            elif part == 1:
                turned[block] = w_out[...].T
            else:
                first = parts_of_load[part][0]
                span = pl.ds(pl.multiple_of((block - first) * width, width), width)
                turned[block] = (w_qkv if part == 0 else w_up)[:, span].T
            return carry

        lax.fori_loop(*parts_of_load[part], one, 0)

    def turn_apart(first, after):
        for block in range(first, after):
            part = (0, 0, 0, 1, 2, 2, 2, 2, 3, 3, 3, 3)[block]
            load_copy(block)[part]().wait()
            span = slice(block % 4 * width, (block % 4 + 1) * width)
            if part == 0:
                turned[block] = w_qkv[:, span].T
            elif part == 1:
                turned[block] = w_out[...].T
            elif part == 2:
                turned[block] = w_up[:, span].T
            else:
                turned[block] = w_down[block - 8].T
            yield 230

    first_rows.wait()

    flag = flag_ref[0, 0].astype(F32)

    def lanes_of(index):
        if isinstance(index, int):
            return pl.ds(index * piece, piece)
        return pl.ds(pl.multiple_of(index * piece, piece), piece)

    def forward_copy(index):
        return pltpu.make_async_remote_copy(
            src_ref=outgoing.at[index],
            dst_ref=x_t.at[:, lanes_of(index)],
            send_sem=seg_send.at[index],
            recv_sem=seg_recv.at[index],
            device_id={"segment": 1 - segment},
            device_id_type=MESH,
        )

    def backward_copy(index):
        return pltpu.make_async_remote_copy(
            src_ref=outgoing.at[index],
            dst_ref=incoming_grad.at[index],
            send_sem=seg_send.at[index],
            recv_sem=seg_recv.at[index],
            device_id={"segment": 1 - segment},
            device_id_type=MESH,
        )

    def ends_copy(index):
        return pltpu.make_async_copy(
            ends_v.at[lax.rem(index, 2)], ends_hbm.at[index], ends_sem.at[index]
        )

    def free_ends(index):
        @pl.when(index >= 2)
        def _():
            ends_copy(index - 2).wait()

    def own_rows(index):
        half = lax.rem(index, 2)
        whole = jnp.where(index < 2, 1.0, 0.0).astype(F32)
        weight = whole * flag + (1.0 - whole) * (1.0 - flag)
        picked = rows_in[half].astype(F32) * weight + rows_in[2 + half].astype(F32) * (1.0 - weight)
        return picked.T

    def by_queries(values):
        half = LANES // 2
        blank = jnp.zeros((half, LANES), values.dtype)
        parts = []
        for part in range(2):
            span = slice(part * LANES, (part + 1) * LANES)
            first = jnp.concatenate([values[:half, span], blank], axis=0)
            second = jnp.concatenate([blank, values[half:, span]], axis=0)
            parts.append(jnp.concatenate([first, second], axis=1))
        return parts

    def against(rows_ref, index, pair, parts, has_off):
        own = rows_ref[index, pair]
        products = [dot_plain(own[:LANES], parts[0]), dot_plain(own, parts[1])]
        if has_off:
            before = rows_ref[0, pair]
            products += [dot_plain(before, parts[0]), dot_plain(before, parts[1])]
        return products

    def tiles_of(products, head, part, has_off):
        lanes = slice(head * LANES, (head + 1) * LANES)
        own = products[part]
        tiles = [own[part * LANES : (part + 1) * LANES, lanes]]
        if part:
            tiles.append(own[:LANES, lanes])
        if has_off:
            off = products[2 + part]
            tiles += [off[:LANES, lanes], off[LANES:, lanes]]
        return tiles

    def joined(lows, has_off):
        blank = jnp.zeros((LANES, LANES), BF16)
        first = jnp.concatenate([lows[0][0], blank], axis=0)
        second = jnp.concatenate([lows[1][1], lows[1][0]], axis=0)
        whole = jnp.concatenate([first, second], axis=1)
        if not has_off:
            return whole, None
        first = jnp.concatenate(lows[0][-2:], axis=0)
        second = jnp.concatenate(lows[1][-2:], axis=0)
        return whole, jnp.concatenate([first, second], axis=1)

    def attend(index, has_off):
        lanes = lanes_of(index)
        half = LANES // 2
        key_at = lax.broadcasted_iota(jnp.int32, (LANES, LANES), 0)
        query_at = lax.broadcasted_iota(jnp.int32, (LANES, LANES), 1)
        allowed = key_at <= query_at

        def scores_of(pair):
            return against(
                keys_rm, index, pair, by_queries(qkv[0, pair, :, lanes]), has_off
            )

        ahead = scores_of(0)
        for pair in range(pairs):
            scores = ahead
            if pair + 1 < pairs:
                ahead = scores_of(pair + 1)
            mixed = []
            for head in range(2):
                rows = slice(head * half, (head + 1) * half)
                lows = []
                for part in range(2):
                    tiles = tiles_of(scores, head, part, has_off)
                    tiles[0] = jnp.where(allowed, tiles[0], -1e30)
                    top = jnp.max(functools.reduce(jnp.maximum, tiles), axis=0, keepdims=True)
                    raised = [jnp.exp(tile - top) for tile in tiles]
                    total = functools.reduce(jnp.add, raised)
                    scale = 1.0 / jnp.sum(total, axis=0, keepdims=True)
                    lows.append([(tile * scale).astype(BF16) for tile in raised])
                low, low_off = joined(lows, has_off)
                share[index, pair, head] = low
                mix = dot_plain(qkv[2, pair, rows, lanes], low)
                if has_off:
                    share_off[pair, head] = low_off
                    mix = mix + dot_plain(qkv[2, pair, rows, :piece], low_off)
                mixed.append(mix.astype(BF16))
            mixture[pair, :, lanes] = jnp.concatenate(mixed, axis=0)
            yield 280

    def part_sum(values):
        return jnp.sum(values.reshape(values.shape[0] // 8, 8, values.shape[1]), axis=0)

    def full_mean(parts):
        return jnp.sum(parts, axis=0, keepdims=True) * (1.0 / width)

    def column(index, rows):
        part = columns[index, rows, :].astype(F32)
        return jnp.concatenate([part] * (piece // LANES), axis=1)

    def gather_sum(index, rows, values):
        sums[index, rows, :] = sums[index, rows, :] + fold(values)

    def norm_chunks(index, which, wide_a, total):
        mean = full_mean(total)
        spread = jnp.zeros((8, piece), F32)
        for rows in chunks:
            centred = wide_a[rows, :] - mean
            spread = spread + part_sum(centred * centred)
        inverse = lax.rsqrt(full_mean(spread) + EPS)
        inverses[index, which] = inverse
        return mean, inverse

    def forward_start(index):
        @pl.when(segment == 0)
        def _():
            x_t[:, lanes_of(index)] = own_rows(index).astype(BF16)

        @pl.when(segment == 1)
        def _():
            forward_copy(index).wait_recv()

    def forward_first(index):
        lanes = lanes_of(index)
        inputs = x_t[:, lanes]
        score_scale = 1.0 / math.sqrt(width // HEADS)
        for block in range(3):
            result = dot_plain(turned[block], inputs)
            for pair in range(pairs):
                low = result[pair * LANES : (pair + 1) * LANES]
                low = (low * score_scale if block == 0 else low).astype(BF16)
                qkv[block, pair, :, lanes] = low
                if block == 1:
                    keys_rm[index, pair] = low.T
                if block == 2:
                    values_rm[index, pair] = low.T
            yield 270

    def forward_rest(index, wide_a):
        lanes = lanes_of(index)
        branch = dot_plain(turned[3], mixture[:, :, lanes].reshape(width, piece))
        yield 250
        total = jnp.zeros((8, piece), F32)
        for rows in chunks:
            sum_one = x_t[rows, lanes].astype(F32) + (branch[rows] + column(BIAS_OUT, rows))
            wide_a[rows, :] = sum_one
            total = total + part_sum(sum_one)
            yield 25
        mean, inverse = norm_chunks(index, 0, wide_a, total)
        yield 150
        for rows in chunks:
            normed = (wide_a[rows, :] - mean) * inverse
            norm_one[rows, lanes] = normed
            hidden = normed * column(GAIN_ONE, rows) + column(BIAS_ONE, rows)
            hidden_low[rows, lanes] = hidden.astype(BF16)
            yield 30

        branch_two = None
        for block in range(4):
            pre_block = dot_plain(turned[4 + block], hidden_low[:, lanes])
            yield 50
            lows = []
            for rows in chunks:
                pre = pre_block[rows] + column(BIAS_UP + block, rows)
                level = (lax.erf(pre * (1.0 / math.sqrt(2.0))) + 1.0) * 0.5
                bell = jnp.exp2(pre * pre * (-0.5 * math.log2(math.e)))
                lows.append((pre * level).astype(BF16))
                active[block, rows, lanes] = lows[-1]
                slope[block, rows, lanes] = (
                    level + pre * bell * (1.0 / math.sqrt(2.0 * math.pi))
                ).astype(BF16)
                yield 65
            part = dot_plain(turned[8 + block], jnp.concatenate(lows, axis=0))
            branch_two = part if branch_two is None else branch_two + part
            yield 100
        total = jnp.zeros((8, piece), F32)
        for rows in chunks:
            hidden = norm_one[rows, lanes] * column(GAIN_ONE, rows) + column(BIAS_ONE, rows)
            sum_two = hidden + (branch_two[rows] + column(BIAS_DOWN, rows))
            wide_a[rows, :] = sum_two
            total = total + part_sum(sum_two)
            yield 25
        mean, inverse = norm_chunks(index, 1, wide_a, total)
        yield 150
        for rows in chunks:
            norm_two[rows, lanes] = (wide_a[rows, :] - mean) * inverse
            yield 20

    def forward_end(index):
        for rows in chunks:
            outgoing[index, rows, :] = output_rows(rows, lanes_of(index)).astype(BF16)
        forward_copy(index).start()

    def off_or_not(index, run):
        @pl.when(index == 1)
        def _():
            drain(run(index, True))

        @pl.when(index != 1)
        def _():
            drain(run(index, False))

    def forward(index):
        forward_start(index)
        drain(forward_first(index))
        off_or_not(index, attend)
        drain(forward_rest(index, wide_a))

        @pl.when(segment == 0)
        def _():
            forward_end(index)

    def output_rows(rows, lanes):
        return norm_two[rows, lanes] * column(GAIN_TWO, rows) + column(BIAS_TWO, rows)

    def last_outputs(index, carry):
        free_ends(index)
        for start in range(0, width, LANES):
            rows = slice(start, start + LANES)
            ends_v[lax.rem(index, 2), :, rows] = output_rows(rows, lanes_of(index)).T
        ends_copy(index).start()
        return carry

    def attend_back(index, has_off):
        lanes = lanes_of(index)
        slot = (1 if index == 0 else 0) if isinstance(index, int) else jnp.where(index == 0, 1, 0)
        half = LANES // 2
        score_scale = 1.0 / math.sqrt(width // HEADS)

        def backs_of(pair):
            return against(values_rm, index, pair, by_queries(grad_mix[pair]), has_off)

        ahead = backs_of(0)
        for pair in range(pairs):
            backs = ahead
            if pair + 1 < pairs:
                ahead = backs_of(pair + 1)
            results = ([], [], [])
            for head in range(2):
                rows = slice(head * half, (head + 1) * half)
                low = share[index, pair, head]
                low_off = share_off[pair, head] if has_off else None
                lows = []
                for part in range(2):
                    place = slice(part * LANES, (part + 1) * LANES)
                    wides = [low[place, place]]
                    if part:
                        wides.append(low[:LANES, place])
                    if has_off:
                        wides += [low_off[:LANES, place], low_off[LANES:, place]]
                    wides = [tile.astype(F32) for tile in wides]
                    tiles = tiles_of(backs, head, part, has_off)
                    products = [wide * tile for wide, tile in zip(wides, tiles)]
                    inner = jnp.sum(functools.reduce(jnp.add, products), axis=0, keepdims=True)
                    lows.append(
                        [
                            (product - wide * inner).astype(BF16)
                            for product, wide in zip(products, wides)
                        ]
                    )
                grad_scores, grad_off = joined(lows, has_off)
                queries = qkv[0, pair, rows, lanes]
                grads = grad_mix[pair, rows]
                grad_query = dot_plain(qkv[1, pair, rows, lanes], grad_scores)
                grad_key = dot_turned(queries, grad_scores) + key_sums[slot, 0, pair, rows]
                grad_value = dot_turned(grads, low) + key_sums[slot, 1, pair, rows]
                if has_off:
                    grad_query = grad_query + dot_plain(qkv[1, pair, rows, :piece], grad_off)
                    key_sums[1, 0, pair, rows] = dot_turned(queries, grad_off)
                    key_sums[1, 1, pair, rows] = dot_turned(grads, low_off)
                for kept, grad in zip(results, (grad_query * score_scale, grad_key, grad_value)):
                    kept.append(grad.astype(BF16))
            for block in range(3):
                qkv[block, pair, :, lanes] = jnp.concatenate(results[block], axis=0)
            yield 440

    def backward_start(index):
        @pl.when(segment == 0)
        def _():
            backward_copy(index).wait_recv()

    def backward_norm(index):
        lanes = lanes_of(index)
        plain = jnp.zeros((8, piece), F32)
        inner = jnp.zeros((8, piece), F32)
        for rows in chunks:
            grad = incoming_grad[index, rows, :].astype(F32)
            product = grad * norm_two[rows, lanes]
            gather_sum(GAIN_TWO, rows, product)
            gather_sum(BIAS_TWO, rows, grad)
            gain = column(GAIN_TWO, rows)
            plain = plain + part_sum(grad * gain)
            inner = inner + part_sum(product * gain)
            yield 40
        plain = full_mean(plain)
        inner = full_mean(inner)
        inverse = inverses[index, 1]
        for rows in chunks:
            scaled = incoming_grad[index, rows, :].astype(F32) * column(GAIN_TWO, rows)
            grad_two = (scaled - plain - norm_two[rows, lanes] * inner) * inverse
            gather_sum(BIAS_DOWN, rows, grad_two)
            wide_a[rows, :] = grad_two
            down_grad[rows, lanes] = grad_two.astype(BF16)
            yield 40

    def backward_feed(index):
        lanes = lanes_of(index)
        for block in range(4):
            back = dot_plain(w_down[block], down_grad[:, lanes])
            for rows in chunks:
                grad_pre = back[rows] * slope[block, rows, lanes].astype(F32)
                gather_sum(BIAS_UP + block, rows, grad_pre)
                slope[block, rows, lanes] = grad_pre.astype(BF16)
            yield 250

        through = dot_plain(w_up[...], slope[:, :, lanes].reshape(4 * width, piece))
        plain = jnp.zeros((8, piece), F32)
        inner = jnp.zeros((8, piece), F32)
        for rows in chunks:
            grad_hidden = wide_a[rows, :] + through[rows]
            wide_a[rows, :] = grad_hidden
            product = grad_hidden * norm_one[rows, lanes]
            gather_sum(GAIN_ONE, rows, product)
            gather_sum(BIAS_ONE, rows, grad_hidden)
            gain = column(GAIN_ONE, rows)
            plain = plain + part_sum(grad_hidden * gain)
            inner = inner + part_sum(product * gain)
            yield 120 if rows.start == 0 else 45
        plain = full_mean(plain)
        inner = full_mean(inner)
        inverse = inverses[index, 0]
        for rows in chunks:
            scaled = wide_a[rows, :] * column(GAIN_ONE, rows)
            grad_one = (scaled - plain - norm_one[rows, lanes] * inner) * inverse
            gather_sum(BIAS_OUT, rows, grad_one)
            wide_b[rows, :] = grad_one
            branch_grad[rows, lanes] = grad_one.astype(BF16)
            yield 40
        grad_mix[...] = (
            dot_plain(w_out[...], branch_grad[:, lanes]).astype(BF16).reshape(pairs, LANES, piece)
        )
        yield 300

    def backward_attention(index):
        off_or_not(index, attend_back)
        through = dot_plain(w_qkv[...], qkv[:, :, :, lanes_of(index)].reshape(3 * width, piece))

        @pl.when(segment == 1)
        def _():
            for rows in chunks:
                outgoing[index, rows, :] = (wide_b[rows, :] + through[rows]).astype(BF16)
            backward_copy(index).start()

        @pl.when(segment == 0)
        def _():
            free_ends(index)
            for start in range(0, width, LANES):
                rows = slice(start, start + LANES)
                ends_v[lax.rem(index, 2), :, rows] = (wide_b[rows, :] + through[rows]).T
            ends_copy(index).start()

    def backward_both(index, forward_index):
        forward_copy(forward_index).wait_recv()

        def back():
            yield from backward_norm(index)
            yield from backward_feed(index)
            yield from attend_back(index, False)
            through = dot_plain(w_qkv[...], qkv[:, :, :, lanes_of(index)].reshape(3 * width, piece))
            for rows in chunks:
                outgoing[index, rows, :] = (wide_b[rows, :] + through[rows]).astype(BF16)
                yield 90

        def ahead():
            yield from forward_first(forward_index)
            yield from attend(forward_index, False)
            yield from forward_rest(forward_index, wide_c)

        side_by_side(back(), ahead())
        backward_copy(index).start()

    split = SPLIT if share_rows % (16 * SPLIT) == 0 else 1
    dp_first = DP_FIRST if split == SPLIT else ()
    orders = (ORDER_ONE, ORDER_TWO, ORDER_THREE) if split == SPLIT else plain_orders()
    jobs = 3 * split
    cut_rows = share_rows // split
    job_rows = width // split

    def base_of(job):
        return (8, 4, 0)[job // split]

    def job_span(job):
        return pl.ds(job % split * job_rows, job_rows)

    def fin_rows(job):
        return pl.ds(job % split * cut_rows, cut_rows)

    def parts_of(job):
        return range(2) if job in dp_first else range(1)

    def core_copies(job):
        return [
            pltpu.make_async_remote_copy(
                src_ref=turned.at[base_of(job) + 2 * (1 - core) + each, job_span(job)],
                dst_ref=core_in.at[job // split, each, job_span(job)],
                send_sem=core_send.at[job, each],
                recv_sem=core_recv.at[job, each],
                device_id={"rep": other_core},
                device_id_type=MESH,
            )
            for each in range(2)
        ]

    def side_copies(job):
        base = base_of(job)
        copies = []
        for each in parts_of(job):
            if job in dp_first:
                source = turned.at[base + 2 * core + each, dp_rows(job, dp_steps - 1)[1]]
                target = side_in.at[
                    job // split, pl.ds(job % split * job_rows + each * cut_rows, cut_rows)
                ]
            else:
                source = turned.at[base + 2 * core + (1 - side), job_span(job)]
                target = side_in.at[job // split, job_span(job)]
            copies.append(
                pltpu.make_async_remote_copy(
                    src_ref=source,
                    dst_ref=target,
                    send_sem=side_send.at[job, each],
                    recv_sem=side_recv.at[job, each],
                    device_id={"rep": other_side},
                    device_id_type=MESH,
                )
            )
        return copies

    def dp_slot(job):
        return sum(len(parts_of(before)) for before in range(job))

    def dp_rows(job, step):
        count = dp_count // 2
        start = 0
        for bit in range(step):
            start = start + lax.rem(lax.div(dp, 2**bit), 2) * count
            count = count // 2
        mine = lax.rem(lax.div(dp, 2**step), 2)
        first = job % split * job_rows
        sent = pl.multiple_of(first + (start + (1 - mine) * count) * cut_rows, cut_rows)
        kept = pl.multiple_of(first + (start + mine * count) * cut_rows, cut_rows)
        return pl.ds(sent, count * cut_rows), pl.ds(kept, count * cut_rows)

    def dp_landing(step):
        count = dp_count // 2 ** (step + 1)
        return pl.ds((dp_count - 2 * count) * cut_rows, count * cut_rows)

    def dp_copies(job, step):
        mine = lax.rem(lax.div(dp, 2**step), 2)
        copies = []
        for each in parts_of(job):
            position = base_of(job) + 2 * core + (each if job in dp_first else side)
            copies.append(
                pltpu.make_async_remote_copy(
                    src_ref=turned.at[position, dp_rows(job, step)[0]],
                    dst_ref=dp_in.at[dp_slot(job) + each, dp_landing(step)],
                    send_sem=dp_send.at[job, step, each],
                    recv_sem=dp_recv.at[job, step, each],
                    device_id={"dp": dp + (1 - 2 * mine) * 2**step},
                    device_id_type=MESH,
                )
            )
        return copies

    def join_copy(job):
        part = fin.at[job // split, 2 * core + side, fin_rows(job)]
        return pltpu.make_async_remote_copy(
            src_ref=part,
            dst_ref=part,
            send_sem=join_send.at[job],
            recv_sem=join_recv.at[job],
            device_id={"rep": other_side},
            device_id_type=MESH,
        )

    def last_copies(job):
        copies = []
        for each in range(2):
            part = fin.at[job // split, 2 * core + each, fin_rows(job)]
            copies.append(
                pltpu.make_async_remote_copy(
                    src_ref=part,
                    dst_ref=part,
                    send_sem=last_send.at[job, each],
                    recv_sem=last_recv.at[job, each],
                    device_id={"rep": other_core},
                    device_id_type=MESH,
                )
            )
        return copies

    def fin_copy(job):
        return pltpu.make_async_copy(
            fin.at[job // split, :, fin_rows(job)],
            fin_hbm.at[job // split, :, fin_rows(job)],
            fin_sem.at[job],
        )

    def arrived(*copies):
        for copy in copies:
            copy.wait_send()
        for copy in copies:
            copy.wait_recv()

    def start_all(copies):
        for copy in copies:
            copy.start()

    def turned_bits(value, count):
        place = 0
        while count > 1:
            place = place * 2 + value % 2
            value = value // 2
            count = count // 2
        return place

    pack = min(2, split)

    def left_rows(source, part):
        count = pack * cut_rows
        start = part * pack * cut_rows
        return jnp.concatenate(
            [source(index * share_rows + start, count) for index in range(dp_count)], axis=0
        )

    def keep_rows(block, part, result):
        for index in range(dp_count):
            for each in range(pack):
                target = (part * pack + each) * job_rows + turned_bits(index, dp_count) * cut_rows
                start = (index * pack + each) * cut_rows
                turned[block, target : target + cut_rows, :] = result[start : start + cut_rows]

    def down_sums(part):
        count = width // (4 * share_rows)

        def one(block, carry):
            pieces = []
            for each in range(4 * count):
                start = each * share_rows + part * pack * cut_rows
                pieces.append(active[block, start : start + pack * cut_rows, :])
            result = dot_turned(jnp.concatenate(pieces, axis=0), down_grad[...]).astype(BF16)
            high = lax.rem(block, 2) * 2 + lax.div(block, 2)
            for each in range(count):
                place = turned_bits(each, count) * 4 + high
                for position in range(4):
                    for job in range(pack):
                        target = (part * pack + job) * job_rows + place * cut_rows
                        start = ((each * 4 + position) * pack + job) * cut_rows
                        turned[
                            8 + position, pl.ds(pl.multiple_of(target, cut_rows), cut_rows), :
                        ] = result[start : start + cut_rows]
            return carry

        lax.fori_loop(0, 4, one, 0)

    def up_sums(part):
        def one(block, carry):
            left = left_rows(lambda start, count: hidden_low[start : start + count, :], part)
            keep_rows(4 + block, part, dot_turned(left, slope[block]).astype(BF16))
            return carry

        lax.fori_loop(0, 4, one, 0)

    def qkv_sums(part):
        def one(block, carry):
            left = left_rows(lambda start, count: x_t[start : start + count, :], part)
            grads = qkv[block].reshape(width, PIECES * piece)
            keep_rows(block, part, dot_turned(left, grads).astype(BF16))
            return carry

        lax.fori_loop(0, 3, one, 0)
        left = left_rows(
            lambda start, count: mixture[start // LANES, start % LANES : start % LANES + count, :], part
        )
        keep_rows(3, part, dot_turned(left, branch_grad[...]).astype(BF16))

    def sums_of(job):
        (down_sums, up_sums, qkv_sums)[job // split](job % split // pack)
        for each in range(pack):
            start_all(core_copies(job + each))

    def after_core(job):
        arrived(*core_copies(job))
        rows = job_span(job)
        for each in parts_of(job):
            place = 1 - side if each == 0 else side
            position = base_of(job) + 2 * core + place
            turned[position, rows, :] = (
                turned[position, rows, :].astype(F32)
                + core_in[job // split, place, rows, :].astype(F32)
            ).astype(BF16)
        if job in dp_first:
            start_all(dp_copies(job, 0))

    def start_side(job):
        start_all(side_copies(job))

    def after_side(job):
        arrived(*side_copies(job))
        rows = job_span(job)
        position = base_of(job) + 2 * core + side
        turned[position, rows, :] = (
            turned[position, rows, :].astype(F32)
            + core_in[job // split, side, rows, :].astype(F32)
            + side_in[job // split, rows, :].astype(F32)
        ).astype(BF16)
        start_all(dp_copies(job, 0))

    def dp_total(job, step, each):
        position = base_of(job) + 2 * core + (each if job in dp_first else side)
        kept = turned[position, dp_rows(job, step)[1], :].astype(F32)
        return position, kept + dp_in[dp_slot(job) + each, dp_landing(step), :].astype(F32)

    def after_dp(job):
        for step in range(dp_steps - 1):
            arrived(*dp_copies(job, step))
            for each in parts_of(job):
                position, total = dp_total(job, step, each)
                turned[position, dp_rows(job, step)[1], :] = total.astype(BF16)
            start_all(dp_copies(job, step + 1))

    def after_last_dp(job):
        step = dp_steps - 1
        arrived(*dp_copies(job, step))
        for each in parts_of(job):
            position, total = dp_total(job, step, each)
            if job in dp_first:
                turned[position, dp_rows(job, step)[1], :] = total.astype(BF16)
            else:
                fin[job // split, 2 * core + side, fin_rows(job), :] = total.astype(BF16)
        if job in dp_first:
            start_side(job)
        else:
            join_copy(job).start()

    def after_join(job):
        if job in dp_first:
            arrived(*side_copies(job))
            for each in range(2):
                rows = pl.ds(job % split * job_rows + each * cut_rows, cut_rows)
                own = turned[base_of(job) + 2 * core + each, dp_rows(job, dp_steps - 1)[1], :]
                total = own.astype(F32) + side_in[job // split, rows, :].astype(F32)
                fin[job // split, 2 * core + each, fin_rows(job), :] = total.astype(BF16)
        else:
            arrived(join_copy(job))
        start_all(last_copies(job))

    def after_last(job):
        arrived(*last_copies(job))
        fin_copy(job).start()

    def small_dp_copy(step):
        target = lax.rem(dp + step, dp_count)
        return pltpu.make_async_remote_copy(
            src_ref=small.at[target],
            dst_ref=small_dp.at[step - 1],
            send_sem=sdp_send.at[step - 1],
            recv_sem=sdp_recv.at[step - 1],
            device_id={"dp": target},
            device_id_type=MESH,
        )

    def small_rep_copy(step):
        return pltpu.make_async_remote_copy(
            src_ref=small_rep.at[rep],
            dst_ref=small_rep.at[rep],
            send_sem=srep_send.at[step - 1],
            recv_sem=srep_recv.at[step - 1],
            device_id={"rep": lax.rem(rep + step, 4)},
            device_id_type=MESH,
        )

    small_copy = pltpu.make_async_copy(small_out, small_hbm, load_sem.at[0])

    def small_step(stage):
        if stage == 0:
            rows_of = [jnp.sum(sums[index].T, axis=0, keepdims=True) for index in range(STATS)]
            small[...] = jnp.zeros(small.shape, F32)
            for share_index in range(dp_count):
                for index in range(BIAS_UP):
                    start = share_index * share_rows
                    small[share_index, index : index + 1, :share_rows] = rows_of[index][
                        :, start : start + share_rows
                    ]
                for part in range(4):
                    start = (share_index * 4 + part) * share_rows
                    block, start = start // width, start % width
                    small[share_index, BIAS_UP + part : BIAS_UP + part + 1, :share_rows] = rows_of[
                        BIAS_UP + block
                    ][:, start : start + share_rows]
            for step in range(1, dp_count):
                small_dp_copy(step).start()
        elif stage == 1:
            total = small[dp]
            for step in range(1, dp_count):
                arrived(small_dp_copy(step))
                total = total + small_dp[step - 1]
            small_rep[rep] = total
            for step in range(1, 4):
                small_rep_copy(step).start()
        else:
            for step in range(1, 4):
                arrived(small_rep_copy(step))
            small_out[...] = (small_rep[0] + small_rep[1]) + (small_rep[2] + small_rep[3])
            small_copy.start()

    def run(order):
        steps = (
            sums_of,
            after_core,
            start_side,
            after_side,
            after_dp,
            after_last_dp,
            after_join,
            after_last,
            small_step,
        )
        for stage, job in order:
            steps[stage](job)

    def one_step(step, carry):
        first_index = jnp.where(step < 4, step, jnp.where(step < 6, 5 - step, step - 4))
        last_index = jnp.where(step < 2, step, jnp.where(step == 2, 1, 3))
        index = jnp.minimum(jnp.where(segment == 0, first_index, last_index), PIECES - 1)
        is_last = jnp.where(step == 2 * PIECES, 1, 0)
        begun = jnp.where(step + segment == 0, 0, 1)
        is_forward = jnp.where(step < jnp.where(segment == 0, 4, 2), begun, 0)
        last_backward = jnp.where(step == 2, 1, 0) + jnp.where(step == 5, 1, 0)
        is_backward = jnp.where(segment == 0, begun * (1 - is_forward) * (1 - is_last), last_backward)
        is_split = jnp.where(step >= 2 * PIECES - 1, 1 - segment, 0)
        is_rest = is_backward * (1 - is_split) + is_last * is_split

        @pl.when(is_forward == 1)
        def _():
            forward(index)

        @pl.when(is_backward == 1)
        def _():
            backward_start(index)
            drain(backward_norm(index))

        @pl.when(segment * step == 3)
        def _():
            backward_both(0, 2)

        @pl.when(segment * step == 4)
        def _():
            backward_both(2, 3)

        @pl.when(is_last == 1)
        def _():
            run(orders[0])

        @pl.when(is_rest == 1)
        def _():
            drain(backward_feed(index))

        @pl.when(is_last == 1)
        def _():
            run(orders[1])

        @pl.when(is_rest == 1)
        def _():
            backward_attention(index)

        return carry

    @pl.when(segment == 1)
    def _():
        for part in range(4):
            turn(part)
        for index in range(PIECES):
            incoming_grad[index] = own_rows(index).astype(BF16)

    @pl.when(segment == 0)
    def _():
        def ahead():
            x_t[:, lanes_of(0)] = own_rows(0).astype(BF16)
            yield from forward_first(0)
            yield from attend(0, False)
            yield from forward_rest(0, wide_a)

        drain(turn_apart(0, 4))
        side_by_side(ahead(), turn_apart(4, 12))

    pl.semaphore_wait(barrier, 4 + dp_count - 1)

    @pl.when(segment == 0)
    def _():
        forward_end(0)

    lax.fori_loop(0, 2 * PIECES + 1, one_step, 0)

    cut = orders[2].index((SMALL, 0))
    run(orders[2][:cut])

    @pl.when(segment == 1)
    def _():
        lax.fori_loop(0, PIECES, last_outputs, 0)

    run(orders[2][cut:])

    for index in range(PIECES):

        @pl.when(segment == 0)
        def _():
            forward_copy(index).wait_send()

        @pl.when(segment == 1)
        def _():
            backward_copy(index).wait_send()

    for index in range(2, PIECES):
        ends_copy(index).wait()
    for job in range(jobs):
        fin_copy(job).wait()
    small_copy.wait()


def finish_kernel(
    flag_ref,
    ends_in,
    fin,
    small,
    ends,
    grad_qkv,
    grad_out,
    grad_up,
    grad_down,
    grad_up_bias,
    grad_gains,
    grad_biases,
    ends_v,
    fin_v,
    wide_qkv,
    wide_out,
    wide_up,
    wide_down,
    small_v,
    up_bias_v,
    gains_v,
    biases_v,
    ends_sem,
    in_sem,
    out_sem,
):
    half = ends_in.shape[0] // 2
    share_rows, width = fin.shape[2:]
    start = pl.multiple_of(half * (1 - flag_ref[0, 0]), half)
    cut = half // 4
    ends_copies = []
    ends_loads = []
    for part in range(8):
        source = pl.ds(part * cut, cut)
        offset = start + part * cut if part < 4 else part * cut - half + (half - start)
        target = pl.ds(pl.multiple_of(offset, cut), cut)
        ends_loads.append(
            pltpu.make_async_copy(ends_in.at[source], ends_v.at[source], ends_sem.at[part])
        )
        ends_copies.append(
            pltpu.make_async_copy(ends_v.at[source], ends.at[0, target], ends_sem.at[8 + part])
        )
    loads = [
        pltpu.make_async_copy(fin.at[group], fin_v.at[group], in_sem.at[group])
        for group in range(3)
    ]
    stores = [
        pltpu.make_async_copy(wide, target.at[0], out_sem.at[index])
        for index, (wide, target) in enumerate(
            ((wide_down, grad_down), (wide_up, grad_up), (wide_qkv, grad_qkv), (wide_out, grad_out))
        )
    ]
    small_load = pltpu.make_async_copy(small, small_v, in_sem.at[3])
    small_stores = [
        pltpu.make_async_copy(narrow, target, out_sem.at[4 + index])
        for index, (narrow, target) in enumerate(
            ((up_bias_v, grad_up_bias), (gains_v, grad_gains), (biases_v, grad_biases))
        )
    ]
    small_load.start()
    for group in range(3):
        loads[group].start()
        for copy in ends_loads[group * 3 : group * 3 + 3]:
            copy.start()

    def ends_on(first, after):
        for load, copy in zip(ends_loads[first:after], ends_copies[first:after]):
            load.wait()
            copy.start()

    loads[0].wait()
    for position in range(4):
        rows = slice(position * share_rows, (position + 1) * share_rows)
        wide_down[rows, :] = fin_v[0, position].astype(F32)
    stores[0].start()
    ends_on(0, 3)
    loads[1].wait()
    for position in range(4):
        wide_up[:, position * width : (position + 1) * width] = fin_v[1, position].astype(F32)
    stores[1].start()
    ends_on(3, 6)
    loads[2].wait()
    for position in range(3):
        wide_qkv[:, position * width : (position + 1) * width] = fin_v[2, position].astype(F32)
    stores[2].start()
    wide_out[...] = fin_v[2, 3].astype(F32)
    stores[3].start()
    ends_on(6, 8)
    small_load.wait()
    for position in range(4):
        rows = slice(position * share_rows, (position + 1) * share_rows)
        up_bias_v[:, rows] = small_v[BIAS_UP + position : BIAS_UP + position + 1, :share_rows]
    gains_v[0] = small_v[:2, :share_rows]
    biases_v[0] = small_v[2:BIAS_UP, :share_rows]
    for copy in small_stores:
        copy.start()
    for copy in stores + ends_copies + small_stores:
        copy.wait()


def on_device(
    dp_count,
    block_input,
    cotangent,
    window_group,
    w_qkv,
    w_out,
    w_up,
    w_down,
    up_bias,
    norm_gains,
    biases,
):
    rows, width = block_input.shape
    piece = rows // PIECES
    pairs = width // LANES
    share_rows = width // dp_count
    small_width = max(share_rows, LANES)
    dp_steps = dp_count.bit_length() - 1
    split = SPLIT if share_rows % (16 * SPLIT) == 0 else 1
    jobs = 3 * split
    slots = jobs + (len(DP_FIRST) if split == SPLIT else 0)
    any_spec = pl.BlockSpec(memory_space=pl.ANY)
    vmem_spec = pl.BlockSpec(memory_space=pltpu.VMEM)
    smem_spec = pl.BlockSpec(memory_space=pltpu.SMEM)
    dma = pltpu.SemaphoreType.DMA
    vmem = pltpu.VMEM
    ends_in, fin, small = pl.pallas_call(
        functools.partial(layer_kernel, dp_count),
        out_shape=(
            jax.ShapeDtypeStruct((PIECES, piece, width), F32),
            jax.ShapeDtypeStruct((3, 4, share_rows, width), BF16),
            jax.ShapeDtypeStruct((16, small_width), F32),
        ),
        in_specs=[smem_spec] + [any_spec] * 6 + [vmem_spec] * 3,
        out_specs=(any_spec,) * 3,
        scratch_shapes=[
            vmem((width, 3 * width), BF16),
            vmem((width, width), BF16),
            vmem((width, 4 * width), BF16),
            vmem((4, width, width), BF16),
            vmem((12, width, width), BF16),
            vmem((PIECES, piece, width), BF16),
            vmem((width, rows), BF16),
            vmem((3, pairs, LANES, rows), BF16),
            vmem((PIECES, pairs, piece, LANES), BF16),
            vmem((PIECES, pairs, piece, LANES), BF16),
            vmem((PIECES, pairs, 2, piece, piece), BF16),
            vmem((pairs, 2, piece, piece), BF16),
            vmem((pairs, LANES, rows), BF16),
            vmem((width, rows), F32),
            vmem((width, rows), F32),
            vmem((PIECES, 2, 1, piece), F32),
            vmem((width, rows), BF16),
            vmem((4, width, rows), BF16),
            vmem((4, width, rows), BF16),
            vmem((width, rows), BF16),
            vmem((width, rows), BF16),
            vmem((pairs, LANES, piece), BF16),
            vmem((PIECES, width, piece), BF16),
            vmem((PIECES, width, piece), BF16),
            vmem((STATS, width, LANES), BF16),
            vmem((STATS, width, LANES), F32),
            vmem((2, 2, pairs, LANES, piece), F32),
            vmem((width, piece), F32),
            vmem((width, piece), F32),
            vmem((width, piece), F32),
            vmem((2, piece, width), F32),
            vmem((3, 2, width, width), BF16),
            vmem((3, width, width), BF16),
            vmem((slots, (width - share_rows) // split, width), BF16),
            vmem((3, 4, share_rows, width), BF16),
            vmem((dp_count, 16, small_width), F32),
            vmem((dp_count - 1, 16, small_width), F32),
            vmem((4, 16, small_width), F32),
            vmem((16, small_width), F32),
            dma((13,)),
            dma((PIECES,)),
            dma((PIECES,)),
            dma((PIECES,)),
            dma((jobs, 2)),
            dma((jobs, 2)),
            dma((jobs, 2)),
            dma((jobs, 2)),
            dma((jobs, dp_steps, 2)),
            dma((jobs, dp_steps, 2)),
            dma((jobs,)),
            dma((jobs,)),
            dma((jobs, 2)),
            dma((jobs, 2)),
            dma((dp_count - 1,)),
            dma((dp_count - 1,)),
            dma((3,)),
            dma((3,)),
            dma((jobs,)),
        ],
        compiler_params=pltpu.CompilerParams(
            collective_id=0, has_side_effects=True, vmem_limit_bytes=63 * 1024 * 1024
        ),
    )(
        window_group,
        block_input.reshape(PIECES, piece, width),
        cotangent.reshape(PIECES, piece, width),
        w_qkv,
        w_out,
        w_up,
        w_down,
        up_bias,
        norm_gains,
        biases,
    )
    return pl.pallas_call(
        finish_kernel,
        out_shape=(
            jax.ShapeDtypeStruct((1, rows, width), F32),
            jax.ShapeDtypeStruct((1, share_rows, 3 * width), F32),
            jax.ShapeDtypeStruct((1, share_rows, width), F32),
            jax.ShapeDtypeStruct((1, share_rows, 4 * width), F32),
            jax.ShapeDtypeStruct((1, 4 * share_rows, width), F32),
            jax.ShapeDtypeStruct((1, 4 * share_rows), F32),
            jax.ShapeDtypeStruct((1, 2, share_rows), F32),
            jax.ShapeDtypeStruct((1, 4, share_rows), F32),
        ),
        in_specs=[smem_spec] + [any_spec] * 3,
        out_specs=(any_spec,) * 8,
        scratch_shapes=[
            vmem((rows, width), F32),
            vmem((3, 4, share_rows, width), BF16),
            vmem((share_rows, 3 * width), F32),
            vmem((share_rows, width), F32),
            vmem((share_rows, 4 * width), F32),
            vmem((4 * share_rows, width), F32),
            vmem((16, small_width), F32),
            vmem((1, 4 * share_rows), F32),
            vmem((1, 2, share_rows), F32),
            vmem((1, 4, share_rows), F32),
            dma((16,)),
            dma((4,)),
            dma((7,)),
        ],
        compiler_params=pltpu.CompilerParams(vmem_limit_bytes=63 * 1024 * 1024),
    )(window_group, ends_in.reshape(rows, width), fin, small)


def solution(mesh):
    return jax.shard_map(
        functools.partial(on_device, mesh.shape["dp"]),
        mesh=mesh,
        in_specs=(
            P(("dp", "rep"), None),
            P(("dp", "rep"), None),
            P(("dp", "rep"), None),
            P("segment", None, None),
            P("segment", None, None),
            P("segment", None, None),
            P("segment", None, None),
            P("segment", None),
            P("segment", None, None),
            P("segment", None, None),
        ),
        out_specs=(
            P("segment", ("dp", "rep"), None),
            P("segment", "dp", None),
            P("segment", "dp", None),
            P("segment", "dp", None),
            P("segment", "dp", None),
            P("segment", "dp"),
            P("segment", None, "dp"),
            P("segment", None, "dp"),
        ),
        check_vma=False,
    )
```

```python
import functools
import math

import jax
import jax.numpy as jnp
from jax import lax
from jax.experimental import pallas as pl
from jax.experimental.pallas import tpu as pltpu
from jax.sharding import PartitionSpec as P

MESH = pl.DeviceIdType.MESH
F32 = jnp.float32
BF16 = jnp.bfloat16
HEADS = 8
LANES = 128
PIECES = 4
EPS = 1e-05
GAIN_ONE, GAIN_TWO, BIAS_OUT, BIAS_ONE, BIAS_DOWN, BIAS_TWO, BIAS_UP = range(7)
STATS = 10
CHUNK = 64
SPLIT = 4
DP_FIRST = (1, 5, 9)
SUM, CORE, SIDE, SIDED, DP, DPED, JOIN, LAST, SMALL = range(9)
ORDER_ONE = (
    (SUM, 0), (SUM, 2),
)
ORDER_TWO = (
    (CORE, 0), (SIDE, 0), (SUM, 4), (CORE, 3), (CORE, 2), (CORE, 1), (SIDE, 3), (SUM, 6), (SIDED, 0),
    (SIDE, 2),
)
ORDER_THREE = (
    (CORE, 4), (SIDED, 3), (CORE, 6), (SIDE, 6), (CORE, 5), (DP, 0), (SIDE, 4), (SUM, 8), (DPED, 0), (DP, 1),
    (SIDED, 2), (CORE, 7), (SIDE, 7), (SUM, 10), (DP, 3), (SIDED, 6), (CORE, 8), (SIDE, 8), (SIDED, 4),
    (DPED, 1), (DP, 2), (CORE, 9), (DP, 6), (DPED, 3), (CORE, 11), (SIDE, 11), (SIDED, 8), (DP, 4),
    (CORE, 10), (SMALL, 0), (DP, 5), (DPED, 6), (JOIN, 1), (JOIN, 3), (SIDED, 7), (DP, 9), (SIDE, 10),
    (SIDED, 11), (DP, 8), (DPED, 4), (DPED, 2), (SIDED, 10), (DP, 7), (DPED, 9), (DP, 11), (JOIN, 6),
    (JOIN, 4), (DPED, 5), (DPED, 8), (DP, 10), (DPED, 7), (SMALL, 1), (LAST, 6), (LAST, 1), (JOIN, 2),
    (DPED, 11), (LAST, 3), (JOIN, 0), (DPED, 10), (JOIN, 7), (JOIN, 8), (JOIN, 11), (JOIN, 9), (JOIN, 5),
    (LAST, 4), (SMALL, 2), (LAST, 0), (JOIN, 10), (LAST, 9), (LAST, 11), (LAST, 5), (LAST, 7), (LAST, 8),
    (LAST, 2), (LAST, 10),
)


def plain_orders():
    one = ((SUM, 0),)
    two = ((SUM, 1), (CORE, 0), (SIDE, 0))
    three = ((SUM, 2), (CORE, 1), (SIDE, 1), (CORE, 2), (SIDE, 2), (SMALL, 0), (SMALL, 1), (SMALL, 2))
    for stage in (SIDED, DP, DPED, JOIN, LAST):
        three += tuple((stage, job) for job in range(3))
    return one, two, three


def dot_plain(left, right):
    return lax.dot_general(left, right, (((1,), (0,)), ((), ())), preferred_element_type=F32)


def drain(parts):
    for _ in parts:
        pass


def side_by_side(one, two, behind):
    spent = [0, behind]
    live = [one, two]
    while live[0] or live[1]:
        which = 0 if live[0] and (not live[1] or spent[0] <= spent[1]) else 1
        cost = next(live[which], None)
        if cost is None:
            live[which] = None
        else:
            spent[which] += cost


def dot_turned(left, right):
    return lax.dot_general(left, right, (((1,), (1,)), ((), ())), preferred_element_type=F32)


def fold(values):
    total = values[:, :LANES]
    for start in range(LANES, values.shape[1], LANES):
        total = total + values[:, start : start + LANES]
    return total


def layer_kernel(
    dp_count,
    flag_ref,
    x_hbm,
    ct_hbm,
    w_qkv_hbm,
    w_out_hbm,
    w_up_hbm,
    w_down_hbm,
    up_bias_ref,
    gains_ref,
    biases_ref,
    ends_hbm,
    fin_hbm,
    small_hbm,
    w_qkv,
    w_out,
    w_up,
    w_down,
    turned,
    rows_in,
    x_t,
    qkv,
    keys_rm,
    values_rm,
    share,
    share_off,
    mixture,
    norm_one,
    norm_two,
    inverses,
    hidden_low,
    slope,
    active,
    down_grad,
    branch_grad,
    grad_mix,
    outgoing,
    incoming_grad,
    columns,
    sums,
    key_sums,
    wide_a,
    wide_b,
    wide_c,
    ends_v,
    core_in,
    side_in,
    dp_in,
    fin,
    small,
    small_dp,
    small_rep,
    small_out,
    load_sem,
    seg_send,
    seg_recv,
    ends_sem,
    core_send,
    core_recv,
    side_send,
    side_recv,
    dp_send,
    dp_recv,
    join_send,
    join_recv,
    last_send,
    last_recv,
    sdp_send,
    sdp_recv,
    srep_send,
    srep_recv,
    fin_sem,
):
    width = w_out.shape[0]
    piece = x_t.shape[1] // PIECES
    pairs = qkv.shape[1]
    share_rows = width // dp_count
    dp_steps = dp_count.bit_length() - 1
    segment = lax.axis_index("segment")
    dp = lax.axis_index("dp")
    rep = lax.axis_index("rep")
    core = lax.rem(rep, 2)
    side = lax.div(rep, 2)
    other_core = side * 2 + (1 - core)
    other_side = (1 - side) * 2 + core

    def load_copy(block):
        def span(first):
            return pl.ds(pl.multiple_of((block - first) * width, width), width)

        def copy_of(source, target):
            return pltpu.make_async_copy(source, target, load_sem.at[1 + block])

        return (
            lambda: copy_of(w_qkv_hbm.at[0, :, span(0)], w_qkv.at[:, span(0)]),
            lambda: copy_of(w_out_hbm.at[0], w_out),
            lambda: copy_of(w_up_hbm.at[0, :, span(4)], w_up.at[:, span(4)]),
            lambda: copy_of(w_down_hbm.at[0, span(8), :], w_down.at[block - 8]),
        )

    parts_of_load = ((0, 3), (3, 4), (4, 8), (8, 12))
    first_rows = pltpu.make_async_copy(x_hbm, rows_in, load_sem.at[0])
    last_rows = pltpu.make_async_copy(ct_hbm, rows_in, load_sem.at[0])

    @pl.when(segment == 0)
    def _():
        first_rows.start()

    @pl.when(segment == 1)
    def _():
        last_rows.start()

    for part, (first, after) in enumerate(parts_of_load):
        for block in range(first, after):
            load_copy(block)[part]().start()

    barrier = pltpu.get_barrier_semaphore()
    pl.semaphore_signal(
        barrier, inc=1, device_id={"segment": 1 - segment}, device_id_type=MESH
    )
    for step in range(1, 4):
        pl.semaphore_signal(
            barrier, inc=1, device_id={"rep": lax.rem(rep + step, 4)}, device_id_type=MESH
        )
    for step in range(1, dp_count):
        pl.semaphore_signal(
            barrier, inc=1, device_id={"dp": lax.rem(dp + step, dp_count)}, device_id_type=MESH
        )

    params = [gains_ref[0].astype(F32), biases_ref[0].astype(F32)]
    for block in range(4):
        params.append(up_bias_ref[:, block * width : (block + 1) * width].astype(F32))
    params.append(jnp.zeros((16 - STATS, width), F32))
    upright = jnp.concatenate(params, axis=0).T
    for index in range(STATS):
        columns[index] = jnp.broadcast_to(upright[:, index : index + 1], (width, LANES)).astype(BF16)
    for index in range(STATS):
        sums[index] = jnp.zeros((width, LANES), F32)
    key_sums[0] = jnp.zeros(key_sums.shape[1:], F32)

    chunks = [slice(start, start + CHUNK) for start in range(0, width, CHUNK)]

    def turn(part):
        def one(block, carry):
            load_copy(block)[part]().wait()
            if part == 3:
                turned[block] = w_down[block - 8].T
            elif part == 1:
                turned[block] = w_out[...].T
            else:
                first = parts_of_load[part][0]
                span = pl.ds(pl.multiple_of((block - first) * width, width), width)
                turned[block] = (w_qkv if part == 0 else w_up)[:, span].T
            return carry

        lax.fori_loop(*parts_of_load[part], one, 0)

    def turn_apart(first, after):
        for block in range(first, after):
            part = (0, 0, 0, 1, 2, 2, 2, 2, 3, 3, 3, 3)[block]
            load_copy(block)[part]().wait()
            span = slice(block % 4 * width, (block % 4 + 1) * width)
            if part == 0:
                turned[block] = w_qkv[:, span].T
            elif part == 1:
                turned[block] = w_out[...].T
            elif part == 2:
                turned[block] = w_up[:, span].T
            else:
                turned[block] = w_down[block - 8].T
            yield 230

    first_rows.wait()

    flag = flag_ref[0, 0].astype(F32)

    def lanes_of(index):
        if isinstance(index, int):
            return pl.ds(index * piece, piece)
        return pl.ds(pl.multiple_of(index * piece, piece), piece)

    def forward_copy(index):
        return pltpu.make_async_remote_copy(
            src_ref=outgoing.at[index],
            dst_ref=x_t.at[:, lanes_of(index)],
            send_sem=seg_send.at[index],
            recv_sem=seg_recv.at[index],
            device_id={"segment": 1 - segment},
            device_id_type=MESH,
        )

    def backward_copy(index):
        return pltpu.make_async_remote_copy(
            src_ref=outgoing.at[index],
            dst_ref=incoming_grad.at[index],
            send_sem=seg_send.at[index],
            recv_sem=seg_recv.at[index],
            device_id={"segment": 1 - segment},
            device_id_type=MESH,
        )

    def ends_copy(index):
        return pltpu.make_async_copy(
            ends_v.at[lax.rem(index, 2)], ends_hbm.at[index], ends_sem.at[index]
        )

    def free_ends(index):
        @pl.when(index >= 2)
        def _():
            ends_copy(index - 2).wait()

    def own_rows(index):
        half = lax.rem(index, 2)
        whole = jnp.where(index < 2, 1.0, 0.0).astype(F32)
        weight = whole * flag + (1.0 - whole) * (1.0 - flag)
        picked = rows_in[half].astype(F32) * weight + rows_in[2 + half].astype(F32) * (1.0 - weight)
        return picked.T

    def by_queries(values):
        half = LANES // 2
        blank = jnp.zeros((half, LANES), values.dtype)
        parts = []
        for part in range(2):
            span = slice(part * LANES, (part + 1) * LANES)
            first = jnp.concatenate([values[:half, span], blank], axis=0)
            second = jnp.concatenate([blank, values[half:, span]], axis=0)
            parts.append(jnp.concatenate([first, second], axis=1))
        return parts

    def against(rows_ref, index, pair, parts, has_off):
        own = rows_ref[index, pair]
        products = [dot_plain(own[:LANES], parts[0]), dot_plain(own, parts[1])]
        if has_off:
            before = rows_ref[0, pair]
            products += [dot_plain(before, parts[0]), dot_plain(before, parts[1])]
        return products

    def tiles_of(products, head, part, has_off):
        lanes = slice(head * LANES, (head + 1) * LANES)
        own = products[part]
        tiles = [own[part * LANES : (part + 1) * LANES, lanes]]
        if part:
            tiles.append(own[:LANES, lanes])
        if has_off:
            off = products[2 + part]
            tiles += [off[:LANES, lanes], off[LANES:, lanes]]
        return tiles

    def joined(lows, has_off):
        blank = jnp.zeros((LANES, LANES), BF16)
        first = jnp.concatenate([lows[0][0], blank], axis=0)
        second = jnp.concatenate([lows[1][1], lows[1][0]], axis=0)
        whole = jnp.concatenate([first, second], axis=1)
        if not has_off:
            return whole, None
        first = jnp.concatenate(lows[0][-2:], axis=0)
        second = jnp.concatenate(lows[1][-2:], axis=0)
        return whole, jnp.concatenate([first, second], axis=1)

    def attend(index, has_off):
        lanes = lanes_of(index)
        half = LANES // 2
        key_at = lax.broadcasted_iota(jnp.int32, (LANES, LANES), 0)
        query_at = lax.broadcasted_iota(jnp.int32, (LANES, LANES), 1)
        allowed = key_at <= query_at

        def scores_of(pair):
            return against(
                keys_rm, index, pair, by_queries(qkv[0, pair, :, lanes]), has_off
            )

        ahead = scores_of(0)
        for pair in range(pairs):
            scores = ahead
            if pair + 1 < pairs:
                ahead = scores_of(pair + 1)
            mixed = []
            for head in range(2):
                rows = slice(head * half, (head + 1) * half)
                lows = []
                for part in range(2):
                    tiles = tiles_of(scores, head, part, has_off)
                    tiles[0] = jnp.where(allowed, tiles[0], -1e30)
                    top = jnp.max(functools.reduce(jnp.maximum, tiles), axis=0, keepdims=True)
                    raised = [jnp.exp(tile - top) for tile in tiles]
                    total = functools.reduce(jnp.add, raised)
                    scale = 1.0 / jnp.sum(total, axis=0, keepdims=True)
                    lows.append([(tile * scale).astype(BF16) for tile in raised])
                low, low_off = joined(lows, has_off)
                share[index, pair, head] = low
                mix = dot_plain(qkv[2, pair, rows, lanes], low)
                if has_off:
                    share_off[pair, head] = low_off
                    mix = mix + dot_plain(qkv[2, pair, rows, :piece], low_off)
                mixed.append(mix.astype(BF16))
            mixture[pair, :, lanes] = jnp.concatenate(mixed, axis=0)
            yield 280

    def part_sum(values):
        return jnp.sum(values.reshape(values.shape[0] // 8, 8, values.shape[1]), axis=0)

    def full_mean(parts):
        return jnp.sum(parts, axis=0, keepdims=True) * (1.0 / width)

    def column(index, rows):
        part = columns[index, rows, :].astype(F32)
        return jnp.concatenate([part] * (piece // LANES), axis=1)

    def gather_sum(index, rows, values):
        sums[index, rows, :] = sums[index, rows, :] + fold(values)

    def norm_chunks(index, which, wide_a, total):
        mean = full_mean(total)
        spread = jnp.zeros((8, piece), F32)
        for rows in chunks:
            centred = wide_a[rows, :] - mean
            spread = spread + part_sum(centred * centred)
        inverse = lax.rsqrt(full_mean(spread) + EPS)
        inverses[index, which] = inverse
        return mean, inverse

    def forward_start(index):
        @pl.when(segment == 0)
        def _():
            x_t[:, lanes_of(index)] = own_rows(index).astype(BF16)

        @pl.when(segment == 1)
        def _():
            forward_copy(index).wait_recv()

    def forward_first(index):
        lanes = lanes_of(index)
        inputs = x_t[:, lanes]
        score_scale = 1.0 / math.sqrt(width // HEADS)
        for block in range(3):
            result = dot_plain(turned[block], inputs)
            for pair in range(pairs):
                low = result[pair * LANES : (pair + 1) * LANES]
                low = (low * score_scale if block == 0 else low).astype(BF16)
                qkv[block, pair, :, lanes] = low
                if block == 1:
                    keys_rm[index, pair] = low.T
                if block == 2:
                    values_rm[index, pair] = low.T
            yield 270

    def forward_rest(index, wide_a):
        lanes = lanes_of(index)
        branch = dot_plain(turned[3], mixture[:, :, lanes].reshape(width, piece))
        yield 250
        total = jnp.zeros((8, piece), F32)
        for rows in chunks:
            sum_one = x_t[rows, lanes].astype(F32) + (branch[rows] + column(BIAS_OUT, rows))
            wide_a[rows, :] = sum_one
            total = total + part_sum(sum_one)
            yield 25
        mean, inverse = norm_chunks(index, 0, wide_a, total)
        yield 150
        for rows in chunks:
            normed = (wide_a[rows, :] - mean) * inverse
            norm_one[rows, lanes] = normed
            hidden = normed * column(GAIN_ONE, rows) + column(BIAS_ONE, rows)
            hidden_low[rows, lanes] = hidden.astype(BF16)
            yield 30

        branch_two = None
        for block in range(4):
            pre_block = dot_plain(turned[4 + block], hidden_low[:, lanes])
            yield 50
            lows = []
            for rows in chunks:
                pre = pre_block[rows] + column(BIAS_UP + block, rows)
                level = (lax.erf(pre * (1.0 / math.sqrt(2.0))) + 1.0) * 0.5
                bell = jnp.exp2(pre * pre * (-0.5 * math.log2(math.e)))
                lows.append((pre * level).astype(BF16))
                active[block, rows, lanes] = lows[-1]
                slope[block, rows, lanes] = (
                    level + pre * bell * (1.0 / math.sqrt(2.0 * math.pi))
                ).astype(BF16)
                yield 65
            part = dot_plain(turned[8 + block], jnp.concatenate(lows, axis=0))
            branch_two = part if branch_two is None else branch_two + part
            yield 100
        total = jnp.zeros((8, piece), F32)
        for rows in chunks:
            hidden = norm_one[rows, lanes] * column(GAIN_ONE, rows) + column(BIAS_ONE, rows)
            sum_two = hidden + (branch_two[rows] + column(BIAS_DOWN, rows))
            wide_a[rows, :] = sum_two
            total = total + part_sum(sum_two)
            yield 25
        mean, inverse = norm_chunks(index, 1, wide_a, total)
        yield 150
        for rows in chunks:
            norm_two[rows, lanes] = (wide_a[rows, :] - mean) * inverse
            yield 20

    def forward_end(index):
        for rows in chunks:
            outgoing[index, rows, :] = output_rows(rows, lanes_of(index)).astype(BF16)
        forward_copy(index).start()

    def off_or_not(index, run):
        @pl.when(index == 1)
        def _():
            drain(run(index, True))

        @pl.when(index != 1)
        def _():
            drain(run(index, False))

    def forward(index):
        forward_start(index)
        drain(forward_first(index))
        off_or_not(index, attend)
        drain(forward_rest(index, wide_a))

        @pl.when(segment == 0)
        def _():
            forward_end(index)

    def output_rows(rows, lanes):
        return norm_two[rows, lanes] * column(GAIN_TWO, rows) + column(BIAS_TWO, rows)

    def last_outputs(index, carry):
        free_ends(index)
        for start in range(0, width, LANES):
            rows = slice(start, start + LANES)
            ends_v[lax.rem(index, 2), :, rows] = output_rows(rows, lanes_of(index)).T
        ends_copy(index).start()
        return carry

    def attend_back(index, has_off):
        lanes = lanes_of(index)
        slot = (1 if index == 0 else 0) if isinstance(index, int) else jnp.where(index == 0, 1, 0)
        half = LANES // 2
        score_scale = 1.0 / math.sqrt(width // HEADS)

        def backs_of(pair):
            return against(values_rm, index, pair, by_queries(grad_mix[pair]), has_off)

        ahead = backs_of(0)
        for pair in range(pairs):
            backs = ahead
            if pair + 1 < pairs:
                ahead = backs_of(pair + 1)
            results = ([], [], [])
            for head in range(2):
                rows = slice(head * half, (head + 1) * half)
                low = share[index, pair, head]
                low_off = share_off[pair, head] if has_off else None
                lows = []
                for part in range(2):
                    place = slice(part * LANES, (part + 1) * LANES)
                    wides = [low[place, place]]
                    if part:
                        wides.append(low[:LANES, place])
                    if has_off:
                        wides += [low_off[:LANES, place], low_off[LANES:, place]]
                    wides = [tile.astype(F32) for tile in wides]
                    tiles = tiles_of(backs, head, part, has_off)
                    products = [wide * tile for wide, tile in zip(wides, tiles)]
                    inner = jnp.sum(functools.reduce(jnp.add, products), axis=0, keepdims=True)
                    lows.append(
                        [
                            (product - wide * inner).astype(BF16)
                            for product, wide in zip(products, wides)
                        ]
                    )
                grad_scores, grad_off = joined(lows, has_off)
                queries = qkv[0, pair, rows, lanes]
                grads = grad_mix[pair, rows]
                grad_query = dot_plain(qkv[1, pair, rows, lanes], grad_scores)
                grad_key = dot_turned(queries, grad_scores) + key_sums[slot, 0, pair, rows]
                grad_value = dot_turned(grads, low) + key_sums[slot, 1, pair, rows]
                if has_off:
                    grad_query = grad_query + dot_plain(qkv[1, pair, rows, :piece], grad_off)
                    key_sums[1, 0, pair, rows] = dot_turned(queries, grad_off)
                    key_sums[1, 1, pair, rows] = dot_turned(grads, low_off)
                for kept, grad in zip(results, (grad_query * score_scale, grad_key, grad_value)):
                    kept.append(grad.astype(BF16))
            for block in range(3):
                qkv[block, pair, :, lanes] = jnp.concatenate(results[block], axis=0)
            yield 440

    def backward_start(index):
        @pl.when(segment == 0)
        def _():
            backward_copy(index).wait_recv()

    def backward_norm(index):
        lanes = lanes_of(index)
        plain = jnp.zeros((8, piece), F32)
        inner = jnp.zeros((8, piece), F32)
        for rows in chunks:
            grad = incoming_grad[index, rows, :].astype(F32)
            product = grad * norm_two[rows, lanes]
            gather_sum(GAIN_TWO, rows, product)
            gather_sum(BIAS_TWO, rows, grad)
            gain = column(GAIN_TWO, rows)
            plain = plain + part_sum(grad * gain)
            inner = inner + part_sum(product * gain)
            yield 40
        plain = full_mean(plain)
        inner = full_mean(inner)
        inverse = inverses[index, 1]
        for rows in chunks:
            scaled = incoming_grad[index, rows, :].astype(F32) * column(GAIN_TWO, rows)
            grad_two = (scaled - plain - norm_two[rows, lanes] * inner) * inverse
            gather_sum(BIAS_DOWN, rows, grad_two)
            wide_a[rows, :] = grad_two
            down_grad[rows, lanes] = grad_two.astype(BF16)
            yield 40

    def backward_feed(index):
        lanes = lanes_of(index)
        for block in range(4):
            back = dot_plain(w_down[block], down_grad[:, lanes])
            for rows in chunks:
                grad_pre = back[rows] * slope[block, rows, lanes].astype(F32)
                gather_sum(BIAS_UP + block, rows, grad_pre)
                slope[block, rows, lanes] = grad_pre.astype(BF16)
            yield 250

        through = dot_plain(w_up[...], slope[:, :, lanes].reshape(4 * width, piece))
        plain = jnp.zeros((8, piece), F32)
        inner = jnp.zeros((8, piece), F32)
        for rows in chunks:
            grad_hidden = wide_a[rows, :] + through[rows]
            wide_a[rows, :] = grad_hidden
            product = grad_hidden * norm_one[rows, lanes]
            gather_sum(GAIN_ONE, rows, product)
            gather_sum(BIAS_ONE, rows, grad_hidden)
            gain = column(GAIN_ONE, rows)
            plain = plain + part_sum(grad_hidden * gain)
            inner = inner + part_sum(product * gain)
            yield 120 if rows.start == 0 else 45
        plain = full_mean(plain)
        inner = full_mean(inner)
        inverse = inverses[index, 0]
        for rows in chunks:
            scaled = wide_a[rows, :] * column(GAIN_ONE, rows)
            grad_one = (scaled - plain - norm_one[rows, lanes] * inner) * inverse
            gather_sum(BIAS_OUT, rows, grad_one)
            wide_b[rows, :] = grad_one
            branch_grad[rows, lanes] = grad_one.astype(BF16)
            yield 40
        grad_mix[...] = (
            dot_plain(w_out[...], branch_grad[:, lanes]).astype(BF16).reshape(pairs, LANES, piece)
        )
        yield 300

    def backward_attention(index):
        off_or_not(index, attend_back)
        through = dot_plain(w_qkv[...], qkv[:, :, :, lanes_of(index)].reshape(3 * width, piece))

        @pl.when(segment == 1)
        def _():
            for rows in chunks:
                outgoing[index, rows, :] = (wide_b[rows, :] + through[rows]).astype(BF16)
            backward_copy(index).start()

        @pl.when(segment == 0)
        def _():
            free_ends(index)
            for start in range(0, width, LANES):
                rows = slice(start, start + LANES)
                ends_v[lax.rem(index, 2), :, rows] = (wide_b[rows, :] + through[rows]).T
            ends_copy(index).start()

    def backward_both(index, forward_index):
        forward_copy(forward_index).wait_recv()

        def back():
            yield from backward_norm(index)
            yield from backward_feed(index)
            yield from attend_back(index, False)
            through = dot_plain(w_qkv[...], qkv[:, :, :, lanes_of(index)].reshape(3 * width, piece))
            for rows in chunks:
                outgoing[index, rows, :] = (wide_b[rows, :] + through[rows]).astype(BF16)
                yield 90

        def ahead():
            yield from forward_first(forward_index)
            yield from attend(forward_index, False)
            yield from forward_rest(forward_index, wide_c)

        side_by_side(back(), ahead(), 300)
        backward_copy(index).start()

    split = SPLIT if share_rows % (16 * SPLIT) == 0 else 1
    dp_first = DP_FIRST if split == SPLIT else ()
    orders = (ORDER_ONE, ORDER_TWO, ORDER_THREE) if split == SPLIT else plain_orders()
    jobs = 3 * split
    cut_rows = share_rows // split
    job_rows = width // split

    def base_of(job):
        return (8, 4, 0)[job // split]

    def job_span(job):
        return pl.ds(job % split * job_rows, job_rows)

    def fin_rows(job):
        return pl.ds(job % split * cut_rows, cut_rows)

    def parts_of(job):
        return range(2) if job in dp_first else range(1)

    def core_copies(job):
        return [
            pltpu.make_async_remote_copy(
                src_ref=turned.at[base_of(job) + 2 * (1 - core) + each, job_span(job)],
                dst_ref=core_in.at[job // split, each, job_span(job)],
                send_sem=core_send.at[job, each],
                recv_sem=core_recv.at[job, each],
                device_id={"rep": other_core},
                device_id_type=MESH,
            )
            for each in range(2)
        ]

    def side_copies(job):
        base = base_of(job)
        copies = []
        for each in parts_of(job):
            if job in dp_first:
                source = turned.at[base + 2 * core + each, dp_rows(job, dp_steps - 1)[1]]
                target = side_in.at[
                    job // split, pl.ds(job % split * job_rows + each * cut_rows, cut_rows)
                ]
            else:
                source = turned.at[base + 2 * core + (1 - side), job_span(job)]
                target = side_in.at[job // split, job_span(job)]
            copies.append(
                pltpu.make_async_remote_copy(
                    src_ref=source,
                    dst_ref=target,
                    send_sem=side_send.at[job, each],
                    recv_sem=side_recv.at[job, each],
                    device_id={"rep": other_side},
                    device_id_type=MESH,
                )
            )
        return copies

    def dp_slot(job):
        return sum(len(parts_of(before)) for before in range(job))

    def dp_rows(job, step):
        count = dp_count // 2
        start = 0
        for bit in range(step):
            start = start + lax.rem(lax.div(dp, 2**bit), 2) * count
            count = count // 2
        mine = lax.rem(lax.div(dp, 2**step), 2)
        first = job % split * job_rows
        sent = pl.multiple_of(first + (start + (1 - mine) * count) * cut_rows, cut_rows)
        kept = pl.multiple_of(first + (start + mine * count) * cut_rows, cut_rows)
        return pl.ds(sent, count * cut_rows), pl.ds(kept, count * cut_rows)

    def dp_landing(step):
        count = dp_count // 2 ** (step + 1)
        return pl.ds((dp_count - 2 * count) * cut_rows, count * cut_rows)

    def dp_copies(job, step):
        mine = lax.rem(lax.div(dp, 2**step), 2)
        copies = []
        for each in parts_of(job):
            position = base_of(job) + 2 * core + (each if job in dp_first else side)
            copies.append(
                pltpu.make_async_remote_copy(
                    src_ref=turned.at[position, dp_rows(job, step)[0]],
                    dst_ref=dp_in.at[dp_slot(job) + each, dp_landing(step)],
                    send_sem=dp_send.at[job, step, each],
                    recv_sem=dp_recv.at[job, step, each],
                    device_id={"dp": dp + (1 - 2 * mine) * 2**step},
                    device_id_type=MESH,
                )
            )
        return copies

    def join_copy(job):
        part = fin.at[job // split, 2 * core + side, fin_rows(job)]
        return pltpu.make_async_remote_copy(
            src_ref=part,
            dst_ref=part,
            send_sem=join_send.at[job],
            recv_sem=join_recv.at[job],
            device_id={"rep": other_side},
            device_id_type=MESH,
        )

    def last_copies(job):
        copies = []
        for each in range(2):
            part = fin.at[job // split, 2 * core + each, fin_rows(job)]
            copies.append(
                pltpu.make_async_remote_copy(
                    src_ref=part,
                    dst_ref=part,
                    send_sem=last_send.at[job, each],
                    recv_sem=last_recv.at[job, each],
                    device_id={"rep": other_core},
                    device_id_type=MESH,
                )
            )
        return copies

    def fin_copy(job):
        return pltpu.make_async_copy(
            fin.at[job // split, :, fin_rows(job)],
            fin_hbm.at[job // split, :, fin_rows(job)],
            fin_sem.at[job],
        )

    def arrived(*copies):
        for copy in copies:
            copy.wait_send()
        for copy in copies:
            copy.wait_recv()

    def start_all(copies):
        for copy in copies:
            copy.start()

    def turned_bits(value, count):
        place = 0
        while count > 1:
            place = place * 2 + value % 2
            value = value // 2
            count = count // 2
        return place

    pack = min(2, split)

    def left_rows(source, part):
        count = pack * cut_rows
        start = part * pack * cut_rows
        return jnp.concatenate(
            [source(index * share_rows + start, count) for index in range(dp_count)], axis=0
        )

    def keep_rows(block, part, result):
        for index in range(dp_count):
            for each in range(pack):
                target = (part * pack + each) * job_rows + turned_bits(index, dp_count) * cut_rows
                start = (index * pack + each) * cut_rows
                turned[block, target : target + cut_rows, :] = result[start : start + cut_rows]

    def down_blocks(part, tokens, add):
        count = width // (4 * share_rows)

        def one(block, carry):
            pieces = []
            for each in range(4 * count):
                start = each * share_rows + part * pack * cut_rows
                pieces.append(active[block, start : start + pack * cut_rows, tokens])
            result = dot_turned(jnp.concatenate(pieces, axis=0), down_grad[:, tokens])
            high = lax.rem(block, 2) * 2 + lax.div(block, 2)
            for each in range(count):
                place = turned_bits(each, count) * 4 + high
                for position in range(4):
                    for job in range(pack):
                        target = (part * pack + job) * job_rows + place * cut_rows
                        rows = pl.ds(pl.multiple_of(target, cut_rows), cut_rows)
                        start = ((each * 4 + position) * pack + job) * cut_rows
                        total = result[start : start + cut_rows]
                        if add:
                            total = total + turned[8 + position, rows, :].astype(F32)
                        turned[8 + position, rows, :] = total.astype(BF16)
            return carry

        lax.fori_loop(0, 4, one, 0)

    half_tokens = PIECES // 2 * piece

    def early_down_sums():
        for part in range(split // pack):
            down_blocks(part, slice(0, half_tokens), False)

    def down_sums(part):
        @pl.when(segment == 0)
        def _():
            down_blocks(part, slice(half_tokens, 2 * half_tokens), True)

        @pl.when(segment == 1)
        def _():
            down_blocks(part, slice(0, 2 * half_tokens), False)

    def up_sums(part):
        def one(block, carry):
            left = left_rows(lambda start, count: hidden_low[start : start + count, :], part)
            keep_rows(4 + block, part, dot_turned(left, slope[block]).astype(BF16))
            return carry

        lax.fori_loop(0, 4, one, 0)

    def qkv_sums(part):
        def one(block, carry):
            left = left_rows(lambda start, count: x_t[start : start + count, :], part)
            grads = qkv[block].reshape(width, PIECES * piece)
            keep_rows(block, part, dot_turned(left, grads).astype(BF16))
            return carry

        lax.fori_loop(0, 3, one, 0)
        left = left_rows(
            lambda start, count: mixture[start // LANES, start % LANES : start % LANES + count, :], part
        )
        keep_rows(3, part, dot_turned(left, branch_grad[...]).astype(BF16))

    def sums_of(job):
        (down_sums, up_sums, qkv_sums)[job // split](job % split // pack)
        for each in range(pack):
            start_all(core_copies(job + each))

    def after_core(job):
        arrived(*core_copies(job))
        rows = job_span(job)
        for each in parts_of(job):
            place = 1 - side if each == 0 else side
            position = base_of(job) + 2 * core + place
            turned[position, rows, :] = (
                turned[position, rows, :].astype(F32)
                + core_in[job // split, place, rows, :].astype(F32)
            ).astype(BF16)
        if job in dp_first:
            start_all(dp_copies(job, 0))

    def start_side(job):
        start_all(side_copies(job))

    def after_side(job):
        arrived(*side_copies(job))
        rows = job_span(job)
        position = base_of(job) + 2 * core + side
        turned[position, rows, :] = (
            turned[position, rows, :].astype(F32)
            + core_in[job // split, side, rows, :].astype(F32)
            + side_in[job // split, rows, :].astype(F32)
        ).astype(BF16)
        start_all(dp_copies(job, 0))

    def dp_total(job, step, each):
        position = base_of(job) + 2 * core + (each if job in dp_first else side)
        kept = turned[position, dp_rows(job, step)[1], :].astype(F32)
        return position, kept + dp_in[dp_slot(job) + each, dp_landing(step), :].astype(F32)

    def after_dp(job):
        for step in range(dp_steps - 1):
            arrived(*dp_copies(job, step))
            for each in parts_of(job):
                position, total = dp_total(job, step, each)
                turned[position, dp_rows(job, step)[1], :] = total.astype(BF16)
            start_all(dp_copies(job, step + 1))

    def after_last_dp(job):
        step = dp_steps - 1
        arrived(*dp_copies(job, step))
        for each in parts_of(job):
            position, total = dp_total(job, step, each)
            if job in dp_first:
                turned[position, dp_rows(job, step)[1], :] = total.astype(BF16)
            else:
                fin[job // split, 2 * core + side, fin_rows(job), :] = total.astype(BF16)
        if job in dp_first:
            start_side(job)
        else:
            join_copy(job).start()

    def after_join(job):
        if job in dp_first:
            arrived(*side_copies(job))
            for each in range(2):
                rows = pl.ds(job % split * job_rows + each * cut_rows, cut_rows)
                own = turned[base_of(job) + 2 * core + each, dp_rows(job, dp_steps - 1)[1], :]
                total = own.astype(F32) + side_in[job // split, rows, :].astype(F32)
                fin[job // split, 2 * core + each, fin_rows(job), :] = total.astype(BF16)
        else:
            arrived(join_copy(job))
        start_all(last_copies(job))

    def after_last(job):
        arrived(*last_copies(job))
        fin_copy(job).start()

    def small_dp_copy(step):
        target = lax.rem(dp + step, dp_count)
        return pltpu.make_async_remote_copy(
            src_ref=small.at[target],
            dst_ref=small_dp.at[step - 1],
            send_sem=sdp_send.at[step - 1],
            recv_sem=sdp_recv.at[step - 1],
            device_id={"dp": target},
            device_id_type=MESH,
        )

    def small_rep_copy(step):
        return pltpu.make_async_remote_copy(
            src_ref=small_rep.at[rep],
            dst_ref=small_rep.at[rep],
            send_sem=srep_send.at[step - 1],
            recv_sem=srep_recv.at[step - 1],
            device_id={"rep": lax.rem(rep + step, 4)},
            device_id_type=MESH,
        )

    small_copy = pltpu.make_async_copy(small_out, small_hbm, load_sem.at[0])

    def small_step(stage):
        if stage == 0:
            rows_of = [jnp.sum(sums[index].T, axis=0, keepdims=True) for index in range(STATS)]
            small[...] = jnp.zeros(small.shape, F32)
            for share_index in range(dp_count):
                for index in range(BIAS_UP):
                    start = share_index * share_rows
                    small[share_index, index : index + 1, :share_rows] = rows_of[index][
                        :, start : start + share_rows
                    ]
                for part in range(4):
                    start = (share_index * 4 + part) * share_rows
                    block, start = start // width, start % width
                    small[share_index, BIAS_UP + part : BIAS_UP + part + 1, :share_rows] = rows_of[
                        BIAS_UP + block
                    ][:, start : start + share_rows]
            for step in range(1, dp_count):
                small_dp_copy(step).start()
        elif stage == 1:
            total = small[dp]
            for step in range(1, dp_count):
                arrived(small_dp_copy(step))
                total = total + small_dp[step - 1]
            small_rep[rep] = total
            for step in range(1, 4):
                small_rep_copy(step).start()
        else:
            for step in range(1, 4):
                arrived(small_rep_copy(step))
            small_out[...] = (small_rep[0] + small_rep[1]) + (small_rep[2] + small_rep[3])
            small_copy.start()

    def run(order):
        steps = (
            sums_of,
            after_core,
            start_side,
            after_side,
            after_dp,
            after_last_dp,
            after_join,
            after_last,
            small_step,
        )
        for stage, job in order:
            steps[stage](job)

    def one_step(step, carry):
        first_index = jnp.where(step < 4, step, jnp.where(step < 6, 5 - step, step - 4))
        last_index = jnp.where(step < 2, step, jnp.where(step == 2, 1, 3))
        index = jnp.minimum(jnp.where(segment == 0, first_index, last_index), PIECES - 1)
        is_last = jnp.where(step == 2 * PIECES, 1, 0)
        begun = jnp.where(step + segment == 0, 0, 1)
        is_forward = jnp.where(step < jnp.where(segment == 0, 4, 2), begun, 0)
        last_backward = jnp.where(step == 2, 1, 0) + jnp.where(step == 5, 1, 0)
        is_backward = jnp.where(segment == 0, begun * (1 - is_forward) * (1 - is_last), last_backward)
        is_split = jnp.where(step >= 2 * PIECES - 1, 1 - segment, 0)
        is_rest = is_backward * (1 - is_split) + is_last * is_split

        @pl.when(is_forward == 1)
        def _():
            forward(index)

        @pl.when(is_backward == 1)
        def _():
            backward_start(index)
            drain(backward_norm(index))

        @pl.when(segment * step == 3)
        def _():
            backward_both(0, 2)

        @pl.when(segment * step == 4)
        def _():
            backward_both(2, 3)

        @pl.when(is_last == 1)
        def _():
            run(orders[0])

        @pl.when(is_rest == 1)
        def _():
            drain(backward_feed(index))

        @pl.when(is_last == 1)
        def _():
            run(orders[1])

        @pl.when(is_rest == 1)
        def _():
            backward_attention(index)

        @pl.when((1 - segment) * step == 5)
        def _():
            early_down_sums()

        return carry

    @pl.when(segment == 1)
    def _():
        for part in range(4):
            turn(part)
        for index in range(PIECES):
            incoming_grad[index] = own_rows(index).astype(BF16)

    @pl.when(segment == 0)
    def _():
        def ahead():
            x_t[:, lanes_of(0)] = own_rows(0).astype(BF16)
            yield from forward_first(0)
            yield from attend(0, False)
            yield from forward_rest(0, wide_a)

        drain(turn_apart(0, 1))
        side_by_side(ahead(), turn_apart(1, 12), -400)

    pl.semaphore_wait(barrier, 4 + dp_count - 1)

    @pl.when(segment == 0)
    def _():
        forward_end(0)

    lax.fori_loop(0, 2 * PIECES + 1, one_step, 0)

    cut = orders[2].index((SMALL, 0))
    run(orders[2][:cut])

    @pl.when(segment == 1)
    def _():
        lax.fori_loop(0, PIECES, last_outputs, 0)

    run(orders[2][cut:])

    for index in range(PIECES):

        @pl.when(segment == 0)
        def _():
            forward_copy(index).wait_send()

        @pl.when(segment == 1)
        def _():
            backward_copy(index).wait_send()

    for index in range(2, PIECES):
        ends_copy(index).wait()
    for job in range(jobs):
        fin_copy(job).wait()
    small_copy.wait()


def finish_kernel(
    flag_ref,
    ends_in,
    fin,
    small,
    ends,
    grad_qkv,
    grad_out,
    grad_up,
    grad_down,
    grad_up_bias,
    grad_gains,
    grad_biases,
    ends_v,
    fin_v,
    wide_qkv,
    wide_out,
    wide_up,
    wide_down,
    small_v,
    up_bias_v,
    gains_v,
    biases_v,
    ends_sem,
    in_sem,
    out_sem,
):
    half = ends_in.shape[0] // 2
    share_rows, width = fin.shape[2:]
    start = pl.multiple_of(half * (1 - flag_ref[0, 0]), half)
    cut = half // 4
    ends_copies = []
    ends_loads = []
    for part in range(8):
        source = pl.ds(part * cut, cut)
        offset = start + part * cut if part < 4 else part * cut - half + (half - start)
        target = pl.ds(pl.multiple_of(offset, cut), cut)
        ends_loads.append(
            pltpu.make_async_copy(ends_in.at[source], ends_v.at[source], ends_sem.at[part])
        )
        ends_copies.append(
            pltpu.make_async_copy(ends_v.at[source], ends.at[0, target], ends_sem.at[8 + part])
        )
    loads = [
        pltpu.make_async_copy(fin.at[group], fin_v.at[group], in_sem.at[group])
        for group in range(3)
    ]
    stores = [
        pltpu.make_async_copy(wide, target.at[0], out_sem.at[index])
        for index, (wide, target) in enumerate(
            ((wide_down, grad_down), (wide_up, grad_up), (wide_qkv, grad_qkv), (wide_out, grad_out))
        )
    ]
    small_load = pltpu.make_async_copy(small, small_v, in_sem.at[3])
    small_stores = [
        pltpu.make_async_copy(narrow, target, out_sem.at[4 + index])
        for index, (narrow, target) in enumerate(
            ((up_bias_v, grad_up_bias), (gains_v, grad_gains), (biases_v, grad_biases))
        )
    ]
    small_load.start()
    for group in range(3):
        loads[group].start()
        for copy in ends_loads[group * 3 : group * 3 + 3]:
            copy.start()

    def ends_on(first, after):
        for load, copy in zip(ends_loads[first:after], ends_copies[first:after]):
            load.wait()
            copy.start()

    loads[0].wait()
    for position in range(4):
        rows = slice(position * share_rows, (position + 1) * share_rows)
        wide_down[rows, :] = fin_v[0, position].astype(F32)
    stores[0].start()
    ends_on(0, 3)
    loads[1].wait()
    for position in range(4):
        wide_up[:, position * width : (position + 1) * width] = fin_v[1, position].astype(F32)
    stores[1].start()
    ends_on(3, 6)
    loads[2].wait()
    for position in range(3):
        wide_qkv[:, position * width : (position + 1) * width] = fin_v[2, position].astype(F32)
    stores[2].start()
    wide_out[...] = fin_v[2, 3].astype(F32)
    stores[3].start()
    ends_on(6, 8)
    small_load.wait()
    for position in range(4):
        rows = slice(position * share_rows, (position + 1) * share_rows)
        up_bias_v[:, rows] = small_v[BIAS_UP + position : BIAS_UP + position + 1, :share_rows]
    gains_v[0] = small_v[:2, :share_rows]
    biases_v[0] = small_v[2:BIAS_UP, :share_rows]
    for copy in small_stores:
        copy.start()
    for copy in stores + ends_copies + small_stores:
        copy.wait()


def on_device(
    dp_count,
    block_input,
    cotangent,
    window_group,
    w_qkv,
    w_out,
    w_up,
    w_down,
    up_bias,
    norm_gains,
    biases,
):
    rows, width = block_input.shape
    piece = rows // PIECES
    pairs = width // LANES
    share_rows = width // dp_count
    small_width = max(share_rows, LANES)
    dp_steps = dp_count.bit_length() - 1
    split = SPLIT if share_rows % (16 * SPLIT) == 0 else 1
    jobs = 3 * split
    slots = jobs + (len(DP_FIRST) if split == SPLIT else 0)
    any_spec = pl.BlockSpec(memory_space=pl.ANY)
    vmem_spec = pl.BlockSpec(memory_space=pltpu.VMEM)
    smem_spec = pl.BlockSpec(memory_space=pltpu.SMEM)
    dma = pltpu.SemaphoreType.DMA
    vmem = pltpu.VMEM
    ends_in, fin, small = pl.pallas_call(
        functools.partial(layer_kernel, dp_count),
        out_shape=(
            jax.ShapeDtypeStruct((PIECES, piece, width), F32),
            jax.ShapeDtypeStruct((3, 4, share_rows, width), BF16),
            jax.ShapeDtypeStruct((16, small_width), F32),
        ),
        in_specs=[smem_spec] + [any_spec] * 6 + [vmem_spec] * 3,
        out_specs=(any_spec,) * 3,
        scratch_shapes=[
            vmem((width, 3 * width), BF16),
            vmem((width, width), BF16),
            vmem((width, 4 * width), BF16),
            vmem((4, width, width), BF16),
            vmem((12, width, width), BF16),
            vmem((PIECES, piece, width), BF16),
            vmem((width, rows), BF16),
            vmem((3, pairs, LANES, rows), BF16),
            vmem((PIECES, pairs, piece, LANES), BF16),
            vmem((PIECES, pairs, piece, LANES), BF16),
            vmem((PIECES, pairs, 2, piece, piece), BF16),
            vmem((pairs, 2, piece, piece), BF16),
            vmem((pairs, LANES, rows), BF16),
            vmem((width, rows), F32),
            vmem((width, rows), F32),
            vmem((PIECES, 2, 1, piece), F32),
            vmem((width, rows), BF16),
            vmem((4, width, rows), BF16),
            vmem((4, width, rows), BF16),
            vmem((width, rows), BF16),
            vmem((width, rows), BF16),
            vmem((pairs, LANES, piece), BF16),
            vmem((PIECES, width, piece), BF16),
            vmem((PIECES, width, piece), BF16),
            vmem((STATS, width, LANES), BF16),
            vmem((STATS, width, LANES), F32),
            vmem((2, 2, pairs, LANES, piece), F32),
            vmem((width, piece), F32),
            vmem((width, piece), F32),
            vmem((width, piece), F32),
            vmem((2, piece, width), F32),
            vmem((3, 2, width, width), BF16),
            vmem((3, width, width), BF16),
            vmem((slots, (width - share_rows) // split, width), BF16),
            vmem((3, 4, share_rows, width), BF16),
            vmem((dp_count, 16, small_width), F32),
            vmem((dp_count - 1, 16, small_width), F32),
            vmem((4, 16, small_width), F32),
            vmem((16, small_width), F32),
            dma((13,)),
            dma((PIECES,)),
            dma((PIECES,)),
            dma((PIECES,)),
            dma((jobs, 2)),
            dma((jobs, 2)),
            dma((jobs, 2)),
            dma((jobs, 2)),
            dma((jobs, dp_steps, 2)),
            dma((jobs, dp_steps, 2)),
            dma((jobs,)),
            dma((jobs,)),
            dma((jobs, 2)),
            dma((jobs, 2)),
            dma((dp_count - 1,)),
            dma((dp_count - 1,)),
            dma((3,)),
            dma((3,)),
            dma((jobs,)),
        ],
        compiler_params=pltpu.CompilerParams(
            collective_id=0, has_side_effects=True, vmem_limit_bytes=63 * 1024 * 1024
        ),
    )(
        window_group,
        block_input.reshape(PIECES, piece, width),
        cotangent.reshape(PIECES, piece, width),
        w_qkv,
        w_out,
        w_up,
        w_down,
        up_bias,
        norm_gains,
        biases,
    )
    return pl.pallas_call(
        finish_kernel,
        out_shape=(
            jax.ShapeDtypeStruct((1, rows, width), F32),
            jax.ShapeDtypeStruct((1, share_rows, 3 * width), F32),
            jax.ShapeDtypeStruct((1, share_rows, width), F32),
            jax.ShapeDtypeStruct((1, share_rows, 4 * width), F32),
            jax.ShapeDtypeStruct((1, 4 * share_rows, width), F32),
            jax.ShapeDtypeStruct((1, 4 * share_rows), F32),
            jax.ShapeDtypeStruct((1, 2, share_rows), F32),
            jax.ShapeDtypeStruct((1, 4, share_rows), F32),
        ),
        in_specs=[smem_spec] + [any_spec] * 3,
        out_specs=(any_spec,) * 8,
        scratch_shapes=[
            vmem((rows, width), F32),
            vmem((3, 4, share_rows, width), BF16),
            vmem((share_rows, 3 * width), F32),
            vmem((share_rows, width), F32),
            vmem((share_rows, 4 * width), F32),
            vmem((4 * share_rows, width), F32),
            vmem((16, small_width), F32),
            vmem((1, 4 * share_rows), F32),
            vmem((1, 2, share_rows), F32),
            vmem((1, 4, share_rows), F32),
            dma((16,)),
            dma((4,)),
            dma((7,)),
        ],
        compiler_params=pltpu.CompilerParams(vmem_limit_bytes=63 * 1024 * 1024),
    )(window_group, ends_in.reshape(rows, width), fin, small)


def solution(mesh):
    return jax.shard_map(
        functools.partial(on_device, mesh.shape["dp"]),
        mesh=mesh,
        in_specs=(
            P(("dp", "rep"), None),
            P(("dp", "rep"), None),
            P(("dp", "rep"), None),
            P("segment", None, None),
            P("segment", None, None),
            P("segment", None, None),
            P("segment", None, None),
            P("segment", None),
            P("segment", None, None),
            P("segment", None, None),
        ),
        out_specs=(
            P("segment", ("dp", "rep"), None),
            P("segment", "dp", None),
            P("segment", "dp", None),
            P("segment", "dp", None),
            P("segment", "dp", None),
            P("segment", "dp"),
            P("segment", None, "dp"),
            P("segment", None, "dp"),
        ),
        check_vma=False,
    )
```

```python
import functools
import math

import jax
import jax.numpy as jnp
from jax import lax
from jax.experimental import pallas as pl
from jax.experimental.pallas import tpu as pltpu
from jax.sharding import PartitionSpec as P

MESH = pl.DeviceIdType.MESH
F32 = jnp.float32
BF16 = jnp.bfloat16
HEADS = 8
LANES = 128
PIECES = 4
EPS = 1e-05
GAIN_ONE, GAIN_TWO, BIAS_OUT, BIAS_ONE, BIAS_DOWN, BIAS_TWO, BIAS_UP = range(7)
STATS = 10
CHUNK = 64
SPLIT = 4
DP_FIRST = (1, 5, 9)
SUM, CORE, SIDE, SIDED, DP, DPED, JOIN, LAST, SMALL = range(9)
ORDER_ONE = (
    (SUM, 0), (SUM, 2),
)
ORDER_TWO = (
    (CORE, 0), (SIDE, 0), (SUM, 4), (CORE, 3), (CORE, 2), (CORE, 1), (SIDE, 3), (SUM, 6), (SIDED, 0),
    (SIDE, 2),
)
ORDER_THREE = (
    (CORE, 4), (SIDED, 3), (CORE, 6), (SIDE, 6), (CORE, 5), (DP, 0), (SIDE, 4), (SUM, 8), (DPED, 0), (DP, 1),
    (SIDED, 2), (CORE, 7), (SIDE, 7), (SUM, 10), (DP, 3), (SIDED, 6), (CORE, 8), (SIDE, 8), (SIDED, 4),
    (DPED, 1), (DP, 2), (CORE, 9), (DP, 6), (DPED, 3), (CORE, 11), (SIDE, 11), (SIDED, 8), (DP, 4),
    (CORE, 10), (SMALL, 0), (DP, 5), (DPED, 6), (JOIN, 1), (JOIN, 3), (SIDED, 7), (DP, 9), (SIDE, 10),
    (SIDED, 11), (DP, 8), (DPED, 4), (DPED, 2), (SIDED, 10), (DP, 7), (DPED, 9), (DP, 11), (JOIN, 6),
    (JOIN, 4), (DPED, 5), (DPED, 8), (DP, 10), (DPED, 7), (SMALL, 1), (LAST, 6), (LAST, 1), (JOIN, 2),
    (DPED, 11), (LAST, 3), (JOIN, 0), (DPED, 10), (JOIN, 7), (JOIN, 8), (JOIN, 11), (JOIN, 9), (JOIN, 5),
    (LAST, 4), (SMALL, 2), (LAST, 0), (JOIN, 10), (LAST, 9), (LAST, 11), (LAST, 5), (LAST, 7), (LAST, 8),
    (LAST, 2), (LAST, 10),
)


def plain_orders():
    one = ((SUM, 0),)
    two = ((SUM, 1), (CORE, 0), (SIDE, 0))
    three = ((SUM, 2), (CORE, 1), (SIDE, 1), (CORE, 2), (SIDE, 2), (SMALL, 0), (SMALL, 1), (SMALL, 2))
    for stage in (SIDED, DP, DPED, JOIN, LAST):
        three += tuple((stage, job) for job in range(3))
    return one, two, three


def dot_plain(left, right):
    return lax.dot_general(left, right, (((1,), (0,)), ((), ())), preferred_element_type=F32)


def drain(parts):
    for _ in parts:
        pass


def side_by_side(one, two, behind):
    spent = [0, behind]
    live = [one, two]
    while live[0] or live[1]:
        which = 0 if live[0] and (not live[1] or spent[0] <= spent[1]) else 1
        cost = next(live[which], None)
        if cost is None:
            live[which] = None
        else:
            spent[which] += cost


def dot_turned(left, right):
    return lax.dot_general(left, right, (((1,), (1,)), ((), ())), preferred_element_type=F32)


def fold(values):
    total = values[:, :LANES]
    for start in range(LANES, values.shape[1], LANES):
        total = total + values[:, start : start + LANES]
    return total


def layer_kernel(
    dp_count,
    flag_ref,
    x_hbm,
    ct_hbm,
    w_qkv_hbm,
    w_out_hbm,
    w_up_hbm,
    w_down_hbm,
    up_bias_ref,
    gains_ref,
    biases_ref,
    ends_hbm,
    fin_hbm,
    small_hbm,
    w_qkv,
    w_out,
    w_up,
    w_down,
    turned,
    rows_in,
    x_t,
    qkv,
    keys_rm,
    values_rm,
    share,
    share_off,
    mixture,
    norm_one,
    norm_two,
    inverses,
    hidden_low,
    slope,
    active,
    down_grad,
    branch_grad,
    grad_mix,
    outgoing,
    incoming_grad,
    columns,
    sums,
    key_sums,
    wide_a,
    wide_b,
    wide_c,
    ends_v,
    core_in,
    side_in,
    dp_in,
    fin,
    small,
    small_dp,
    small_rep,
    small_out,
    load_sem,
    seg_send,
    seg_recv,
    ends_sem,
    core_send,
    core_recv,
    side_send,
    side_recv,
    dp_send,
    dp_recv,
    join_send,
    join_recv,
    last_send,
    last_recv,
    sdp_send,
    sdp_recv,
    srep_send,
    srep_recv,
    fin_sem,
):
    width = w_out.shape[0]
    piece = x_t.shape[1] // PIECES
    pairs = qkv.shape[1]
    share_rows = width // dp_count
    dp_steps = dp_count.bit_length() - 1
    segment = lax.axis_index("segment")
    dp = lax.axis_index("dp")
    rep = lax.axis_index("rep")
    core = lax.rem(rep, 2)
    side = lax.div(rep, 2)
    other_core = side * 2 + (1 - core)
    other_side = (1 - side) * 2 + core

    def load_copy(block):
        def span(first):
            return pl.ds(pl.multiple_of((block - first) * width, width), width)

        def copy_of(source, target):
            return pltpu.make_async_copy(source, target, load_sem.at[1 + block])

        return (
            lambda: copy_of(w_qkv_hbm.at[0, :, span(0)], w_qkv.at[:, span(0)]),
            lambda: copy_of(w_out_hbm.at[0], w_out),
            lambda: copy_of(w_up_hbm.at[0, :, span(4)], w_up.at[:, span(4)]),
            lambda: copy_of(w_down_hbm.at[0, span(8), :], w_down.at[block - 8]),
        )

    parts_of_load = ((0, 3), (3, 4), (4, 8), (8, 12))
    first_rows = pltpu.make_async_copy(x_hbm, rows_in, load_sem.at[0])
    last_rows = pltpu.make_async_copy(ct_hbm, rows_in, load_sem.at[0])

    @pl.when(segment == 0)
    def _():
        first_rows.start()

    @pl.when(segment == 1)
    def _():
        last_rows.start()

    for part, (first, after) in enumerate(parts_of_load):
        for block in range(first, after):
            load_copy(block)[part]().start()

    barrier = pltpu.get_barrier_semaphore()
    pl.semaphore_signal(
        barrier, inc=1, device_id={"segment": 1 - segment}, device_id_type=MESH
    )
    for step in range(1, 4):
        pl.semaphore_signal(
            barrier, inc=1, device_id={"rep": lax.rem(rep + step, 4)}, device_id_type=MESH
        )
    for step in range(1, dp_count):
        pl.semaphore_signal(
            barrier, inc=1, device_id={"dp": lax.rem(dp + step, dp_count)}, device_id_type=MESH
        )

    params = [gains_ref[0].astype(F32), biases_ref[0].astype(F32)]
    for block in range(4):
        params.append(up_bias_ref[:, block * width : (block + 1) * width].astype(F32))
    params.append(jnp.zeros((16 - STATS, width), F32))
    upright = jnp.concatenate(params, axis=0).T
    for index in range(STATS):
        columns[index] = jnp.broadcast_to(upright[:, index : index + 1], (width, LANES)).astype(BF16)
    for index in range(STATS):
        sums[index] = jnp.zeros((width, LANES), F32)
    key_sums[0] = jnp.zeros(key_sums.shape[1:], F32)

    chunks = [slice(start, start + CHUNK) for start in range(0, width, CHUNK)]

    def turn(part):
        def one(block, carry):
            load_copy(block)[part]().wait()
            if part == 3:
                turned[block] = w_down[block - 8].T
            elif part == 1:
                turned[block] = w_out[...].T
            else:
                first = parts_of_load[part][0]
                span = pl.ds(pl.multiple_of((block - first) * width, width), width)
                turned[block] = (w_qkv if part == 0 else w_up)[:, span].T
            return carry

        lax.fori_loop(*parts_of_load[part], one, 0)

    def turn_apart(first, after):
        for block in range(first, after):
            part = (0, 0, 0, 1, 2, 2, 2, 2, 3, 3, 3, 3)[block]
            load_copy(block)[part]().wait()
            span = slice(block % 4 * width, (block % 4 + 1) * width)
            if part == 0:
                turned[block] = w_qkv[:, span].T
            elif part == 1:
                turned[block] = w_out[...].T
            elif part == 2:
                turned[block] = w_up[:, span].T
            else:
                turned[block] = w_down[block - 8].T
            yield 230

    first_rows.wait()

    flag = flag_ref[0, 0].astype(F32)

    def lanes_of(index):
        if isinstance(index, int):
            return pl.ds(index * piece, piece)
        return pl.ds(pl.multiple_of(index * piece, piece), piece)

    def forward_copy(index):
        return pltpu.make_async_remote_copy(
            src_ref=outgoing.at[index],
            dst_ref=x_t.at[:, lanes_of(index)],
            send_sem=seg_send.at[index],
            recv_sem=seg_recv.at[index],
            device_id={"segment": 1 - segment},
            device_id_type=MESH,
        )

    def backward_copy(index):
        return pltpu.make_async_remote_copy(
            src_ref=outgoing.at[index],
            dst_ref=incoming_grad.at[index],
            send_sem=seg_send.at[index],
            recv_sem=seg_recv.at[index],
            device_id={"segment": 1 - segment},
            device_id_type=MESH,
        )

    def ends_copy(index):
        return pltpu.make_async_copy(
            ends_v.at[lax.rem(index, 2)], ends_hbm.at[index], ends_sem.at[index]
        )

    def free_ends(index):
        @pl.when(index >= 2)
        def _():
            ends_copy(index - 2).wait()

    def own_rows(index):
        half = lax.rem(index, 2)
        whole = jnp.where(index < 2, 1.0, 0.0).astype(F32)
        weight = whole * flag + (1.0 - whole) * (1.0 - flag)
        picked = rows_in[half].astype(F32) * weight + rows_in[2 + half].astype(F32) * (1.0 - weight)
        return picked.T

    def by_queries(values):
        half = LANES // 2
        blank = jnp.zeros((half, LANES), values.dtype)
        parts = []
        for part in range(2):
            span = slice(part * LANES, (part + 1) * LANES)
            first = jnp.concatenate([values[:half, span], blank], axis=0)
            second = jnp.concatenate([blank, values[half:, span]], axis=0)
            parts.append(jnp.concatenate([first, second], axis=1))
        return parts

    def against(rows_ref, index, pair, parts, has_off):
        own = rows_ref[index, pair]
        products = [dot_plain(own[:LANES], parts[0]), dot_plain(own, parts[1])]
        if has_off:
            before = rows_ref[0, pair]
            products += [dot_plain(before, parts[0]), dot_plain(before, parts[1])]
        return products

    def tiles_of(products, head, part, has_off):
        lanes = slice(head * LANES, (head + 1) * LANES)
        own = products[part]
        tiles = [own[part * LANES : (part + 1) * LANES, lanes]]
        if part:
            tiles.append(own[:LANES, lanes])
        if has_off:
            off = products[2 + part]
            tiles += [off[:LANES, lanes], off[LANES:, lanes]]
        return tiles

    def joined(lows, has_off):
        blank = jnp.zeros((LANES, LANES), BF16)
        first = jnp.concatenate([lows[0][0], blank], axis=0)
        second = jnp.concatenate([lows[1][1], lows[1][0]], axis=0)
        whole = jnp.concatenate([first, second], axis=1)
        if not has_off:
            return whole, None
        first = jnp.concatenate(lows[0][-2:], axis=0)
        second = jnp.concatenate(lows[1][-2:], axis=0)
        return whole, jnp.concatenate([first, second], axis=1)

    def attend(index, has_off):
        lanes = lanes_of(index)
        half = LANES // 2
        key_at = lax.broadcasted_iota(jnp.int32, (LANES, LANES), 0)
        query_at = lax.broadcasted_iota(jnp.int32, (LANES, LANES), 1)
        allowed = key_at <= query_at

        def scores_of(pair):
            return against(
                keys_rm, index, pair, by_queries(qkv[0, pair, :, lanes]), has_off
            )

        ahead = scores_of(0)
        for pair in range(pairs):
            scores = ahead
            if pair + 1 < pairs:
                ahead = scores_of(pair + 1)
            mixed = []
            for head in range(2):
                rows = slice(head * half, (head + 1) * half)
                lows = []
                for part in range(2):
                    tiles = tiles_of(scores, head, part, has_off)
                    tiles[0] = jnp.where(allowed, tiles[0], -1e30)
                    top = jnp.max(functools.reduce(jnp.maximum, tiles), axis=0, keepdims=True)
                    raised = [jnp.exp(tile - top) for tile in tiles]
                    total = functools.reduce(jnp.add, raised)
                    scale = 1.0 / jnp.sum(total, axis=0, keepdims=True)
                    lows.append([(tile * scale).astype(BF16) for tile in raised])
                low, low_off = joined(lows, has_off)
                share[index, pair, head] = low
                mix = dot_plain(qkv[2, pair, rows, lanes], low)
                if has_off:
                    share_off[pair, head] = low_off
                    mix = mix + dot_plain(qkv[2, pair, rows, :piece], low_off)
                mixed.append(mix.astype(BF16))
            mixture[pair, :, lanes] = jnp.concatenate(mixed, axis=0)
            yield 280

    def part_sum(values):
        return jnp.sum(values.reshape(values.shape[0] // 8, 8, values.shape[1]), axis=0)

    def full_mean(parts):
        return jnp.sum(parts, axis=0, keepdims=True) * (1.0 / width)

    def column(index, rows):
        part = columns[index, rows, :].astype(F32)
        return jnp.concatenate([part] * (piece // LANES), axis=1)

    def gather_sum(index, rows, values):
        sums[index, rows, :] = sums[index, rows, :] + fold(values)

    def norm_chunks(index, which, wide_a, total):
        mean = full_mean(total)
        spread = jnp.zeros((8, piece), F32)
        for rows in chunks:
            centred = wide_a[rows, :] - mean
            spread = spread + part_sum(centred * centred)
        inverse = lax.rsqrt(full_mean(spread) + EPS)
        inverses[index, which] = inverse
        return mean, inverse

    def forward_start(index):
        @pl.when(segment == 0)
        def _():
            x_t[:, lanes_of(index)] = own_rows(index).astype(BF16)

        @pl.when(segment == 1)
        def _():
            forward_copy(index).wait_recv()

    def forward_first(index):
        lanes = lanes_of(index)
        inputs = x_t[:, lanes]
        score_scale = 1.0 / math.sqrt(width // HEADS)
        for block in range(3):
            result = dot_plain(turned[block], inputs)
            for pair in range(pairs):
                low = result[pair * LANES : (pair + 1) * LANES]
                low = (low * score_scale if block == 0 else low).astype(BF16)
                qkv[block, pair, :, lanes] = low
                if block == 1:
                    keys_rm[index, pair] = low.T
                if block == 2:
                    values_rm[index, pair] = low.T
            yield 270

    def forward_rest(index, wide_a):
        lanes = lanes_of(index)
        branch = dot_plain(turned[3], mixture[:, :, lanes].reshape(width, piece))
        yield 250
        total = jnp.zeros((8, piece), F32)
        for rows in chunks:
            sum_one = x_t[rows, lanes].astype(F32) + (branch[rows] + column(BIAS_OUT, rows))
            wide_a[rows, :] = sum_one
            total = total + part_sum(sum_one)
            yield 25
        mean, inverse = norm_chunks(index, 0, wide_a, total)
        yield 150
        for rows in chunks:
            normed = (wide_a[rows, :] - mean) * inverse
            norm_one[rows, lanes] = normed
            hidden = normed * column(GAIN_ONE, rows) + column(BIAS_ONE, rows)
            hidden_low[rows, lanes] = hidden.astype(BF16)
            yield 30

        branch_two = None
        for block in range(4):
            pre_block = dot_plain(turned[4 + block], hidden_low[:, lanes])
            yield 50
            lows = []
            for rows in chunks:
                pre = pre_block[rows] + column(BIAS_UP + block, rows)
                level = (lax.erf(pre * (1.0 / math.sqrt(2.0))) + 1.0) * 0.5
                bell = jnp.exp2(pre * pre * (-0.5 * math.log2(math.e)))
                lows.append((pre * level).astype(BF16))
                active[block, rows, lanes] = lows[-1]
                slope[block, rows, lanes] = (
                    level + pre * bell * (1.0 / math.sqrt(2.0 * math.pi))
                ).astype(BF16)
                yield 65
            part = dot_plain(turned[8 + block], jnp.concatenate(lows, axis=0))
            branch_two = part if branch_two is None else branch_two + part
            yield 100
        total = jnp.zeros((8, piece), F32)
        for rows in chunks:
            hidden = norm_one[rows, lanes] * column(GAIN_ONE, rows) + column(BIAS_ONE, rows)
            sum_two = hidden + (branch_two[rows] + column(BIAS_DOWN, rows))
            wide_a[rows, :] = sum_two
            total = total + part_sum(sum_two)
            yield 25
        mean, inverse = norm_chunks(index, 1, wide_a, total)
        yield 150
        for rows in chunks:
            norm_two[rows, lanes] = (wide_a[rows, :] - mean) * inverse
            yield 20

    def forward_end(index):
        for rows in chunks:
            outgoing[index, rows, :] = output_rows(rows, lanes_of(index)).astype(BF16)
        forward_copy(index).start()

    def off_or_not(index, run):
        @pl.when(index == 1)
        def _():
            drain(run(index, True))

        @pl.when(index != 1)
        def _():
            drain(run(index, False))

    def forward(index):
        forward_start(index)
        drain(forward_first(index))
        off_or_not(index, attend)
        drain(forward_rest(index, wide_a))

        @pl.when(segment == 0)
        def _():
            forward_end(index)

    def output_rows(rows, lanes):
        return norm_two[rows, lanes] * column(GAIN_TWO, rows) + column(BIAS_TWO, rows)

    def last_outputs(index, carry):
        free_ends(index)
        for start in range(0, width, LANES):
            rows = slice(start, start + LANES)
            ends_v[lax.rem(index, 2), :, rows] = output_rows(rows, lanes_of(index)).T
        ends_copy(index).start()
        return carry

    def attend_back(index, has_off):
        lanes = lanes_of(index)
        slot = (1 if index == 0 else 0) if isinstance(index, int) else jnp.where(index == 0, 1, 0)
        half = LANES // 2
        score_scale = 1.0 / math.sqrt(width // HEADS)

        def backs_of(pair):
            return against(values_rm, index, pair, by_queries(grad_mix[pair]), has_off)

        ahead = backs_of(0)
        for pair in range(pairs):
            backs = ahead
            if pair + 1 < pairs:
                ahead = backs_of(pair + 1)
            results = ([], [], [])
            for head in range(2):
                rows = slice(head * half, (head + 1) * half)
                low = share[index, pair, head]
                low_off = share_off[pair, head] if has_off else None
                lows = []
                for part in range(2):
                    place = slice(part * LANES, (part + 1) * LANES)
                    wides = [low[place, place]]
                    if part:
                        wides.append(low[:LANES, place])
                    if has_off:
                        wides += [low_off[:LANES, place], low_off[LANES:, place]]
                    wides = [tile.astype(F32) for tile in wides]
                    tiles = tiles_of(backs, head, part, has_off)
                    products = [wide * tile for wide, tile in zip(wides, tiles)]
                    inner = jnp.sum(functools.reduce(jnp.add, products), axis=0, keepdims=True)
                    lows.append(
                        [
                            (product - wide * inner).astype(BF16)
                            for product, wide in zip(products, wides)
                        ]
                    )
                grad_scores, grad_off = joined(lows, has_off)
                queries = qkv[0, pair, rows, lanes]
                grads = grad_mix[pair, rows]
                grad_query = dot_plain(qkv[1, pair, rows, lanes], grad_scores)
                grad_key = dot_turned(queries, grad_scores) + key_sums[slot, 0, pair, rows]
                grad_value = dot_turned(grads, low) + key_sums[slot, 1, pair, rows]
                if has_off:
                    grad_query = grad_query + dot_plain(qkv[1, pair, rows, :piece], grad_off)
                    key_sums[1, 0, pair, rows] = dot_turned(queries, grad_off)
                    key_sums[1, 1, pair, rows] = dot_turned(grads, low_off)
                for kept, grad in zip(results, (grad_query * score_scale, grad_key, grad_value)):
                    kept.append(grad.astype(BF16))
            for block in range(3):
                qkv[block, pair, :, lanes] = jnp.concatenate(results[block], axis=0)
            yield 440

    def backward_start(index):
        @pl.when(segment == 0)
        def _():
            backward_copy(index).wait_recv()

    def backward_norm(index):
        lanes = lanes_of(index)
        plain = jnp.zeros((8, piece), F32)
        inner = jnp.zeros((8, piece), F32)
        for rows in chunks:
            grad = incoming_grad[index, rows, :].astype(F32)
            product = grad * norm_two[rows, lanes]
            gather_sum(GAIN_TWO, rows, product)
            gather_sum(BIAS_TWO, rows, grad)
            gain = column(GAIN_TWO, rows)
            plain = plain + part_sum(grad * gain)
            inner = inner + part_sum(product * gain)
            yield 40
        plain = full_mean(plain)
        inner = full_mean(inner)
        inverse = inverses[index, 1]
        for rows in chunks:
            scaled = incoming_grad[index, rows, :].astype(F32) * column(GAIN_TWO, rows)
            grad_two = (scaled - plain - norm_two[rows, lanes] * inner) * inverse
            gather_sum(BIAS_DOWN, rows, grad_two)
            wide_a[rows, :] = grad_two
            down_grad[rows, lanes] = grad_two.astype(BF16)
            yield 40

    def backward_feed(index):
        lanes = lanes_of(index)
        for block in range(4):
            back = dot_plain(w_down[block], down_grad[:, lanes])
            for rows in chunks:
                grad_pre = back[rows] * slope[block, rows, lanes].astype(F32)
                gather_sum(BIAS_UP + block, rows, grad_pre)
                slope[block, rows, lanes] = grad_pre.astype(BF16)
            yield 250

        through = dot_plain(w_up[...], slope[:, :, lanes].reshape(4 * width, piece))
        plain = jnp.zeros((8, piece), F32)
        inner = jnp.zeros((8, piece), F32)
        for rows in chunks:
            grad_hidden = wide_a[rows, :] + through[rows]
            wide_a[rows, :] = grad_hidden
            product = grad_hidden * norm_one[rows, lanes]
            gather_sum(GAIN_ONE, rows, product)
            gather_sum(BIAS_ONE, rows, grad_hidden)
            gain = column(GAIN_ONE, rows)
            plain = plain + part_sum(grad_hidden * gain)
            inner = inner + part_sum(product * gain)
            yield 120 if rows.start == 0 else 45
        plain = full_mean(plain)
        inner = full_mean(inner)
        inverse = inverses[index, 0]
        for rows in chunks:
            scaled = wide_a[rows, :] * column(GAIN_ONE, rows)
            grad_one = (scaled - plain - norm_one[rows, lanes] * inner) * inverse
            gather_sum(BIAS_OUT, rows, grad_one)
            wide_b[rows, :] = grad_one
            branch_grad[rows, lanes] = grad_one.astype(BF16)
            yield 40
        grad_mix[...] = (
            dot_plain(w_out[...], branch_grad[:, lanes]).astype(BF16).reshape(pairs, LANES, piece)
        )
        yield 300

    def backward_attention(index):
        off_or_not(index, attend_back)
        through = dot_plain(w_qkv[...], qkv[:, :, :, lanes_of(index)].reshape(3 * width, piece))

        @pl.when(segment == 1)
        def _():
            for rows in chunks:
                outgoing[index, rows, :] = (wide_b[rows, :] + through[rows]).astype(BF16)
            backward_copy(index).start()

        @pl.when(segment == 0)
        def _():
            free_ends(index)
            for start in range(0, width, LANES):
                rows = slice(start, start + LANES)
                ends_v[lax.rem(index, 2), :, rows] = (wide_b[rows, :] + through[rows]).T
            ends_copy(index).start()

    def backward_both(index, forward_index):
        forward_copy(forward_index).wait_recv()

        def back():
            yield from backward_norm(index)
            yield from backward_feed(index)
            yield from attend_back(index, False)
            through = dot_plain(w_qkv[...], qkv[:, :, :, lanes_of(index)].reshape(3 * width, piece))
            for rows in chunks:
                outgoing[index, rows, :] = (wide_b[rows, :] + through[rows]).astype(BF16)
                yield 90

        def ahead():
            yield from forward_first(forward_index)
            yield from attend(forward_index, False)
            yield from forward_rest(forward_index, wide_c)

        side_by_side(back(), ahead(), 300)
        backward_copy(index).start()

    split = SPLIT if share_rows % (16 * SPLIT) == 0 else 1
    dp_first = DP_FIRST if split == SPLIT else ()
    orders = (ORDER_ONE, ORDER_TWO, ORDER_THREE) if split == SPLIT else plain_orders()
    jobs = 3 * split
    cut_rows = share_rows // split
    job_rows = width // split

    def base_of(job):
        return (8, 4, 0)[job // split]

    def job_span(job):
        return pl.ds(job % split * job_rows, job_rows)

    def fin_rows(job):
        return pl.ds(job % split * cut_rows, cut_rows)

    def parts_of(job):
        return range(2) if job in dp_first else range(1)

    def core_copies(job):
        return [
            pltpu.make_async_remote_copy(
                src_ref=turned.at[base_of(job) + 2 * (1 - core) + each, job_span(job)],
                dst_ref=core_in.at[job // split, each, job_span(job)],
                send_sem=core_send.at[job, each],
                recv_sem=core_recv.at[job, each],
                device_id={"rep": other_core},
                device_id_type=MESH,
            )
            for each in range(2)
        ]

    def side_copies(job):
        base = base_of(job)
        copies = []
        for each in parts_of(job):
            if job in dp_first:
                source = turned.at[base + 2 * core + each, dp_rows(job, dp_steps - 1)[1]]
                target = side_in.at[
                    job // split, pl.ds(job % split * job_rows + each * cut_rows, cut_rows)
                ]
            else:
                source = turned.at[base + 2 * core + (1 - side), job_span(job)]
                target = side_in.at[job // split, job_span(job)]
            copies.append(
                pltpu.make_async_remote_copy(
                    src_ref=source,
                    dst_ref=target,
                    send_sem=side_send.at[job, each],
                    recv_sem=side_recv.at[job, each],
                    device_id={"rep": other_side},
                    device_id_type=MESH,
                )
            )
        return copies

    def dp_slot(job):
        return sum(len(parts_of(before)) for before in range(job))

    def dp_rows(job, step):
        count = dp_count // 2
        start = 0
        for bit in range(step):
            start = start + lax.rem(lax.div(dp, 2**bit), 2) * count
            count = count // 2
        mine = lax.rem(lax.div(dp, 2**step), 2)
        first = job % split * job_rows
        sent = pl.multiple_of(first + (start + (1 - mine) * count) * cut_rows, cut_rows)
        kept = pl.multiple_of(first + (start + mine * count) * cut_rows, cut_rows)
        return pl.ds(sent, count * cut_rows), pl.ds(kept, count * cut_rows)

    def dp_landing(step):
        count = dp_count // 2 ** (step + 1)
        return pl.ds((dp_count - 2 * count) * cut_rows, count * cut_rows)

    def dp_copies(job, step):
        mine = lax.rem(lax.div(dp, 2**step), 2)
        copies = []
        for each in parts_of(job):
            position = base_of(job) + 2 * core + (each if job in dp_first else side)
            copies.append(
                pltpu.make_async_remote_copy(
                    src_ref=turned.at[position, dp_rows(job, step)[0]],
                    dst_ref=dp_in.at[dp_slot(job) + each, dp_landing(step)],
                    send_sem=dp_send.at[job, step, each],
                    recv_sem=dp_recv.at[job, step, each],
                    device_id={"dp": dp + (1 - 2 * mine) * 2**step},
                    device_id_type=MESH,
                )
            )
        return copies

    def join_copy(job):
        part = fin.at[job // split, 2 * core + side, fin_rows(job)]
        return pltpu.make_async_remote_copy(
            src_ref=part,
            dst_ref=part,
            send_sem=join_send.at[job],
            recv_sem=join_recv.at[job],
            device_id={"rep": other_side},
            device_id_type=MESH,
        )

    def last_copies(job):
        copies = []
        for each in range(2):
            part = fin.at[job // split, 2 * core + each, fin_rows(job)]
            copies.append(
                pltpu.make_async_remote_copy(
                    src_ref=part,
                    dst_ref=part,
                    send_sem=last_send.at[job, each],
                    recv_sem=last_recv.at[job, each],
                    device_id={"rep": other_core},
                    device_id_type=MESH,
                )
            )
        return copies

    def fin_copy(job):
        return pltpu.make_async_copy(
            fin.at[job // split, :, fin_rows(job)],
            fin_hbm.at[job // split, :, fin_rows(job)],
            fin_sem.at[job],
        )

    def arrived(*copies):
        for copy in copies:
            copy.wait_send()
        for copy in copies:
            copy.wait_recv()

    def start_all(copies):
        for copy in copies:
            copy.start()

    def turned_bits(value, count):
        place = 0
        while count > 1:
            place = place * 2 + value % 2
            value = value // 2
            count = count // 2
        return place

    pack = min(2, split)

    def left_rows(source, part):
        count = pack * cut_rows
        start = part * pack * cut_rows
        return jnp.concatenate(
            [source(index * share_rows + start, count) for index in range(dp_count)], axis=0
        )

    def keep_rows(block, part, result):
        for index in range(dp_count):
            for each in range(pack):
                target = (part * pack + each) * job_rows + turned_bits(index, dp_count) * cut_rows
                start = (index * pack + each) * cut_rows
                turned[block, target : target + cut_rows, :] = result[start : start + cut_rows]

    def down_block(part, block, tokens, add):
        count = width // (4 * share_rows)
        pieces = []
        for each in range(4 * count):
            start = pl.multiple_of(each * share_rows + part * (pack * cut_rows), pack * cut_rows)
            pieces.append(active[block, pl.ds(start, pack * cut_rows), tokens])
        result = dot_turned(jnp.concatenate(pieces, axis=0), down_grad[:, tokens])
        high = lax.rem(block, 2) * 2 + lax.div(block, 2)
        for each in range(count):
            place = turned_bits(each, count) * 4 + high
            for position in range(4):
                for job in range(pack):
                    target = (part * pack + job) * job_rows + place * cut_rows
                    rows = pl.ds(pl.multiple_of(target, cut_rows), cut_rows)
                    start = ((each * 4 + position) * pack + job) * cut_rows
                    total = result[start : start + cut_rows]
                    if add:
                        total = total + turned[8 + position, rows, :].astype(F32)
                    turned[8 + position, rows, :] = total.astype(BF16)

    half_tokens = PIECES // 2 * piece

    def early_down_sums():
        def one(step, carry):
            down_block(lax.div(step, 4), lax.rem(step, 4), slice(0, half_tokens), False)
            return carry

        lax.fori_loop(0, 4 * (split // pack), one, 0)

    def down_sums(part):
        def one(block, carry):
            down_block(part, block, slice(half_tokens, 2 * half_tokens), True)
            return carry

        lax.fori_loop(0, 4, one, 0)

    def up_sums(part):
        def one(block, carry):
            left = left_rows(lambda start, count: hidden_low[start : start + count, :], part)
            keep_rows(4 + block, part, dot_turned(left, slope[block]).astype(BF16))
            return carry

        lax.fori_loop(0, 4, one, 0)

    def qkv_sums(part):
        def one(block, carry):
            left = left_rows(lambda start, count: x_t[start : start + count, :], part)
            grads = qkv[block].reshape(width, PIECES * piece)
            keep_rows(block, part, dot_turned(left, grads).astype(BF16))
            return carry

        lax.fori_loop(0, 3, one, 0)
        left = left_rows(
            lambda start, count: mixture[start // LANES, start % LANES : start % LANES + count, :], part
        )
        keep_rows(3, part, dot_turned(left, branch_grad[...]).astype(BF16))

    def sums_of(job):
        (down_sums, up_sums, qkv_sums)[job // split](job % split // pack)
        for each in range(pack):
            start_all(core_copies(job + each))

    def after_core(job):
        arrived(*core_copies(job))
        rows = job_span(job)
        for each in parts_of(job):
            place = 1 - side if each == 0 else side
            position = base_of(job) + 2 * core + place
            turned[position, rows, :] = (
                turned[position, rows, :].astype(F32)
                + core_in[job // split, place, rows, :].astype(F32)
            ).astype(BF16)
        if job in dp_first:
            start_all(dp_copies(job, 0))

    def start_side(job):
        start_all(side_copies(job))

    def after_side(job):
        arrived(*side_copies(job))
        rows = job_span(job)
        position = base_of(job) + 2 * core + side
        turned[position, rows, :] = (
            turned[position, rows, :].astype(F32)
            + core_in[job // split, side, rows, :].astype(F32)
            + side_in[job // split, rows, :].astype(F32)
        ).astype(BF16)
        start_all(dp_copies(job, 0))

    def dp_total(job, step, each):
        position = base_of(job) + 2 * core + (each if job in dp_first else side)
        kept = turned[position, dp_rows(job, step)[1], :].astype(F32)
        return position, kept + dp_in[dp_slot(job) + each, dp_landing(step), :].astype(F32)

    def after_dp(job):
        for step in range(dp_steps - 1):
            arrived(*dp_copies(job, step))
            for each in parts_of(job):
                position, total = dp_total(job, step, each)
                turned[position, dp_rows(job, step)[1], :] = total.astype(BF16)
            start_all(dp_copies(job, step + 1))

    def after_last_dp(job):
        step = dp_steps - 1
        arrived(*dp_copies(job, step))
        for each in parts_of(job):
            position, total = dp_total(job, step, each)
            if job in dp_first:
                turned[position, dp_rows(job, step)[1], :] = total.astype(BF16)
            else:
                fin[job // split, 2 * core + side, fin_rows(job), :] = total.astype(BF16)
        if job in dp_first:
            start_side(job)
        else:
            join_copy(job).start()

    def after_join(job):
        if job in dp_first:
            arrived(*side_copies(job))
            for each in range(2):
                rows = pl.ds(job % split * job_rows + each * cut_rows, cut_rows)
                own = turned[base_of(job) + 2 * core + each, dp_rows(job, dp_steps - 1)[1], :]
                total = own.astype(F32) + side_in[job // split, rows, :].astype(F32)
                fin[job // split, 2 * core + each, fin_rows(job), :] = total.astype(BF16)
        else:
            arrived(join_copy(job))
        start_all(last_copies(job))

    def after_last(job):
        arrived(*last_copies(job))
        fin_copy(job).start()

    def small_dp_copy(step):
        target = lax.rem(dp + step, dp_count)
        return pltpu.make_async_remote_copy(
            src_ref=small.at[target],
            dst_ref=small_dp.at[step - 1],
            send_sem=sdp_send.at[step - 1],
            recv_sem=sdp_recv.at[step - 1],
            device_id={"dp": target},
            device_id_type=MESH,
        )

    def small_rep_copy(step):
        return pltpu.make_async_remote_copy(
            src_ref=small_rep.at[rep],
            dst_ref=small_rep.at[rep],
            send_sem=srep_send.at[step - 1],
            recv_sem=srep_recv.at[step - 1],
            device_id={"rep": lax.rem(rep + step, 4)},
            device_id_type=MESH,
        )

    small_copy = pltpu.make_async_copy(small_out, small_hbm, load_sem.at[0])

    def small_step(stage):
        if stage == 0:
            rows_of = [jnp.sum(sums[index].T, axis=0, keepdims=True) for index in range(STATS)]
            small[...] = jnp.zeros(small.shape, F32)
            for share_index in range(dp_count):
                for index in range(BIAS_UP):
                    start = share_index * share_rows
                    small[share_index, index : index + 1, :share_rows] = rows_of[index][
                        :, start : start + share_rows
                    ]
                for part in range(4):
                    start = (share_index * 4 + part) * share_rows
                    block, start = start // width, start % width
                    small[share_index, BIAS_UP + part : BIAS_UP + part + 1, :share_rows] = rows_of[
                        BIAS_UP + block
                    ][:, start : start + share_rows]
            for step in range(1, dp_count):
                small_dp_copy(step).start()
        elif stage == 1:
            total = small[dp]
            for step in range(1, dp_count):
                arrived(small_dp_copy(step))
                total = total + small_dp[step - 1]
            small_rep[rep] = total
            for step in range(1, 4):
                small_rep_copy(step).start()
        else:
            for step in range(1, 4):
                arrived(small_rep_copy(step))
            small_out[...] = (small_rep[0] + small_rep[1]) + (small_rep[2] + small_rep[3])
            small_copy.start()

    def run(order):
        steps = (
            sums_of,
            after_core,
            start_side,
            after_side,
            after_dp,
            after_last_dp,
            after_join,
            after_last,
            small_step,
        )
        for stage, job in order:
            steps[stage](job)

    def one_step(step, carry):
        first_index = jnp.where(step < 4, step, jnp.where(step < 6, 5 - step, step - 4))
        last_index = jnp.where(step < 2, step, jnp.where(step == 2, 1, 3))
        index = jnp.minimum(jnp.where(segment == 0, first_index, last_index), PIECES - 1)
        is_last = jnp.where(step == 2 * PIECES, 1, 0)
        begun = jnp.where(step + segment == 0, 0, 1)
        is_forward = jnp.where(step < jnp.where(segment == 0, 4, 2), begun, 0)
        last_backward = jnp.where(step == 2, 1, 0) + jnp.where(step == 5, 1, 0)
        is_backward = jnp.where(segment == 0, begun * (1 - is_forward) * (1 - is_last), last_backward)
        is_split = jnp.where(step >= 2 * PIECES - 1, 1 - segment, 0)
        is_rest = is_backward * (1 - is_split) + is_last * is_split

        @pl.when(is_forward == 1)
        def _():
            forward(index)

        @pl.when(is_backward == 1)
        def _():
            backward_start(index)
            drain(backward_norm(index))

        @pl.when(segment * step == 3)
        def _():
            backward_both(0, 2)

        @pl.when(segment * step == 4)
        def _():
            backward_both(2, 3)

        @pl.when(is_last == 1)
        def _():
            run(orders[0])

        @pl.when(is_rest == 1)
        def _():
            drain(backward_feed(index))

        @pl.when(is_last == 1)
        def _():
            run(orders[1])

        @pl.when(is_rest == 1)
        def _():
            backward_attention(index)

        @pl.when(step - segment == 5)
        def _():
            early_down_sums()

        return carry

    @pl.when(segment == 1)
    def _():
        for part in range(4):
            turn(part)

        def one_cotangent(index, carry):
            incoming_grad[index] = own_rows(index).astype(BF16)
            return carry

        lax.fori_loop(0, PIECES, one_cotangent, 0)

    @pl.when(segment == 0)
    def _():
        def ahead():
            x_t[:, lanes_of(0)] = own_rows(0).astype(BF16)
            yield from forward_first(0)
            yield from attend(0, False)
            yield from forward_rest(0, wide_a)

        drain(turn_apart(0, 1))
        side_by_side(ahead(), turn_apart(1, 12), -400)

    pl.semaphore_wait(barrier, 4 + dp_count - 1)

    @pl.when(segment == 0)
    def _():
        forward_end(0)

    lax.fori_loop(0, 2 * PIECES + 1, one_step, 0)

    cut = orders[2].index((SMALL, 0))
    run(orders[2][:cut])

    @pl.when(segment == 1)
    def _():
        lax.fori_loop(0, PIECES, last_outputs, 0)

    run(orders[2][cut:])

    for index in range(PIECES):

        @pl.when(segment == 0)
        def _():
            forward_copy(index).wait_send()

        @pl.when(segment == 1)
        def _():
            backward_copy(index).wait_send()

    for index in range(2, PIECES):
        ends_copy(index).wait()
    for job in range(jobs):
        fin_copy(job).wait()
    small_copy.wait()


def finish_kernel(
    flag_ref,
    ends_in,
    fin,
    small,
    ends,
    grad_qkv,
    grad_out,
    grad_up,
    grad_down,
    grad_up_bias,
    grad_gains,
    grad_biases,
    ends_v,
    fin_v,
    wide_qkv,
    wide_out,
    wide_up,
    wide_down,
    small_v,
    up_bias_v,
    gains_v,
    biases_v,
    ends_sem,
    in_sem,
    out_sem,
):
    half = ends_in.shape[0] // 2
    share_rows, width = fin.shape[2:]
    start = pl.multiple_of(half * (1 - flag_ref[0, 0]), half)
    cut = half // 4
    ends_copies = []
    ends_loads = []
    for part in range(8):
        source = pl.ds(part * cut, cut)
        offset = start + part * cut if part < 4 else part * cut - half + (half - start)
        target = pl.ds(pl.multiple_of(offset, cut), cut)
        ends_loads.append(
            pltpu.make_async_copy(ends_in.at[source], ends_v.at[source], ends_sem.at[part])
        )
        ends_copies.append(
            pltpu.make_async_copy(ends_v.at[source], ends.at[0, target], ends_sem.at[8 + part])
        )
    loads = [
        pltpu.make_async_copy(fin.at[group], fin_v.at[group], in_sem.at[group])
        for group in range(3)
    ]
    stores = [
        pltpu.make_async_copy(wide, target.at[0], out_sem.at[index])
        for index, (wide, target) in enumerate(
            ((wide_down, grad_down), (wide_up, grad_up), (wide_qkv, grad_qkv), (wide_out, grad_out))
        )
    ]
    small_load = pltpu.make_async_copy(small, small_v, in_sem.at[3])
    small_stores = [
        pltpu.make_async_copy(narrow, target, out_sem.at[4 + index])
        for index, (narrow, target) in enumerate(
            ((up_bias_v, grad_up_bias), (gains_v, grad_gains), (biases_v, grad_biases))
        )
    ]
    small_load.start()
    for group in range(3):
        loads[group].start()
        for copy in ends_loads[group * 3 : group * 3 + 3]:
            copy.start()

    def ends_on(first, after):
        for load, copy in zip(ends_loads[first:after], ends_copies[first:after]):
            load.wait()
            copy.start()

    loads[0].wait()
    for position in range(4):
        rows = slice(position * share_rows, (position + 1) * share_rows)
        wide_down[rows, :] = fin_v[0, position].astype(F32)
    stores[0].start()
    ends_on(0, 3)
    loads[1].wait()
    for position in range(4):
        wide_up[:, position * width : (position + 1) * width] = fin_v[1, position].astype(F32)
    stores[1].start()
    ends_on(3, 6)
    loads[2].wait()
    for position in range(3):
        wide_qkv[:, position * width : (position + 1) * width] = fin_v[2, position].astype(F32)
    stores[2].start()
    wide_out[...] = fin_v[2, 3].astype(F32)
    stores[3].start()
    ends_on(6, 8)
    small_load.wait()
    for position in range(4):
        rows = slice(position * share_rows, (position + 1) * share_rows)
        up_bias_v[:, rows] = small_v[BIAS_UP + position : BIAS_UP + position + 1, :share_rows]
    gains_v[0] = small_v[:2, :share_rows]
    biases_v[0] = small_v[2:BIAS_UP, :share_rows]
    for copy in small_stores:
        copy.start()
    for copy in stores + ends_copies + small_stores:
        copy.wait()


def on_device(
    dp_count,
    block_input,
    cotangent,
    window_group,
    w_qkv,
    w_out,
    w_up,
    w_down,
    up_bias,
    norm_gains,
    biases,
):
    rows, width = block_input.shape
    piece = rows // PIECES
    pairs = width // LANES
    share_rows = width // dp_count
    small_width = max(share_rows, LANES)
    dp_steps = dp_count.bit_length() - 1
    split = SPLIT if share_rows % (16 * SPLIT) == 0 else 1
    jobs = 3 * split
    slots = jobs + (len(DP_FIRST) if split == SPLIT else 0)
    any_spec = pl.BlockSpec(memory_space=pl.ANY)
    vmem_spec = pl.BlockSpec(memory_space=pltpu.VMEM)
    smem_spec = pl.BlockSpec(memory_space=pltpu.SMEM)
    dma = pltpu.SemaphoreType.DMA
    vmem = pltpu.VMEM
    ends_in, fin, small = pl.pallas_call(
        functools.partial(layer_kernel, dp_count),
        out_shape=(
            jax.ShapeDtypeStruct((PIECES, piece, width), F32),
            jax.ShapeDtypeStruct((3, 4, share_rows, width), BF16),
            jax.ShapeDtypeStruct((16, small_width), F32),
        ),
        in_specs=[smem_spec] + [any_spec] * 6 + [vmem_spec] * 3,
        out_specs=(any_spec,) * 3,
        scratch_shapes=[
            vmem((width, 3 * width), BF16),
            vmem((width, width), BF16),
            vmem((width, 4 * width), BF16),
            vmem((4, width, width), BF16),
            vmem((12, width, width), BF16),
            vmem((PIECES, piece, width), BF16),
            vmem((width, rows), BF16),
            vmem((3, pairs, LANES, rows), BF16),
            vmem((PIECES, pairs, piece, LANES), BF16),
            vmem((PIECES, pairs, piece, LANES), BF16),
            vmem((PIECES, pairs, 2, piece, piece), BF16),
            vmem((pairs, 2, piece, piece), BF16),
            vmem((pairs, LANES, rows), BF16),
            vmem((width, rows), F32),
            vmem((width, rows), F32),
            vmem((PIECES, 2, 1, piece), F32),
            vmem((width, rows), BF16),
            vmem((4, width, rows), BF16),
            vmem((4, width, rows), BF16),
            vmem((width, rows), BF16),
            vmem((width, rows), BF16),
            vmem((pairs, LANES, piece), BF16),
            vmem((PIECES, width, piece), BF16),
            vmem((PIECES, width, piece), BF16),
            vmem((STATS, width, LANES), BF16),
            vmem((STATS, width, LANES), F32),
            vmem((2, 2, pairs, LANES, piece), F32),
            vmem((width, piece), F32),
            vmem((width, piece), F32),
            vmem((width, piece), F32),
            vmem((2, piece, width), F32),
            vmem((3, 2, width, width), BF16),
            vmem((3, width, width), BF16),
            vmem((slots, (width - share_rows) // split, width), BF16),
            vmem((3, 4, share_rows, width), BF16),
            vmem((dp_count, 16, small_width), F32),
            vmem((dp_count - 1, 16, small_width), F32),
            vmem((4, 16, small_width), F32),
            vmem((16, small_width), F32),
            dma((13,)),
            dma((PIECES,)),
            dma((PIECES,)),
            dma((PIECES,)),
            dma((jobs, 2)),
            dma((jobs, 2)),
            dma((jobs, 2)),
            dma((jobs, 2)),
            dma((jobs, dp_steps, 2)),
            dma((jobs, dp_steps, 2)),
            dma((jobs,)),
            dma((jobs,)),
            dma((jobs, 2)),
            dma((jobs, 2)),
            dma((dp_count - 1,)),
            dma((dp_count - 1,)),
            dma((3,)),
            dma((3,)),
            dma((jobs,)),
        ],
        compiler_params=pltpu.CompilerParams(
            collective_id=0, has_side_effects=True, vmem_limit_bytes=63 * 1024 * 1024
        ),
    )(
        window_group,
        block_input.reshape(PIECES, piece, width),
        cotangent.reshape(PIECES, piece, width),
        w_qkv,
        w_out,
        w_up,
        w_down,
        up_bias,
        norm_gains,
        biases,
    )
    return pl.pallas_call(
        finish_kernel,
        out_shape=(
            jax.ShapeDtypeStruct((1, rows, width), F32),
            jax.ShapeDtypeStruct((1, share_rows, 3 * width), F32),
            jax.ShapeDtypeStruct((1, share_rows, width), F32),
            jax.ShapeDtypeStruct((1, share_rows, 4 * width), F32),
            jax.ShapeDtypeStruct((1, 4 * share_rows, width), F32),
            jax.ShapeDtypeStruct((1, 4 * share_rows), F32),
            jax.ShapeDtypeStruct((1, 2, share_rows), F32),
            jax.ShapeDtypeStruct((1, 4, share_rows), F32),
        ),
        in_specs=[smem_spec] + [any_spec] * 3,
        out_specs=(any_spec,) * 8,
        scratch_shapes=[
            vmem((rows, width), F32),
            vmem((3, 4, share_rows, width), BF16),
            vmem((share_rows, 3 * width), F32),
            vmem((share_rows, width), F32),
            vmem((share_rows, 4 * width), F32),
            vmem((4 * share_rows, width), F32),
            vmem((16, small_width), F32),
            vmem((1, 4 * share_rows), F32),
            vmem((1, 2, share_rows), F32),
            vmem((1, 4, share_rows), F32),
            dma((16,)),
            dma((4,)),
            dma((7,)),
        ],
        compiler_params=pltpu.CompilerParams(vmem_limit_bytes=63 * 1024 * 1024),
    )(window_group, ends_in.reshape(rows, width), fin, small)


def solution(mesh):
    return jax.shard_map(
        functools.partial(on_device, mesh.shape["dp"]),
        mesh=mesh,
        in_specs=(
            P(("dp", "rep"), None),
            P(("dp", "rep"), None),
            P(("dp", "rep"), None),
            P("segment", None, None),
            P("segment", None, None),
            P("segment", None, None),
            P("segment", None, None),
            P("segment", None),
            P("segment", None, None),
            P("segment", None, None),
        ),
        out_specs=(
            P("segment", ("dp", "rep"), None),
            P("segment", "dp", None),
            P("segment", "dp", None),
            P("segment", "dp", None),
            P("segment", "dp", None),
            P("segment", "dp"),
            P("segment", None, "dp"),
            P("segment", None, "dp"),
        ),
        check_vma=False,
    )
```

```python
import functools
import math

import jax
import jax.numpy as jnp
from jax import lax
from jax.experimental import pallas as pl
from jax.experimental.pallas import tpu as pltpu
from jax.sharding import PartitionSpec as P

MESH = pl.DeviceIdType.MESH
F32 = jnp.float32
BF16 = jnp.bfloat16
HEADS = 8
LANES = 128
PIECES = 4
EPS = 1e-05
GAIN_ONE, GAIN_TWO, BIAS_OUT, BIAS_ONE, BIAS_DOWN, BIAS_TWO, BIAS_UP = range(7)
STATS = 10
CHUNK = 64
SPLIT = 4
DP_FIRST = (1, 5, 9)
SUM, CORE, SIDE, SIDED, DP, DPED, JOIN, LAST, SMALL = range(9)
ORDER_ONE = (
    (SUM, 0), (SUM, 2), (CORE, 0), (SIDE, 0),
)
ORDER_TWO = (
    (SUM, 4), (CORE, 3), (CORE, 2), (CORE, 1), (SIDE, 3), (SUM, 6), (SIDED, 0),
    (SIDE, 2),
)
ORDER_THREE = (
    (CORE, 4), (SIDED, 3), (CORE, 6), (SIDE, 6), (CORE, 5), (DP, 0), (SIDE, 4), (SUM, 8), (DPED, 0), (DP, 1),
    (SIDED, 2), (CORE, 7), (SIDE, 7), (SUM, 10), (DP, 3), (SIDED, 6), (CORE, 8), (SIDE, 8), (SIDED, 4),
    (DPED, 1), (DP, 2), (CORE, 9), (DP, 6), (DPED, 3), (CORE, 11), (SIDE, 11), (SIDED, 8), (DP, 4),
    (CORE, 10), (SMALL, 0), (DP, 5), (DPED, 6), (JOIN, 1), (JOIN, 3), (SIDED, 7), (DP, 9), (SIDE, 10),
    (SIDED, 11), (DP, 8), (DPED, 4), (DPED, 2), (SIDED, 10), (DP, 7), (DPED, 9), (DP, 11), (JOIN, 6),
    (JOIN, 4), (DPED, 5), (DPED, 8), (DP, 10), (DPED, 7), (SMALL, 1), (LAST, 6), (LAST, 1), (JOIN, 2),
    (DPED, 11), (LAST, 3), (JOIN, 0), (DPED, 10), (JOIN, 7), (JOIN, 8), (JOIN, 11), (JOIN, 9), (JOIN, 5),
    (LAST, 4), (SMALL, 2), (LAST, 0), (JOIN, 10), (LAST, 9), (LAST, 11), (LAST, 5), (LAST, 7), (LAST, 8),
    (LAST, 2), (LAST, 10),
)


def plain_orders():
    one = ((SUM, 0),)
    two = ((SUM, 1), (CORE, 0), (SIDE, 0))
    three = ((SUM, 2), (CORE, 1), (SIDE, 1), (CORE, 2), (SIDE, 2), (SMALL, 0), (SMALL, 1), (SMALL, 2))
    for stage in (SIDED, DP, DPED, JOIN, LAST):
        three += tuple((stage, job) for job in range(3))
    return one, two, three


def dot_plain(left, right):
    return lax.dot_general(left, right, (((1,), (0,)), ((), ())), preferred_element_type=F32)


def drain(parts):
    for _ in parts:
        pass


def side_by_side(one, two, behind):
    spent = [0, behind]
    live = [one, two]
    while live[0] or live[1]:
        which = 0 if live[0] and (not live[1] or spent[0] <= spent[1]) else 1
        cost = next(live[which], None)
        if cost is None:
            live[which] = None
        else:
            spent[which] += cost


def dot_turned(left, right):
    return lax.dot_general(left, right, (((1,), (1,)), ((), ())), preferred_element_type=F32)


def fold(values):
    total = values[:, :LANES]
    for start in range(LANES, values.shape[1], LANES):
        total = total + values[:, start : start + LANES]
    return total


def layer_kernel(
    dp_count,
    flag_ref,
    x_hbm,
    ct_hbm,
    w_qkv_hbm,
    w_out_hbm,
    w_up_hbm,
    w_down_hbm,
    up_bias_ref,
    gains_ref,
    biases_ref,
    ends_hbm,
    fin_hbm,
    small_hbm,
    w_qkv,
    w_out,
    w_up,
    w_down,
    turned,
    rows_in,
    x_t,
    qkv,
    keys_rm,
    values_rm,
    share,
    share_off,
    mixture,
    norm_one,
    norm_two,
    inverses,
    hidden_low,
    slope,
    active,
    down_grad,
    branch_grad,
    grad_mix,
    outgoing,
    incoming_grad,
    columns,
    sums,
    key_sums,
    wide_a,
    wide_b,
    wide_c,
    ends_v,
    core_in,
    side_in,
    dp_in,
    fin,
    small,
    small_dp,
    small_rep,
    small_out,
    load_sem,
    seg_send,
    seg_recv,
    ends_sem,
    core_send,
    core_recv,
    side_send,
    side_recv,
    dp_send,
    dp_recv,
    join_send,
    join_recv,
    last_send,
    last_recv,
    sdp_send,
    sdp_recv,
    srep_send,
    srep_recv,
    fin_sem,
):
    width = w_out.shape[0]
    piece = x_t.shape[1] // PIECES
    pairs = qkv.shape[1]
    share_rows = width // dp_count
    dp_steps = dp_count.bit_length() - 1
    segment = lax.axis_index("segment")
    dp = lax.axis_index("dp")
    rep = lax.axis_index("rep")
    core = lax.rem(rep, 2)
    side = lax.div(rep, 2)
    other_core = side * 2 + (1 - core)
    other_side = (1 - side) * 2 + core

    def load_copy(block):
        def span(first):
            return pl.ds(pl.multiple_of((block - first) * width, width), width)

        def copy_of(source, target):
            return pltpu.make_async_copy(source, target, load_sem.at[1 + block])

        return (
            lambda: copy_of(w_qkv_hbm.at[0, :, span(0)], w_qkv.at[:, span(0)]),
            lambda: copy_of(w_out_hbm.at[0], w_out),
            lambda: copy_of(w_up_hbm.at[0, :, span(4)], w_up.at[:, span(4)]),
            lambda: copy_of(w_down_hbm.at[0, span(8), :], w_down.at[block - 8]),
        )

    parts_of_load = ((0, 3), (3, 4), (4, 8), (8, 12))
    first_rows = pltpu.make_async_copy(x_hbm, rows_in, load_sem.at[0])
    last_rows = pltpu.make_async_copy(ct_hbm, rows_in, load_sem.at[0])

    @pl.when(segment == 0)
    def _():
        first_rows.start()

    @pl.when(segment == 1)
    def _():
        last_rows.start()

    for part, (first, after) in enumerate(parts_of_load):
        for block in range(first, after):
            load_copy(block)[part]().start()

    barrier = pltpu.get_barrier_semaphore()
    pl.semaphore_signal(
        barrier, inc=1, device_id={"segment": 1 - segment}, device_id_type=MESH
    )
    for step in range(1, 4):
        pl.semaphore_signal(
            barrier, inc=1, device_id={"rep": lax.rem(rep + step, 4)}, device_id_type=MESH
        )
    for step in range(1, dp_count):
        pl.semaphore_signal(
            barrier, inc=1, device_id={"dp": lax.rem(dp + step, dp_count)}, device_id_type=MESH
        )

    params = [gains_ref[0].astype(F32), biases_ref[0].astype(F32)]
    for block in range(4):
        params.append(up_bias_ref[:, block * width : (block + 1) * width].astype(F32))
    params.append(jnp.zeros((16 - STATS, width), F32))
    upright = jnp.concatenate(params, axis=0).T
    for index in range(STATS):
        columns[index] = jnp.broadcast_to(upright[:, index : index + 1], (width, LANES)).astype(BF16)
    for index in range(STATS):
        sums[index] = jnp.zeros((width, LANES), F32)
    key_sums[0] = jnp.zeros(key_sums.shape[1:], F32)

    chunks = [slice(start, start + CHUNK) for start in range(0, width, CHUNK)]

    def turn(part):
        def one(block, carry):
            load_copy(block)[part]().wait()
            if part == 3:
                turned[block] = w_down[block - 8].T
            elif part == 1:
                turned[block] = w_out[...].T
            else:
                first = parts_of_load[part][0]
                span = pl.ds(pl.multiple_of((block - first) * width, width), width)
                turned[block] = (w_qkv if part == 0 else w_up)[:, span].T
            return carry

        lax.fori_loop(*parts_of_load[part], one, 0)

    def turn_apart(first, after):
        for block in range(first, after):
            part = (0, 0, 0, 1, 2, 2, 2, 2, 3, 3, 3, 3)[block]
            load_copy(block)[part]().wait()
            span = slice(block % 4 * width, (block % 4 + 1) * width)
            if part == 0:
                turned[block] = w_qkv[:, span].T
            elif part == 1:
                turned[block] = w_out[...].T
            elif part == 2:
                turned[block] = w_up[:, span].T
            else:
                turned[block] = w_down[block - 8].T
            yield 230

    first_rows.wait()

    flag = flag_ref[0, 0].astype(F32)

    def lanes_of(index):
        if isinstance(index, int):
            return pl.ds(index * piece, piece)
        return pl.ds(pl.multiple_of(index * piece, piece), piece)

    def forward_copy(index):
        return pltpu.make_async_remote_copy(
            src_ref=outgoing.at[index],
            dst_ref=x_t.at[:, lanes_of(index)],
            send_sem=seg_send.at[index],
            recv_sem=seg_recv.at[index],
            device_id={"segment": 1 - segment},
            device_id_type=MESH,
        )

    def backward_copy(index):
        return pltpu.make_async_remote_copy(
            src_ref=outgoing.at[index],
            dst_ref=incoming_grad.at[index],
            send_sem=seg_send.at[index],
            recv_sem=seg_recv.at[index],
            device_id={"segment": 1 - segment},
            device_id_type=MESH,
        )

    def ends_copy(index):
        return pltpu.make_async_copy(
            ends_v.at[lax.rem(index, 2)], ends_hbm.at[index], ends_sem.at[index]
        )

    def free_ends(index):
        @pl.when(index >= 2)
        def _():
            ends_copy(index - 2).wait()

    def own_rows(index):
        half = lax.rem(index, 2)
        whole = jnp.where(index < 2, 1.0, 0.0).astype(F32)
        weight = whole * flag + (1.0 - whole) * (1.0 - flag)
        picked = rows_in[half].astype(F32) * weight + rows_in[2 + half].astype(F32) * (1.0 - weight)
        return picked.T

    def by_queries(values):
        half = LANES // 2
        blank = jnp.zeros((half, LANES), values.dtype)
        parts = []
        for part in range(2):
            span = slice(part * LANES, (part + 1) * LANES)
            first = jnp.concatenate([values[:half, span], blank], axis=0)
            second = jnp.concatenate([blank, values[half:, span]], axis=0)
            parts.append(jnp.concatenate([first, second], axis=1))
        return parts

    def against(rows_ref, index, pair, parts, has_off):
        own = rows_ref[index, pair]
        products = [dot_plain(own[:LANES], parts[0]), dot_plain(own, parts[1])]
        if has_off:
            before = rows_ref[0, pair]
            products += [dot_plain(before, parts[0]), dot_plain(before, parts[1])]
        return products

    def tiles_of(products, head, part, has_off):
        lanes = slice(head * LANES, (head + 1) * LANES)
        own = products[part]
        tiles = [own[part * LANES : (part + 1) * LANES, lanes]]
        if part:
            tiles.append(own[:LANES, lanes])
        if has_off:
            off = products[2 + part]
            tiles += [off[:LANES, lanes], off[LANES:, lanes]]
        return tiles

    def joined(lows, has_off):
        blank = jnp.zeros((LANES, LANES), BF16)
        first = jnp.concatenate([lows[0][0], blank], axis=0)
        second = jnp.concatenate([lows[1][1], lows[1][0]], axis=0)
        whole = jnp.concatenate([first, second], axis=1)
        if not has_off:
            return whole, None
        first = jnp.concatenate(lows[0][-2:], axis=0)
        second = jnp.concatenate(lows[1][-2:], axis=0)
        return whole, jnp.concatenate([first, second], axis=1)

    def attend(index, has_off):
        lanes = lanes_of(index)
        half = LANES // 2
        key_at = lax.broadcasted_iota(jnp.int32, (LANES, LANES), 0)
        query_at = lax.broadcasted_iota(jnp.int32, (LANES, LANES), 1)
        allowed = key_at <= query_at

        def scores_of(pair):
            return against(
                keys_rm, index, pair, by_queries(qkv[0, pair, :, lanes]), has_off
            )

        ahead = scores_of(0)
        for pair in range(pairs):
            scores = ahead
            if pair + 1 < pairs:
                ahead = scores_of(pair + 1)
            mixed = []
            for head in range(2):
                rows = slice(head * half, (head + 1) * half)
                lows = []
                for part in range(2):
                    tiles = tiles_of(scores, head, part, has_off)
                    tiles[0] = jnp.where(allowed, tiles[0], -1e30)
                    top = jnp.max(functools.reduce(jnp.maximum, tiles), axis=0, keepdims=True)
                    raised = [jnp.exp(tile - top) for tile in tiles]
                    total = functools.reduce(jnp.add, raised)
                    scale = 1.0 / jnp.sum(total, axis=0, keepdims=True)
                    lows.append([(tile * scale).astype(BF16) for tile in raised])
                low, low_off = joined(lows, has_off)
                share[index, pair, head] = low
                mix = dot_plain(qkv[2, pair, rows, lanes], low)
                if has_off:
                    share_off[pair, head] = low_off
                    mix = mix + dot_plain(qkv[2, pair, rows, :piece], low_off)
                mixed.append(mix.astype(BF16))
            mixture[pair, :, lanes] = jnp.concatenate(mixed, axis=0)
            yield 280

    def part_sum(values):
        return jnp.sum(values.reshape(values.shape[0] // 8, 8, values.shape[1]), axis=0)

    def full_mean(parts):
        return jnp.sum(parts, axis=0, keepdims=True) * (1.0 / width)

    def column(index, rows):
        part = columns[index, rows, :].astype(F32)
        return jnp.concatenate([part] * (piece // LANES), axis=1)

    def gather_sum(index, rows, values):
        sums[index, rows, :] = sums[index, rows, :] + fold(values)

    def norm_chunks(index, which, wide_a, total):
        mean = full_mean(total)
        spread = jnp.zeros((8, piece), F32)
        for rows in chunks:
            centred = wide_a[rows, :] - mean
            spread = spread + part_sum(centred * centred)
        inverse = lax.rsqrt(full_mean(spread) + EPS)
        inverses[index, which] = inverse
        return mean, inverse

    def forward_start(index):
        @pl.when(segment == 0)
        def _():
            x_t[:, lanes_of(index)] = own_rows(index).astype(BF16)

        @pl.when(segment == 1)
        def _():
            forward_copy(index).wait_recv()

    def forward_first(index):
        lanes = lanes_of(index)
        inputs = x_t[:, lanes]
        score_scale = 1.0 / math.sqrt(width // HEADS)
        for block in range(3):
            result = dot_plain(turned[block], inputs)
            for pair in range(pairs):
                low = result[pair * LANES : (pair + 1) * LANES]
                low = (low * score_scale if block == 0 else low).astype(BF16)
                qkv[block, pair, :, lanes] = low
                if block == 1:
                    keys_rm[index, pair] = low.T
                if block == 2:
                    values_rm[index, pair] = low.T
            yield 270

    def forward_rest(index, wide_a):
        lanes = lanes_of(index)
        branch = dot_plain(turned[3], mixture[:, :, lanes].reshape(width, piece))
        yield 250
        total = jnp.zeros((8, piece), F32)
        for rows in chunks:
            sum_one = x_t[rows, lanes].astype(F32) + (branch[rows] + column(BIAS_OUT, rows))
            wide_a[rows, :] = sum_one
            total = total + part_sum(sum_one)
            yield 25
        mean, inverse = norm_chunks(index, 0, wide_a, total)
        yield 150
        for rows in chunks:
            normed = (wide_a[rows, :] - mean) * inverse
            norm_one[rows, lanes] = normed
            hidden = normed * column(GAIN_ONE, rows) + column(BIAS_ONE, rows)
            hidden_low[rows, lanes] = hidden.astype(BF16)
            yield 30

        branch_two = None
        for block in range(4):
            pre_block = dot_plain(turned[4 + block], hidden_low[:, lanes])
            yield 50
            lows = []
            for rows in chunks:
                pre = pre_block[rows] + column(BIAS_UP + block, rows)
                level = (lax.erf(pre * (1.0 / math.sqrt(2.0))) + 1.0) * 0.5
                bell = jnp.exp2(pre * pre * (-0.5 * math.log2(math.e)))
                lows.append((pre * level).astype(BF16))
                active[block, rows, lanes] = lows[-1]
                slope[block, rows, lanes] = (
                    level + pre * bell * (1.0 / math.sqrt(2.0 * math.pi))
                ).astype(BF16)
                yield 65
            part = dot_plain(turned[8 + block], jnp.concatenate(lows, axis=0))
            branch_two = part if branch_two is None else branch_two + part
            yield 100
        total = jnp.zeros((8, piece), F32)
        for rows in chunks:
            hidden = norm_one[rows, lanes] * column(GAIN_ONE, rows) + column(BIAS_ONE, rows)
            sum_two = hidden + (branch_two[rows] + column(BIAS_DOWN, rows))
            wide_a[rows, :] = sum_two
            total = total + part_sum(sum_two)
            yield 25
        mean, inverse = norm_chunks(index, 1, wide_a, total)
        yield 150
        for rows in chunks:
            norm_two[rows, lanes] = (wide_a[rows, :] - mean) * inverse
            yield 20

    def forward_end(index):
        for rows in chunks:
            outgoing[index, rows, :] = output_rows(rows, lanes_of(index)).astype(BF16)
        forward_copy(index).start()

    def off_or_not(index, run):
        @pl.when(index == 1)
        def _():
            drain(run(index, True))

        @pl.when(index != 1)
        def _():
            drain(run(index, False))

    def forward(index):
        forward_start(index)
        drain(forward_first(index))
        off_or_not(index, attend)
        drain(forward_rest(index, wide_a))

        @pl.when(segment == 0)
        def _():
            forward_end(index)

    def output_rows(rows, lanes):
        return norm_two[rows, lanes] * column(GAIN_TWO, rows) + column(BIAS_TWO, rows)

    def last_outputs(index, carry):
        free_ends(index)
        for start in range(0, width, LANES):
            rows = slice(start, start + LANES)
            ends_v[lax.rem(index, 2), :, rows] = output_rows(rows, lanes_of(index)).T
        ends_copy(index).start()
        return carry

    def attend_back(index, has_off):
        lanes = lanes_of(index)
        slot = (1 if index == 0 else 0) if isinstance(index, int) else jnp.where(index == 0, 1, 0)
        half = LANES // 2
        score_scale = 1.0 / math.sqrt(width // HEADS)

        def backs_of(pair):
            return against(values_rm, index, pair, by_queries(grad_mix[pair]), has_off)

        ahead = backs_of(0)
        for pair in range(pairs):
            backs = ahead
            if pair + 1 < pairs:
                ahead = backs_of(pair + 1)
            results = ([], [], [])
            for head in range(2):
                rows = slice(head * half, (head + 1) * half)
                low = share[index, pair, head]
                low_off = share_off[pair, head] if has_off else None
                lows = []
                for part in range(2):
                    place = slice(part * LANES, (part + 1) * LANES)
                    wides = [low[place, place]]
                    if part:
                        wides.append(low[:LANES, place])
                    if has_off:
                        wides += [low_off[:LANES, place], low_off[LANES:, place]]
                    wides = [tile.astype(F32) for tile in wides]
                    tiles = tiles_of(backs, head, part, has_off)
                    products = [wide * tile for wide, tile in zip(wides, tiles)]
                    inner = jnp.sum(functools.reduce(jnp.add, products), axis=0, keepdims=True)
                    lows.append(
                        [
                            (product - wide * inner).astype(BF16)
                            for product, wide in zip(products, wides)
                        ]
                    )
                grad_scores, grad_off = joined(lows, has_off)
                queries = qkv[0, pair, rows, lanes]
                grads = grad_mix[pair, rows]
                grad_query = dot_plain(qkv[1, pair, rows, lanes], grad_scores)
                grad_key = dot_turned(queries, grad_scores) + key_sums[slot, 0, pair, rows]
                grad_value = dot_turned(grads, low) + key_sums[slot, 1, pair, rows]
                if has_off:
                    grad_query = grad_query + dot_plain(qkv[1, pair, rows, :piece], grad_off)
                    key_sums[1, 0, pair, rows] = dot_turned(queries, grad_off)
                    key_sums[1, 1, pair, rows] = dot_turned(grads, low_off)
                for kept, grad in zip(results, (grad_query * score_scale, grad_key, grad_value)):
                    kept.append(grad.astype(BF16))
            for block in range(3):
                qkv[block, pair, :, lanes] = jnp.concatenate(results[block], axis=0)
            yield 440

    def backward_start(index):
        @pl.when(segment == 0)
        def _():
            backward_copy(index).wait_recv()

    def backward_norm(index):
        lanes = lanes_of(index)
        plain = jnp.zeros((8, piece), F32)
        inner = jnp.zeros((8, piece), F32)
        for rows in chunks:
            grad = incoming_grad[index, rows, :].astype(F32)
            product = grad * norm_two[rows, lanes]
            gather_sum(GAIN_TWO, rows, product)
            gather_sum(BIAS_TWO, rows, grad)
            gain = column(GAIN_TWO, rows)
            plain = plain + part_sum(grad * gain)
            inner = inner + part_sum(product * gain)
            yield 40
        plain = full_mean(plain)
        inner = full_mean(inner)
        inverse = inverses[index, 1]
        for rows in chunks:
            scaled = incoming_grad[index, rows, :].astype(F32) * column(GAIN_TWO, rows)
            grad_two = (scaled - plain - norm_two[rows, lanes] * inner) * inverse
            gather_sum(BIAS_DOWN, rows, grad_two)
            wide_a[rows, :] = grad_two
            down_grad[rows, lanes] = grad_two.astype(BF16)
            yield 40

    def backward_feed(index):
        lanes = lanes_of(index)
        for block in range(4):
            back = dot_plain(w_down[block], down_grad[:, lanes])
            for rows in chunks:
                grad_pre = back[rows] * slope[block, rows, lanes].astype(F32)
                gather_sum(BIAS_UP + block, rows, grad_pre)
                slope[block, rows, lanes] = grad_pre.astype(BF16)
            yield 250

        through = dot_plain(w_up[...], slope[:, :, lanes].reshape(4 * width, piece))
        plain = jnp.zeros((8, piece), F32)
        inner = jnp.zeros((8, piece), F32)
        for rows in chunks:
            grad_hidden = wide_a[rows, :] + through[rows]
            wide_a[rows, :] = grad_hidden
            product = grad_hidden * norm_one[rows, lanes]
            gather_sum(GAIN_ONE, rows, product)
            gather_sum(BIAS_ONE, rows, grad_hidden)
            gain = column(GAIN_ONE, rows)
            plain = plain + part_sum(grad_hidden * gain)
            inner = inner + part_sum(product * gain)
            yield 120 if rows.start == 0 else 45
        plain = full_mean(plain)
        inner = full_mean(inner)
        inverse = inverses[index, 0]
        for rows in chunks:
            scaled = wide_a[rows, :] * column(GAIN_ONE, rows)
            grad_one = (scaled - plain - norm_one[rows, lanes] * inner) * inverse
            gather_sum(BIAS_OUT, rows, grad_one)
            wide_b[rows, :] = grad_one
            branch_grad[rows, lanes] = grad_one.astype(BF16)
            yield 40
        grad_mix[...] = (
            dot_plain(w_out[...], branch_grad[:, lanes]).astype(BF16).reshape(pairs, LANES, piece)
        )
        yield 300

    def backward_attention(index):
        off_or_not(index, attend_back)
        through = dot_plain(w_qkv[...], qkv[:, :, :, lanes_of(index)].reshape(3 * width, piece))

        @pl.when(segment == 1)
        def _():
            for rows in chunks:
                outgoing[index, rows, :] = (wide_b[rows, :] + through[rows]).astype(BF16)
            backward_copy(index).start()

        @pl.when(segment == 0)
        def _():
            free_ends(index)
            for start in range(0, width, LANES):
                rows = slice(start, start + LANES)
                ends_v[lax.rem(index, 2), :, rows] = (wide_b[rows, :] + through[rows]).T
            ends_copy(index).start()

    def backward_both(index, forward_index):
        forward_copy(forward_index).wait_recv()

        def back():
            yield from backward_norm(index)
            yield from backward_feed(index)
            yield from attend_back(index, False)
            through = dot_plain(w_qkv[...], qkv[:, :, :, lanes_of(index)].reshape(3 * width, piece))
            for rows in chunks:
                outgoing[index, rows, :] = (wide_b[rows, :] + through[rows]).astype(BF16)
                yield 90

        def ahead():
            yield from forward_first(forward_index)
            yield from attend(forward_index, False)
            yield from forward_rest(forward_index, wide_c)

        side_by_side(back(), ahead(), 300)
        backward_copy(index).start()

    split = SPLIT if share_rows % (16 * SPLIT) == 0 else 1
    dp_first = DP_FIRST if split == SPLIT else ()
    orders = (ORDER_ONE, ORDER_TWO, ORDER_THREE) if split == SPLIT else plain_orders()
    jobs = 3 * split
    cut_rows = share_rows // split
    job_rows = width // split

    def base_of(job):
        return (8, 4, 0)[job // split]

    def job_span(job):
        return pl.ds(job % split * job_rows, job_rows)

    def fin_rows(job):
        return pl.ds(job % split * cut_rows, cut_rows)

    def parts_of(job):
        return range(2) if job in dp_first else range(1)

    def core_copies(job):
        return [
            pltpu.make_async_remote_copy(
                src_ref=turned.at[base_of(job) + 2 * (1 - core) + each, job_span(job)],
                dst_ref=core_in.at[job // split, each, job_span(job)],
                send_sem=core_send.at[job, each],
                recv_sem=core_recv.at[job, each],
                device_id={"rep": other_core},
                device_id_type=MESH,
            )
            for each in range(2)
        ]

    def side_copies(job):
        base = base_of(job)
        copies = []
        for each in parts_of(job):
            if job in dp_first:
                source = turned.at[base + 2 * core + each, dp_rows(job, dp_steps - 1)[1]]
                target = side_in.at[
                    job // split, pl.ds(job % split * job_rows + each * cut_rows, cut_rows)
                ]
            else:
                source = turned.at[base + 2 * core + (1 - side), job_span(job)]
                target = side_in.at[job // split, job_span(job)]
            copies.append(
                pltpu.make_async_remote_copy(
                    src_ref=source,
                    dst_ref=target,
                    send_sem=side_send.at[job, each],
                    recv_sem=side_recv.at[job, each],
                    device_id={"rep": other_side},
                    device_id_type=MESH,
                )
            )
        return copies

    def dp_slot(job):
        return sum(len(parts_of(before)) for before in range(job))

    def dp_rows(job, step):
        count = dp_count // 2
        start = 0
        for bit in range(step):
            start = start + lax.rem(lax.div(dp, 2**bit), 2) * count
            count = count // 2
        mine = lax.rem(lax.div(dp, 2**step), 2)
        first = job % split * job_rows
        sent = pl.multiple_of(first + (start + (1 - mine) * count) * cut_rows, cut_rows)
        kept = pl.multiple_of(first + (start + mine * count) * cut_rows, cut_rows)
        return pl.ds(sent, count * cut_rows), pl.ds(kept, count * cut_rows)

    def dp_landing(step):
        count = dp_count // 2 ** (step + 1)
        return pl.ds((dp_count - 2 * count) * cut_rows, count * cut_rows)

    def dp_copies(job, step):
        mine = lax.rem(lax.div(dp, 2**step), 2)
        copies = []
        for each in parts_of(job):
            position = base_of(job) + 2 * core + (each if job in dp_first else side)
            copies.append(
                pltpu.make_async_remote_copy(
                    src_ref=turned.at[position, dp_rows(job, step)[0]],
                    dst_ref=dp_in.at[dp_slot(job) + each, dp_landing(step)],
                    send_sem=dp_send.at[job, step, each],
                    recv_sem=dp_recv.at[job, step, each],
                    device_id={"dp": dp + (1 - 2 * mine) * 2**step},
                    device_id_type=MESH,
                )
            )
        return copies

    def join_copy(job):
        part = fin.at[job // split, 2 * core + side, fin_rows(job)]
        return pltpu.make_async_remote_copy(
            src_ref=part,
            dst_ref=part,
            send_sem=join_send.at[job],
            recv_sem=join_recv.at[job],
            device_id={"rep": other_side},
            device_id_type=MESH,
        )

    def last_copies(job):
        copies = []
        for each in range(2):
            part = fin.at[job // split, 2 * core + each, fin_rows(job)]
            copies.append(
                pltpu.make_async_remote_copy(
                    src_ref=part,
                    dst_ref=part,
                    send_sem=last_send.at[job, each],
                    recv_sem=last_recv.at[job, each],
                    device_id={"rep": other_core},
                    device_id_type=MESH,
                )
            )
        return copies

    def fin_copy(job):
        return pltpu.make_async_copy(
            fin.at[job // split, :, fin_rows(job)],
            fin_hbm.at[job // split, :, fin_rows(job)],
            fin_sem.at[job],
        )

    def arrived(*copies):
        for copy in copies:
            copy.wait_send()
        for copy in copies:
            copy.wait_recv()

    def start_all(copies):
        for copy in copies:
            copy.start()

    def turned_bits(value, count):
        place = 0
        while count > 1:
            place = place * 2 + value % 2
            value = value // 2
            count = count // 2
        return place

    pack = min(2, split)

    def left_rows(source, part):
        count = pack * cut_rows
        start = part * pack * cut_rows
        return jnp.concatenate(
            [source(index * share_rows + start, count) for index in range(dp_count)], axis=0
        )

    def keep_rows(block, part, result):
        for index in range(dp_count):
            for each in range(pack):
                target = (part * pack + each) * job_rows + turned_bits(index, dp_count) * cut_rows
                start = (index * pack + each) * cut_rows
                turned[block, target : target + cut_rows, :] = result[start : start + cut_rows]

    def down_block(part, block, tokens, add):
        count = width // (4 * share_rows)
        pieces = []
        for each in range(4 * count):
            start = pl.multiple_of(each * share_rows + part * (pack * cut_rows), pack * cut_rows)
            pieces.append(active[block, pl.ds(start, pack * cut_rows), tokens])
        result = dot_turned(jnp.concatenate(pieces, axis=0), down_grad[:, tokens])
        high = lax.rem(block, 2) * 2 + lax.div(block, 2)
        for each in range(count):
            place = turned_bits(each, count) * 4 + high
            for position in range(4):
                for job in range(pack):
                    target = (part * pack + job) * job_rows + place * cut_rows
                    rows = pl.ds(pl.multiple_of(target, cut_rows), cut_rows)
                    start = ((each * 4 + position) * pack + job) * cut_rows
                    total = result[start : start + cut_rows]
                    if add:
                        total = total + turned[8 + position, rows, :].astype(F32)
                    turned[8 + position, rows, :] = total.astype(BF16)

    half_tokens = PIECES // 2 * piece

    def early_down_sums():
        def one(step, carry):
            down_block(lax.div(step, 4), lax.rem(step, 4), slice(0, half_tokens), False)
            return carry

        lax.fori_loop(0, 4 * (split // pack), one, 0)

    def down_sums(part):
        def one(block, carry):
            down_block(part, block, slice(half_tokens, 2 * half_tokens), True)
            return carry

        lax.fori_loop(0, 4, one, 0)

    def up_sums(part):
        def one(block, carry):
            left = left_rows(lambda start, count: hidden_low[start : start + count, :], part)
            keep_rows(4 + block, part, dot_turned(left, slope[block]).astype(BF16))
            return carry

        lax.fori_loop(0, 4, one, 0)

    def qkv_sums(part):
        def one(block, carry):
            left = left_rows(lambda start, count: x_t[start : start + count, :], part)
            grads = qkv[block].reshape(width, PIECES * piece)
            keep_rows(block, part, dot_turned(left, grads).astype(BF16))
            return carry

        lax.fori_loop(0, 3, one, 0)
        left = left_rows(
            lambda start, count: mixture[start // LANES, start % LANES : start % LANES + count, :], part
        )
        keep_rows(3, part, dot_turned(left, branch_grad[...]).astype(BF16))

    def sums_of(job):
        (down_sums, up_sums, qkv_sums)[job // split](job % split // pack)
        for each in range(pack):
            start_all(core_copies(job + each))

    def after_core(job):
        arrived(*core_copies(job))
        rows = job_span(job)
        for each in parts_of(job):
            place = 1 - side if each == 0 else side
            position = base_of(job) + 2 * core + place
            turned[position, rows, :] = (
                turned[position, rows, :].astype(F32)
                + core_in[job // split, place, rows, :].astype(F32)
            ).astype(BF16)
        if job in dp_first:
            start_all(dp_copies(job, 0))

    def start_side(job):
        start_all(side_copies(job))

    def after_side(job):
        arrived(*side_copies(job))
        rows = job_span(job)
        position = base_of(job) + 2 * core + side
        turned[position, rows, :] = (
            turned[position, rows, :].astype(F32)
            + core_in[job // split, side, rows, :].astype(F32)
            + side_in[job // split, rows, :].astype(F32)
        ).astype(BF16)
        start_all(dp_copies(job, 0))

    def dp_total(job, step, each):
        position = base_of(job) + 2 * core + (each if job in dp_first else side)
        kept = turned[position, dp_rows(job, step)[1], :].astype(F32)
        return position, kept + dp_in[dp_slot(job) + each, dp_landing(step), :].astype(F32)

    def after_dp(job):
        for step in range(dp_steps - 1):
            arrived(*dp_copies(job, step))
            for each in parts_of(job):
                position, total = dp_total(job, step, each)
                turned[position, dp_rows(job, step)[1], :] = total.astype(BF16)
            start_all(dp_copies(job, step + 1))

    def after_last_dp(job):
        step = dp_steps - 1
        arrived(*dp_copies(job, step))
        for each in parts_of(job):
            position, total = dp_total(job, step, each)
            if job in dp_first:
                turned[position, dp_rows(job, step)[1], :] = total.astype(BF16)
            else:
                fin[job // split, 2 * core + side, fin_rows(job), :] = total.astype(BF16)
        if job in dp_first:
            start_side(job)
        else:
            join_copy(job).start()

    def after_join(job):
        if job in dp_first:
            arrived(*side_copies(job))
            for each in range(2):
                rows = pl.ds(job % split * job_rows + each * cut_rows, cut_rows)
                own = turned[base_of(job) + 2 * core + each, dp_rows(job, dp_steps - 1)[1], :]
                total = own.astype(F32) + side_in[job // split, rows, :].astype(F32)
                fin[job // split, 2 * core + each, fin_rows(job), :] = total.astype(BF16)
        else:
            arrived(join_copy(job))
        start_all(last_copies(job))

    def after_last(job):
        arrived(*last_copies(job))
        fin_copy(job).start()

    def small_dp_copy(step):
        target = lax.rem(dp + step, dp_count)
        return pltpu.make_async_remote_copy(
            src_ref=small.at[target],
            dst_ref=small_dp.at[step - 1],
            send_sem=sdp_send.at[step - 1],
            recv_sem=sdp_recv.at[step - 1],
            device_id={"dp": target},
            device_id_type=MESH,
        )

    def small_rep_copy(step):
        return pltpu.make_async_remote_copy(
            src_ref=small_rep.at[rep],
            dst_ref=small_rep.at[rep],
            send_sem=srep_send.at[step - 1],
            recv_sem=srep_recv.at[step - 1],
            device_id={"rep": lax.rem(rep + step, 4)},
            device_id_type=MESH,
        )

    small_copy = pltpu.make_async_copy(small_out, small_hbm, load_sem.at[0])

    def small_step(stage):
        if stage == 0:
            rows_of = [jnp.sum(sums[index].T, axis=0, keepdims=True) for index in range(STATS)]
            small[...] = jnp.zeros(small.shape, F32)
            for share_index in range(dp_count):
                for index in range(BIAS_UP):
                    start = share_index * share_rows
                    small[share_index, index : index + 1, :share_rows] = rows_of[index][
                        :, start : start + share_rows
                    ]
                for part in range(4):
                    start = (share_index * 4 + part) * share_rows
                    block, start = start // width, start % width
                    small[share_index, BIAS_UP + part : BIAS_UP + part + 1, :share_rows] = rows_of[
                        BIAS_UP + block
                    ][:, start : start + share_rows]
            for step in range(1, dp_count):
                small_dp_copy(step).start()
        elif stage == 1:
            total = small[dp]
            for step in range(1, dp_count):
                arrived(small_dp_copy(step))
                total = total + small_dp[step - 1]
            small_rep[rep] = total
            for step in range(1, 4):
                small_rep_copy(step).start()
        else:
            for step in range(1, 4):
                arrived(small_rep_copy(step))
            small_out[...] = (small_rep[0] + small_rep[1]) + (small_rep[2] + small_rep[3])
            small_copy.start()

    def run(order):
        steps = (
            sums_of,
            after_core,
            start_side,
            after_side,
            after_dp,
            after_last_dp,
            after_join,
            after_last,
            small_step,
        )
        for stage, job in order:
            steps[stage](job)

    def one_step(step, carry):
        first_index = jnp.where(step < 4, step, jnp.where(step < 6, 5 - step, step - 4))
        last_index = jnp.where(step < 2, step, jnp.where(step == 2, 1, 3))
        index = jnp.minimum(jnp.where(segment == 0, first_index, last_index), PIECES - 1)
        is_last = jnp.where(step == 2 * PIECES, 1, 0)
        begun = jnp.where(step + segment == 0, 0, 1)
        is_forward = jnp.where(step < jnp.where(segment == 0, 4, 2), begun, 0)
        last_backward = jnp.where(step == 2, 1, 0) + jnp.where(step == 5, 1, 0)
        is_backward = jnp.where(segment == 0, begun * (1 - is_forward) * (1 - is_last), last_backward)
        is_split = jnp.where(step >= 2 * PIECES - 1, 1 - segment, 0)
        is_rest = is_backward * (1 - is_split) + is_last * is_split

        @pl.when(is_forward == 1)
        def _():
            forward(index)

        @pl.when(is_backward == 1)
        def _():
            backward_start(index)
            drain(backward_norm(index))

        @pl.when(segment * step == 3)
        def _():
            backward_both(0, 2)

        @pl.when(segment * step == 4)
        def _():
            backward_both(2, 3)

        @pl.when(is_last == 1)
        def _():
            run(orders[0])

        @pl.when(is_rest == 1)
        def _():
            drain(backward_feed(index))

        @pl.when(is_last == 1)
        def _():
            run(orders[1])

        @pl.when(is_rest == 1)
        def _():
            backward_attention(index)

        @pl.when(step - segment == 5)
        def _():
            early_down_sums()

        return carry

    @pl.when(segment == 1)
    def _():
        for part in range(4):
            turn(part)

        def one_cotangent(index, carry):
            incoming_grad[index] = own_rows(index).astype(BF16)
            return carry

        lax.fori_loop(0, PIECES, one_cotangent, 0)

    @pl.when(segment == 0)
    def _():
        def ahead():
            x_t[:, lanes_of(0)] = own_rows(0).astype(BF16)
            yield from forward_first(0)
            yield from attend(0, False)
            yield from forward_rest(0, wide_a)

        drain(turn_apart(0, 1))
        side_by_side(ahead(), turn_apart(1, 12), -400)

    pl.semaphore_wait(barrier, 4 + dp_count - 1)

    @pl.when(segment == 0)
    def _():
        forward_end(0)

    lax.fori_loop(0, 2 * PIECES + 1, one_step, 0)

    cut = orders[2].index((SMALL, 0))
    run(orders[2][:cut])

    @pl.when(segment == 1)
    def _():
        lax.fori_loop(0, PIECES, last_outputs, 0)

    run(orders[2][cut:])

    for index in range(PIECES):

        @pl.when(segment == 0)
        def _():
            forward_copy(index).wait_send()

        @pl.when(segment == 1)
        def _():
            backward_copy(index).wait_send()

    for index in range(2, PIECES):
        ends_copy(index).wait()
    for job in range(jobs):
        fin_copy(job).wait()
    small_copy.wait()


def finish_kernel(
    flag_ref,
    ends_in,
    fin,
    small,
    ends,
    grad_qkv,
    grad_out,
    grad_up,
    grad_down,
    grad_up_bias,
    grad_gains,
    grad_biases,
    ends_v,
    fin_v,
    wide_qkv,
    wide_out,
    wide_up,
    wide_down,
    small_v,
    up_bias_v,
    gains_v,
    biases_v,
    ends_sem,
    in_sem,
    out_sem,
):
    half = ends_in.shape[0] // 2
    share_rows, width = fin.shape[2:]
    start = pl.multiple_of(half * (1 - flag_ref[0, 0]), half)
    cut = half // 4
    ends_copies = []
    ends_loads = []
    for part in range(8):
        source = pl.ds(part * cut, cut)
        offset = start + part * cut if part < 4 else part * cut - half + (half - start)
        target = pl.ds(pl.multiple_of(offset, cut), cut)
        ends_loads.append(
            pltpu.make_async_copy(ends_in.at[source], ends_v.at[source], ends_sem.at[part])
        )
        ends_copies.append(
            pltpu.make_async_copy(ends_v.at[source], ends.at[0, target], ends_sem.at[8 + part])
        )
    loads = [
        pltpu.make_async_copy(fin.at[group], fin_v.at[group], in_sem.at[group])
        for group in range(3)
    ]
    stores = [
        pltpu.make_async_copy(wide, target.at[0], out_sem.at[index])
        for index, (wide, target) in enumerate(
            ((wide_down, grad_down), (wide_up, grad_up), (wide_qkv, grad_qkv), (wide_out, grad_out))
        )
    ]
    small_load = pltpu.make_async_copy(small, small_v, in_sem.at[3])
    small_stores = [
        pltpu.make_async_copy(narrow, target, out_sem.at[4 + index])
        for index, (narrow, target) in enumerate(
            ((up_bias_v, grad_up_bias), (gains_v, grad_gains), (biases_v, grad_biases))
        )
    ]
    small_load.start()
    for group in range(3):
        loads[group].start()
        for copy in ends_loads[group * 3 : group * 3 + 3]:
            copy.start()

    def ends_on(first, after):
        for load, copy in zip(ends_loads[first:after], ends_copies[first:after]):
            load.wait()
            copy.start()

    loads[0].wait()
    for position in range(4):
        rows = slice(position * share_rows, (position + 1) * share_rows)
        wide_down[rows, :] = fin_v[0, position].astype(F32)
    stores[0].start()
    ends_on(0, 3)
    loads[1].wait()
    for position in range(4):
        wide_up[:, position * width : (position + 1) * width] = fin_v[1, position].astype(F32)
    stores[1].start()
    ends_on(3, 6)
    loads[2].wait()
    for position in range(3):
        wide_qkv[:, position * width : (position + 1) * width] = fin_v[2, position].astype(F32)
    stores[2].start()
    wide_out[...] = fin_v[2, 3].astype(F32)
    stores[3].start()
    ends_on(6, 8)
    small_load.wait()
    for position in range(4):
        rows = slice(position * share_rows, (position + 1) * share_rows)
        up_bias_v[:, rows] = small_v[BIAS_UP + position : BIAS_UP + position + 1, :share_rows]
    gains_v[0] = small_v[:2, :share_rows]
    biases_v[0] = small_v[2:BIAS_UP, :share_rows]
    for copy in small_stores:
        copy.start()
    for copy in stores + ends_copies + small_stores:
        copy.wait()


def on_device(
    dp_count,
    block_input,
    cotangent,
    window_group,
    w_qkv,
    w_out,
    w_up,
    w_down,
    up_bias,
    norm_gains,
    biases,
):
    rows, width = block_input.shape
    piece = rows // PIECES
    pairs = width // LANES
    share_rows = width // dp_count
    small_width = max(share_rows, LANES)
    dp_steps = dp_count.bit_length() - 1
    split = SPLIT if share_rows % (16 * SPLIT) == 0 else 1
    jobs = 3 * split
    slots = jobs + (len(DP_FIRST) if split == SPLIT else 0)
    any_spec = pl.BlockSpec(memory_space=pl.ANY)
    vmem_spec = pl.BlockSpec(memory_space=pltpu.VMEM)
    smem_spec = pl.BlockSpec(memory_space=pltpu.SMEM)
    dma = pltpu.SemaphoreType.DMA
    vmem = pltpu.VMEM
    ends_in, fin, small = pl.pallas_call(
        functools.partial(layer_kernel, dp_count),
        out_shape=(
            jax.ShapeDtypeStruct((PIECES, piece, width), F32),
            jax.ShapeDtypeStruct((3, 4, share_rows, width), BF16),
            jax.ShapeDtypeStruct((16, small_width), F32),
        ),
        in_specs=[smem_spec] + [any_spec] * 6 + [vmem_spec] * 3,
        out_specs=(any_spec,) * 3,
        scratch_shapes=[
            vmem((width, 3 * width), BF16),
            vmem((width, width), BF16),
            vmem((width, 4 * width), BF16),
            vmem((4, width, width), BF16),
            vmem((12, width, width), BF16),
            vmem((PIECES, piece, width), BF16),
            vmem((width, rows), BF16),
            vmem((3, pairs, LANES, rows), BF16),
            vmem((PIECES, pairs, piece, LANES), BF16),
            vmem((PIECES, pairs, piece, LANES), BF16),
            vmem((PIECES, pairs, 2, piece, piece), BF16),
            vmem((pairs, 2, piece, piece), BF16),
            vmem((pairs, LANES, rows), BF16),
            vmem((width, rows), F32),
            vmem((width, rows), F32),
            vmem((PIECES, 2, 1, piece), F32),
            vmem((width, rows), BF16),
            vmem((4, width, rows), BF16),
            vmem((4, width, rows), BF16),
            vmem((width, rows), BF16),
            vmem((width, rows), BF16),
            vmem((pairs, LANES, piece), BF16),
            vmem((PIECES, width, piece), BF16),
            vmem((PIECES, width, piece), BF16),
            vmem((STATS, width, LANES), BF16),
            vmem((STATS, width, LANES), F32),
            vmem((2, 2, pairs, LANES, piece), F32),
            vmem((width, piece), F32),
            vmem((width, piece), F32),
            vmem((width, piece), F32),
            vmem((2, piece, width), F32),
            vmem((3, 2, width, width), BF16),
            vmem((3, width, width), BF16),
            vmem((slots, (width - share_rows) // split, width), BF16),
            vmem((3, 4, share_rows, width), BF16),
            vmem((dp_count, 16, small_width), F32),
            vmem((dp_count - 1, 16, small_width), F32),
            vmem((4, 16, small_width), F32),
            vmem((16, small_width), F32),
            dma((13,)),
            dma((PIECES,)),
            dma((PIECES,)),
            dma((PIECES,)),
            dma((jobs, 2)),
            dma((jobs, 2)),
            dma((jobs, 2)),
            dma((jobs, 2)),
            dma((jobs, dp_steps, 2)),
            dma((jobs, dp_steps, 2)),
            dma((jobs,)),
            dma((jobs,)),
            dma((jobs, 2)),
            dma((jobs, 2)),
            dma((dp_count - 1,)),
            dma((dp_count - 1,)),
            dma((3,)),
            dma((3,)),
            dma((jobs,)),
        ],
        compiler_params=pltpu.CompilerParams(
            collective_id=0, has_side_effects=True, vmem_limit_bytes=63 * 1024 * 1024
        ),
    )(
        window_group,
        block_input.reshape(PIECES, piece, width),
        cotangent.reshape(PIECES, piece, width),
        w_qkv,
        w_out,
        w_up,
        w_down,
        up_bias,
        norm_gains,
        biases,
    )
    return pl.pallas_call(
        finish_kernel,
        out_shape=(
            jax.ShapeDtypeStruct((1, rows, width), F32),
            jax.ShapeDtypeStruct((1, share_rows, 3 * width), F32),
            jax.ShapeDtypeStruct((1, share_rows, width), F32),
            jax.ShapeDtypeStruct((1, share_rows, 4 * width), F32),
            jax.ShapeDtypeStruct((1, 4 * share_rows, width), F32),
            jax.ShapeDtypeStruct((1, 4 * share_rows), F32),
            jax.ShapeDtypeStruct((1, 2, share_rows), F32),
            jax.ShapeDtypeStruct((1, 4, share_rows), F32),
        ),
        in_specs=[smem_spec] + [any_spec] * 3,
        out_specs=(any_spec,) * 8,
        scratch_shapes=[
            vmem((rows, width), F32),
            vmem((3, 4, share_rows, width), BF16),
            vmem((share_rows, 3 * width), F32),
            vmem((share_rows, width), F32),
            vmem((share_rows, 4 * width), F32),
            vmem((4 * share_rows, width), F32),
            vmem((16, small_width), F32),
            vmem((1, 4 * share_rows), F32),
            vmem((1, 2, share_rows), F32),
            vmem((1, 4, share_rows), F32),
            dma((16,)),
            dma((4,)),
            dma((7,)),
        ],
        compiler_params=pltpu.CompilerParams(vmem_limit_bytes=63 * 1024 * 1024),
    )(window_group, ends_in.reshape(rows, width), fin, small)


def solution(mesh):
    return jax.shard_map(
        functools.partial(on_device, mesh.shape["dp"]),
        mesh=mesh,
        in_specs=(
            P(("dp", "rep"), None),
            P(("dp", "rep"), None),
            P(("dp", "rep"), None),
            P("segment", None, None),
            P("segment", None, None),
            P("segment", None, None),
            P("segment", None, None),
            P("segment", None),
            P("segment", None, None),
            P("segment", None, None),
        ),
        out_specs=(
            P("segment", ("dp", "rep"), None),
            P("segment", "dp", None),
            P("segment", "dp", None),
            P("segment", "dp", None),
            P("segment", "dp", None),
            P("segment", "dp"),
            P("segment", None, "dp"),
            P("segment", None, "dp"),
        ),
        check_vma=False,
    )
```
